32 devices in a mesh: crop: 2 (over y), dap: 8 (over z, x), sub: 2 (over core).
Axes of the slice: x: 2, y: 2, z: 4, core: 2. Of those that a mesh axis runs over, the one named last changes fastest.
Arguments:
- pairwise_state: bfloat16 [64, 32, 128], P(('crop', 'dap', 'sub')), parts along dimension 0, may hold values from -27 to 27, as said below
- alignment_state: bfloat16 [64, 32, 256], P('crop', ('dap', 'sub')), parts along dimension 0, may hold values from -27 to 27, as said below
- alignment_mask: int32 [64, 32], P('crop', ('dap', 'sub')), parts along dimension 0, may hold values 0 or 1
- residue_crop_mask: int32 [64], P('crop'), parts along dimension 0, may hold values from 0 to 1, as said below
- outer_input_weight: bfloat16 [2, 256, 32], replicated, may hold values from -0.375 to 0.375
- outer_output_weight: bfloat16 [32, 32, 128], replicated, may hold values from -0.1875 to 0.1875
- triangle_input_weight: bfloat16 [4, 128, 128], replicated, may hold values from -0.5 to 0.5
- triangle_gate: bfloat16 [128, 128], replicated, may hold values from -0.5 to 0.5
- triangle_output_weight: bfloat16 [128, 128], replicated, may hold values from -0.5 to 0.5
- transition_up_weight: bfloat16 [128, 512], replicated, may hold values from -0.5 to 0.5
- transition_down_weight: bfloat16 [512, 128], replicated, may hold values from -0.25 to 0.25
Outputs:
- pair_out: bfloat16 [64, 32, 128], P(('crop', 'dap', 'sub')), parts along dimension 0
The draws below stay inside these ranges and needn't reach their ends.
There are 2 independent parts, one for each index of `crop`. The reference program is written for one: setup_inputs(seed, part) draws one part's arguments, and reference() takes and returns one part's arrays. A program takes and returns all parts, laid end to end along the dimension named above; an argument that names none is the same for every part. Nothing has to cross between parts.
Inputs may be any that keep to these rules, and one draw needn't show every extreme that they name: `residue_crop_mask`: 0 on every residue after the crop's end, which lies at 16 or later and before 32; inside the crop a residue may also be 0. `pairwise_state`: finite real values. `alignment_state`: finite real values.
All inputs are finite; a program needn't handle non-finite values. No bound on the sum of `alignment_mask` on one device may be relied on, other than what follows from the above.
Results may differ from the reference program's by a relative error of at most 0.0075.
Values may be sent and summed in bfloat16 or wider, within the bound.
No kernel may reach another device: no remote copies, remote signals or barrier semaphores. Data moves between devices by JAX's collectives and lax.ppermute only.
A program may use at most 64 MiB of HBM per device.

```python
import math
import jax
import jax.numpy as jnp
from jax import lax

C_M = 256
C_Z = 128
C_OPM = 32
C_TRI = 128
C_TRANS = 512
SEQUENCE_COUNT = 32
RESIDUE_COUNT = 32


def scaled_field(key_cell, key_chan, values, shape_cells, channels):
    cell_scale = jnp.exp(jax.random.uniform(key_cell, shape_cells + (1,), jnp.float32, math.log(0.3), math.log(3.0)))
    chan_scale = jnp.exp(jax.random.uniform(key_chan, (channels,), jnp.float32, math.log(0.3), math.log(3.0)))
    return values * cell_scale * chan_scale


def draw_pairwise_state(key, part):
    key = jax.random.fold_in(key, 5)
    key_base, key_cell, key_chan = jax.random.split(key, 3)
    values = jax.random.truncated_normal(key_base, -3.0, 3.0, (RESIDUE_COUNT, RESIDUE_COUNT, C_Z), jnp.float32)
    return scaled_field(key_cell, key_chan, values, (RESIDUE_COUNT, RESIDUE_COUNT), C_Z).astype(jnp.bfloat16)


def draw_alignment_state(key, part):
    key = jax.random.fold_in(key, 7)
    key_base, key_cell, key_chan = jax.random.split(key, 3)
    values = jax.random.truncated_normal(key_base, -3.0, 3.0, (SEQUENCE_COUNT, RESIDUE_COUNT, C_M), jnp.float32)
    return scaled_field(key_cell, key_chan, values, (SEQUENCE_COUNT, RESIDUE_COUNT), C_M).astype(jnp.bfloat16)


def draw_residue_crop_mask(key, part):
    key = jax.random.fold_in(key, 9)
    key_len, key_gap = jax.random.split(key, 2)
    length = jax.random.randint(key_len, (), RESIDUE_COUNT // 2, RESIDUE_COUNT)
    inside = (jnp.arange(RESIDUE_COUNT, dtype=jnp.int32) < length).astype(jnp.int32)
    present = (jax.random.randint(key_gap, (RESIDUE_COUNT,), 0, 8) != 0).astype(jnp.int32)
    return inside * present


def place_ends(values, key, least, top_value):
    longest = values.shape.index(max(values.shape))
    spots = []
    for shift in (0, 1):
        where = [jax.random.randint(jax.random.fold_in(key, axis), (), 0, length) for axis, length in enumerate(values.shape)]
        where[longest] = (where[longest] + shift) % values.shape[longest]
        spots.append(tuple(where))
    return values.at[spots[0]].set(least).at[spots[1]].set(top_value)


def gaussian(own_key, extent, deviation, reach, kind=jnp.bfloat16):
    return jnp.clip(deviation * jax.random.normal(own_key, extent, jnp.float32), -reach, reach).astype(kind)


def setup_inputs(seed: int = 0, part: int = 0) -> dict:
    key_of = jax.random.split(jax.random.key(seed), 12)
    part_keys = jax.random.split(jax.random.fold_in(key_of[11], part), 12)
    pairwise_state = draw_pairwise_state(jax.random.fold_in(jax.random.fold_in(key_of[11], part), 71), part)
    alignment_state = draw_alignment_state(jax.random.fold_in(jax.random.fold_in(key_of[11], part), 71), part)
    alignment_mask = place_ends((jax.random.randint(part_keys[2], (SEQUENCE_COUNT, RESIDUE_COUNT), 0, 4) < 3).astype(jnp.int32), jax.random.fold_in(part_keys[2], 1), 0, 1)
    residue_crop_mask = draw_residue_crop_mask(jax.random.fold_in(jax.random.fold_in(key_of[11], part), 71), part)
    outer_input_weight = gaussian(key_of[4], (2, C_M, C_OPM), C_M ** -0.5, 0.375)
    outer_output_weight = gaussian(key_of[5], (C_OPM, C_OPM, C_Z), (C_OPM * C_OPM) ** -0.5, 0.1875)
    triangle_input_weight = gaussian(key_of[6], (4, C_Z, C_TRI), C_Z ** -0.5, 0.5)
    triangle_gate = gaussian(key_of[7], (C_Z, C_Z), C_Z ** -0.5, 0.5)
    triangle_output_weight = gaussian(key_of[8], (C_TRI, C_Z), C_TRI ** -0.5, 0.5)
    transition_up_weight = gaussian(key_of[9], (C_Z, C_TRANS), C_Z ** -0.5, 0.5)
    transition_down_weight = gaussian(key_of[10], (C_TRANS, C_Z), C_TRANS ** -0.5, 0.25)
    return {"pairwise_state": pairwise_state, "alignment_state": alignment_state, "alignment_mask": alignment_mask, "residue_crop_mask": residue_crop_mask, "outer_input_weight": outer_input_weight, "outer_output_weight": outer_output_weight, "triangle_input_weight": triangle_input_weight, "triangle_gate": triangle_gate, "triangle_output_weight": triangle_output_weight, "transition_up_weight": transition_up_weight, "transition_down_weight": transition_down_weight}


def norm_layer(values, reduce_axis):
    average = lax.optimization_barrier(jnp.mean(values, axis=reduce_axis, keepdims=True))
    centered = values - average
    variance = lax.optimization_barrier(jnp.mean(centered * centered, axis=reduce_axis, keepdims=True))
    return centered * lax.rsqrt(variance + 1e-05)

def reference(pairwise_state, alignment_state, alignment_mask, residue_crop_mask, outer_input_weight, outer_output_weight, triangle_input_weight, triangle_gate, triangle_output_weight, transition_up_weight, transition_down_weight):
    residue_keep = residue_crop_mask.astype(jnp.float32)
    alignment_keep = alignment_mask.astype(jnp.float32) * residue_keep[None, :]
    pair_keep = residue_keep[:, None] * residue_keep[None, :]
    alignment_normed = norm_layer(alignment_state.astype(jnp.float32), -1).astype(jnp.bfloat16)
    left_alignment = (jnp.einsum('pxm,my->pxy', alignment_normed.astype(jnp.float32), outer_input_weight[0].astype(jnp.float32)) * alignment_keep[:, :, None]).astype(jnp.bfloat16)
    right_alignment = (jnp.einsum('pxm,my->pxy', alignment_normed.astype(jnp.float32), outer_input_weight[1].astype(jnp.float32)) * alignment_keep[:, :, None]).astype(jnp.bfloat16)
    inner_alignment = jnp.einsum('tqu,ulx->tqlx', left_alignment.astype(jnp.float32), outer_output_weight.astype(jnp.float32)).astype(jnp.bfloat16)
    numerator_sum = jnp.einsum('zkwv,znw->knv', inner_alignment.astype(jnp.float32), right_alignment.astype(jnp.float32))
    pair_norm_count = jnp.einsum('cf,cg->fg', alignment_keep, alignment_keep)
    opm = numerator_sum / jnp.maximum(pair_norm_count, 1.0)[:, :, None]
    pair_one = (pairwise_state.astype(jnp.float32) + opm).astype(jnp.bfloat16)
    ln_one = norm_layer(pair_one.astype(jnp.float32), -1).astype(jnp.bfloat16)
    ln_wide = ln_one.astype(jnp.float32)

    def operand(gate_w, proj_w):
        gate_val = jnp.einsum('ijc,cd->dij', ln_wide, gate_w.astype(jnp.float32))
        proj_val = jnp.einsum('ijc,cd->dij', ln_wide, proj_w.astype(jnp.float32))
        return (jax.nn.sigmoid(gate_val) * proj_val * pair_keep[None]).astype(jnp.bfloat16)
    left_tri = operand(triangle_input_weight[0], triangle_input_weight[1])
    right_tri = operand(triangle_input_weight[2], triangle_input_weight[3])

    def channel_product(operands):
        left_one, right_one = operands
        return jnp.dot(left_one.astype(jnp.float32), right_one.astype(jnp.float32).T, preferred_element_type=jnp.float32).astype(jnp.bfloat16)
    product = lax.map(channel_product, (left_tri, right_tri))
    normed = norm_layer(product.astype(jnp.float32), 0).astype(jnp.bfloat16)
    update = jnp.einsum('cij,cd->ijd', normed.astype(jnp.float32), triangle_output_weight.astype(jnp.float32))
    gate_out = jax.nn.sigmoid(jnp.einsum('ijc,cd->ijd', ln_wide, triangle_gate.astype(jnp.float32)))
    pair_two = (pair_one.astype(jnp.float32) + gate_out * update).astype(jnp.bfloat16)
    ln_two = norm_layer(pair_two.astype(jnp.float32), -1).astype(jnp.bfloat16)

    def transition(row_pair):
        row_ln, row_base = row_pair
        hidden = jax.nn.relu(jnp.dot(row_ln, transition_up_weight, preferred_element_type=jnp.float32)).astype(jnp.bfloat16)
        return (row_base.astype(jnp.float32) + jnp.dot(hidden, transition_down_weight, preferred_element_type=jnp.float32)).astype(jnp.bfloat16)
    return lax.map(transition, (ln_two, pair_two))
```

```python
import jax
import jax.numpy as jnp
from jax import lax
from jax.sharding import PartitionSpec as P

REPLICATED_PAIR_BYTES = 1 << 20


def norm_layer(values, reduce_axis):
    average = jnp.mean(values, axis=reduce_axis, keepdims=True)
    centered = values - average
    variance = jnp.mean(centered * centered, axis=reduce_axis, keepdims=True)
    return centered * lax.rsqrt(variance + 1e-05)


def transition(ln_two, pair_two, transition_up_weight, transition_down_weight):
    hidden = jax.nn.relu(
        jnp.dot(ln_two, transition_up_weight, preferred_element_type=jnp.float32)
    ).astype(jnp.bfloat16)
    return (
        pair_two.astype(jnp.float32)
        + jnp.dot(hidden, transition_down_weight, preferred_element_type=jnp.float32)
    ).astype(jnp.bfloat16)


def gather_rows(block, dap_count):
    me = lax.axis_index("dap")
    got = [block]
    for offset in range(1, dap_count):
        got.append(
            lax.ppermute(block, "dap", [(src, src ^ offset) for src in range(dap_count)])
        )
    step = 1
    while step < dap_count:
        swap = (me & step) != 0
        got = [
            jnp.where(swap, got[place ^ step], got[place]) for place in range(dap_count)
        ]
        step *= 2
    stacked = jnp.stack(got)
    both = lax.all_gather(stacked, "sub", axis=1)
    return both.reshape((-1,) + block.shape[1:])


def shards_replicated(
    dap_count,
    pairwise_state,
    alignment_state,
    alignment_mask,
    residue_crop_mask,
    outer_input_weight,
    outer_output_weight,
    triangle_input_weight,
    triangle_gate,
    triangle_output_weight,
    transition_up_weight,
    transition_down_weight,
):
    row_count = pairwise_state.shape[0]
    start_row = lax.axis_index(("dap", "sub")) * row_count
    full_mask = residue_crop_mask.astype(jnp.float32)
    row_mask = lax.dynamic_slice_in_dim(full_mask, start_row, row_count, 0)
    pair_all = gather_rows(pairwise_state, dap_count)
    alignment_keep = alignment_mask.astype(jnp.float32) * row_mask[None, :]
    alignment_normed = norm_layer(alignment_state.astype(jnp.float32), -1).astype(jnp.bfloat16)
    projected = jnp.einsum(
        "pxm,qmy->xqyp", alignment_normed, outer_input_weight, preferred_element_type=jnp.float32
    )
    projected = (projected * alignment_keep.T[:, None, None, :]).astype(jnp.bfloat16)
    channels = projected.shape[2]
    sent = jnp.concatenate(
        [
            projected.reshape(row_count, 2 * channels, -1),
            alignment_keep.T[:, None, :].astype(jnp.bfloat16),
        ],
        axis=1,
    )
    msa_all = gather_rows(sent, dap_count)
    left = msa_all[:, :channels]
    right = msa_all[:, channels : 2 * channels]
    keep = msa_all[:, 2 * channels]
    inner = jnp.einsum(
        "iut,ulx->iltx", left, outer_output_weight, preferred_element_type=jnp.float32
    ).astype(jnp.bfloat16)
    numerator = jnp.einsum("iltx,jlt->ijx", inner, right, preferred_element_type=jnp.float32)
    count = jnp.einsum("it,jt->ij", keep, keep, preferred_element_type=jnp.float32)
    opm = numerator / jnp.maximum(count, 1.0)[:, :, None]
    pair_one = (pair_all.astype(jnp.float32) + opm).astype(jnp.bfloat16)
    ln_one = norm_layer(pair_one.astype(jnp.float32), -1).astype(jnp.bfloat16)
    pair_keep = full_mask[:, None] * full_mask[None, :]

    def operand(source, keep_rows, gate_w, proj_w):
        gate_val = jnp.einsum("ijc,cd->ijd", source, gate_w, preferred_element_type=jnp.float32)
        proj_val = jnp.einsum("ijc,cd->ijd", source, proj_w, preferred_element_type=jnp.float32)
        return (jax.nn.sigmoid(gate_val) * proj_val * keep_rows[:, :, None]).astype(jnp.bfloat16)

    own_ln = lax.dynamic_slice_in_dim(ln_one, start_row, row_count, 0)
    own_pair = lax.dynamic_slice_in_dim(pair_one, start_row, row_count, 0)
    left_tri = operand(
        own_ln,
        row_mask[:, None] * full_mask[None, :],
        triangle_input_weight[0],
        triangle_input_weight[1],
    )
    right_tri = operand(ln_one, pair_keep, triangle_input_weight[2], triangle_input_weight[3])
    product = jnp.einsum(
        "ikc,jkc->ijc", left_tri, right_tri, preferred_element_type=jnp.float32
    ).astype(jnp.bfloat16)
    normed = norm_layer(product.astype(jnp.float32), -1).astype(jnp.bfloat16)
    update = jnp.einsum(
        "ijc,cd->ijd", normed, triangle_output_weight, preferred_element_type=jnp.float32
    )
    gate_out = jax.nn.sigmoid(
        jnp.einsum("ijc,cd->ijd", own_ln, triangle_gate, preferred_element_type=jnp.float32)
    )
    pair_two = (own_pair.astype(jnp.float32) + gate_out * update).astype(jnp.bfloat16)
    ln_two = norm_layer(pair_two.astype(jnp.float32), -1).astype(jnp.bfloat16)
    return transition(ln_two, pair_two, transition_up_weight, transition_down_weight)


def shards(
    pairwise_state,
    alignment_state,
    alignment_mask,
    residue_crop_mask,
    outer_input_weight,
    outer_output_weight,
    triangle_input_weight,
    triangle_gate,
    triangle_output_weight,
    transition_up_weight,
    transition_down_weight,
):
    row_count = pairwise_state.shape[0]
    start_row = lax.axis_index(("dap", "sub")) * row_count
    row_presence_mask = lax.dynamic_slice_in_dim(residue_crop_mask, start_row, row_count, 0).astype(
        jnp.float32
    )
    full_mask = residue_crop_mask.astype(jnp.float32)
    alignment_keep = alignment_mask.astype(jnp.float32) * row_presence_mask[None, :]
    alignment_normed = norm_layer(alignment_state.astype(jnp.float32), -1).astype(jnp.bfloat16)
    left_alignment = (
        jnp.einsum(
            "pxm,my->pxy",
            alignment_normed,
            outer_input_weight[0],
            preferred_element_type=jnp.float32,
        )
        * alignment_keep[:, :, None]
    ).astype(jnp.bfloat16)
    right_alignment = (
        jnp.einsum(
            "pxm,my->pxy",
            alignment_normed,
            outer_input_weight[1],
            preferred_element_type=jnp.float32,
        )
        * alignment_keep[:, :, None]
    ).astype(jnp.bfloat16)
    inner_alignment = jnp.einsum(
        "tqu,ulx->tqlx", left_alignment, outer_output_weight, preferred_element_type=jnp.float32
    ).astype(jnp.bfloat16)
    right_portion = lax.all_gather(right_alignment, ("dap", "sub"), axis=1, tiled=True)
    keep_portion = lax.all_gather(
        alignment_keep.astype(jnp.bfloat16), ("dap", "sub"), axis=1, tiled=True
    )
    numerator_sum = jnp.einsum(
        "zkwv,znw->knv", inner_alignment, right_portion, preferred_element_type=jnp.float32
    )
    pair_norm_count = jnp.einsum("cf,cg->fg", alignment_keep, keep_portion.astype(jnp.float32))
    block_part = numerator_sum / jnp.maximum(pair_norm_count, 1.0)[:, :, None]
    pair_one = (pairwise_state.astype(jnp.float32) + block_part).astype(jnp.bfloat16)
    ln_one = norm_layer(pair_one.astype(jnp.float32), -1).astype(jnp.bfloat16)
    pair_keep = row_presence_mask[:, None] * full_mask[None, :]

    def operand(gate_w, proj_w):
        gate_val = jnp.einsum("ijc,cd->dij", ln_one, gate_w, preferred_element_type=jnp.float32)
        proj_val = jnp.einsum("ijc,cd->dij", ln_one, proj_w, preferred_element_type=jnp.float32)
        return (jax.nn.sigmoid(gate_val) * proj_val * pair_keep[None]).astype(jnp.bfloat16)

    left_tri = operand(triangle_input_weight[0], triangle_input_weight[1])
    right_tri = operand(triangle_input_weight[2], triangle_input_weight[3])
    near_right = lax.all_gather(right_tri, "sub", axis=1, tiled=True)
    left_cols, right_all = (
        lax.all_to_all(left_tri, "dap", split_axis=0, concat_axis=1, tiled=True),
        lax.all_to_all(near_right, "dap", split_axis=0, concat_axis=1, tiled=True),
    )
    product = jnp.einsum(
        "cik,cjk->cij", left_cols, right_all, preferred_element_type=jnp.float32
    ).astype(jnp.bfloat16)
    returned = lax.all_to_all(product, "dap", split_axis=1, concat_axis=0, tiled=True)
    normed = norm_layer(returned.astype(jnp.float32), 0).astype(jnp.bfloat16)
    update = jnp.einsum(
        "cij,cd->ijd", normed, triangle_output_weight, preferred_element_type=jnp.float32
    )
    gate_out = jax.nn.sigmoid(
        jnp.einsum("ijc,cd->ijd", ln_one, triangle_gate, preferred_element_type=jnp.float32)
    )
    pair_two = (pair_one.astype(jnp.float32) + gate_out * update).astype(jnp.bfloat16)
    ln_two = norm_layer(pair_two.astype(jnp.float32), -1).astype(jnp.bfloat16)

    def step(row_pair):
        return transition(*row_pair, transition_up_weight, transition_down_weight)

    return lax.map(step, (ln_two, pair_two))


def solution(mesh):
    placed = (
        P(("crop", "dap", "sub"), None, None),
        P("crop", ("dap", "sub"), None),
        P("crop", ("dap", "sub")),
        P("crop"),
        P(),
        P(),
        P(),
        P(),
        P(),
        P(),
        P(),
    )
    dap_count = mesh.shape["dap"]

    def body(pairwise_state, *rest):
        residues, channels = pairwise_state.shape[1:]
        if residues * residues * channels * 2 <= REPLICATED_PAIR_BYTES:
            return shards_replicated(dap_count, pairwise_state, *rest)
        return shards(pairwise_state, *rest)

    return jax.shard_map(
        body,
        mesh=mesh,
        in_specs=placed,
        out_specs=P(("crop", "dap", "sub"), None, None),
        check_vma=False,
    )
```

```python
import jax
import jax.numpy as jnp
from jax import lax
from jax.sharding import Mesh, PartitionSpec as P

REPLICATED_PAIR_BYTES = 1 << 20


def norm_layer(values, reduce_axis):
    average = jnp.mean(values, axis=reduce_axis, keepdims=True)
    centered = values - average
    variance = jnp.mean(centered * centered, axis=reduce_axis, keepdims=True)
    return centered * lax.rsqrt(variance + 1e-05)


def transition(ln_two, pair_two, transition_up_weight, transition_down_weight):
    hidden = jax.nn.relu(
        jnp.dot(ln_two, transition_up_weight, preferred_element_type=jnp.float32)
    ).astype(jnp.bfloat16)
    return (
        pair_two.astype(jnp.float32)
        + jnp.dot(hidden, transition_down_weight, preferred_element_type=jnp.float32)
    ).astype(jnp.bfloat16)


def gather_all(block):
    held = block[None]
    for axis in ("x", "z_low", "z_high"):
        held = lax.all_gather(held, axis, axis=0, tiled=True)
    both = lax.all_gather(held, "sub", axis=0).swapaxes(0, 1)
    return both.reshape((-1,) + block.shape)


def shards_replicated(
    pairwise_state,
    alignment_state,
    alignment_mask,
    residue_crop_mask,
    outer_input_weight,
    outer_output_weight,
    triangle_input_weight,
    triangle_gate,
    triangle_output_weight,
    transition_up_weight,
    transition_down_weight,
):
    row_count = pairwise_state.shape[0]
    start_row = lax.axis_index(("z_high", "z_low", "x", "sub")) * row_count
    full_mask = residue_crop_mask.astype(jnp.float32)
    row_mask = lax.dynamic_slice_in_dim(full_mask, start_row, row_count, 0)
    alignment_keep = alignment_mask.astype(jnp.float32) * row_mask[None, :]
    alignment_normed = norm_layer(alignment_state.astype(jnp.float32), -1).astype(jnp.bfloat16)
    projected = jnp.einsum(
        "pxm,qmy->pxqy", alignment_normed, outer_input_weight, preferred_element_type=jnp.float32
    )
    projected = (projected * alignment_keep[:, :, None, None]).astype(jnp.bfloat16)
    sequences, _, _, channels = projected.shape
    wide = pairwise_state.shape[-1]
    pair_rows = row_count * pairwise_state.shape[1]
    sent = jnp.concatenate(
        [
            pairwise_state.reshape(pair_rows, wide),
            projected.reshape(-1, wide),
            jnp.pad(alignment_keep.T.astype(jnp.bfloat16), ((0, 0), (0, wide - sequences))),
        ],
        axis=0,
    )
    held = gather_all(sent)
    pair_all = held[:, :pair_rows].reshape((-1,) + pairwise_state.shape[1:])
    msa_all = held[:, pair_rows:-row_count].reshape(-1, sequences, row_count, 2, channels)
    left, right = (
        msa_all[:, :, :, q].transpose(0, 2, 1, 3).reshape(-1, sequences, channels) for q in (0, 1)
    )
    left = left.transpose(0, 2, 1)
    right = right.transpose(0, 2, 1)
    keep = held[:, -row_count:, :sequences].reshape(-1, sequences)
    inner = jnp.einsum(
        "iut,ulx->iltx", left, outer_output_weight, preferred_element_type=jnp.float32
    ).astype(jnp.bfloat16)
    numerator = jnp.einsum("iltx,jlt->ijx", inner, right, preferred_element_type=jnp.float32)
    count = jnp.einsum("it,jt->ij", keep, keep, preferred_element_type=jnp.float32)
    opm = numerator / jnp.maximum(count, 1.0)[:, :, None]
    pair_one = (pair_all.astype(jnp.float32) + opm).astype(jnp.bfloat16)
    ln_one = norm_layer(pair_one.astype(jnp.float32), -1).astype(jnp.bfloat16)
    pair_keep = full_mask[:, None] * full_mask[None, :]

    def operand(source, keep_rows, gate_w, proj_w):
        gate_val = jnp.einsum("ijc,cd->ijd", source, gate_w, preferred_element_type=jnp.float32)
        proj_val = jnp.einsum("ijc,cd->ijd", source, proj_w, preferred_element_type=jnp.float32)
        return (jax.nn.sigmoid(gate_val) * proj_val * keep_rows[:, :, None]).astype(jnp.bfloat16)

    own_ln = lax.dynamic_slice_in_dim(ln_one, start_row, row_count, 0)
    own_pair = lax.dynamic_slice_in_dim(pair_one, start_row, row_count, 0)
    left_tri = operand(
        own_ln,
        row_mask[:, None] * full_mask[None, :],
        triangle_input_weight[0],
        triangle_input_weight[1],
    )
    right_tri = operand(ln_one, pair_keep, triangle_input_weight[2], triangle_input_weight[3])
    product = jnp.einsum(
        "ikc,jkc->ijc", left_tri, right_tri, preferred_element_type=jnp.float32
    ).astype(jnp.bfloat16)
    normed = norm_layer(product.astype(jnp.float32), -1).astype(jnp.bfloat16)
    update = jnp.einsum(
        "ijc,cd->ijd", normed, triangle_output_weight, preferred_element_type=jnp.float32
    )
    gate_out = jax.nn.sigmoid(
        jnp.einsum("ijc,cd->ijd", own_ln, triangle_gate, preferred_element_type=jnp.float32)
    )
    pair_two = (own_pair.astype(jnp.float32) + gate_out * update).astype(jnp.bfloat16)
    ln_two = norm_layer(pair_two.astype(jnp.float32), -1).astype(jnp.bfloat16)
    return transition(ln_two, pair_two, transition_up_weight, transition_down_weight)


def shards(
    pairwise_state,
    alignment_state,
    alignment_mask,
    residue_crop_mask,
    outer_input_weight,
    outer_output_weight,
    triangle_input_weight,
    triangle_gate,
    triangle_output_weight,
    transition_up_weight,
    transition_down_weight,
):
    row_count = pairwise_state.shape[0]
    start_row = lax.axis_index(("dap", "sub")) * row_count
    row_presence_mask = lax.dynamic_slice_in_dim(residue_crop_mask, start_row, row_count, 0).astype(
        jnp.float32
    )
    full_mask = residue_crop_mask.astype(jnp.float32)
    alignment_keep = alignment_mask.astype(jnp.float32) * row_presence_mask[None, :]
    alignment_normed = norm_layer(alignment_state.astype(jnp.float32), -1).astype(jnp.bfloat16)
    left_alignment = (
        jnp.einsum(
            "pxm,my->pxy",
            alignment_normed,
            outer_input_weight[0],
            preferred_element_type=jnp.float32,
        )
        * alignment_keep[:, :, None]
    ).astype(jnp.bfloat16)
    right_alignment = (
        jnp.einsum(
            "pxm,my->pxy",
            alignment_normed,
            outer_input_weight[1],
            preferred_element_type=jnp.float32,
        )
        * alignment_keep[:, :, None]
    ).astype(jnp.bfloat16)
    inner_alignment = jnp.einsum(
        "tqu,ulx->tqlx", left_alignment, outer_output_weight, preferred_element_type=jnp.float32
    ).astype(jnp.bfloat16)
    right_portion = lax.all_gather(right_alignment, ("dap", "sub"), axis=1, tiled=True)
    keep_portion = lax.all_gather(
        alignment_keep.astype(jnp.bfloat16), ("dap", "sub"), axis=1, tiled=True
    )
    numerator_sum = jnp.einsum(
        "zkwv,znw->knv", inner_alignment, right_portion, preferred_element_type=jnp.float32
    )
    pair_norm_count = jnp.einsum("cf,cg->fg", alignment_keep, keep_portion.astype(jnp.float32))
    block_part = numerator_sum / jnp.maximum(pair_norm_count, 1.0)[:, :, None]
    pair_one = (pairwise_state.astype(jnp.float32) + block_part).astype(jnp.bfloat16)
    ln_one = norm_layer(pair_one.astype(jnp.float32), -1).astype(jnp.bfloat16)
    pair_keep = row_presence_mask[:, None] * full_mask[None, :]

    def operand(gate_w, proj_w):
        gate_val = jnp.einsum("ijc,cd->dij", ln_one, gate_w, preferred_element_type=jnp.float32)
        proj_val = jnp.einsum("ijc,cd->dij", ln_one, proj_w, preferred_element_type=jnp.float32)
        return (jax.nn.sigmoid(gate_val) * proj_val * pair_keep[None]).astype(jnp.bfloat16)

    left_tri = operand(triangle_input_weight[0], triangle_input_weight[1])
    right_tri = operand(triangle_input_weight[2], triangle_input_weight[3])
    near_right = lax.all_gather(right_tri, "sub", axis=1, tiled=True)
    left_cols, right_all = (
        lax.all_to_all(left_tri, "dap", split_axis=0, concat_axis=1, tiled=True),
        lax.all_to_all(near_right, "dap", split_axis=0, concat_axis=1, tiled=True),
    )
    product = jnp.einsum(
        "cik,cjk->cij", left_cols, right_all, preferred_element_type=jnp.float32
    ).astype(jnp.bfloat16)
    returned = lax.all_to_all(product, "dap", split_axis=1, concat_axis=0, tiled=True)
    normed = norm_layer(returned.astype(jnp.float32), 0).astype(jnp.bfloat16)
    update = jnp.einsum(
        "cij,cd->ijd", normed, triangle_output_weight, preferred_element_type=jnp.float32
    )
    gate_out = jax.nn.sigmoid(
        jnp.einsum("ijc,cd->ijd", ln_one, triangle_gate, preferred_element_type=jnp.float32)
    )
    pair_two = (pair_one.astype(jnp.float32) + gate_out * update).astype(jnp.bfloat16)
    ln_two = norm_layer(pair_two.astype(jnp.float32), -1).astype(jnp.bfloat16)

    def step(row_pair):
        return transition(*row_pair, transition_up_weight, transition_down_weight)

    return lax.map(step, (ln_two, pair_two))


def solution(mesh):
    placed = (
        P(("crop", "dap", "sub"), None, None),
        P("crop", ("dap", "sub"), None),
        P("crop", ("dap", "sub")),
        P("crop"),
        P(),
        P(),
        P(),
        P(),
        P(),
        P(),
        P(),
    )

    def distributed(*arrays):
        return jax.shard_map(
            shards,
            mesh=mesh,
            in_specs=placed,
            out_specs=P(("crop", "dap", "sub"), None, None),
            check_vma=False,
        )(*arrays)

    def replicated(*arrays):
        dap = ("z_high", "z_low", "x")
        fine = Mesh(
            mesh.devices.reshape(mesh.shape["crop"], 2, 2, -1, mesh.shape["sub"]),
            ("crop",) + dap + ("sub",),
        )
        rows = ("crop",) + dap + ("sub",)
        return jax.shard_map(
            shards_replicated,
            mesh=fine,
            in_specs=(P(rows, None, None), P("crop", rows[1:], None), P("crop", rows[1:]))
            + placed[3:],
            out_specs=P(rows, None, None),
            check_vma=False,
        )(*arrays)

    def whole(pairwise_state, *rest):
        residues, channels = pairwise_state.shape[1:]
        if residues * residues * channels * 2 <= REPLICATED_PAIR_BYTES:
            return replicated(pairwise_state, *rest)
        return distributed(pairwise_state, *rest)

    return whole
```

```python
import jax
import jax.numpy as jnp
from jax import lax
from jax.sharding import PartitionSpec as P

REPLICATED_PAIR_BYTES = 1 << 20


def norm_layer(values, reduce_axis):
    average = jnp.mean(values, axis=reduce_axis, keepdims=True)
    centered = values - average
    variance = jnp.mean(centered * centered, axis=reduce_axis, keepdims=True)
    return centered * lax.rsqrt(variance + 1e-05)


def transition(ln_two, pair_two, transition_up_weight, transition_down_weight):
    hidden = jax.nn.relu(
        jnp.dot(ln_two, transition_up_weight, preferred_element_type=jnp.float32)
    ).astype(jnp.bfloat16)
    return (
        pair_two.astype(jnp.float32)
        + jnp.dot(hidden, transition_down_weight, preferred_element_type=jnp.float32)
    ).astype(jnp.bfloat16)


def gather_all(block):
    dap_count = lax.axis_size("dap")
    copies = jnp.broadcast_to(block, (dap_count,) + block.shape)
    held = lax.all_to_all(copies, "dap", split_axis=0, concat_axis=0)
    both = lax.all_gather(held, "sub", axis=0).swapaxes(0, 1)
    return both.reshape((-1,) + block.shape)


def shards_replicated(
    pairwise_state,
    alignment_state,
    alignment_mask,
    residue_crop_mask,
    outer_input_weight,
    outer_output_weight,
    triangle_input_weight,
    triangle_gate,
    triangle_output_weight,
    transition_up_weight,
    transition_down_weight,
):
    row_count = pairwise_state.shape[0]
    start_row = lax.axis_index(("dap", "sub")) * row_count
    full_mask = residue_crop_mask.astype(jnp.float32)
    row_mask = lax.dynamic_slice_in_dim(full_mask, start_row, row_count, 0)
    alignment_keep = alignment_mask.astype(jnp.float32) * row_mask[None, :]
    alignment_normed = norm_layer(alignment_state.astype(jnp.float32), -1).astype(jnp.bfloat16)
    projected = jnp.einsum(
        "pxm,qmy->pxqy", alignment_normed, outer_input_weight, preferred_element_type=jnp.float32
    )
    projected = (projected * alignment_keep[:, :, None, None]).astype(jnp.bfloat16)
    sequences, _, _, channels = projected.shape
    wide = pairwise_state.shape[-1]
    pair_rows = row_count * pairwise_state.shape[1]
    sent = jnp.concatenate(
        [
            pairwise_state.reshape(pair_rows, wide),
            projected.reshape(-1, wide),
            jnp.pad(alignment_keep.T.astype(jnp.bfloat16), ((0, 0), (0, wide - sequences))),
        ],
        axis=0,
    )
    held = gather_all(sent)
    pair_all = held[:, :pair_rows].reshape((-1,) + pairwise_state.shape[1:])
    msa_all = held[:, pair_rows:-row_count].reshape(-1, sequences, row_count, 2, channels)
    left, right = (
        msa_all[:, :, :, q].transpose(0, 2, 1, 3).reshape(-1, sequences, channels) for q in (0, 1)
    )
    left = left.transpose(0, 2, 1)
    right = right.transpose(0, 2, 1)
    keep = held[:, -row_count:, :sequences].reshape(-1, sequences)
    inner = jnp.einsum(
        "iut,ulx->iltx", left, outer_output_weight, preferred_element_type=jnp.float32
    ).astype(jnp.bfloat16)
    numerator = jnp.einsum("iltx,jlt->ijx", inner, right, preferred_element_type=jnp.float32)
    count = jnp.einsum("it,jt->ij", keep, keep, preferred_element_type=jnp.float32)
    opm = numerator / jnp.maximum(count, 1.0)[:, :, None]
    pair_one = (pair_all.astype(jnp.float32) + opm).astype(jnp.bfloat16)
    ln_one = norm_layer(pair_one.astype(jnp.float32), -1).astype(jnp.bfloat16)
    pair_keep = full_mask[:, None] * full_mask[None, :]

    def operand(source, keep_rows, gate_w, proj_w):
        gate_val = jnp.einsum("ijc,cd->ijd", source, gate_w, preferred_element_type=jnp.float32)
        proj_val = jnp.einsum("ijc,cd->ijd", source, proj_w, preferred_element_type=jnp.float32)
        return (jax.nn.sigmoid(gate_val) * proj_val * keep_rows[:, :, None]).astype(jnp.bfloat16)

    own_ln = lax.dynamic_slice_in_dim(ln_one, start_row, row_count, 0)
    own_pair = lax.dynamic_slice_in_dim(pair_one, start_row, row_count, 0)
    left_tri = operand(
        own_ln,
        row_mask[:, None] * full_mask[None, :],
        triangle_input_weight[0],
        triangle_input_weight[1],
    )
    right_tri = operand(ln_one, pair_keep, triangle_input_weight[2], triangle_input_weight[3])
    product = jnp.einsum(
        "ikc,jkc->ijc", left_tri, right_tri, preferred_element_type=jnp.float32
    ).astype(jnp.bfloat16)
    normed = norm_layer(product.astype(jnp.float32), -1).astype(jnp.bfloat16)
    update = jnp.einsum(
        "ijc,cd->ijd", normed, triangle_output_weight, preferred_element_type=jnp.float32
    )
    gate_out = jax.nn.sigmoid(
        jnp.einsum("ijc,cd->ijd", own_ln, triangle_gate, preferred_element_type=jnp.float32)
    )
    pair_two = (own_pair.astype(jnp.float32) + gate_out * update).astype(jnp.bfloat16)
    ln_two = norm_layer(pair_two.astype(jnp.float32), -1).astype(jnp.bfloat16)
    return transition(ln_two, pair_two, transition_up_weight, transition_down_weight)


def shards(
    pairwise_state,
    alignment_state,
    alignment_mask,
    residue_crop_mask,
    outer_input_weight,
    outer_output_weight,
    triangle_input_weight,
    triangle_gate,
    triangle_output_weight,
    transition_up_weight,
    transition_down_weight,
):
    row_count = pairwise_state.shape[0]
    start_row = lax.axis_index(("dap", "sub")) * row_count
    row_presence_mask = lax.dynamic_slice_in_dim(residue_crop_mask, start_row, row_count, 0).astype(
        jnp.float32
    )
    full_mask = residue_crop_mask.astype(jnp.float32)
    alignment_keep = alignment_mask.astype(jnp.float32) * row_presence_mask[None, :]
    alignment_normed = norm_layer(alignment_state.astype(jnp.float32), -1).astype(jnp.bfloat16)
    left_alignment = (
        jnp.einsum(
            "pxm,my->pxy",
            alignment_normed,
            outer_input_weight[0],
            preferred_element_type=jnp.float32,
        )
        * alignment_keep[:, :, None]
    ).astype(jnp.bfloat16)
    right_alignment = (
        jnp.einsum(
            "pxm,my->pxy",
            alignment_normed,
            outer_input_weight[1],
            preferred_element_type=jnp.float32,
        )
        * alignment_keep[:, :, None]
    ).astype(jnp.bfloat16)
    inner_alignment = jnp.einsum(
        "tqu,ulx->tqlx", left_alignment, outer_output_weight, preferred_element_type=jnp.float32
    ).astype(jnp.bfloat16)
    right_portion = lax.all_gather(right_alignment, ("dap", "sub"), axis=1, tiled=True)
    keep_portion = lax.all_gather(
        alignment_keep.astype(jnp.bfloat16), ("dap", "sub"), axis=1, tiled=True
    )
    numerator_sum = jnp.einsum(
        "zkwv,znw->knv", inner_alignment, right_portion, preferred_element_type=jnp.float32
    )
    pair_norm_count = jnp.einsum("cf,cg->fg", alignment_keep, keep_portion.astype(jnp.float32))
    block_part = numerator_sum / jnp.maximum(pair_norm_count, 1.0)[:, :, None]
    pair_one = (pairwise_state.astype(jnp.float32) + block_part).astype(jnp.bfloat16)
    ln_one = norm_layer(pair_one.astype(jnp.float32), -1).astype(jnp.bfloat16)
    pair_keep = row_presence_mask[:, None] * full_mask[None, :]

    def operand(gate_w, proj_w):
        gate_val = jnp.einsum("ijc,cd->dij", ln_one, gate_w, preferred_element_type=jnp.float32)
        proj_val = jnp.einsum("ijc,cd->dij", ln_one, proj_w, preferred_element_type=jnp.float32)
        return (jax.nn.sigmoid(gate_val) * proj_val * pair_keep[None]).astype(jnp.bfloat16)

    left_tri = operand(triangle_input_weight[0], triangle_input_weight[1])
    right_tri = operand(triangle_input_weight[2], triangle_input_weight[3])
    near_right = lax.all_gather(right_tri, "sub", axis=1, tiled=True)
    left_cols, right_all = (
        lax.all_to_all(left_tri, "dap", split_axis=0, concat_axis=1, tiled=True),
        lax.all_to_all(near_right, "dap", split_axis=0, concat_axis=1, tiled=True),
    )
    product = jnp.einsum(
        "cik,cjk->cij", left_cols, right_all, preferred_element_type=jnp.float32
    ).astype(jnp.bfloat16)
    returned = lax.all_to_all(product, "dap", split_axis=1, concat_axis=0, tiled=True)
    normed = norm_layer(returned.astype(jnp.float32), 0).astype(jnp.bfloat16)
    update = jnp.einsum(
        "cij,cd->ijd", normed, triangle_output_weight, preferred_element_type=jnp.float32
    )
    gate_out = jax.nn.sigmoid(
        jnp.einsum("ijc,cd->ijd", ln_one, triangle_gate, preferred_element_type=jnp.float32)
    )
    pair_two = (pair_one.astype(jnp.float32) + gate_out * update).astype(jnp.bfloat16)
    ln_two = norm_layer(pair_two.astype(jnp.float32), -1).astype(jnp.bfloat16)

    def step(row_pair):
        return transition(*row_pair, transition_up_weight, transition_down_weight)

    return lax.map(step, (ln_two, pair_two))


def solution(mesh):
    placed = (
        P(("crop", "dap", "sub"), None, None),
        P("crop", ("dap", "sub"), None),
        P("crop", ("dap", "sub")),
        P("crop"),
        P(),
        P(),
        P(),
        P(),
        P(),
        P(),
        P(),
    )

    def body(pairwise_state, *rest):
        residues, channels = pairwise_state.shape[1:]
        if residues * residues * channels * 2 <= REPLICATED_PAIR_BYTES:
            return shards_replicated(pairwise_state, *rest)
        return shards(pairwise_state, *rest)

    return jax.shard_map(
        body,
        mesh=mesh,
        in_specs=placed,
        out_specs=P(("crop", "dap", "sub"), None, None),
        check_vma=False,
    )
```

```python
import jax
import jax.numpy as jnp
from jax import lax
from jax.experimental import pallas as pl
from jax.experimental.pallas import tpu as pltpu
from jax.sharding import PartitionSpec as P

REPLICATED_PAIR_BYTES = 1 << 20


def norm_layer(values, reduce_axis):
    average = jnp.mean(values, axis=reduce_axis, keepdims=True)
    centered = values - average
    variance = jnp.mean(centered * centered, axis=reduce_axis, keepdims=True)
    return centered * lax.rsqrt(variance + 1e-05)


def transition(ln_two, pair_two, transition_up_weight, transition_down_weight):
    hidden = jax.nn.relu(
        jnp.dot(ln_two, transition_up_weight, preferred_element_type=jnp.float32)
    ).astype(jnp.bfloat16)
    return (
        pair_two.astype(jnp.float32)
        + jnp.dot(hidden, transition_down_weight, preferred_element_type=jnp.float32)
    ).astype(jnp.bfloat16)


def layer_norm(values):
    count = values.shape[-1]
    centered = values - jnp.sum(values, axis=-1, keepdims=True) * (1.0 / count)
    variance = jnp.sum(centered * centered, axis=-1, keepdims=True) * (1.0 / count)
    return centered * lax.rsqrt(variance + 1e-05)


def pack_kernel(place_ref, mask_ref, keep_ref, state_ref, weight_ref, pair_ref, out_ref, normed_ref):
    rows, residues, wide = pair_ref.shape
    sequences = state_ref.shape[0]
    channels = weight_ref.shape[1]
    base = rows * residues
    start = place_ref[0]
    second_core = place_ref[1] == 1
    for row in range(rows):
        out_ref[row * residues : (row + 1) * residues] = pair_ref[row]
    normed_ref[...] = layer_norm(state_ref[...].astype(jnp.float32))
    eye = lax.broadcasted_iota(jnp.int32, (sequences, sequences), 0) == lax.broadcasted_iota(
        jnp.int32, (sequences, sequences), 1
    )
    lefts, rights, keeps = [], [], []
    for row in range(rows):
        present = mask_ref[start + row].astype(jnp.float32)
        keep_row = keep_ref[row : row + 1].astype(jnp.float32) * present
        keep_column = jnp.sum(
            jnp.where(eye, jnp.broadcast_to(keep_row, eye.shape), 0.0), axis=1, keepdims=True
        )
        normed = normed_ref[:, row].astype(jnp.bfloat16)
        last = (((1,), (1,)), ((), ()))
        left = lax.dot_general(weight_ref[0], normed, last, preferred_element_type=jnp.float32)
        right = lax.dot_general(normed, weight_ref[1], last, preferred_element_type=jnp.float32)
        lefts.append(left * keep_row)
        rights.append(right * keep_column)
        keeps.append(keep_row)
    left = jnp.concatenate(lefts, axis=1)
    right = jnp.concatenate(rights, axis=1)
    first = jnp.concatenate([right, left], axis=1)
    other = jnp.concatenate([left, right], axis=1)
    out_ref[base : base + sequences] = jnp.where(second_core, other, first).astype(jnp.bfloat16)
    keep = jnp.concatenate(
        keeps + [jnp.zeros((16 - rows, sequences), jnp.float32)], axis=0
    )
    out_ref[base + sequences :] = jnp.concatenate(
        [keep, jnp.zeros((16, wide - sequences), jnp.float32)], axis=1
    ).astype(jnp.bfloat16)


def update_kernel(
    place_ref,
    mask_ref,
    held_ref,
    outer_ref,
    triangle_ref,
    gate_ref,
    output_ref,
    up_ref,
    down_ref,
    out_ref,
    block_ref,
    left_ref,
    right_ref,
    keep_ref,
    outer_product_ref,
    pair_ref,
    pair_one_ref,
    ln_one_ref,
):
    rows, residues, wide = out_ref.shape
    cores, chips = held_ref.shape[:2]
    channels = outer_ref.shape[0]
    sequences = channels
    base = rows * residues
    group = cores * rows
    start = place_ref[0]
    bf16 = jnp.bfloat16
    f32 = jnp.float32

    block_ref[...] = jnp.zeros_like(block_ref)
    for d in range(channels):
        weight = outer_ref[d]
        for part in range(group):
            block_ref[
                (d * group + part) * channels : (d * group + part + 1) * channels,
                part * wide : (part + 1) * wide,
            ] = weight

    lane = lax.broadcasted_iota(jnp.int32, (channels, wide), 1)
    lane_block = lane // channels
    for chip in range(chips):
        packed = [held_ref[core, chip, base : base + sequences].astype(f32) for core in range(cores)]
        right = jnp.where(lane < wide // 2, packed[0], packed[1]).astype(bf16)
        for copy in range(group):
            right_ref[copy * sequences : (copy + 1) * sequences, chip * wide : (chip + 1) * wide] = right
        for core in range(cores):
            for row in range(rows):
                residue = (chip * cores + core) * rows + row
                at = (rows if core == 0 else 0) + row
                left_ref[residue] = jnp.where(lane_block == at, packed[core], 0.0)
            presence = held_ref[core, chip, base + sequences :].astype(f32)
            keep_ref[(chip * cores + core) * rows : (chip * cores + core + 1) * rows] = presence[:rows]
            pair_ref[(chip * cores + core) * rows : (chip * cores + core + 1) * rows] = (
                held_ref[core, chip, :base].astype(f32).reshape(rows, residues, wide)
            )

    last = (((1,), (1,)), ((), ()))
    keep = keep_ref[...].astype(bf16)
    count = lax.dot_general(keep, keep, last, preferred_element_type=f32)
    inverse = 1.0 / jnp.maximum(count, 1.0)

    step = 8
    for first in range(0, channels, step):
        left = jnp.concatenate(
            [left_ref[:, d] for d in range(first, first + step)], axis=0
        ).astype(bf16)
        outer = jnp.dot(left, right_ref[...], preferred_element_type=f32).astype(bf16)
        for d in range(first, first + step):
            for chip in range(chips):
                outer_product_ref[
                    chip * residues : (chip + 1) * residues, d * wide : (d + 1) * wide
                ] = outer[
                    (d - first) * residues : (d - first + 1) * residues,
                    chip * wide : (chip + 1) * wide,
                ]
    numerator = jnp.dot(outer_product_ref[...], block_ref[...], preferred_element_type=f32)

    for k in range(residues):
        chip, part = k // group, k % group
        opm = numerator[
            chip * residues : (chip + 1) * residues, part * wide : (part + 1) * wide
        ] * jnp.broadcast_to(inverse[:, k : k + 1], (residues, wide))
        pair_one = (pair_ref[:, k] + opm).astype(bf16).astype(f32)
        pair_one_ref[k] = pair_one
        ln_one_ref[k] = layer_norm(pair_one)

    ln_all = ln_one_ref[...].reshape(residues * residues, wide).astype(bf16)
    gate_value = jnp.dot(ln_all, triangle_ref[2], preferred_element_type=f32)
    value = jnp.dot(ln_all, triangle_ref[3], preferred_element_type=f32)
    right_tri = (jax.nn.sigmoid(gate_value) * value).astype(bf16).astype(f32)

    mask_column = jnp.zeros((residues, 1), f32)
    place = lax.broadcasted_iota(jnp.int32, (residues, 1), 0)
    for k in range(residues):
        mask_column = jnp.where(place == k, mask_ref[k].astype(f32), mask_column)

    own_pair = jnp.concatenate([pair_one_ref[:, start + row] for row in range(rows)], axis=0)
    own_ln = jnp.concatenate([ln_one_ref[:, start + row] for row in range(rows)], axis=0).astype(bf16)
    gate_value = jnp.dot(own_ln, triangle_ref[0], preferred_element_type=f32)
    value = jnp.dot(own_ln, triangle_ref[1], preferred_element_type=f32)
    left_tri = jax.nn.sigmoid(gate_value) * value * jnp.concatenate([mask_column] * rows, axis=0)
    left_tri = left_tri.astype(bf16).astype(f32)
    products = []
    for row in range(rows):
        total = jnp.zeros((residues, wide), f32)
        for k in range(residues):
            at = row * residues + k
            total += left_tri[at : at + 1] * right_tri[k * residues : (k + 1) * residues]
        products.append(total * (mask_column * mask_ref[start + row].astype(f32)))
    product = jnp.concatenate(products, axis=0).astype(bf16).astype(f32)
    normed = layer_norm(product).astype(bf16)
    update = jnp.dot(normed, output_ref[...], preferred_element_type=f32)
    gate_out = jax.nn.sigmoid(jnp.dot(own_ln, gate_ref[...], preferred_element_type=f32))
    pair_two = (own_pair + gate_out * update).astype(bf16).astype(f32)
    ln_two = layer_norm(pair_two).astype(bf16)
    hidden = jnp.maximum(jnp.dot(ln_two, up_ref[...], preferred_element_type=f32), 0.0).astype(bf16)
    result = pair_two + jnp.dot(hidden, down_ref[...], preferred_element_type=f32)
    out_ref[...] = result.astype(bf16).reshape(rows, residues, wide)


def gather_all(block):
    dap_count = lax.axis_size("dap")
    copies = jnp.broadcast_to(block, (dap_count,) + block.shape)
    held = lax.all_to_all(copies, "dap", split_axis=0, concat_axis=0)
    return lax.all_gather(held, "sub", axis=0)


def shards_replicated(
    pairwise_state,
    alignment_state,
    alignment_mask,
    residue_crop_mask,
    outer_input_weight,
    outer_output_weight,
    triangle_input_weight,
    triangle_gate,
    triangle_output_weight,
    transition_up_weight,
    transition_down_weight,
):
    rows, residues, wide = pairwise_state.shape
    sequences = alignment_state.shape[0]
    channels = outer_input_weight.shape[2]
    sub = lax.axis_index("sub")
    start = (lax.axis_index("dap") * lax.axis_size("sub") + sub) * rows
    place = jnp.stack([start, sub]).astype(jnp.int32)
    scalar = pl.BlockSpec(memory_space=pltpu.SMEM)
    vector = pl.BlockSpec(memory_space=pltpu.VMEM)
    params = pltpu.CompilerParams(vmem_limit_bytes=40 << 20)
    packed = pl.pallas_call(
        pack_kernel,
        out_shape=jax.ShapeDtypeStruct((rows * residues + sequences + 16, wide), jnp.bfloat16),
        in_specs=[scalar] * 2 + [vector] * 4,
        out_specs=vector,
        scratch_shapes=[pltpu.VMEM(alignment_state.shape, jnp.float32)],
        compiler_params=params,
    )(
        place,
        residue_crop_mask,
        alignment_mask.T,
        alignment_state,
        outer_input_weight.transpose(0, 2, 1),
        pairwise_state,
    )
    held = gather_all(packed)
    cores, chips = held.shape[:2]
    group = cores * rows
    return pl.pallas_call(
        update_kernel,
        out_shape=jax.ShapeDtypeStruct(pairwise_state.shape, jnp.bfloat16),
        in_specs=[scalar] * 2 + [vector] * 7,
        out_specs=vector,
        scratch_shapes=[
            pltpu.VMEM((channels * group * channels, group * wide), jnp.bfloat16),
            pltpu.VMEM((residues, channels, wide), jnp.float32),
            pltpu.VMEM((group * sequences, chips * wide), jnp.bfloat16),
            pltpu.VMEM((residues, wide), jnp.float32),
            pltpu.VMEM((chips * residues, channels * wide), jnp.bfloat16),
            pltpu.VMEM((residues, residues, wide), jnp.float32),
            pltpu.VMEM((residues, residues, wide), jnp.float32),
            pltpu.VMEM((residues, residues, wide), jnp.float32),
        ],
        compiler_params=params,
    )(
        place,
        residue_crop_mask,
        held,
        outer_output_weight,
        triangle_input_weight,
        triangle_gate,
        triangle_output_weight,
        transition_up_weight,
        transition_down_weight,
    )


def shards(
    pairwise_state,
    alignment_state,
    alignment_mask,
    residue_crop_mask,
    outer_input_weight,
    outer_output_weight,
    triangle_input_weight,
    triangle_gate,
    triangle_output_weight,
    transition_up_weight,
    transition_down_weight,
):
    row_count = pairwise_state.shape[0]
    start_row = lax.axis_index(("dap", "sub")) * row_count
    row_presence_mask = lax.dynamic_slice_in_dim(residue_crop_mask, start_row, row_count, 0).astype(
        jnp.float32
    )
    full_mask = residue_crop_mask.astype(jnp.float32)
    alignment_keep = alignment_mask.astype(jnp.float32) * row_presence_mask[None, :]
    alignment_normed = norm_layer(alignment_state.astype(jnp.float32), -1).astype(jnp.bfloat16)
    left_alignment = (
        jnp.einsum(
            "pxm,my->pxy",
            alignment_normed,
            outer_input_weight[0],
            preferred_element_type=jnp.float32,
        )
        * alignment_keep[:, :, None]
    ).astype(jnp.bfloat16)
    right_alignment = (
        jnp.einsum(
            "pxm,my->pxy",
            alignment_normed,
            outer_input_weight[1],
            preferred_element_type=jnp.float32,
        )
        * alignment_keep[:, :, None]
    ).astype(jnp.bfloat16)
    inner_alignment = jnp.einsum(
        "tqu,ulx->tqlx", left_alignment, outer_output_weight, preferred_element_type=jnp.float32
    ).astype(jnp.bfloat16)
    right_portion = lax.all_gather(right_alignment, ("dap", "sub"), axis=1, tiled=True)
    keep_portion = lax.all_gather(
        alignment_keep.astype(jnp.bfloat16), ("dap", "sub"), axis=1, tiled=True
    )
    numerator_sum = jnp.einsum(
        "zkwv,znw->knv", inner_alignment, right_portion, preferred_element_type=jnp.float32
    )
    pair_norm_count = jnp.einsum("cf,cg->fg", alignment_keep, keep_portion.astype(jnp.float32))
    block_part = numerator_sum / jnp.maximum(pair_norm_count, 1.0)[:, :, None]
    pair_one = (pairwise_state.astype(jnp.float32) + block_part).astype(jnp.bfloat16)
    ln_one = norm_layer(pair_one.astype(jnp.float32), -1).astype(jnp.bfloat16)
    pair_keep = row_presence_mask[:, None] * full_mask[None, :]

    def operand(gate_w, proj_w):
        gate_val = jnp.einsum("ijc,cd->dij", ln_one, gate_w, preferred_element_type=jnp.float32)
        proj_val = jnp.einsum("ijc,cd->dij", ln_one, proj_w, preferred_element_type=jnp.float32)
        return (jax.nn.sigmoid(gate_val) * proj_val * pair_keep[None]).astype(jnp.bfloat16)

    left_tri = operand(triangle_input_weight[0], triangle_input_weight[1])
    right_tri = operand(triangle_input_weight[2], triangle_input_weight[3])
    near_right = lax.all_gather(right_tri, "sub", axis=1, tiled=True)
    left_cols, right_all = (
        lax.all_to_all(left_tri, "dap", split_axis=0, concat_axis=1, tiled=True),
        lax.all_to_all(near_right, "dap", split_axis=0, concat_axis=1, tiled=True),
    )
    product = jnp.einsum(
        "cik,cjk->cij", left_cols, right_all, preferred_element_type=jnp.float32
    ).astype(jnp.bfloat16)
    returned = lax.all_to_all(product, "dap", split_axis=1, concat_axis=0, tiled=True)
    normed = norm_layer(returned.astype(jnp.float32), 0).astype(jnp.bfloat16)
    update = jnp.einsum(
        "cij,cd->ijd", normed, triangle_output_weight, preferred_element_type=jnp.float32
    )
    gate_out = jax.nn.sigmoid(
        jnp.einsum("ijc,cd->ijd", ln_one, triangle_gate, preferred_element_type=jnp.float32)
    )
    pair_two = (pair_one.astype(jnp.float32) + gate_out * update).astype(jnp.bfloat16)
    ln_two = norm_layer(pair_two.astype(jnp.float32), -1).astype(jnp.bfloat16)

    def step(row_pair):
        return transition(*row_pair, transition_up_weight, transition_down_weight)

    return lax.map(step, (ln_two, pair_two))


def solution(mesh):
    placed = (
        P(("crop", "dap", "sub"), None, None),
        P("crop", ("dap", "sub"), None),
        P("crop", ("dap", "sub")),
        P("crop"),
        P(),
        P(),
        P(),
        P(),
        P(),
        P(),
        P(),
    )

    def body(pairwise_state, *rest):
        residues, channels = pairwise_state.shape[1:]
        if residues * residues * channels * 2 <= REPLICATED_PAIR_BYTES:
            return shards_replicated(pairwise_state, *rest)
        return shards(pairwise_state, *rest)

    return jax.shard_map(
        body,
        mesh=mesh,
        in_specs=placed,
        out_specs=P(("crop", "dap", "sub"), None, None),
        check_vma=False,
    )
```

```python
import jax
import jax.numpy as jnp
from jax import lax
from jax.experimental import pallas as pl
from jax.experimental.pallas import tpu as pltpu
from jax.sharding import PartitionSpec as P

REPLICATED_PAIR_BYTES = 1 << 20


def norm_layer(values, reduce_axis):
    average = jnp.mean(values, axis=reduce_axis, keepdims=True)
    centered = values - average
    variance = jnp.mean(centered * centered, axis=reduce_axis, keepdims=True)
    return centered * lax.rsqrt(variance + 1e-05)


def transition(ln_two, pair_two, transition_up_weight, transition_down_weight):
    hidden = jax.nn.relu(
        jnp.dot(ln_two, transition_up_weight, preferred_element_type=jnp.float32)
    ).astype(jnp.bfloat16)
    return (
        pair_two.astype(jnp.float32)
        + jnp.dot(hidden, transition_down_weight, preferred_element_type=jnp.float32)
    ).astype(jnp.bfloat16)


def layer_norm(values):
    count = values.shape[-1]
    centered = values - jnp.sum(values, axis=-1, keepdims=True) * (1.0 / count)
    variance = jnp.sum(centered * centered, axis=-1, keepdims=True) * (1.0 / count)
    return centered * lax.rsqrt(variance + 1e-05)


def first_row(rows):
    return (lax.axis_index("dap") * lax.axis_size("sub") + lax.axis_index("sub")) * rows


def pack_kernel(
    mask_ref,
    keep_hbm,
    state_hbm,
    weight_hbm,
    pair_hbm,
    out_ref,
    keep_ref,
    state_ref,
    weight_ref,
    normed_ref,
    sems,
):
    rows, residues, wide = pair_hbm.shape
    sequences = state_ref.shape[0]
    base = rows * residues
    start = first_row(rows)
    second_core = lax.axis_index("sub") == 1
    loads = [
        pltpu.make_async_copy(state_hbm, state_ref, sems.at[0]),
        pltpu.make_async_copy(weight_hbm, weight_ref, sems.at[1]),
        pltpu.make_async_copy(keep_hbm, keep_ref, sems.at[2]),
    ] + [
        pltpu.make_async_copy(
            pair_hbm.at[row], out_ref.at[pl.ds(row * residues, residues)], sems.at[3 + row]
        )
        for row in range(rows)
    ]
    for load in loads:
        load.start()
    loads[0].wait()
    normed_ref[...] = layer_norm(state_ref[...].astype(jnp.float32))
    eye = lax.broadcasted_iota(jnp.int32, (sequences, sequences), 0) == lax.broadcasted_iota(
        jnp.int32, (sequences, sequences), 1
    )
    lefts, rights, keeps = [], [], []
    for load in loads[1:]:
        load.wait()
    for row in range(rows):
        present = mask_ref[start + row].astype(jnp.float32)
        keep_row = keep_ref[row : row + 1].astype(jnp.float32) * present
        keep_column = jnp.sum(
            jnp.where(eye, jnp.broadcast_to(keep_row, eye.shape), 0.0), axis=1, keepdims=True
        )
        normed = normed_ref[:, row].astype(jnp.bfloat16)
        last = (((1,), (1,)), ((), ()))
        left = lax.dot_general(weight_ref[0], normed, last, preferred_element_type=jnp.float32)
        right = lax.dot_general(normed, weight_ref[1], last, preferred_element_type=jnp.float32)
        lefts.append(left * keep_row)
        rights.append(right * keep_column)
        keeps.append(keep_row)
    left = jnp.concatenate(lefts, axis=1)
    right = jnp.concatenate(rights, axis=1)
    first = jnp.concatenate([right, left], axis=1)
    other = jnp.concatenate([left, right], axis=1)
    out_ref[base : base + sequences] = jnp.where(second_core, other, first).astype(jnp.bfloat16)
    keep = jnp.concatenate(
        keeps + [jnp.zeros((16 - rows, sequences), jnp.float32)], axis=0
    )
    out_ref[base + sequences :] = jnp.concatenate(
        [keep, jnp.zeros((16, wide - sequences), jnp.float32)], axis=1
    ).astype(jnp.bfloat16)


def update_kernel(
    mask_ref,
    held_ref,
    outer_ref,
    triangle_ref,
    gate_ref,
    output_ref,
    up_ref,
    down_ref,
    out_ref,
    block_ref,
    left_ref,
    right_ref,
    keep_ref,
    outer_product_ref,
    pair_ref,
    pair_one_ref,
    ln_one_ref,
):
    rows, residues, wide = out_ref.shape
    cores, chips = held_ref.shape[:2]
    channels = outer_ref.shape[0]
    sequences = channels
    base = rows * residues
    group = cores * rows
    start = first_row(rows)
    bf16 = jnp.bfloat16
    f32 = jnp.float32

    block_ref[...] = jnp.zeros_like(block_ref)
    for d in range(channels):
        weight = outer_ref[d]
        for part in range(group):
            block_ref[
                (d * group + part) * channels : (d * group + part + 1) * channels,
                part * wide : (part + 1) * wide,
            ] = weight

    lane = lax.broadcasted_iota(jnp.int32, (channels, wide), 1)
    lane_block = lane // channels
    for chip in range(chips):
        packed = [held_ref[core, chip, base : base + sequences].astype(f32) for core in range(cores)]
        right = jnp.where(lane < wide // 2, packed[0], packed[1]).astype(bf16)
        for copy in range(group):
            right_ref[copy * sequences : (copy + 1) * sequences, chip * wide : (chip + 1) * wide] = right
        for core in range(cores):
            for row in range(rows):
                residue = (chip * cores + core) * rows + row
                at = (rows if core == 0 else 0) + row
                left_ref[residue] = jnp.where(lane_block == at, packed[core], 0.0)
            presence = held_ref[core, chip, base + sequences :].astype(f32)
            keep_ref[(chip * cores + core) * rows : (chip * cores + core + 1) * rows] = presence[:rows]
            pair_ref[(chip * cores + core) * rows : (chip * cores + core + 1) * rows] = (
                held_ref[core, chip, :base].astype(f32).reshape(rows, residues, wide)
            )

    last = (((1,), (1,)), ((), ()))
    keep = keep_ref[...].astype(bf16)
    count = lax.dot_general(keep, keep, last, preferred_element_type=f32)
    inverse = 1.0 / jnp.maximum(count, 1.0)

    step = 8
    for first in range(0, channels, step):
        left = jnp.concatenate(
            [left_ref[:, d] for d in range(first, first + step)], axis=0
        ).astype(bf16)
        outer = jnp.dot(left, right_ref[...], preferred_element_type=f32).astype(bf16)
        for d in range(first, first + step):
            for chip in range(chips):
                outer_product_ref[
                    chip * residues : (chip + 1) * residues, d * wide : (d + 1) * wide
                ] = outer[
                    (d - first) * residues : (d - first + 1) * residues,
                    chip * wide : (chip + 1) * wide,
                ]
    numerator = jnp.dot(outer_product_ref[...], block_ref[...], preferred_element_type=f32)

    for k in range(residues):
        chip, part = k // group, k % group
        opm = numerator[
            chip * residues : (chip + 1) * residues, part * wide : (part + 1) * wide
        ] * jnp.broadcast_to(inverse[:, k : k + 1], (residues, wide))
        pair_one = (pair_ref[:, k] + opm).astype(bf16).astype(f32)
        pair_one_ref[k] = pair_one
        ln_one_ref[k] = layer_norm(pair_one)

    ln_all = ln_one_ref[...].reshape(residues * residues, wide).astype(bf16)
    gate_value = jnp.dot(ln_all, triangle_ref[2], preferred_element_type=f32)
    value = jnp.dot(ln_all, triangle_ref[3], preferred_element_type=f32)
    right_tri = (jax.nn.sigmoid(gate_value) * value).astype(bf16).astype(f32)

    mask_column = jnp.zeros((residues, 1), f32)
    place = lax.broadcasted_iota(jnp.int32, (residues, 1), 0)
    for k in range(residues):
        mask_column = jnp.where(place == k, mask_ref[k].astype(f32), mask_column)

    own_pair = jnp.concatenate([pair_one_ref[:, start + row] for row in range(rows)], axis=0)
    own_ln = jnp.concatenate([ln_one_ref[:, start + row] for row in range(rows)], axis=0).astype(bf16)
    gate_value = jnp.dot(own_ln, triangle_ref[0], preferred_element_type=f32)
    value = jnp.dot(own_ln, triangle_ref[1], preferred_element_type=f32)
    left_tri = jax.nn.sigmoid(gate_value) * value * jnp.concatenate([mask_column] * rows, axis=0)
    left_tri = left_tri.astype(bf16).astype(f32)
    products = []
    for row in range(rows):
        total = jnp.zeros((residues, wide), f32)
        for k in range(residues):
            at = row * residues + k
            total += left_tri[at : at + 1] * right_tri[k * residues : (k + 1) * residues]
        products.append(total * (mask_column * mask_ref[start + row].astype(f32)))
    product = jnp.concatenate(products, axis=0).astype(bf16).astype(f32)
    normed = layer_norm(product).astype(bf16)
    update = jnp.dot(normed, output_ref[...], preferred_element_type=f32)
    gate_out = jax.nn.sigmoid(jnp.dot(own_ln, gate_ref[...], preferred_element_type=f32))
    pair_two = (own_pair + gate_out * update).astype(bf16).astype(f32)
    ln_two = layer_norm(pair_two).astype(bf16)
    hidden = jnp.maximum(jnp.dot(ln_two, up_ref[...], preferred_element_type=f32), 0.0).astype(bf16)
    result = pair_two + jnp.dot(hidden, down_ref[...], preferred_element_type=f32)
    out_ref[...] = result.astype(bf16).reshape(rows, residues, wide)


def gather_all(block):
    return lax.all_gather(lax.all_gather(block, "dap", axis=0), "sub", axis=0)


def shards_replicated(
    pairwise_state,
    alignment_state,
    alignment_mask,
    residue_crop_mask,
    outer_input_weight,
    outer_output_weight,
    triangle_input_weight,
    triangle_gate,
    triangle_output_weight,
    transition_up_weight,
    transition_down_weight,
):
    rows, residues, wide = pairwise_state.shape
    sequences = alignment_state.shape[0]
    channels = outer_input_weight.shape[2]
    scalar = pl.BlockSpec(memory_space=pltpu.SMEM)
    vector = pl.BlockSpec(memory_space=pltpu.VMEM)
    params = pltpu.CompilerParams(vmem_limit_bytes=40 << 20)
    hbm = pl.BlockSpec(memory_space=pltpu.HBM)
    packed = pl.pallas_call(
        pack_kernel,
        out_shape=jax.ShapeDtypeStruct((rows * residues + sequences + 16, wide), jnp.bfloat16),
        in_specs=[scalar] + [hbm] * 4,
        out_specs=vector,
        scratch_shapes=[
            pltpu.VMEM((rows, sequences), jnp.int32),
            pltpu.VMEM(alignment_state.shape, jnp.bfloat16),
            pltpu.VMEM((2, channels, alignment_state.shape[2]), jnp.bfloat16),
            pltpu.VMEM(alignment_state.shape, jnp.float32),
            pltpu.SemaphoreType.DMA((3 + rows,)),
        ],
        compiler_params=pltpu.CompilerParams(vmem_limit_bytes=63 << 20),
    )(
        residue_crop_mask,
        alignment_mask.T,
        alignment_state,
        outer_input_weight.transpose(0, 2, 1),
        pairwise_state,
    )
    held = gather_all(packed)
    cores, chips = held.shape[:2]
    group = cores * rows
    return pl.pallas_call(
        update_kernel,
        out_shape=jax.ShapeDtypeStruct(pairwise_state.shape, jnp.bfloat16),
        in_specs=[scalar] + [vector] * 7,
        out_specs=vector,
        scratch_shapes=[
            pltpu.VMEM((channels * group * channels, group * wide), jnp.bfloat16),
            pltpu.VMEM((residues, channels, wide), jnp.float32),
            pltpu.VMEM((group * sequences, chips * wide), jnp.bfloat16),
            pltpu.VMEM((residues, wide), jnp.float32),
            pltpu.VMEM((chips * residues, channels * wide), jnp.bfloat16),
            pltpu.VMEM((residues, residues, wide), jnp.float32),
            pltpu.VMEM((residues, residues, wide), jnp.float32),
            pltpu.VMEM((residues, residues, wide), jnp.float32),
        ],
        compiler_params=params,
    )(
        residue_crop_mask,
        held,
        outer_output_weight,
        triangle_input_weight,
        triangle_gate,
        triangle_output_weight,
        transition_up_weight,
        transition_down_weight,
    )


def shards(
    pairwise_state,
    alignment_state,
    alignment_mask,
    residue_crop_mask,
    outer_input_weight,
    outer_output_weight,
    triangle_input_weight,
    triangle_gate,
    triangle_output_weight,
    transition_up_weight,
    transition_down_weight,
):
    row_count = pairwise_state.shape[0]
    start_row = lax.axis_index(("dap", "sub")) * row_count
    row_presence_mask = lax.dynamic_slice_in_dim(residue_crop_mask, start_row, row_count, 0).astype(
        jnp.float32
    )
    full_mask = residue_crop_mask.astype(jnp.float32)
    alignment_keep = alignment_mask.astype(jnp.float32) * row_presence_mask[None, :]
    alignment_normed = norm_layer(alignment_state.astype(jnp.float32), -1).astype(jnp.bfloat16)
    left_alignment = (
        jnp.einsum(
            "pxm,my->pxy",
            alignment_normed,
            outer_input_weight[0],
            preferred_element_type=jnp.float32,
        )
        * alignment_keep[:, :, None]
    ).astype(jnp.bfloat16)
    right_alignment = (
        jnp.einsum(
            "pxm,my->pxy",
            alignment_normed,
            outer_input_weight[1],
            preferred_element_type=jnp.float32,
        )
        * alignment_keep[:, :, None]
    ).astype(jnp.bfloat16)
    inner_alignment = jnp.einsum(
        "tqu,ulx->tqlx", left_alignment, outer_output_weight, preferred_element_type=jnp.float32
    ).astype(jnp.bfloat16)
    right_portion = lax.all_gather(right_alignment, ("dap", "sub"), axis=1, tiled=True)
    keep_portion = lax.all_gather(
        alignment_keep.astype(jnp.bfloat16), ("dap", "sub"), axis=1, tiled=True
    )
    numerator_sum = jnp.einsum(
        "zkwv,znw->knv", inner_alignment, right_portion, preferred_element_type=jnp.float32
    )
    pair_norm_count = jnp.einsum("cf,cg->fg", alignment_keep, keep_portion.astype(jnp.float32))
    block_part = numerator_sum / jnp.maximum(pair_norm_count, 1.0)[:, :, None]
    pair_one = (pairwise_state.astype(jnp.float32) + block_part).astype(jnp.bfloat16)
    ln_one = norm_layer(pair_one.astype(jnp.float32), -1).astype(jnp.bfloat16)
    pair_keep = row_presence_mask[:, None] * full_mask[None, :]

    def operand(gate_w, proj_w):
        gate_val = jnp.einsum("ijc,cd->dij", ln_one, gate_w, preferred_element_type=jnp.float32)
        proj_val = jnp.einsum("ijc,cd->dij", ln_one, proj_w, preferred_element_type=jnp.float32)
        return (jax.nn.sigmoid(gate_val) * proj_val * pair_keep[None]).astype(jnp.bfloat16)

    left_tri = operand(triangle_input_weight[0], triangle_input_weight[1])
    right_tri = operand(triangle_input_weight[2], triangle_input_weight[3])
    near_right = lax.all_gather(right_tri, "sub", axis=1, tiled=True)
    left_cols, right_all = (
        lax.all_to_all(left_tri, "dap", split_axis=0, concat_axis=1, tiled=True),
        lax.all_to_all(near_right, "dap", split_axis=0, concat_axis=1, tiled=True),
    )
    product = jnp.einsum(
        "cik,cjk->cij", left_cols, right_all, preferred_element_type=jnp.float32
    ).astype(jnp.bfloat16)
    returned = lax.all_to_all(product, "dap", split_axis=1, concat_axis=0, tiled=True)
    normed = norm_layer(returned.astype(jnp.float32), 0).astype(jnp.bfloat16)
    update = jnp.einsum(
        "cij,cd->ijd", normed, triangle_output_weight, preferred_element_type=jnp.float32
    )
    gate_out = jax.nn.sigmoid(
        jnp.einsum("ijc,cd->ijd", ln_one, triangle_gate, preferred_element_type=jnp.float32)
    )
    pair_two = (pair_one.astype(jnp.float32) + gate_out * update).astype(jnp.bfloat16)
    ln_two = norm_layer(pair_two.astype(jnp.float32), -1).astype(jnp.bfloat16)

    def step(row_pair):
        return transition(*row_pair, transition_up_weight, transition_down_weight)

    return lax.map(step, (ln_two, pair_two))


def solution(mesh):
    placed = (
        P(("crop", "dap", "sub"), None, None),
        P("crop", ("dap", "sub"), None),
        P("crop", ("dap", "sub")),
        P("crop"),
        P(),
        P(),
        P(),
        P(),
        P(),
        P(),
        P(),
    )

    def body(pairwise_state, *rest):
        residues, channels = pairwise_state.shape[1:]
        if residues * residues * channels * 2 <= REPLICATED_PAIR_BYTES:
            return shards_replicated(pairwise_state, *rest)
        return shards(pairwise_state, *rest)

    return jax.shard_map(
        body,
        mesh=mesh,
        in_specs=placed,
        out_specs=P(("crop", "dap", "sub"), None, None),
        check_vma=False,
    )
```

```python
import jax
import jax.numpy as jnp
from jax import lax
from jax.experimental import pallas as pl
from jax.experimental.pallas import tpu as pltpu
from jax.sharding import PartitionSpec as P

REPLICATED_PAIR_BYTES = 1 << 20


def norm_layer(values, reduce_axis):
    average = jnp.mean(values, axis=reduce_axis, keepdims=True)
    centered = values - average
    variance = jnp.mean(centered * centered, axis=reduce_axis, keepdims=True)
    return centered * lax.rsqrt(variance + 1e-05)


def transition(ln_two, pair_two, transition_up_weight, transition_down_weight):
    hidden = jax.nn.relu(
        jnp.dot(ln_two, transition_up_weight, preferred_element_type=jnp.float32)
    ).astype(jnp.bfloat16)
    return (
        pair_two.astype(jnp.float32)
        + jnp.dot(hidden, transition_down_weight, preferred_element_type=jnp.float32)
    ).astype(jnp.bfloat16)


def layer_norm(values):
    count = values.shape[-1]
    centered = values - jnp.sum(values, axis=-1, keepdims=True) * (1.0 / count)
    variance = jnp.sum(centered * centered, axis=-1, keepdims=True) * (1.0 / count)
    return centered * lax.rsqrt(variance + 1e-05)


def first_row(rows):
    return (lax.axis_index("dap") * lax.axis_size("sub") + lax.axis_index("sub")) * rows


def pack_kernel(
    mask_hbm,
    keep_hbm,
    state_hbm,
    weight_hbm,
    pair_hbm,
    out_ref,
    mask_ref,
    keep_ref,
    state_ref,
    weight_ref,
    wide_ref,
    sems,
):
    rows, residues, wide = pair_hbm.shape
    sequences = state_ref.shape[0]
    base = rows * residues
    start = first_row(rows)
    second_core = lax.axis_index("sub") == 1
    loads = [
        pltpu.make_async_copy(state_hbm, state_ref, sems.at[0]),
        pltpu.make_async_copy(weight_hbm, weight_ref, sems.at[1]),
        pltpu.make_async_copy(keep_hbm, keep_ref, sems.at[2]),
        pltpu.make_async_copy(mask_hbm, mask_ref, sems.at[3]),
    ] + [
        pltpu.make_async_copy(
            pair_hbm.at[row], out_ref.at[pl.ds(row * residues, residues)], sems.at[4 + row]
        )
        for row in range(rows)
    ]
    for load in loads:
        load.start()
    loads[0].wait()
    wide_ref[...] = state_ref[...].astype(jnp.float32)
    normed_rows = [layer_norm(wide_ref[:, row]).astype(jnp.bfloat16) for row in range(rows)]
    eye = lax.broadcasted_iota(jnp.int32, (sequences, sequences), 0) == lax.broadcasted_iota(
        jnp.int32, (sequences, sequences), 1
    )
    lefts, rights, keeps = [], [], []
    for load in loads[1:]:
        load.wait()
    for row in range(rows):
        present = mask_ref[start + row].astype(jnp.float32)
        keep_row = keep_ref[row : row + 1].astype(jnp.float32) * present
        keep_column = jnp.sum(
            jnp.where(eye, jnp.broadcast_to(keep_row, eye.shape), 0.0), axis=1, keepdims=True
        )
        normed = normed_rows[row]
        last = (((1,), (1,)), ((), ()))
        left = lax.dot_general(weight_ref[0], normed, last, preferred_element_type=jnp.float32)
        right = lax.dot_general(normed, weight_ref[1], last, preferred_element_type=jnp.float32)
        lefts.append(left * keep_row)
        rights.append(right * keep_column)
        keeps.append(keep_row)
    left = jnp.concatenate(lefts, axis=1)
    right = jnp.concatenate(rights, axis=1)
    first = jnp.concatenate([right, left], axis=1)
    other = jnp.concatenate([left, right], axis=1)
    out_ref[base : base + sequences] = jnp.where(second_core, other, first).astype(jnp.bfloat16)
    keep = jnp.concatenate(
        keeps + [jnp.zeros((16 - rows, sequences), jnp.float32)], axis=0
    )
    out_ref[base + sequences :] = jnp.concatenate(
        [keep, jnp.zeros((16, wide - sequences), jnp.float32)], axis=1
    ).astype(jnp.bfloat16)


def update_kernel(
    mask_ref,
    held_ref,
    other_ref,
    outer_ref,
    triangle_ref,
    gate_ref,
    output_ref,
    up_ref,
    down_ref,
    out_ref,
    block_ref,
    left_ref,
    right_ref,
    keep_ref,
    outer_product_ref,
    pair_ref,
    pair_one_ref,
    ln_one_ref,
):
    rows, residues, wide = out_ref.shape
    cores, chips = 2, held_ref.shape[0]
    channels = outer_ref.shape[0]
    sequences = channels
    base = rows * residues
    group = cores * rows
    start = first_row(rows)
    second_core = lax.axis_index("sub") == 1
    bf16 = jnp.bfloat16
    f32 = jnp.float32

    block_ref[...] = jnp.zeros_like(block_ref)
    for d in range(channels):
        weight = outer_ref[d]
        for part in range(group):
            block_ref[
                (d * group + part) * channels : (d * group + part + 1) * channels,
                part * wide : (part + 1) * wide,
            ] = weight

    lane = lax.broadcasted_iota(jnp.int32, (channels, wide), 1)
    lane_block = lane // channels
    for chip in range(chips):
        place = xor_place(chip, chips)
        mine, other = held_ref[place], other_ref[place]
        blocks = [jnp.where(second_core, other, mine), jnp.where(second_core, mine, other)]
        packed = [block[base : base + sequences].astype(f32) for block in blocks]
        right = jnp.where(lane < wide // 2, packed[0], packed[1]).astype(bf16)
        for copy in range(group):
            right_ref[copy * sequences : (copy + 1) * sequences, chip * wide : (chip + 1) * wide] = right
        for core in range(cores):
            for row in range(rows):
                residue = (chip * cores + core) * rows + row
                at = (rows if core == 0 else 0) + row
                left_ref[residue] = jnp.where(lane_block == at, packed[core], 0.0)
            presence = blocks[core][base + sequences :].astype(f32)
            keep_ref[(chip * cores + core) * rows : (chip * cores + core + 1) * rows] = presence[:rows]
            pair_ref[(chip * cores + core) * rows : (chip * cores + core + 1) * rows] = (
                blocks[core][:base].astype(f32).reshape(rows, residues, wide)
            )

    last = (((1,), (1,)), ((), ()))
    keep = keep_ref[...].astype(bf16)
    count = lax.dot_general(keep, keep, last, preferred_element_type=f32)
    inverse = 1.0 / jnp.maximum(count, 1.0)

    step = 8
    for first in range(0, channels, step):
        left = jnp.concatenate(
            [left_ref[:, d] for d in range(first, first + step)], axis=0
        ).astype(bf16)
        outer = jnp.dot(left, right_ref[...], preferred_element_type=f32).astype(bf16)
        for d in range(first, first + step):
            for chip in range(chips):
                outer_product_ref[
                    chip * residues : (chip + 1) * residues, d * wide : (d + 1) * wide
                ] = outer[
                    (d - first) * residues : (d - first + 1) * residues,
                    chip * wide : (chip + 1) * wide,
                ]
    numerator = jnp.dot(outer_product_ref[...], block_ref[...], preferred_element_type=f32)

    for k in range(residues):
        chip, part = k // group, k % group
        opm = numerator[
            chip * residues : (chip + 1) * residues, part * wide : (part + 1) * wide
        ] * jnp.broadcast_to(inverse[:, k : k + 1], (residues, wide))
        pair_one = (pair_ref[:, k] + opm).astype(bf16).astype(f32)
        pair_one_ref[k] = pair_one
        ln_one_ref[k] = layer_norm(pair_one)

    ln_all = ln_one_ref[...].reshape(residues * residues, wide).astype(bf16)
    gate_value = jnp.dot(ln_all, triangle_ref[2], preferred_element_type=f32)
    value = jnp.dot(ln_all, triangle_ref[3], preferred_element_type=f32)
    right_tri = (jax.nn.sigmoid(gate_value) * value).astype(bf16).astype(f32)

    mask_column = jnp.zeros((residues, 1), f32)
    place = lax.broadcasted_iota(jnp.int32, (residues, 1), 0)
    for k in range(residues):
        mask_column = jnp.where(place == k, mask_ref[k].astype(f32), mask_column)

    own_pair = jnp.concatenate([pair_one_ref[:, start + row] for row in range(rows)], axis=0)
    own_ln = jnp.concatenate([ln_one_ref[:, start + row] for row in range(rows)], axis=0).astype(bf16)
    gate_value = jnp.dot(own_ln, triangle_ref[0], preferred_element_type=f32)
    value = jnp.dot(own_ln, triangle_ref[1], preferred_element_type=f32)
    left_tri = jax.nn.sigmoid(gate_value) * value * jnp.concatenate([mask_column] * rows, axis=0)
    left_tri = left_tri.astype(bf16).astype(f32)
    products = []
    for row in range(rows):
        total = jnp.zeros((residues, wide), f32)
        for k in range(residues):
            at = row * residues + k
            total += left_tri[at : at + 1] * right_tri[k * residues : (k + 1) * residues]
        products.append(total * (mask_column * mask_ref[start + row].astype(f32)))
    product = jnp.concatenate(products, axis=0).astype(bf16).astype(f32)
    normed = layer_norm(product).astype(bf16)
    update = jnp.dot(normed, output_ref[...], preferred_element_type=f32)
    gate_out = jax.nn.sigmoid(jnp.dot(own_ln, gate_ref[...], preferred_element_type=f32))
    pair_two = (own_pair + gate_out * update).astype(bf16).astype(f32)
    ln_two = layer_norm(pair_two).astype(bf16)
    hidden = jnp.maximum(jnp.dot(ln_two, up_ref[...], preferred_element_type=f32), 0.0).astype(bf16)
    result = pair_two + jnp.dot(hidden, down_ref[...], preferred_element_type=f32)
    out_ref[...] = result.astype(bf16).reshape(rows, residues, wide)


def gather_all(block):
    dap_count = lax.axis_size("dap")
    held = block[None]
    step = dap_count // 2
    while step:
        got = lax.ppermute(held, "dap", [(src, src ^ step) for src in range(dap_count)])
        held = jnp.concatenate([held, got], axis=0)
        step //= 2
    return held, lax.ppermute(held, "sub", [(0, 1), (1, 0)])


def xor_place(chip, chips):
    difference = lax.bitwise_xor(lax.axis_index("dap"), chip)
    place = 0
    step, bit = chips // 2, 1
    while step:
        place = place + jnp.where(lax.bitwise_and(difference, step) != 0, bit, 0)
        step //= 2
        bit *= 2
    return place


def shards_replicated(
    pairwise_state,
    alignment_state,
    alignment_mask,
    residue_crop_mask,
    outer_input_weight,
    outer_output_weight,
    triangle_input_weight,
    triangle_gate,
    triangle_output_weight,
    transition_up_weight,
    transition_down_weight,
):
    rows, residues, wide = pairwise_state.shape
    sequences = alignment_state.shape[0]
    channels = outer_input_weight.shape[2]
    scalar = pl.BlockSpec(memory_space=pltpu.SMEM)
    vector = pl.BlockSpec(memory_space=pltpu.VMEM)
    params = pltpu.CompilerParams(vmem_limit_bytes=40 << 20)
    hbm = pl.BlockSpec(memory_space=pltpu.HBM)
    packed = pl.pallas_call(
        pack_kernel,
        out_shape=jax.ShapeDtypeStruct((rows * residues + sequences + 16, wide), jnp.bfloat16),
        in_specs=[hbm] * 5,
        out_specs=vector,
        scratch_shapes=[
            pltpu.SMEM((residues,), jnp.int32),
            pltpu.VMEM((rows, sequences), jnp.int32),
            pltpu.VMEM(alignment_state.shape, jnp.bfloat16),
            pltpu.VMEM((2, channels, alignment_state.shape[2]), jnp.bfloat16),
            pltpu.VMEM(alignment_state.shape, jnp.float32),
            pltpu.SemaphoreType.DMA((4 + rows,)),
        ],
        compiler_params=pltpu.CompilerParams(vmem_limit_bytes=63 << 20),
    )(
        residue_crop_mask,
        alignment_mask.T,
        alignment_state,
        outer_input_weight.transpose(0, 2, 1),
        pairwise_state,
    )
    held, other = gather_all(packed)
    cores, chips = 2, held.shape[0]
    group = cores * rows
    return pl.pallas_call(
        update_kernel,
        out_shape=jax.ShapeDtypeStruct(pairwise_state.shape, jnp.bfloat16),
        in_specs=[scalar] + [vector] * 8,
        out_specs=vector,
        scratch_shapes=[
            pltpu.VMEM((channels * group * channels, group * wide), jnp.bfloat16),
            pltpu.VMEM((residues, channels, wide), jnp.float32),
            pltpu.VMEM((group * sequences, chips * wide), jnp.bfloat16),
            pltpu.VMEM((residues, wide), jnp.float32),
            pltpu.VMEM((chips * residues, channels * wide), jnp.bfloat16),
            pltpu.VMEM((residues, residues, wide), jnp.float32),
            pltpu.VMEM((residues, residues, wide), jnp.float32),
            pltpu.VMEM((residues, residues, wide), jnp.float32),
        ],
        compiler_params=params,
    )(
        residue_crop_mask,
        held,
        other,
        outer_output_weight,
        triangle_input_weight,
        triangle_gate,
        triangle_output_weight,
        transition_up_weight,
        transition_down_weight,
    )


def shards(
    pairwise_state,
    alignment_state,
    alignment_mask,
    residue_crop_mask,
    outer_input_weight,
    outer_output_weight,
    triangle_input_weight,
    triangle_gate,
    triangle_output_weight,
    transition_up_weight,
    transition_down_weight,
):
    row_count = pairwise_state.shape[0]
    start_row = lax.axis_index(("dap", "sub")) * row_count
    row_presence_mask = lax.dynamic_slice_in_dim(residue_crop_mask, start_row, row_count, 0).astype(
        jnp.float32
    )
    full_mask = residue_crop_mask.astype(jnp.float32)
    alignment_keep = alignment_mask.astype(jnp.float32) * row_presence_mask[None, :]
    alignment_normed = norm_layer(alignment_state.astype(jnp.float32), -1).astype(jnp.bfloat16)
    left_alignment = (
        jnp.einsum(
            "pxm,my->pxy",
            alignment_normed,
            outer_input_weight[0],
            preferred_element_type=jnp.float32,
        )
        * alignment_keep[:, :, None]
    ).astype(jnp.bfloat16)
    right_alignment = (
        jnp.einsum(
            "pxm,my->pxy",
            alignment_normed,
            outer_input_weight[1],
            preferred_element_type=jnp.float32,
        )
        * alignment_keep[:, :, None]
    ).astype(jnp.bfloat16)
    inner_alignment = jnp.einsum(
        "tqu,ulx->tqlx", left_alignment, outer_output_weight, preferred_element_type=jnp.float32
    ).astype(jnp.bfloat16)
    right_portion = lax.all_gather(right_alignment, ("dap", "sub"), axis=1, tiled=True)
    keep_portion = lax.all_gather(
        alignment_keep.astype(jnp.bfloat16), ("dap", "sub"), axis=1, tiled=True
    )
    numerator_sum = jnp.einsum(
        "zkwv,znw->knv", inner_alignment, right_portion, preferred_element_type=jnp.float32
    )
    pair_norm_count = jnp.einsum("cf,cg->fg", alignment_keep, keep_portion.astype(jnp.float32))
    block_part = numerator_sum / jnp.maximum(pair_norm_count, 1.0)[:, :, None]
    pair_one = (pairwise_state.astype(jnp.float32) + block_part).astype(jnp.bfloat16)
    ln_one = norm_layer(pair_one.astype(jnp.float32), -1).astype(jnp.bfloat16)
    pair_keep = row_presence_mask[:, None] * full_mask[None, :]

    def operand(gate_w, proj_w):
        gate_val = jnp.einsum("ijc,cd->dij", ln_one, gate_w, preferred_element_type=jnp.float32)
        proj_val = jnp.einsum("ijc,cd->dij", ln_one, proj_w, preferred_element_type=jnp.float32)
        return (jax.nn.sigmoid(gate_val) * proj_val * pair_keep[None]).astype(jnp.bfloat16)

    left_tri = operand(triangle_input_weight[0], triangle_input_weight[1])
    right_tri = operand(triangle_input_weight[2], triangle_input_weight[3])
    near_right = lax.all_gather(right_tri, "sub", axis=1, tiled=True)
    left_cols, right_all = (
        lax.all_to_all(left_tri, "dap", split_axis=0, concat_axis=1, tiled=True),
        lax.all_to_all(near_right, "dap", split_axis=0, concat_axis=1, tiled=True),
    )
    product = jnp.einsum(
        "cik,cjk->cij", left_cols, right_all, preferred_element_type=jnp.float32
    ).astype(jnp.bfloat16)
    returned = lax.all_to_all(product, "dap", split_axis=1, concat_axis=0, tiled=True)
    normed = norm_layer(returned.astype(jnp.float32), 0).astype(jnp.bfloat16)
    update = jnp.einsum(
        "cij,cd->ijd", normed, triangle_output_weight, preferred_element_type=jnp.float32
    )
    gate_out = jax.nn.sigmoid(
        jnp.einsum("ijc,cd->ijd", ln_one, triangle_gate, preferred_element_type=jnp.float32)
    )
    pair_two = (pair_one.astype(jnp.float32) + gate_out * update).astype(jnp.bfloat16)
    ln_two = norm_layer(pair_two.astype(jnp.float32), -1).astype(jnp.bfloat16)

    def step(row_pair):
        return transition(*row_pair, transition_up_weight, transition_down_weight)

    return lax.map(step, (ln_two, pair_two))


def solution(mesh):
    placed = (
        P(("crop", "dap", "sub"), None, None),
        P("crop", ("dap", "sub"), None),
        P("crop", ("dap", "sub")),
        P("crop"),
        P(),
        P(),
        P(),
        P(),
        P(),
        P(),
        P(),
    )

    def body(pairwise_state, *rest):
        residues, channels = pairwise_state.shape[1:]
        if residues * residues * channels * 2 <= REPLICATED_PAIR_BYTES:
            return shards_replicated(pairwise_state, *rest)
        return shards(pairwise_state, *rest)

    return jax.shard_map(
        body,
        mesh=mesh,
        in_specs=placed,
        out_specs=P(("crop", "dap", "sub"), None, None),
        check_vma=False,
    )
```

```python
import jax
import jax.numpy as jnp
from jax import lax
from jax.experimental import pallas as pl
from jax.experimental.pallas import tpu as pltpu
from jax.sharding import PartitionSpec as P

REPLICATED_PAIR_BYTES = 1 << 20


def norm_layer(values, reduce_axis):
    average = jnp.mean(values, axis=reduce_axis, keepdims=True)
    centered = values - average
    variance = jnp.mean(centered * centered, axis=reduce_axis, keepdims=True)
    return centered * lax.rsqrt(variance + 1e-05)


def transition(ln_two, pair_two, transition_up_weight, transition_down_weight):
    hidden = jax.nn.relu(
        jnp.dot(ln_two, transition_up_weight, preferred_element_type=jnp.float32)
    ).astype(jnp.bfloat16)
    return (
        pair_two.astype(jnp.float32)
        + jnp.dot(hidden, transition_down_weight, preferred_element_type=jnp.float32)
    ).astype(jnp.bfloat16)


def layer_norm(values):
    count = values.shape[-1]
    centered = values - jnp.sum(values, axis=-1, keepdims=True) * (1.0 / count)
    variance = jnp.sum(centered * centered, axis=-1, keepdims=True) * (1.0 / count)
    return centered * lax.rsqrt(variance + 1e-05)


def first_row(rows):
    return (lax.axis_index("dap") * lax.axis_size("sub") + lax.axis_index("sub")) * rows


def pack_kernel(
    mask_hbm,
    keep_hbm,
    state_hbm,
    weight_hbm,
    pair_hbm,
    out_ref,
    mask_ref,
    keep_ref,
    state_ref,
    weight_ref,
    wide_ref,
    sems,
):
    rows, residues, wide = pair_hbm.shape
    sequences = state_ref.shape[0]
    base = rows * residues
    start = first_row(rows)
    second_core = lax.axis_index("sub") == 1
    loads = [
        pltpu.make_async_copy(state_hbm, state_ref, sems.at[0]),
        pltpu.make_async_copy(weight_hbm, weight_ref, sems.at[1]),
        pltpu.make_async_copy(keep_hbm, keep_ref, sems.at[2]),
        pltpu.make_async_copy(mask_hbm, mask_ref, sems.at[3]),
    ] + [
        pltpu.make_async_copy(
            pair_hbm.at[row], out_ref.at[pl.ds(row * residues, residues)], sems.at[4 + row]
        )
        for row in range(rows)
    ]
    for load in loads:
        load.start()
    loads[0].wait()
    wide_ref[...] = state_ref[...].astype(jnp.float32)
    normed_rows = [layer_norm(wide_ref[:, row]).astype(jnp.bfloat16) for row in range(rows)]
    eye = lax.broadcasted_iota(jnp.int32, (sequences, sequences), 0) == lax.broadcasted_iota(
        jnp.int32, (sequences, sequences), 1
    )
    lefts, rights, keeps = [], [], []
    for load in loads[1:]:
        load.wait()
    for row in range(rows):
        present = mask_ref[start + row].astype(jnp.float32)
        keep_row = keep_ref[row : row + 1].astype(jnp.float32) * present
        keep_column = jnp.sum(
            jnp.where(eye, jnp.broadcast_to(keep_row, eye.shape), 0.0), axis=1, keepdims=True
        )
        normed = normed_rows[row]
        last = (((1,), (1,)), ((), ()))
        left = lax.dot_general(weight_ref[0], normed, last, preferred_element_type=jnp.float32)
        right = lax.dot_general(normed, weight_ref[1], last, preferred_element_type=jnp.float32)
        lefts.append(left * keep_row)
        rights.append(right * keep_column)
        keeps.append(keep_row)
    left = jnp.concatenate(lefts, axis=1)
    right = jnp.concatenate(rights, axis=1)
    first = jnp.concatenate([right, left], axis=1)
    other = jnp.concatenate([left, right], axis=1)
    out_ref[base : base + sequences] = jnp.where(second_core, other, first).astype(jnp.bfloat16)
    keep = jnp.concatenate(
        keeps + [jnp.zeros((16 - rows, sequences), jnp.float32)], axis=0
    )
    out_ref[base + sequences :] = jnp.concatenate(
        [keep, jnp.zeros((16, wide - sequences), jnp.float32)], axis=1
    ).astype(jnp.bfloat16)


def weight_kernel(outer_ref, packed_ref, block_ref, held_ref):
    channels, _, wide = outer_ref.shape
    group = block_ref.shape[1] // wide
    held_ref[0] = packed_ref[...]
    block_ref[...] = jnp.zeros_like(block_ref)
    for d in range(channels):
        weight = outer_ref[d]
        for part in range(group):
            block_ref[
                (d * group + part) * channels : (d * group + part + 1) * channels,
                part * wide : (part + 1) * wide,
            ] = weight


def update_kernel(
    mask_ref,
    held_ref,
    other_ref,
    block_ref,
    triangle_ref,
    gate_ref,
    output_ref,
    up_ref,
    down_ref,
    out_ref,
    left_ref,
    right_ref,
    keep_ref,
    outer_product_ref,
    pair_ref,
    pair_one_ref,
    ln_one_ref,
):
    rows, residues, wide = out_ref.shape
    cores, chips = 2, held_ref.shape[0]
    sequences, channels = left_ref.shape[2] // (cores * rows), left_ref.shape[1]
    base = rows * residues
    group = cores * rows
    start = first_row(rows)
    second_core = lax.axis_index("sub") == 1
    bf16 = jnp.bfloat16
    f32 = jnp.float32

    lane = lax.broadcasted_iota(jnp.int32, (channels, wide), 1)
    lane_block = lane // channels
    for chip in range(chips):
        places = [block_place(chip, core, chips) for core in range(cores)]
        blocks = [
            jnp.where(second_core, other_ref[places[0]], held_ref[places[0]]),
            jnp.where(second_core, held_ref[places[1]], other_ref[places[1]]),
        ]
        packed = [block[base : base + sequences].astype(f32) for block in blocks]
        right = jnp.where(lane < wide // 2, packed[0], packed[1]).astype(bf16)
        for copy in range(group):
            right_ref[copy * sequences : (copy + 1) * sequences, chip * wide : (chip + 1) * wide] = right
        for core in range(cores):
            for row in range(rows):
                residue = (chip * cores + core) * rows + row
                at = (rows if core == 0 else 0) + row
                left_ref[residue] = jnp.where(lane_block == at, packed[core], 0.0)
            presence = blocks[core][base + sequences :].astype(f32)
            keep_ref[(chip * cores + core) * rows : (chip * cores + core + 1) * rows] = presence[:rows]
            pair_ref[(chip * cores + core) * rows : (chip * cores + core + 1) * rows] = (
                blocks[core][:base].astype(f32).reshape(rows, residues, wide)
            )

    last = (((1,), (1,)), ((), ()))
    keep = keep_ref[...].astype(bf16)
    count = lax.dot_general(keep, keep, last, preferred_element_type=f32)
    inverse = 1.0 / jnp.maximum(count, 1.0)

    step = 8
    for first in range(0, channels, step):
        left = jnp.concatenate(
            [left_ref[:, d] for d in range(first, first + step)], axis=0
        ).astype(bf16)
        outer = jnp.dot(left, right_ref[...], preferred_element_type=f32).astype(bf16)
        for d in range(first, first + step):
            for chip in range(chips):
                outer_product_ref[
                    chip * residues : (chip + 1) * residues, d * wide : (d + 1) * wide
                ] = outer[
                    (d - first) * residues : (d - first + 1) * residues,
                    chip * wide : (chip + 1) * wide,
                ]
    numerator = jnp.dot(outer_product_ref[...], block_ref[...], preferred_element_type=f32)

    for k in range(residues):
        chip, part = k // group, k % group
        opm = numerator[
            chip * residues : (chip + 1) * residues, part * wide : (part + 1) * wide
        ] * jnp.broadcast_to(inverse[:, k : k + 1], (residues, wide))
        pair_one = (pair_ref[:, k] + opm).astype(bf16).astype(f32)
        pair_one_ref[k] = pair_one
        ln_one_ref[k] = layer_norm(pair_one)

    ln_all = ln_one_ref[...].reshape(residues * residues, wide).astype(bf16)
    gate_value = jnp.dot(ln_all, triangle_ref[2], preferred_element_type=f32)
    value = jnp.dot(ln_all, triangle_ref[3], preferred_element_type=f32)
    right_tri = (jax.nn.sigmoid(gate_value) * value).astype(bf16).astype(f32)

    mask_column = jnp.zeros((residues, 1), f32)
    place = lax.broadcasted_iota(jnp.int32, (residues, 1), 0)
    for k in range(residues):
        mask_column = jnp.where(place == k, mask_ref[k].astype(f32), mask_column)

    own_pair = jnp.concatenate([pair_one_ref[:, start + row] for row in range(rows)], axis=0)
    own_ln = jnp.concatenate([ln_one_ref[:, start + row] for row in range(rows)], axis=0).astype(bf16)
    gate_value = jnp.dot(own_ln, triangle_ref[0], preferred_element_type=f32)
    value = jnp.dot(own_ln, triangle_ref[1], preferred_element_type=f32)
    left_tri = jax.nn.sigmoid(gate_value) * value * jnp.concatenate([mask_column] * rows, axis=0)
    left_tri = left_tri.astype(bf16).astype(f32)
    products = []
    for row in range(rows):
        total = jnp.zeros((residues, wide), f32)
        for k in range(residues):
            at = row * residues + k
            total += left_tri[at : at + 1] * right_tri[k * residues : (k + 1) * residues]
        products.append(total * (mask_column * mask_ref[start + row].astype(f32)))
    product = jnp.concatenate(products, axis=0).astype(bf16).astype(f32)
    normed = layer_norm(product).astype(bf16)
    update = jnp.dot(normed, output_ref[...], preferred_element_type=f32)
    gate_out = jax.nn.sigmoid(jnp.dot(own_ln, gate_ref[...], preferred_element_type=f32))
    pair_two = (own_pair + gate_out * update).astype(bf16).astype(f32)
    ln_two = layer_norm(pair_two).astype(bf16)
    hidden = jnp.maximum(jnp.dot(ln_two, up_ref[...], preferred_element_type=f32), 0.0).astype(bf16)
    result = pair_two + jnp.dot(hidden, down_ref[...], preferred_element_type=f32)
    out_ref[...] = result.astype(bf16).reshape(rows, residues, wide)


def stage_steps(dap_count, core):
    low = [1 << bit for bit in range(dap_count.bit_length() - 2)]
    steps = [dap_count // 2] + low
    return steps if core == 0 else steps[-1:] + steps[:-1]


def double(held, dap_count, stage):
    pairs = []
    for core in range(2):
        step = stage_steps(dap_count, core)[stage]
        pairs += [(2 * chip + core, 2 * (chip ^ step) + core) for chip in range(dap_count)]
    return lax.ppermute(held, ("dap", "sub"), pairs)


def block_place(chip, core, chips):
    difference = lax.bitwise_xor(lax.axis_index("dap"), chip)
    place = 0
    for stage, step in enumerate(stage_steps(chips, core)):
        place = place + jnp.where(lax.bitwise_and(difference, step) != 0, 1 << stage, 0)
    return place


def shards_replicated(
    pairwise_state,
    alignment_state,
    alignment_mask,
    residue_crop_mask,
    outer_input_weight,
    outer_output_weight,
    triangle_input_weight,
    triangle_gate,
    triangle_output_weight,
    transition_up_weight,
    transition_down_weight,
):
    rows, residues, wide = pairwise_state.shape
    sequences = alignment_state.shape[0]
    channels = outer_input_weight.shape[2]
    scalar = pl.BlockSpec(memory_space=pltpu.SMEM)
    vector = pl.BlockSpec(memory_space=pltpu.VMEM)
    params = pltpu.CompilerParams(vmem_limit_bytes=32 << 20)
    hbm = pl.BlockSpec(memory_space=pltpu.HBM)
    packed = pl.pallas_call(
        pack_kernel,
        out_shape=jax.ShapeDtypeStruct((rows * residues + sequences + 16, wide), jnp.bfloat16),
        in_specs=[hbm] * 5,
        out_specs=vector,
        scratch_shapes=[
            pltpu.SMEM((residues,), jnp.int32),
            pltpu.VMEM((rows, sequences), jnp.int32),
            pltpu.VMEM(alignment_state.shape, jnp.bfloat16),
            pltpu.VMEM((2, channels, alignment_state.shape[2]), jnp.bfloat16),
            pltpu.VMEM(alignment_state.shape, jnp.float32),
            pltpu.SemaphoreType.DMA((4 + rows,)),
        ],
        compiler_params=pltpu.CompilerParams(vmem_limit_bytes=63 << 20),
    )(
        residue_crop_mask,
        alignment_mask.T,
        alignment_state,
        outer_input_weight.transpose(0, 2, 1),
        pairwise_state,
    )
    dap_count, cores = lax.axis_size("dap"), lax.axis_size("sub")
    group = cores * rows
    got = double(packed[None], dap_count, 0)
    block_weight, held = pl.pallas_call(
        weight_kernel,
        out_shape=(
            jax.ShapeDtypeStruct((channels * group * channels, group * wide), jnp.bfloat16),
            jax.ShapeDtypeStruct((1,) + packed.shape, jnp.bfloat16),
        ),
        in_specs=[vector] * 2,
        out_specs=(vector, vector),
        compiler_params=pltpu.CompilerParams(vmem_limit_bytes=16 << 20),
        cost_estimate=pl.CostEstimate(flops=0, bytes_accessed=6 << 20, transcendentals=0),
    )(outer_output_weight, packed)
    for stage in range(1, dap_count.bit_length()):
        held = jnp.concatenate([held, got], axis=0)
        if stage < dap_count.bit_length() - 1:
            got = double(held, dap_count, stage)
    other = lax.ppermute(held, "sub", [(0, 1), (1, 0)])
    chips = held.shape[0]
    return pl.pallas_call(
        update_kernel,
        out_shape=jax.ShapeDtypeStruct(pairwise_state.shape, jnp.bfloat16),
        in_specs=[scalar] + [vector] * 8,
        out_specs=vector,
        scratch_shapes=[
            pltpu.VMEM((residues, channels, wide), jnp.float32),
            pltpu.VMEM((group * sequences, chips * wide), jnp.bfloat16),
            pltpu.VMEM((residues, wide), jnp.float32),
            pltpu.VMEM((chips * residues, channels * wide), jnp.bfloat16),
            pltpu.VMEM((residues, residues, wide), jnp.float32),
            pltpu.VMEM((residues, residues, wide), jnp.float32),
            pltpu.VMEM((residues, residues, wide), jnp.float32),
        ],
        compiler_params=params,
    )(
        residue_crop_mask,
        held,
        other,
        block_weight,
        triangle_input_weight,
        triangle_gate,
        triangle_output_weight,
        transition_up_weight,
        transition_down_weight,
    )


def shards(
    pairwise_state,
    alignment_state,
    alignment_mask,
    residue_crop_mask,
    outer_input_weight,
    outer_output_weight,
    triangle_input_weight,
    triangle_gate,
    triangle_output_weight,
    transition_up_weight,
    transition_down_weight,
):
    row_count = pairwise_state.shape[0]
    start_row = lax.axis_index(("dap", "sub")) * row_count
    row_presence_mask = lax.dynamic_slice_in_dim(residue_crop_mask, start_row, row_count, 0).astype(
        jnp.float32
    )
    full_mask = residue_crop_mask.astype(jnp.float32)
    alignment_keep = alignment_mask.astype(jnp.float32) * row_presence_mask[None, :]
    alignment_normed = norm_layer(alignment_state.astype(jnp.float32), -1).astype(jnp.bfloat16)
    left_alignment = (
        jnp.einsum(
            "pxm,my->pxy",
            alignment_normed,
            outer_input_weight[0],
            preferred_element_type=jnp.float32,
        )
        * alignment_keep[:, :, None]
    ).astype(jnp.bfloat16)
    right_alignment = (
        jnp.einsum(
            "pxm,my->pxy",
            alignment_normed,
            outer_input_weight[1],
            preferred_element_type=jnp.float32,
        )
        * alignment_keep[:, :, None]
    ).astype(jnp.bfloat16)
    inner_alignment = jnp.einsum(
        "tqu,ulx->tqlx", left_alignment, outer_output_weight, preferred_element_type=jnp.float32
    ).astype(jnp.bfloat16)
    right_portion = lax.all_gather(right_alignment, ("dap", "sub"), axis=1, tiled=True)
    keep_portion = lax.all_gather(
        alignment_keep.astype(jnp.bfloat16), ("dap", "sub"), axis=1, tiled=True
    )
    numerator_sum = jnp.einsum(
        "zkwv,znw->knv", inner_alignment, right_portion, preferred_element_type=jnp.float32
    )
    pair_norm_count = jnp.einsum("cf,cg->fg", alignment_keep, keep_portion.astype(jnp.float32))
    block_part = numerator_sum / jnp.maximum(pair_norm_count, 1.0)[:, :, None]
    pair_one = (pairwise_state.astype(jnp.float32) + block_part).astype(jnp.bfloat16)
    ln_one = norm_layer(pair_one.astype(jnp.float32), -1).astype(jnp.bfloat16)
    pair_keep = row_presence_mask[:, None] * full_mask[None, :]

    def operand(gate_w, proj_w):
        gate_val = jnp.einsum("ijc,cd->dij", ln_one, gate_w, preferred_element_type=jnp.float32)
        proj_val = jnp.einsum("ijc,cd->dij", ln_one, proj_w, preferred_element_type=jnp.float32)
        return (jax.nn.sigmoid(gate_val) * proj_val * pair_keep[None]).astype(jnp.bfloat16)

    left_tri = operand(triangle_input_weight[0], triangle_input_weight[1])
    right_tri = operand(triangle_input_weight[2], triangle_input_weight[3])
    near_right = lax.all_gather(right_tri, "sub", axis=1, tiled=True)
    left_cols, right_all = (
        lax.all_to_all(left_tri, "dap", split_axis=0, concat_axis=1, tiled=True),
        lax.all_to_all(near_right, "dap", split_axis=0, concat_axis=1, tiled=True),
    )
    product = jnp.einsum(
        "cik,cjk->cij", left_cols, right_all, preferred_element_type=jnp.float32
    ).astype(jnp.bfloat16)
    returned = lax.all_to_all(product, "dap", split_axis=1, concat_axis=0, tiled=True)
    normed = norm_layer(returned.astype(jnp.float32), 0).astype(jnp.bfloat16)
    update = jnp.einsum(
        "cij,cd->ijd", normed, triangle_output_weight, preferred_element_type=jnp.float32
    )
    gate_out = jax.nn.sigmoid(
        jnp.einsum("ijc,cd->ijd", ln_one, triangle_gate, preferred_element_type=jnp.float32)
    )
    pair_two = (pair_one.astype(jnp.float32) + gate_out * update).astype(jnp.bfloat16)
    ln_two = norm_layer(pair_two.astype(jnp.float32), -1).astype(jnp.bfloat16)

    def step(row_pair):
        return transition(*row_pair, transition_up_weight, transition_down_weight)

    return lax.map(step, (ln_two, pair_two))


def solution(mesh):
    placed = (
        P(("crop", "dap", "sub"), None, None),
        P("crop", ("dap", "sub"), None),
        P("crop", ("dap", "sub")),
        P("crop"),
        P(),
        P(),
        P(),
        P(),
        P(),
        P(),
        P(),
    )

    small = mesh.shape["sub"] == 2 and mesh.shape["dap"] == 8

    def body(pairwise_state, *rest):
        residues, channels = pairwise_state.shape[1:]
        if small and residues * residues * channels * 2 <= REPLICATED_PAIR_BYTES:
            return shards_replicated(pairwise_state, *rest)
        return shards(pairwise_state, *rest)

    return jax.shard_map(
        body,
        mesh=mesh,
        in_specs=placed,
        out_specs=P(("crop", "dap", "sub"), None, None),
        check_vma=False,
    )
```

```python
import jax
import jax.numpy as jnp
from jax import lax
from jax.experimental import pallas as pl
from jax.experimental.pallas import tpu as pltpu
from jax.sharding import PartitionSpec as P

REPLICATED_PAIR_BYTES = 1 << 20


def norm_layer(values, reduce_axis):
    average = jnp.mean(values, axis=reduce_axis, keepdims=True)
    centered = values - average
    variance = jnp.mean(centered * centered, axis=reduce_axis, keepdims=True)
    return centered * lax.rsqrt(variance + 1e-05)


def transition(ln_two, pair_two, transition_up_weight, transition_down_weight):
    hidden = jax.nn.relu(
        jnp.dot(ln_two, transition_up_weight, preferred_element_type=jnp.float32)
    ).astype(jnp.bfloat16)
    return (
        pair_two.astype(jnp.float32)
        + jnp.dot(hidden, transition_down_weight, preferred_element_type=jnp.float32)
    ).astype(jnp.bfloat16)


def layer_norm(values):
    count = values.shape[-1]
    centered = values - jnp.sum(values, axis=-1, keepdims=True) * (1.0 / count)
    variance = jnp.sum(centered * centered, axis=-1, keepdims=True) * (1.0 / count)
    return centered * lax.rsqrt(variance + 1e-05)


def first_row(rows):
    return (lax.axis_index("dap") * lax.axis_size("sub") + lax.axis_index("sub")) * rows


def pack_kernel(
    mask_hbm,
    keep_hbm,
    state_hbm,
    weight_hbm,
    pair_hbm,
    out_ref,
    mask_ref,
    keep_ref,
    state_ref,
    weight_ref,
    wide_ref,
    sems,
):
    rows, residues, wide = pair_hbm.shape
    sequences = state_ref.shape[0]
    base = rows * residues
    start = first_row(rows)
    second_core = lax.axis_index("sub") == 1
    loads = [
        pltpu.make_async_copy(state_hbm, state_ref, sems.at[0]),
        pltpu.make_async_copy(weight_hbm, weight_ref, sems.at[1]),
        pltpu.make_async_copy(keep_hbm, keep_ref, sems.at[2]),
        pltpu.make_async_copy(mask_hbm, mask_ref, sems.at[3]),
    ] + [
        pltpu.make_async_copy(
            pair_hbm.at[row], out_ref.at[pl.ds(row * residues, residues)], sems.at[4 + row]
        )
        for row in range(rows)
    ]
    for load in loads:
        load.start()
    loads[0].wait()
    wide_ref[...] = state_ref[...].astype(jnp.float32)
    normed_rows = [layer_norm(wide_ref[:, row]).astype(jnp.bfloat16) for row in range(rows)]
    eye = lax.broadcasted_iota(jnp.int32, (sequences, sequences), 0) == lax.broadcasted_iota(
        jnp.int32, (sequences, sequences), 1
    )
    lefts, rights, keeps = [], [], []
    for load in loads[1:]:
        load.wait()
    for row in range(rows):
        present = mask_ref[start + row].astype(jnp.float32)
        keep_row = keep_ref[row : row + 1].astype(jnp.float32) * present
        keep_column = jnp.sum(
            jnp.where(eye, jnp.broadcast_to(keep_row, eye.shape), 0.0), axis=1, keepdims=True
        )
        normed = normed_rows[row]
        last = (((1,), (1,)), ((), ()))
        left = lax.dot_general(weight_ref[0], normed, last, preferred_element_type=jnp.float32)
        right = lax.dot_general(normed, weight_ref[1], last, preferred_element_type=jnp.float32)
        lefts.append(left * keep_row)
        rights.append(right * keep_column)
        keeps.append(keep_row)
    left = jnp.concatenate(lefts, axis=1)
    right = jnp.concatenate(rights, axis=1)
    first = jnp.concatenate([right, left], axis=1)
    other = jnp.concatenate([left, right], axis=1)
    out_ref[base : base + sequences] = jnp.where(second_core, other, first).astype(jnp.bfloat16)
    keep = jnp.concatenate(
        keeps + [jnp.zeros((16 - rows, sequences), jnp.float32)], axis=0
    )
    out_ref[base + sequences :] = jnp.concatenate(
        [keep, jnp.zeros((16, wide - sequences), jnp.float32)], axis=1
    ).astype(jnp.bfloat16)


def update_kernel(
    mask_ref,
    both_ref,
    mine_ref,
    other_ref,
    outer_ref,
    triangle_ref,
    gate_ref,
    output_ref,
    up_ref,
    down_ref,
    out_ref,
    block_ref,
    left_ref,
    right_ref,
    keep_ref,
    outer_product_ref,
    pair_ref,
    pair_one_ref,
    ln_one_ref,
):
    rows, residues, wide = out_ref.shape
    cores, chips = both_ref.shape[0], lax.axis_size("dap")
    channels = outer_ref.shape[0]
    sequences = channels
    base = rows * residues
    group = cores * rows
    start = first_row(rows)
    bf16 = jnp.bfloat16
    f32 = jnp.float32

    block_ref[...] = jnp.zeros_like(block_ref)
    for d in range(channels):
        weight = outer_ref[d]
        for part in range(group):
            block_ref[
                (d * group + part) * channels : (d * group + part + 1) * channels,
                part * wide : (part + 1) * wide,
            ] = weight

    lane = lax.broadcasted_iota(jnp.int32, (channels, wide), 1)
    lane_block = lane // channels
    for chip in range(chips):
        blocks = [
            chip_block(both_ref, mine_ref, other_ref, chip, core) for core in range(cores)
        ]
        packed = [block[base : base + sequences].astype(f32) for block in blocks]
        right = jnp.where(lane < wide // 2, packed[0], packed[1]).astype(bf16)
        for copy in range(group):
            right_ref[copy * sequences : (copy + 1) * sequences, chip * wide : (chip + 1) * wide] = right
        for core in range(cores):
            for row in range(rows):
                residue = (chip * cores + core) * rows + row
                at = (rows if core == 0 else 0) + row
                left_ref[residue] = jnp.where(lane_block == at, packed[core], 0.0)
            presence = blocks[core][base + sequences :].astype(f32)
            keep_ref[(chip * cores + core) * rows : (chip * cores + core + 1) * rows] = presence[:rows]
            pair_ref[(chip * cores + core) * rows : (chip * cores + core + 1) * rows] = (
                blocks[core][:base].astype(f32).reshape(rows, residues, wide)
            )

    last = (((1,), (1,)), ((), ()))
    keep = keep_ref[...].astype(bf16)
    count = lax.dot_general(keep, keep, last, preferred_element_type=f32)
    inverse = 1.0 / jnp.maximum(count, 1.0)

    step = 8
    for first in range(0, channels, step):
        left = jnp.concatenate(
            [left_ref[:, d] for d in range(first, first + step)], axis=0
        ).astype(bf16)
        outer = jnp.dot(left, right_ref[...], preferred_element_type=f32).astype(bf16)
        for d in range(first, first + step):
            for chip in range(chips):
                outer_product_ref[
                    chip * residues : (chip + 1) * residues, d * wide : (d + 1) * wide
                ] = outer[
                    (d - first) * residues : (d - first + 1) * residues,
                    chip * wide : (chip + 1) * wide,
                ]
    numerator = jnp.dot(outer_product_ref[...], block_ref[...], preferred_element_type=f32)

    for k in range(residues):
        chip, part = k // group, k % group
        opm = numerator[
            chip * residues : (chip + 1) * residues, part * wide : (part + 1) * wide
        ] * jnp.broadcast_to(inverse[:, k : k + 1], (residues, wide))
        pair_one = (pair_ref[:, k] + opm).astype(bf16).astype(f32)
        pair_one_ref[k] = pair_one
        ln_one_ref[k] = layer_norm(pair_one)

    ln_all = ln_one_ref[...].reshape(residues * residues, wide).astype(bf16)
    gate_value = jnp.dot(ln_all, triangle_ref[2], preferred_element_type=f32)
    value = jnp.dot(ln_all, triangle_ref[3], preferred_element_type=f32)
    right_tri = (jax.nn.sigmoid(gate_value) * value).astype(bf16).astype(f32)

    mask_column = jnp.zeros((residues, 1), f32)
    place = lax.broadcasted_iota(jnp.int32, (residues, 1), 0)
    for k in range(residues):
        mask_column = jnp.where(place == k, mask_ref[k].astype(f32), mask_column)

    own_pair = jnp.concatenate([pair_one_ref[:, start + row] for row in range(rows)], axis=0)
    own_ln = jnp.concatenate([ln_one_ref[:, start + row] for row in range(rows)], axis=0).astype(bf16)
    gate_value = jnp.dot(own_ln, triangle_ref[0], preferred_element_type=f32)
    value = jnp.dot(own_ln, triangle_ref[1], preferred_element_type=f32)
    left_tri = jax.nn.sigmoid(gate_value) * value * jnp.concatenate([mask_column] * rows, axis=0)
    left_tri = left_tri.astype(bf16).astype(f32)
    products = []
    for row in range(rows):
        total = jnp.zeros((residues, wide), f32)
        for k in range(residues):
            at = row * residues + k
            total += left_tri[at : at + 1] * right_tri[k * residues : (k + 1) * residues]
        products.append(total * (mask_column * mask_ref[start + row].astype(f32)))
    product = jnp.concatenate(products, axis=0).astype(bf16).astype(f32)
    normed = layer_norm(product).astype(bf16)
    update = jnp.dot(normed, output_ref[...], preferred_element_type=f32)
    gate_out = jax.nn.sigmoid(jnp.dot(own_ln, gate_ref[...], preferred_element_type=f32))
    pair_two = (own_pair + gate_out * update).astype(bf16).astype(f32)
    ln_two = layer_norm(pair_two).astype(bf16)
    hidden = jnp.maximum(jnp.dot(ln_two, up_ref[...], preferred_element_type=f32), 0.0).astype(bf16)
    result = pair_two + jnp.dot(hidden, down_ref[...], preferred_element_type=f32)
    out_ref[...] = result.astype(bf16).reshape(rows, residues, wide)


def copy_kernel(packed_ref, out_ref):
    out_ref[0] = packed_ref[...]


def chip_offsets(dap_count, core):
    near = dap_count // 2 - 1
    return list(range(1, near + 1)) if core == 0 else list(range(near + 1, dap_count))


def gather_all(packed):
    dap_count = lax.axis_size("dap")
    sibling = [(0, 1), (1, 0)]
    near = lax.ppermute(packed[None], "sub", sibling)
    own = pl.pallas_call(
        copy_kernel,
        out_shape=jax.ShapeDtypeStruct((1,) + packed.shape, packed.dtype),
        in_specs=[pl.BlockSpec(memory_space=pltpu.VMEM)],
        out_specs=pl.BlockSpec(memory_space=pltpu.VMEM),
        compiler_params=pltpu.CompilerParams(vmem_limit_bytes=4 << 20),
    )(packed)
    both = jnp.concatenate([own, near], axis=0)
    offsets = [chip_offsets(dap_count, core) for core in range(2)]
    got = []
    for turn in range(max(map(len, offsets))):
        pairs = [
            (2 * chip + core, 2 * (chip ^ offsets[core][turn]) + core)
            for core in range(2)
            for chip in range(dap_count)
            if turn < len(offsets[core])
        ]
        got.append(lax.ppermute(both, ("dap", "sub"), pairs))
    mine = jnp.concatenate(got, axis=0)
    return both, mine, lax.ppermute(mine, "sub", sibling)


def chip_block(both_ref, mine_ref, other_ref, chip, core):
    chips = lax.axis_size("dap")
    sub = lax.axis_index("sub")
    offset = lax.bitwise_xor(lax.axis_index("dap"), chip)
    near = len(chip_offsets(chips, 0))
    carrier = jnp.where(offset > near, 1, 0)
    turn = jnp.where(offset > near, offset - near, jnp.maximum(offset, 1)) - 1
    place = 2 * turn + jnp.where(carrier == core, 0, 1)
    away = jnp.where(carrier == sub, mine_ref[place], other_ref[place])
    return jnp.where(offset == 0, both_ref[jnp.where(sub == core, 0, 1)], away)


def shards_replicated(
    pairwise_state,
    alignment_state,
    alignment_mask,
    residue_crop_mask,
    outer_input_weight,
    outer_output_weight,
    triangle_input_weight,
    triangle_gate,
    triangle_output_weight,
    transition_up_weight,
    transition_down_weight,
):
    rows, residues, wide = pairwise_state.shape
    sequences = alignment_state.shape[0]
    channels = outer_input_weight.shape[2]
    scalar = pl.BlockSpec(memory_space=pltpu.SMEM)
    vector = pl.BlockSpec(memory_space=pltpu.VMEM)
    params = pltpu.CompilerParams(vmem_limit_bytes=40 << 20)
    hbm = pl.BlockSpec(memory_space=pltpu.HBM)
    packed = pl.pallas_call(
        pack_kernel,
        out_shape=jax.ShapeDtypeStruct((rows * residues + sequences + 16, wide), jnp.bfloat16),
        in_specs=[hbm] * 5,
        out_specs=vector,
        scratch_shapes=[
            pltpu.SMEM((residues,), jnp.int32),
            pltpu.VMEM((rows, sequences), jnp.int32),
            pltpu.VMEM(alignment_state.shape, jnp.bfloat16),
            pltpu.VMEM((2, channels, alignment_state.shape[2]), jnp.bfloat16),
            pltpu.VMEM(alignment_state.shape, jnp.float32),
            pltpu.SemaphoreType.DMA((4 + rows,)),
        ],
        compiler_params=pltpu.CompilerParams(vmem_limit_bytes=63 << 20),
    )(
        residue_crop_mask,
        alignment_mask.T,
        alignment_state,
        outer_input_weight.transpose(0, 2, 1),
        pairwise_state,
    )
    both, mine, other = gather_all(packed)
    cores, chips = lax.axis_size("sub"), lax.axis_size("dap")
    group = cores * rows
    return pl.pallas_call(
        update_kernel,
        out_shape=jax.ShapeDtypeStruct(pairwise_state.shape, jnp.bfloat16),
        in_specs=[scalar] + [vector] * 9,
        out_specs=vector,
        scratch_shapes=[
            pltpu.VMEM((channels * group * channels, group * wide), jnp.bfloat16),
            pltpu.VMEM((residues, channels, wide), jnp.float32),
            pltpu.VMEM((group * sequences, chips * wide), jnp.bfloat16),
            pltpu.VMEM((residues, wide), jnp.float32),
            pltpu.VMEM((chips * residues, channels * wide), jnp.bfloat16),
            pltpu.VMEM((residues, residues, wide), jnp.float32),
            pltpu.VMEM((residues, residues, wide), jnp.float32),
            pltpu.VMEM((residues, residues, wide), jnp.float32),
        ],
        compiler_params=params,
    )(
        residue_crop_mask,
        both,
        mine,
        other,
        outer_output_weight,
        triangle_input_weight,
        triangle_gate,
        triangle_output_weight,
        transition_up_weight,
        transition_down_weight,
    )


def shards(
    pairwise_state,
    alignment_state,
    alignment_mask,
    residue_crop_mask,
    outer_input_weight,
    outer_output_weight,
    triangle_input_weight,
    triangle_gate,
    triangle_output_weight,
    transition_up_weight,
    transition_down_weight,
):
    row_count = pairwise_state.shape[0]
    start_row = lax.axis_index(("dap", "sub")) * row_count
    row_presence_mask = lax.dynamic_slice_in_dim(residue_crop_mask, start_row, row_count, 0).astype(
        jnp.float32
    )
    full_mask = residue_crop_mask.astype(jnp.float32)
    alignment_keep = alignment_mask.astype(jnp.float32) * row_presence_mask[None, :]
    alignment_normed = norm_layer(alignment_state.astype(jnp.float32), -1).astype(jnp.bfloat16)
    left_alignment = (
        jnp.einsum(
            "pxm,my->pxy",
            alignment_normed,
            outer_input_weight[0],
            preferred_element_type=jnp.float32,
        )
        * alignment_keep[:, :, None]
    ).astype(jnp.bfloat16)
    right_alignment = (
        jnp.einsum(
            "pxm,my->pxy",
            alignment_normed,
            outer_input_weight[1],
            preferred_element_type=jnp.float32,
        )
        * alignment_keep[:, :, None]
    ).astype(jnp.bfloat16)
    inner_alignment = jnp.einsum(
        "tqu,ulx->tqlx", left_alignment, outer_output_weight, preferred_element_type=jnp.float32
    ).astype(jnp.bfloat16)
    right_portion = lax.all_gather(right_alignment, ("dap", "sub"), axis=1, tiled=True)
    keep_portion = lax.all_gather(
        alignment_keep.astype(jnp.bfloat16), ("dap", "sub"), axis=1, tiled=True
    )
    numerator_sum = jnp.einsum(
        "zkwv,znw->knv", inner_alignment, right_portion, preferred_element_type=jnp.float32
    )
    pair_norm_count = jnp.einsum("cf,cg->fg", alignment_keep, keep_portion.astype(jnp.float32))
    block_part = numerator_sum / jnp.maximum(pair_norm_count, 1.0)[:, :, None]
    pair_one = (pairwise_state.astype(jnp.float32) + block_part).astype(jnp.bfloat16)
    ln_one = norm_layer(pair_one.astype(jnp.float32), -1).astype(jnp.bfloat16)
    pair_keep = row_presence_mask[:, None] * full_mask[None, :]

    def operand(gate_w, proj_w):
        gate_val = jnp.einsum("ijc,cd->dij", ln_one, gate_w, preferred_element_type=jnp.float32)
        proj_val = jnp.einsum("ijc,cd->dij", ln_one, proj_w, preferred_element_type=jnp.float32)
        return (jax.nn.sigmoid(gate_val) * proj_val * pair_keep[None]).astype(jnp.bfloat16)

    left_tri = operand(triangle_input_weight[0], triangle_input_weight[1])
    right_tri = operand(triangle_input_weight[2], triangle_input_weight[3])
    near_right = lax.all_gather(right_tri, "sub", axis=1, tiled=True)
    left_cols, right_all = (
        lax.all_to_all(left_tri, "dap", split_axis=0, concat_axis=1, tiled=True),
        lax.all_to_all(near_right, "dap", split_axis=0, concat_axis=1, tiled=True),
    )
    product = jnp.einsum(
        "cik,cjk->cij", left_cols, right_all, preferred_element_type=jnp.float32
    ).astype(jnp.bfloat16)
    returned = lax.all_to_all(product, "dap", split_axis=1, concat_axis=0, tiled=True)
    normed = norm_layer(returned.astype(jnp.float32), 0).astype(jnp.bfloat16)
    update = jnp.einsum(
        "cij,cd->ijd", normed, triangle_output_weight, preferred_element_type=jnp.float32
    )
    gate_out = jax.nn.sigmoid(
        jnp.einsum("ijc,cd->ijd", ln_one, triangle_gate, preferred_element_type=jnp.float32)
    )
    pair_two = (pair_one.astype(jnp.float32) + gate_out * update).astype(jnp.bfloat16)
    ln_two = norm_layer(pair_two.astype(jnp.float32), -1).astype(jnp.bfloat16)

    def step(row_pair):
        return transition(*row_pair, transition_up_weight, transition_down_weight)

    return lax.map(step, (ln_two, pair_two))


def solution(mesh):
    placed = (
        P(("crop", "dap", "sub"), None, None),
        P("crop", ("dap", "sub"), None),
        P("crop", ("dap", "sub")),
        P("crop"),
        P(),
        P(),
        P(),
        P(),
        P(),
        P(),
        P(),
    )

    small = mesh.shape["sub"] == 2 and mesh.shape["dap"] == 8

    def body(pairwise_state, *rest):
        residues, channels = pairwise_state.shape[1:]
        if small and residues * residues * channels * 2 <= REPLICATED_PAIR_BYTES:
            return shards_replicated(pairwise_state, *rest)
        return shards(pairwise_state, *rest)

    return jax.shard_map(
        body,
        mesh=mesh,
        in_specs=placed,
        out_specs=P(("crop", "dap", "sub"), None, None),
        check_vma=False,
    )
```

```python
import jax
import jax.numpy as jnp
from jax import lax
from jax.experimental import pallas as pl
from jax.experimental.pallas import tpu as pltpu
from jax.sharding import PartitionSpec as P

REPLICATED_PAIR_BYTES = 1 << 20


def norm_layer(values, reduce_axis):
    average = jnp.mean(values, axis=reduce_axis, keepdims=True)
    centered = values - average
    variance = jnp.mean(centered * centered, axis=reduce_axis, keepdims=True)
    return centered * lax.rsqrt(variance + 1e-05)


def transition(ln_two, pair_two, transition_up_weight, transition_down_weight):
    hidden = jax.nn.relu(
        jnp.dot(ln_two, transition_up_weight, preferred_element_type=jnp.float32)
    ).astype(jnp.bfloat16)
    return (
        pair_two.astype(jnp.float32)
        + jnp.dot(hidden, transition_down_weight, preferred_element_type=jnp.float32)
    ).astype(jnp.bfloat16)


def layer_norm(values):
    count = values.shape[-1]
    centered = values - jnp.sum(values, axis=-1, keepdims=True) * (1.0 / count)
    variance = jnp.sum(centered * centered, axis=-1, keepdims=True) * (1.0 / count)
    return centered * lax.rsqrt(variance + 1e-05)


def first_row(rows):
    return (lax.axis_index("dap") * lax.axis_size("sub") + lax.axis_index("sub")) * rows


def pack_kernel(
    mask_hbm,
    keep_hbm,
    state_hbm,
    weight_hbm,
    pair_hbm,
    out_ref,
    mask_ref,
    keep_ref,
    state_ref,
    weight_ref,
    wide_ref,
    sems,
):
    rows, residues, wide = pair_hbm.shape
    sequences = state_ref.shape[0]
    base = rows * residues
    start = first_row(rows)
    second_core = lax.axis_index("sub") == 1
    loads = [
        pltpu.make_async_copy(state_hbm, state_ref, sems.at[0]),
        pltpu.make_async_copy(weight_hbm, weight_ref, sems.at[1]),
        pltpu.make_async_copy(keep_hbm, keep_ref, sems.at[2]),
        pltpu.make_async_copy(mask_hbm, mask_ref, sems.at[3]),
    ] + [
        pltpu.make_async_copy(
            pair_hbm.at[row], out_ref.at[pl.ds(row * residues, residues)], sems.at[4 + row]
        )
        for row in range(rows)
    ]
    for load in loads:
        load.start()
    loads[0].wait()
    wide_ref[...] = state_ref[...].astype(jnp.float32)
    normed_rows = [layer_norm(wide_ref[:, row]).astype(jnp.bfloat16) for row in range(rows)]
    eye = lax.broadcasted_iota(jnp.int32, (sequences, sequences), 0) == lax.broadcasted_iota(
        jnp.int32, (sequences, sequences), 1
    )
    lefts, rights, keeps = [], [], []
    for load in loads[1:]:
        load.wait()
    for row in range(rows):
        present = mask_ref[start + row].astype(jnp.float32)
        keep_row = keep_ref[row : row + 1].astype(jnp.float32) * present
        keep_column = jnp.sum(
            jnp.where(eye, jnp.broadcast_to(keep_row, eye.shape), 0.0), axis=1, keepdims=True
        )
        normed = normed_rows[row]
        last = (((1,), (1,)), ((), ()))
        left = lax.dot_general(weight_ref[0], normed, last, preferred_element_type=jnp.float32)
        right = lax.dot_general(normed, weight_ref[1], last, preferred_element_type=jnp.float32)
        lefts.append(left * keep_row)
        rights.append(right * keep_column)
        keeps.append(keep_row)
    left = jnp.concatenate(lefts, axis=1)
    right = jnp.concatenate(rights, axis=1)
    first = jnp.concatenate([right, left], axis=1)
    other = jnp.concatenate([left, right], axis=1)
    out_ref[base : base + sequences] = jnp.where(second_core, other, first).astype(jnp.bfloat16)
    keep = jnp.concatenate(
        keeps + [jnp.zeros((16 - rows, sequences), jnp.float32)], axis=0
    )
    out_ref[base + sequences :] = jnp.concatenate(
        [keep, jnp.zeros((16, wide - sequences), jnp.float32)], axis=1
    ).astype(jnp.bfloat16)


def update_kernel(
    mask_ref,
    held_ref,
    other_ref,
    outer_ref,
    triangle_ref,
    gate_ref,
    output_ref,
    up_ref,
    down_ref,
    out_ref,
    block_ref,
    left_ref,
    right_ref,
    keep_ref,
    outer_product_ref,
    pair_ref,
    pair_one_ref,
    ln_one_ref,
):
    rows, residues, wide = out_ref.shape
    cores, chips = 2, lax.axis_size("dap")
    channels = outer_ref.shape[0]
    sequences = channels
    base = rows * residues
    group = cores * rows
    start = first_row(rows)
    second_core = lax.axis_index("sub") == 1
    bf16 = jnp.bfloat16
    f32 = jnp.float32

    block_ref[...] = jnp.zeros_like(block_ref)
    for d in range(channels):
        weight = outer_ref[d]
        for part in range(group):
            block_ref[
                (d * group + part) * channels : (d * group + part + 1) * channels,
                part * wide : (part + 1) * wide,
            ] = weight

    lane = lax.broadcasted_iota(jnp.int32, (channels, wide), 1)
    lane_block = lane // channels
    for chip in range(chips):
        place = block_place(chip, chips)
        mine, other = held_ref[place], other_ref[place]
        blocks = [jnp.where(second_core, other, mine), jnp.where(second_core, mine, other)]
        packed = [block[base : base + sequences].astype(f32) for block in blocks]
        right = jnp.where(lane < wide // 2, packed[0], packed[1]).astype(bf16)
        for copy in range(group):
            right_ref[copy * sequences : (copy + 1) * sequences, chip * wide : (chip + 1) * wide] = right
        for core in range(cores):
            for row in range(rows):
                residue = (chip * cores + core) * rows + row
                at = (rows if core == 0 else 0) + row
                left_ref[residue] = jnp.where(lane_block == at, packed[core], 0.0)
            presence = blocks[core][base + sequences :].astype(f32)
            keep_ref[(chip * cores + core) * rows : (chip * cores + core + 1) * rows] = presence[:rows]
            pair_ref[(chip * cores + core) * rows : (chip * cores + core + 1) * rows] = (
                blocks[core][:base].astype(f32).reshape(rows, residues, wide)
            )

    last = (((1,), (1,)), ((), ()))
    keep = keep_ref[...].astype(bf16)
    count = lax.dot_general(keep, keep, last, preferred_element_type=f32)
    inverse = 1.0 / jnp.maximum(count, 1.0)

    step = 8
    for first in range(0, channels, step):
        left = jnp.concatenate(
            [left_ref[:, d] for d in range(first, first + step)], axis=0
        ).astype(bf16)
        outer = jnp.dot(left, right_ref[...], preferred_element_type=f32).astype(bf16)
        for d in range(first, first + step):
            for chip in range(chips):
                outer_product_ref[
                    chip * residues : (chip + 1) * residues, d * wide : (d + 1) * wide
                ] = outer[
                    (d - first) * residues : (d - first + 1) * residues,
                    chip * wide : (chip + 1) * wide,
                ]
    numerator = jnp.dot(outer_product_ref[...], block_ref[...], preferred_element_type=f32)

    for k in range(residues):
        chip, part = k // group, k % group
        opm = numerator[
            chip * residues : (chip + 1) * residues, part * wide : (part + 1) * wide
        ] * jnp.broadcast_to(inverse[:, k : k + 1], (residues, wide))
        pair_one = (pair_ref[:, k] + opm).astype(bf16).astype(f32)
        pair_one_ref[k] = pair_one
        ln_one_ref[k] = layer_norm(pair_one)

    ln_all = ln_one_ref[...].reshape(residues * residues, wide).astype(bf16)
    gate_value = jnp.dot(ln_all, triangle_ref[2], preferred_element_type=f32)
    value = jnp.dot(ln_all, triangle_ref[3], preferred_element_type=f32)
    right_tri = (jax.nn.sigmoid(gate_value) * value).astype(bf16).astype(f32)

    mask_column = jnp.zeros((residues, 1), f32)
    place = lax.broadcasted_iota(jnp.int32, (residues, 1), 0)
    for k in range(residues):
        mask_column = jnp.where(place == k, mask_ref[k].astype(f32), mask_column)

    own_pair = jnp.concatenate([pair_one_ref[:, start + row] for row in range(rows)], axis=0)
    own_ln = jnp.concatenate([ln_one_ref[:, start + row] for row in range(rows)], axis=0).astype(bf16)
    gate_value = jnp.dot(own_ln, triangle_ref[0], preferred_element_type=f32)
    value = jnp.dot(own_ln, triangle_ref[1], preferred_element_type=f32)
    left_tri = jax.nn.sigmoid(gate_value) * value * jnp.concatenate([mask_column] * rows, axis=0)
    left_tri = left_tri.astype(bf16).astype(f32)
    products = []
    for row in range(rows):
        total = jnp.zeros((residues, wide), f32)
        for k in range(residues):
            at = row * residues + k
            total += left_tri[at : at + 1] * right_tri[k * residues : (k + 1) * residues]
        products.append(total * (mask_column * mask_ref[start + row].astype(f32)))
    product = jnp.concatenate(products, axis=0).astype(bf16).astype(f32)
    normed = layer_norm(product).astype(bf16)
    update = jnp.dot(normed, output_ref[...], preferred_element_type=f32)
    gate_out = jax.nn.sigmoid(jnp.dot(own_ln, gate_ref[...], preferred_element_type=f32))
    pair_two = (own_pair + gate_out * update).astype(bf16).astype(f32)
    ln_two = layer_norm(pair_two).astype(bf16)
    hidden = jnp.maximum(jnp.dot(ln_two, up_ref[...], preferred_element_type=f32), 0.0).astype(bf16)
    result = pair_two + jnp.dot(hidden, down_ref[...], preferred_element_type=f32)
    out_ref[...] = result.astype(bf16).reshape(rows, residues, wide)


def copy_kernel(packed_ref, out_ref):
    out_ref[0] = packed_ref[...]


def gather_all(packed):
    dap_count = lax.axis_size("dap")
    half = dap_count // 2
    far = lax.ppermute(packed[None], "dap", [(src, src ^ half) for src in range(dap_count)])
    own = pl.pallas_call(
        copy_kernel,
        out_shape=jax.ShapeDtypeStruct((1,) + packed.shape, packed.dtype),
        in_specs=[pl.BlockSpec(memory_space=pltpu.VMEM)],
        out_specs=pl.BlockSpec(memory_space=pltpu.VMEM),
        compiler_params=pltpu.CompilerParams(vmem_limit_bytes=4 << 20),
    )(packed)
    both = jnp.concatenate([own, far], axis=0)
    held = [both] + [
        lax.ppermute(both, "dap", [(src, src ^ offset) for src in range(dap_count)])
        for offset in range(1, half)
    ]
    held = jnp.concatenate(held, axis=0)
    return held, lax.ppermute(held, "sub", [(0, 1), (1, 0)])


def block_place(chip, chips):
    offset = lax.bitwise_xor(lax.axis_index("dap"), chip)
    half = chips // 2
    return jnp.where(offset >= half, 2 * (offset - half) + 1, 2 * offset)


def shards_replicated(
    pairwise_state,
    alignment_state,
    alignment_mask,
    residue_crop_mask,
    outer_input_weight,
    outer_output_weight,
    triangle_input_weight,
    triangle_gate,
    triangle_output_weight,
    transition_up_weight,
    transition_down_weight,
):
    rows, residues, wide = pairwise_state.shape
    sequences = alignment_state.shape[0]
    channels = outer_input_weight.shape[2]
    scalar = pl.BlockSpec(memory_space=pltpu.SMEM)
    vector = pl.BlockSpec(memory_space=pltpu.VMEM)
    params = pltpu.CompilerParams(vmem_limit_bytes=40 << 20)
    hbm = pl.BlockSpec(memory_space=pltpu.HBM)
    packed = pl.pallas_call(
        pack_kernel,
        out_shape=jax.ShapeDtypeStruct((rows * residues + sequences + 16, wide), jnp.bfloat16),
        in_specs=[hbm] * 5,
        out_specs=vector,
        scratch_shapes=[
            pltpu.SMEM((residues,), jnp.int32),
            pltpu.VMEM((rows, sequences), jnp.int32),
            pltpu.VMEM(alignment_state.shape, jnp.bfloat16),
            pltpu.VMEM((2, channels, alignment_state.shape[2]), jnp.bfloat16),
            pltpu.VMEM(alignment_state.shape, jnp.float32),
            pltpu.SemaphoreType.DMA((4 + rows,)),
        ],
        compiler_params=pltpu.CompilerParams(vmem_limit_bytes=63 << 20),
    )(
        residue_crop_mask,
        alignment_mask.T,
        alignment_state,
        outer_input_weight.transpose(0, 2, 1),
        pairwise_state,
    )
    held, other = gather_all(packed)
    cores, chips = lax.axis_size("sub"), lax.axis_size("dap")
    group = cores * rows
    return pl.pallas_call(
        update_kernel,
        out_shape=jax.ShapeDtypeStruct(pairwise_state.shape, jnp.bfloat16),
        in_specs=[scalar] + [vector] * 8,
        out_specs=vector,
        scratch_shapes=[
            pltpu.VMEM((channels * group * channels, group * wide), jnp.bfloat16),
            pltpu.VMEM((residues, channels, wide), jnp.float32),
            pltpu.VMEM((group * sequences, chips * wide), jnp.bfloat16),
            pltpu.VMEM((residues, wide), jnp.float32),
            pltpu.VMEM((chips * residues, channels * wide), jnp.bfloat16),
            pltpu.VMEM((residues, residues, wide), jnp.float32),
            pltpu.VMEM((residues, residues, wide), jnp.float32),
            pltpu.VMEM((residues, residues, wide), jnp.float32),
        ],
        compiler_params=params,
    )(
        residue_crop_mask,
        held,
        other,
        outer_output_weight,
        triangle_input_weight,
        triangle_gate,
        triangle_output_weight,
        transition_up_weight,
        transition_down_weight,
    )


def shards(
    pairwise_state,
    alignment_state,
    alignment_mask,
    residue_crop_mask,
    outer_input_weight,
    outer_output_weight,
    triangle_input_weight,
    triangle_gate,
    triangle_output_weight,
    transition_up_weight,
    transition_down_weight,
):
    row_count = pairwise_state.shape[0]
    start_row = lax.axis_index(("dap", "sub")) * row_count
    row_presence_mask = lax.dynamic_slice_in_dim(residue_crop_mask, start_row, row_count, 0).astype(
        jnp.float32
    )
    full_mask = residue_crop_mask.astype(jnp.float32)
    alignment_keep = alignment_mask.astype(jnp.float32) * row_presence_mask[None, :]
    alignment_normed = norm_layer(alignment_state.astype(jnp.float32), -1).astype(jnp.bfloat16)
    left_alignment = (
        jnp.einsum(
            "pxm,my->pxy",
            alignment_normed,
            outer_input_weight[0],
            preferred_element_type=jnp.float32,
        )
        * alignment_keep[:, :, None]
    ).astype(jnp.bfloat16)
    right_alignment = (
        jnp.einsum(
            "pxm,my->pxy",
            alignment_normed,
            outer_input_weight[1],
            preferred_element_type=jnp.float32,
        )
        * alignment_keep[:, :, None]
    ).astype(jnp.bfloat16)
    inner_alignment = jnp.einsum(
        "tqu,ulx->tqlx", left_alignment, outer_output_weight, preferred_element_type=jnp.float32
    ).astype(jnp.bfloat16)
    right_portion = lax.all_gather(right_alignment, ("dap", "sub"), axis=1, tiled=True)
    keep_portion = lax.all_gather(
        alignment_keep.astype(jnp.bfloat16), ("dap", "sub"), axis=1, tiled=True
    )
    numerator_sum = jnp.einsum(
        "zkwv,znw->knv", inner_alignment, right_portion, preferred_element_type=jnp.float32
    )
    pair_norm_count = jnp.einsum("cf,cg->fg", alignment_keep, keep_portion.astype(jnp.float32))
    block_part = numerator_sum / jnp.maximum(pair_norm_count, 1.0)[:, :, None]
    pair_one = (pairwise_state.astype(jnp.float32) + block_part).astype(jnp.bfloat16)
    ln_one = norm_layer(pair_one.astype(jnp.float32), -1).astype(jnp.bfloat16)
    pair_keep = row_presence_mask[:, None] * full_mask[None, :]

    def operand(gate_w, proj_w):
        gate_val = jnp.einsum("ijc,cd->dij", ln_one, gate_w, preferred_element_type=jnp.float32)
        proj_val = jnp.einsum("ijc,cd->dij", ln_one, proj_w, preferred_element_type=jnp.float32)
        return (jax.nn.sigmoid(gate_val) * proj_val * pair_keep[None]).astype(jnp.bfloat16)

    left_tri = operand(triangle_input_weight[0], triangle_input_weight[1])
    right_tri = operand(triangle_input_weight[2], triangle_input_weight[3])
    near_right = lax.all_gather(right_tri, "sub", axis=1, tiled=True)
    left_cols, right_all = (
        lax.all_to_all(left_tri, "dap", split_axis=0, concat_axis=1, tiled=True),
        lax.all_to_all(near_right, "dap", split_axis=0, concat_axis=1, tiled=True),
    )
    product = jnp.einsum(
        "cik,cjk->cij", left_cols, right_all, preferred_element_type=jnp.float32
    ).astype(jnp.bfloat16)
    returned = lax.all_to_all(product, "dap", split_axis=1, concat_axis=0, tiled=True)
    normed = norm_layer(returned.astype(jnp.float32), 0).astype(jnp.bfloat16)
    update = jnp.einsum(
        "cij,cd->ijd", normed, triangle_output_weight, preferred_element_type=jnp.float32
    )
    gate_out = jax.nn.sigmoid(
        jnp.einsum("ijc,cd->ijd", ln_one, triangle_gate, preferred_element_type=jnp.float32)
    )
    pair_two = (pair_one.astype(jnp.float32) + gate_out * update).astype(jnp.bfloat16)
    ln_two = norm_layer(pair_two.astype(jnp.float32), -1).astype(jnp.bfloat16)

    def step(row_pair):
        return transition(*row_pair, transition_up_weight, transition_down_weight)

    return lax.map(step, (ln_two, pair_two))


def solution(mesh):
    placed = (
        P(("crop", "dap", "sub"), None, None),
        P("crop", ("dap", "sub"), None),
        P("crop", ("dap", "sub")),
        P("crop"),
        P(),
        P(),
        P(),
        P(),
        P(),
        P(),
        P(),
    )

    small = mesh.shape["sub"] == 2 and mesh.shape["dap"] == 8

    def body(pairwise_state, *rest):
        residues, channels = pairwise_state.shape[1:]
        if small and residues * residues * channels * 2 <= REPLICATED_PAIR_BYTES:
            return shards_replicated(pairwise_state, *rest)
        return shards(pairwise_state, *rest)

    return jax.shard_map(
        body,
        mesh=mesh,
        in_specs=placed,
        out_specs=P(("crop", "dap", "sub"), None, None),
        check_vma=False,
    )
```

```python
import jax
import jax.numpy as jnp
from jax import lax
from jax.experimental import pallas as pl
from jax.experimental.pallas import tpu as pltpu
from jax.sharding import PartitionSpec as P

REPLICATED_PAIR_BYTES = 1 << 20


def norm_layer(values, reduce_axis):
    average = jnp.mean(values, axis=reduce_axis, keepdims=True)
    centered = values - average
    variance = jnp.mean(centered * centered, axis=reduce_axis, keepdims=True)
    return centered * lax.rsqrt(variance + 1e-05)


def transition(ln_two, pair_two, transition_up_weight, transition_down_weight):
    hidden = jax.nn.relu(
        jnp.dot(ln_two, transition_up_weight, preferred_element_type=jnp.float32)
    ).astype(jnp.bfloat16)
    return (
        pair_two.astype(jnp.float32)
        + jnp.dot(hidden, transition_down_weight, preferred_element_type=jnp.float32)
    ).astype(jnp.bfloat16)


def layer_norm(values):
    count = values.shape[-1]
    centered = values - jnp.sum(values, axis=-1, keepdims=True) * (1.0 / count)
    variance = jnp.sum(centered * centered, axis=-1, keepdims=True) * (1.0 / count)
    return centered * lax.rsqrt(variance + 1e-05)


def first_row(rows):
    return (lax.axis_index("dap") * lax.axis_size("sub") + lax.axis_index("sub")) * rows


def pack_kernel(
    mask_hbm,
    keep_hbm,
    state_hbm,
    weight_hbm,
    pair_hbm,
    out_ref,
    column_ref,
    mask_ref,
    keep_ref,
    state_ref,
    weight_ref,
    wide_ref,
    sems,
):
    rows, residues, wide = pair_hbm.shape
    sequences = state_ref.shape[0]
    base = rows * residues
    start = first_row(rows)
    second_core = lax.axis_index("sub") == 1
    loads = [
        pltpu.make_async_copy(state_hbm, state_ref, sems.at[0]),
        pltpu.make_async_copy(weight_hbm, weight_ref, sems.at[1]),
        pltpu.make_async_copy(keep_hbm, keep_ref, sems.at[2]),
        pltpu.make_async_copy(mask_hbm, mask_ref, sems.at[3]),
    ] + [
        pltpu.make_async_copy(
            pair_hbm.at[row], out_ref.at[pl.ds(row * residues, residues)], sems.at[4 + row]
        )
        for row in range(rows)
    ]
    for load in loads:
        load.start()
    loads[0].wait()
    wide_ref[...] = state_ref[...].astype(jnp.float32)
    normed_rows = [layer_norm(wide_ref[:, row]).astype(jnp.bfloat16) for row in range(rows)]
    eye = lax.broadcasted_iota(jnp.int32, (sequences, sequences), 0) == lax.broadcasted_iota(
        jnp.int32, (sequences, sequences), 1
    )
    lefts, rights, keeps = [], [], []
    for load in loads[1:]:
        load.wait()
    for row in range(rows):
        present = mask_ref[start + row].astype(jnp.float32)
        keep_row = keep_ref[row : row + 1].astype(jnp.float32) * present
        keep_column = jnp.sum(
            jnp.where(eye, jnp.broadcast_to(keep_row, eye.shape), 0.0), axis=1, keepdims=True
        )
        normed = normed_rows[row]
        last = (((1,), (1,)), ((), ()))
        left = lax.dot_general(weight_ref[0], normed, last, preferred_element_type=jnp.float32)
        right = lax.dot_general(normed, weight_ref[1], last, preferred_element_type=jnp.float32)
        lefts.append(left * keep_row)
        rights.append(right * keep_column)
        keeps.append(keep_row)
    left = jnp.concatenate(lefts, axis=1)
    right = jnp.concatenate(rights, axis=1)
    first = jnp.concatenate([right, left], axis=1)
    other = jnp.concatenate([left, right], axis=1)
    out_ref[base : base + sequences] = jnp.where(second_core, other, first).astype(jnp.bfloat16)
    keep = jnp.concatenate(
        keeps + [jnp.zeros((16 - rows, sequences), jnp.float32)], axis=0
    )
    place = lax.broadcasted_iota(jnp.int32, (residues, 1), 0)
    column = jnp.zeros((residues, 1), jnp.float32)
    for k in range(residues):
        column = jnp.where(place == k, mask_ref[k].astype(jnp.float32), column)
    column_ref[...] = jnp.broadcast_to(column, (residues, wide))
    out_ref[base + sequences :] = jnp.concatenate(
        [keep, jnp.zeros((16, wide - sequences), jnp.float32)], axis=1
    ).astype(jnp.bfloat16)


def sigmoid(values):
    return 0.5 * jnp.tanh(0.5 * values) + 0.5


def update_kernel(
    mask_ref,
    held_ref,
    other_ref,
    outer_ref,
    triangle_ref,
    gate_ref,
    output_ref,
    up_ref,
    down_ref,
    out_ref,
    block_ref,
    left_ref,
    right_ref,
    keep_ref,
    first_ref,
    second_ref,
    pair_ref,
    pair_one_ref,
    ln_one_ref,
):
    rows, residues, wide = out_ref.shape
    cores, chips = 2, lax.axis_size("dap")
    channels = outer_ref.shape[0]
    sequences = channels
    base = rows * residues
    half = wide // 2
    group = cores * rows
    start = first_row(rows)
    second_core = lax.axis_index("sub") == 1
    bf16 = jnp.bfloat16
    f32 = jnp.float32

    parts = block_ref.shape[0]
    span = channels // parts
    nothing = jnp.zeros((channels, wide), bf16)
    for part in range(parts):
        for step in range(span + 1):
            weight = outer_ref[part * span + step % span]
            at = step * 2 * channels
            block_ref[part, at : at + channels, :wide] = weight
            block_ref[part, at : at + channels, wide:] = nothing
            block_ref[part, at + channels : at + 2 * channels, :wide] = nothing
            block_ref[part, at + channels : at + 2 * channels, wide:] = weight

    lane = lax.broadcasted_iota(jnp.int32, (channels, wide), 1)
    lane_block = lane // channels
    low = lane < half
    for chip in range(chips):
        place = block_place(chip, chips)
        mine, other = held_ref[place], other_ref[place]
        blocks = [jnp.where(second_core, other, mine), jnp.where(second_core, mine, other)]
        packed = [block[base : base + sequences].astype(f32) for block in blocks]
        right = jnp.where(low, packed[0], packed[1])
        for turn, value in enumerate((right, pltpu.roll(right, half, 1))):
            for copy in range(group):
                right_ref[
                    turn,
                    copy * sequences : (copy + 1) * sequences,
                    chip * wide : (chip + 1) * wide,
                ] = value.astype(bf16)
        for core in range(cores):
            residue = (chip * cores + core) * rows
            for row in range(rows):
                at = (rows if core == 0 else 0) + row
                left_ref[residue + row] = jnp.where(lane_block == at, packed[core], 0.0)
            keep_ref[residue : residue + rows] = blocks[core][base + sequences :].astype(f32)[:rows]
            pair_ref[residue : residue + rows] = (
                blocks[core][:base].astype(f32).reshape(rows, residues, wide)
            )

    last = (((1,), (1,)), ((), ()))
    keep = keep_ref[...].astype(bf16)
    count = lax.dot_general(keep, keep, last, preferred_element_type=f32)
    inverse = 1.0 / jnp.maximum(count, 1.0)

    low = lax.broadcasted_iota(jnp.int32, (residues, wide), 1) < half
    totals = [0.0, 0.0]
    for part in range(parts):
        outer = []
        for turn in range(2):
            left = jnp.concatenate(
                [left_ref[:, d] for d in range(part * span + turn, (part + 1) * span, 2)], axis=0
            ).astype(bf16)
            outer.append(jnp.dot(left, right_ref[turn], preferred_element_type=f32))

        def piece(turn, at, chip):
            return outer[turn][
                at * residues : (at + 1) * residues, chip * wide : (chip + 1) * wide
            ]

        for at in range(span // 2):
            follow = (at + 1) % (span // 2)
            for chip in range(chips):
                place = (
                    part,
                    slice(chip * residues, (chip + 1) * residues),
                    slice(at * wide, (at + 1) * wide),
                )
                first_ref[place] = jnp.where(low, piece(0, at, chip), piece(1, at, chip)).astype(bf16)
                second_ref[place] = jnp.where(
                    low, piece(1, at, chip), piece(0, follow, chip)
                ).astype(bf16)
        depth = span * 2 * channels
        totals[0] += jnp.dot(first_ref[part], block_ref[part, :depth], preferred_element_type=f32)
        totals[1] += jnp.dot(
            second_ref[part], block_ref[part, 2 * channels :], preferred_element_type=f32
        )

    right_weight = jnp.concatenate([triangle_ref[2], triangle_ref[3]], axis=1)
    right_tri = []
    stride = 8
    for first in range(0, residues, stride):
        normed = []
        for k in range(first, first + stride):
            chip, pick = k // group, k % group
            at = (pick % 2) * wide
            numerator = totals[pick // 2][chip * residues : (chip + 1) * residues, at : at + wide]
            opm = numerator * jnp.broadcast_to(inverse[:, k : k + 1], (residues, wide))
            pair_one = (pair_ref[:, k] + opm).astype(bf16).astype(f32)
            pair_one_ref[k] = pair_one
            ln_one = layer_norm(pair_one)
            ln_one_ref[k] = ln_one
            normed.append(ln_one.astype(bf16))
        both = jnp.dot(
            jnp.concatenate(normed, axis=0), right_weight, preferred_element_type=f32
        )
        right_tri.append((sigmoid(both[:, :wide]) * both[:, wide:]).astype(bf16).astype(f32))

    mask = mask_ref[...]
    own_pair = jnp.concatenate([pair_one_ref[:, start + row] for row in range(rows)], axis=0)
    own_ln = jnp.concatenate([ln_one_ref[:, start + row] for row in range(rows)], axis=0).astype(bf16)
    left_weight = jnp.concatenate([triangle_ref[0], triangle_ref[1]], axis=1)
    both = jnp.dot(own_ln, left_weight, preferred_element_type=f32)
    left_tri = sigmoid(both[:, :wide]) * both[:, wide:] * jnp.concatenate([mask] * rows, axis=0)
    left_tri = left_tri.astype(bf16).astype(f32)
    products = []
    for row in range(rows):
        sums = [jnp.zeros((residues, wide), f32) for _ in range(4)]
        for k in range(residues):
            at = row * residues + k
            place = (k % stride) * residues
            sums[k % 4] += left_tri[at : at + 1] * right_tri[k // stride][place : place + residues]
        total = (sums[0] + sums[1]) + (sums[2] + sums[3])
        products.append(total * (mask * mask_ref[pl.ds(start + row, 1), :]))
    product = jnp.concatenate(products, axis=0).astype(bf16).astype(f32)
    normed = layer_norm(product).astype(bf16)
    update = jnp.dot(normed, output_ref[...], preferred_element_type=f32)
    gate_out = sigmoid(jnp.dot(own_ln, gate_ref[...], preferred_element_type=f32))
    pair_two = (own_pair + gate_out * update).astype(bf16).astype(f32)
    ln_two = layer_norm(pair_two).astype(bf16)
    hidden = jnp.maximum(jnp.dot(ln_two, up_ref[...], preferred_element_type=f32), 0.0).astype(bf16)
    result = pair_two + jnp.dot(hidden, down_ref[...], preferred_element_type=f32)
    out_ref[...] = result.astype(bf16).reshape(rows, residues, wide)


def copy_kernel(packed_ref, out_ref):
    out_ref[0] = packed_ref[...]


def gather_all(packed):
    dap_count = lax.axis_size("dap")
    half = dap_count // 2
    far = lax.ppermute(packed[None], "dap", [(src, src ^ half) for src in range(dap_count)])
    own = pl.pallas_call(
        copy_kernel,
        out_shape=jax.ShapeDtypeStruct((1,) + packed.shape, packed.dtype),
        in_specs=[pl.BlockSpec(memory_space=pltpu.VMEM)],
        out_specs=pl.BlockSpec(memory_space=pltpu.VMEM),
        compiler_params=pltpu.CompilerParams(vmem_limit_bytes=4 << 20),
    )(packed)
    both = jnp.concatenate([own, far], axis=0)
    held = [both] + [
        lax.ppermute(both, "dap", [(src, src ^ offset) for src in range(dap_count)])
        for offset in range(1, half)
    ]
    held = jnp.concatenate(held, axis=0)
    return held, lax.ppermute(held, "sub", [(0, 1), (1, 0)])


def block_place(chip, chips):
    offset = lax.bitwise_xor(lax.axis_index("dap"), chip)
    half = chips // 2
    return jnp.where(offset >= half, 2 * (offset - half) + 1, 2 * offset)


def shards_replicated(
    pairwise_state,
    alignment_state,
    alignment_mask,
    residue_crop_mask,
    outer_input_weight,
    outer_output_weight,
    triangle_input_weight,
    triangle_gate,
    triangle_output_weight,
    transition_up_weight,
    transition_down_weight,
):
    rows, residues, wide = pairwise_state.shape
    sequences = alignment_state.shape[0]
    channels = outer_input_weight.shape[2]
    vector = pl.BlockSpec(memory_space=pltpu.VMEM)
    params = pltpu.CompilerParams(vmem_limit_bytes=40 << 20)
    hbm = pl.BlockSpec(memory_space=pltpu.HBM)
    packed, mask = pl.pallas_call(
        pack_kernel,
        out_shape=(
            jax.ShapeDtypeStruct((rows * residues + sequences + 16, wide), jnp.bfloat16),
            jax.ShapeDtypeStruct((residues, wide), jnp.float32),
        ),
        in_specs=[hbm] * 5,
        out_specs=(vector, vector),
        scratch_shapes=[
            pltpu.SMEM((residues,), jnp.int32),
            pltpu.VMEM((rows, sequences), jnp.int32),
            pltpu.VMEM(alignment_state.shape, jnp.bfloat16),
            pltpu.VMEM((2, channels, alignment_state.shape[2]), jnp.bfloat16),
            pltpu.VMEM(alignment_state.shape, jnp.float32),
            pltpu.SemaphoreType.DMA((4 + rows,)),
        ],
        compiler_params=pltpu.CompilerParams(vmem_limit_bytes=63 << 20),
    )(
        residue_crop_mask,
        alignment_mask.T,
        alignment_state,
        outer_input_weight.transpose(0, 2, 1),
        pairwise_state,
    )
    held, other = gather_all(packed)
    cores, chips = lax.axis_size("sub"), lax.axis_size("dap")
    group = cores * rows
    parts = 2
    return pl.pallas_call(
        update_kernel,
        out_shape=jax.ShapeDtypeStruct(pairwise_state.shape, jnp.bfloat16),
        in_specs=[vector] * 9,
        out_specs=vector,
        scratch_shapes=[
            pltpu.VMEM((parts, (channels // parts + 1) * 2 * channels, 2 * wide), jnp.bfloat16),
            pltpu.VMEM((residues, channels, wide), jnp.float32),
            pltpu.VMEM((2, group * sequences, chips * wide), jnp.bfloat16),
            pltpu.VMEM((residues, wide), jnp.float32),
            pltpu.VMEM((parts, chips * residues, channels // parts * wide // 2), jnp.bfloat16),
            pltpu.VMEM((parts, chips * residues, channels // parts * wide // 2), jnp.bfloat16),
            pltpu.VMEM((residues, residues, wide), jnp.float32),
            pltpu.VMEM((residues, residues, wide), jnp.float32),
            pltpu.VMEM((residues, residues, wide), jnp.float32),
        ],
        compiler_params=params,
    )(
        mask,
        held,
        other,
        outer_output_weight,
        triangle_input_weight,
        triangle_gate,
        triangle_output_weight,
        transition_up_weight,
        transition_down_weight,
    )


def shards(
    pairwise_state,
    alignment_state,
    alignment_mask,
    residue_crop_mask,
    outer_input_weight,
    outer_output_weight,
    triangle_input_weight,
    triangle_gate,
    triangle_output_weight,
    transition_up_weight,
    transition_down_weight,
):
    row_count = pairwise_state.shape[0]
    start_row = lax.axis_index(("dap", "sub")) * row_count
    row_presence_mask = lax.dynamic_slice_in_dim(residue_crop_mask, start_row, row_count, 0).astype(
        jnp.float32
    )
    full_mask = residue_crop_mask.astype(jnp.float32)
    alignment_keep = alignment_mask.astype(jnp.float32) * row_presence_mask[None, :]
    alignment_normed = norm_layer(alignment_state.astype(jnp.float32), -1).astype(jnp.bfloat16)
    left_alignment = (
        jnp.einsum(
            "pxm,my->pxy",
            alignment_normed,
            outer_input_weight[0],
            preferred_element_type=jnp.float32,
        )
        * alignment_keep[:, :, None]
    ).astype(jnp.bfloat16)
    right_alignment = (
        jnp.einsum(
            "pxm,my->pxy",
            alignment_normed,
            outer_input_weight[1],
            preferred_element_type=jnp.float32,
        )
        * alignment_keep[:, :, None]
    ).astype(jnp.bfloat16)
    inner_alignment = jnp.einsum(
        "tqu,ulx->tqlx", left_alignment, outer_output_weight, preferred_element_type=jnp.float32
    ).astype(jnp.bfloat16)
    right_portion = lax.all_gather(right_alignment, ("dap", "sub"), axis=1, tiled=True)
    keep_portion = lax.all_gather(
        alignment_keep.astype(jnp.bfloat16), ("dap", "sub"), axis=1, tiled=True
    )
    numerator_sum = jnp.einsum(
        "zkwv,znw->knv", inner_alignment, right_portion, preferred_element_type=jnp.float32
    )
    pair_norm_count = jnp.einsum("cf,cg->fg", alignment_keep, keep_portion.astype(jnp.float32))
    block_part = numerator_sum / jnp.maximum(pair_norm_count, 1.0)[:, :, None]
    pair_one = (pairwise_state.astype(jnp.float32) + block_part).astype(jnp.bfloat16)
    ln_one = norm_layer(pair_one.astype(jnp.float32), -1).astype(jnp.bfloat16)
    pair_keep = row_presence_mask[:, None] * full_mask[None, :]

    def operand(gate_w, proj_w):
        gate_val = jnp.einsum("ijc,cd->dij", ln_one, gate_w, preferred_element_type=jnp.float32)
        proj_val = jnp.einsum("ijc,cd->dij", ln_one, proj_w, preferred_element_type=jnp.float32)
        return (jax.nn.sigmoid(gate_val) * proj_val * pair_keep[None]).astype(jnp.bfloat16)

    left_tri = operand(triangle_input_weight[0], triangle_input_weight[1])
    right_tri = operand(triangle_input_weight[2], triangle_input_weight[3])
    near_right = lax.all_gather(right_tri, "sub", axis=1, tiled=True)
    left_cols, right_all = (
        lax.all_to_all(left_tri, "dap", split_axis=0, concat_axis=1, tiled=True),
        lax.all_to_all(near_right, "dap", split_axis=0, concat_axis=1, tiled=True),
    )
    product = jnp.einsum(
        "cik,cjk->cij", left_cols, right_all, preferred_element_type=jnp.float32
    ).astype(jnp.bfloat16)
    returned = lax.all_to_all(product, "dap", split_axis=1, concat_axis=0, tiled=True)
    normed = norm_layer(returned.astype(jnp.float32), 0).astype(jnp.bfloat16)
    update = jnp.einsum(
        "cij,cd->ijd", normed, triangle_output_weight, preferred_element_type=jnp.float32
    )
    gate_out = jax.nn.sigmoid(
        jnp.einsum("ijc,cd->ijd", ln_one, triangle_gate, preferred_element_type=jnp.float32)
    )
    pair_two = (pair_one.astype(jnp.float32) + gate_out * update).astype(jnp.bfloat16)
    ln_two = norm_layer(pair_two.astype(jnp.float32), -1).astype(jnp.bfloat16)

    def step(row_pair):
        return transition(*row_pair, transition_up_weight, transition_down_weight)

    return lax.map(step, (ln_two, pair_two))


def solution(mesh):
    placed = (
        P(("crop", "dap", "sub"), None, None),
        P("crop", ("dap", "sub"), None),
        P("crop", ("dap", "sub")),
        P("crop"),
        P(),
        P(),
        P(),
        P(),
        P(),
        P(),
        P(),
    )

    small = mesh.shape["sub"] == 2 and mesh.shape["dap"] == 8

    def body(pairwise_state, *rest):
        residues, channels = pairwise_state.shape[1:]
        if small and residues * residues * channels * 2 <= REPLICATED_PAIR_BYTES:
            return shards_replicated(pairwise_state, *rest)
        return shards(pairwise_state, *rest)

    return jax.shard_map(
        body,
        mesh=mesh,
        in_specs=placed,
        out_specs=P(("crop", "dap", "sub"), None, None),
        check_vma=False,
    )
```

```python
import jax
import jax.numpy as jnp
from jax import lax
from jax.experimental import pallas as pl
from jax.experimental.pallas import tpu as pltpu
from jax.sharding import PartitionSpec as P

REPLICATED_PAIR_BYTES = 1 << 20


def norm_layer(values, reduce_axis):
    average = jnp.mean(values, axis=reduce_axis, keepdims=True)
    centered = values - average
    variance = jnp.mean(centered * centered, axis=reduce_axis, keepdims=True)
    return centered * lax.rsqrt(variance + 1e-05)


def transition(ln_two, pair_two, transition_up_weight, transition_down_weight):
    hidden = jax.nn.relu(
        jnp.dot(ln_two, transition_up_weight, preferred_element_type=jnp.float32)
    ).astype(jnp.bfloat16)
    return (
        pair_two.astype(jnp.float32)
        + jnp.dot(hidden, transition_down_weight, preferred_element_type=jnp.float32)
    ).astype(jnp.bfloat16)


def layer_norm(values):
    count = values.shape[-1]
    centered = values - jnp.sum(values, axis=-1, keepdims=True) * (1.0 / count)
    variance = jnp.sum(centered * centered, axis=-1, keepdims=True) * (1.0 / count)
    return centered * lax.rsqrt(variance + 1e-05)


def first_row(rows):
    return (lax.axis_index("dap") * lax.axis_size("sub") + lax.axis_index("sub")) * rows


def pack_kernel(
    mask_hbm,
    keep_hbm,
    state_hbm,
    weight_hbm,
    pair_hbm,
    out_hbm,
    mask_ref,
    keep_ref,
    state_ref,
    weight_ref,
    wide_ref,
    out_ref,
    sems,
):
    rows, residues, wide = pair_hbm.shape
    sequences = state_ref.shape[0]
    base = rows * residues
    start = first_row(rows)
    second_core = lax.axis_index("sub") == 1
    loads = [
        pltpu.make_async_copy(state_hbm, state_ref, sems.at[0]),
        pltpu.make_async_copy(weight_hbm, weight_ref, sems.at[1]),
        pltpu.make_async_copy(keep_hbm, keep_ref, sems.at[2]),
        pltpu.make_async_copy(mask_hbm, mask_ref, sems.at[3]),
    ] + [
        pltpu.make_async_copy(
            pair_hbm.at[row], out_hbm.at[pl.ds(row * residues, residues)], sems.at[5 + row]
        )
        for row in range(rows)
    ]
    for load in loads:
        load.start()
    loads[0].wait()
    wide_ref[...] = state_ref[...].astype(jnp.float32)
    normed_rows = [layer_norm(wide_ref[:, row]).astype(jnp.bfloat16) for row in range(rows)]
    eye = lax.broadcasted_iota(jnp.int32, (sequences, sequences), 0) == lax.broadcasted_iota(
        jnp.int32, (sequences, sequences), 1
    )
    lefts, rights, keeps = [], [], []
    for load in loads[1:4]:
        load.wait()
    for row in range(rows):
        present = mask_ref[start + row].astype(jnp.float32)
        keep_row = keep_ref[row : row + 1].astype(jnp.float32) * present
        keep_column = jnp.sum(
            jnp.where(eye, jnp.broadcast_to(keep_row, eye.shape), 0.0), axis=1, keepdims=True
        )
        normed = normed_rows[row]
        last = (((1,), (1,)), ((), ()))
        left = lax.dot_general(weight_ref[0], normed, last, preferred_element_type=jnp.float32)
        right = lax.dot_general(normed, weight_ref[1], last, preferred_element_type=jnp.float32)
        lefts.append(left * keep_row)
        rights.append(right * keep_column)
        keeps.append(
            jnp.concatenate(
                [keep_row, jnp.full((1, wide - sequences), present, jnp.float32)], axis=1
            )
        )
    left = jnp.concatenate(lefts, axis=1)
    right = jnp.concatenate(rights, axis=1)
    first = jnp.concatenate([right, left], axis=1)
    other = jnp.concatenate([left, right], axis=1)
    out_ref[:sequences] = jnp.where(second_core, other, first).astype(jnp.bfloat16)
    out_ref[sequences:] = jnp.concatenate(
        keeps + [jnp.zeros((16 - rows, wide), jnp.float32)], axis=0
    ).astype(jnp.bfloat16)
    store = pltpu.make_async_copy(
        out_ref, out_hbm.at[pl.ds(base, sequences + 16)], sems.at[4]
    )
    store.start()
    store.wait()
    for load in loads[4:]:
        load.wait()


def sigmoid(values):
    return 0.5 * jnp.tanh(0.5 * values) + 0.5


def update_kernel(
    held_ref,
    other_ref,
    outer_ref,
    triangle_ref,
    gate_ref,
    output_ref,
    up_ref,
    down_ref,
    out_ref,
    block_ref,
    left_ref,
    right_ref,
    keep_ref,
    first_ref,
    second_ref,
    pair_ref,
    pair_one_ref,
    ln_one_ref,
):
    rows, residues, wide = out_ref.shape
    cores, chips = 2, lax.axis_size("dap")
    channels = outer_ref.shape[0]
    sequences = channels
    base = rows * residues
    half = wide // 2
    group = cores * rows
    start = first_row(rows)
    second_core = lax.axis_index("sub") == 1
    bf16 = jnp.bfloat16
    f32 = jnp.float32

    parts = block_ref.shape[0]
    span = channels // parts
    nothing = jnp.zeros((channels, wide), bf16)
    for part in range(parts):
        for step in range(span + 1):
            weight = outer_ref[part * span + step % span]
            at = step * 2 * channels
            block_ref[part, at : at + channels, :wide] = weight
            block_ref[part, at : at + channels, wide:] = nothing
            block_ref[part, at + channels : at + 2 * channels, :wide] = nothing
            block_ref[part, at + channels : at + 2 * channels, wide:] = weight

    lane = lax.broadcasted_iota(jnp.int32, (channels, wide), 1)
    lane_block = lane // channels
    low = lane < half
    for chip in range(chips):
        place = block_place(chip, chips)
        mine, other = held_ref[place], other_ref[place]
        blocks = [jnp.where(second_core, other, mine), jnp.where(second_core, mine, other)]
        packed = [block[base : base + sequences].astype(f32) for block in blocks]
        right = jnp.where(low, packed[0], packed[1])
        for turn, value in enumerate((right, pltpu.roll(right, half, 1))):
            for copy in range(group):
                right_ref[
                    turn,
                    copy * sequences : (copy + 1) * sequences,
                    chip * wide : (chip + 1) * wide,
                ] = value.astype(bf16)
        for core in range(cores):
            residue = (chip * cores + core) * rows
            for row in range(rows):
                at = (rows if core == 0 else 0) + row
                left_ref[residue + row] = jnp.where(lane_block == at, packed[core], 0.0)
            keep_ref[residue : residue + rows] = blocks[core][base + sequences :].astype(f32)[:rows]
            pair_ref[residue : residue + rows] = (
                blocks[core][:base].astype(f32).reshape(rows, residues, wide)
            )

    last = (((1,), (1,)), ((), ()))
    keep = keep_ref[...]
    mask = jnp.broadcast_to(keep[:, sequences : sequences + 1], (residues, wide))
    counted = lax.broadcasted_iota(jnp.int32, (residues, wide), 1) < sequences
    count = lax.dot_general(
        jnp.where(counted, keep, 0.0).astype(bf16),
        keep.astype(bf16),
        last,
        preferred_element_type=f32,
    )
    inverse = 1.0 / jnp.maximum(count, 1.0)

    low = lax.broadcasted_iota(jnp.int32, (residues, wide), 1) < half
    totals = [0.0, 0.0]
    for part in range(parts):
        outer = []
        for turn in range(2):
            left = jnp.concatenate(
                [left_ref[:, d] for d in range(part * span + turn, (part + 1) * span, 2)], axis=0
            ).astype(bf16)
            outer.append(jnp.dot(left, right_ref[turn], preferred_element_type=f32))

        def piece(turn, at, chip):
            return outer[turn][
                at * residues : (at + 1) * residues, chip * wide : (chip + 1) * wide
            ]

        for at in range(span // 2):
            follow = (at + 1) % (span // 2)
            for chip in range(chips):
                place = (
                    part,
                    slice(chip * residues, (chip + 1) * residues),
                    slice(at * wide, (at + 1) * wide),
                )
                first_ref[place] = jnp.where(low, piece(0, at, chip), piece(1, at, chip)).astype(bf16)
                second_ref[place] = jnp.where(
                    low, piece(1, at, chip), piece(0, follow, chip)
                ).astype(bf16)
        depth = span * 2 * channels
        totals[0] += jnp.dot(first_ref[part], block_ref[part, :depth], preferred_element_type=f32)
        totals[1] += jnp.dot(
            second_ref[part], block_ref[part, 2 * channels :], preferred_element_type=f32
        )

    right_weight = jnp.concatenate([triangle_ref[2], triangle_ref[3]], axis=1)
    right_tri = []
    stride = 8
    for first in range(0, residues, stride):
        normed = []
        for k in range(first, first + stride):
            chip, pick = k // group, k % group
            at = (pick % 2) * wide
            numerator = totals[pick // 2][chip * residues : (chip + 1) * residues, at : at + wide]
            opm = numerator * jnp.broadcast_to(inverse[:, k : k + 1], (residues, wide))
            pair_one = (pair_ref[:, k] + opm).astype(bf16).astype(f32)
            pair_one_ref[k] = pair_one
            ln_one = layer_norm(pair_one)
            ln_one_ref[k] = ln_one
            normed.append(ln_one.astype(bf16))
        both = jnp.dot(
            jnp.concatenate(normed, axis=0), right_weight, preferred_element_type=f32
        )
        right_tri.append((sigmoid(both[:, :wide]) * both[:, wide:]).astype(bf16).astype(f32))

    own_pair = jnp.concatenate([pair_one_ref[:, start + row] for row in range(rows)], axis=0)
    own_ln = jnp.concatenate([ln_one_ref[:, start + row] for row in range(rows)], axis=0).astype(bf16)
    left_weight = jnp.concatenate([triangle_ref[0], triangle_ref[1]], axis=1)
    both = jnp.dot(own_ln, left_weight, preferred_element_type=f32)
    left_tri = sigmoid(both[:, :wide]) * both[:, wide:] * jnp.concatenate([mask] * rows, axis=0)
    left_tri = left_tri.astype(bf16).astype(f32)
    products = []
    for row in range(rows):
        sums = [jnp.zeros((residues, wide), f32) for _ in range(4)]
        for k in range(residues):
            at = row * residues + k
            place = (k % stride) * residues
            sums[k % 4] += left_tri[at : at + 1] * right_tri[k // stride][place : place + residues]
        total = (sums[0] + sums[1]) + (sums[2] + sums[3])
        own_mask = keep_ref[pl.ds(start + row, 1), :][:, sequences : sequences + 1]
        products.append(total * (mask * own_mask))
    product = jnp.concatenate(products, axis=0).astype(bf16).astype(f32)
    normed = layer_norm(product).astype(bf16)
    update = jnp.dot(normed, output_ref[...], preferred_element_type=f32)
    gate_out = sigmoid(jnp.dot(own_ln, gate_ref[...], preferred_element_type=f32))
    pair_two = (own_pair + gate_out * update).astype(bf16).astype(f32)
    ln_two = layer_norm(pair_two).astype(bf16)
    hidden = jnp.maximum(jnp.dot(ln_two, up_ref[...], preferred_element_type=f32), 0.0).astype(bf16)
    result = pair_two + jnp.dot(hidden, down_ref[...], preferred_element_type=f32)
    out_ref[...] = result.astype(bf16).reshape(rows, residues, wide)


def copy_kernel(packed_ref, out_ref):
    out_ref[0] = packed_ref[...]


def gather_all(packed):
    dap_count = lax.axis_size("dap")
    half = dap_count // 2
    far = lax.ppermute(packed[None], "dap", [(src, src ^ half) for src in range(dap_count)])
    own = pl.pallas_call(
        copy_kernel,
        out_shape=jax.ShapeDtypeStruct((1,) + packed.shape, packed.dtype),
        in_specs=[pl.BlockSpec(memory_space=pltpu.VMEM)],
        out_specs=pl.BlockSpec(memory_space=pltpu.VMEM),
        compiler_params=pltpu.CompilerParams(vmem_limit_bytes=4 << 20),
    )(packed)
    both = jnp.concatenate([own, far], axis=0)
    held = [both] + [
        lax.ppermute(both, "dap", [(src, src ^ offset) for src in range(dap_count)])
        for offset in range(1, half)
    ]
    held = jnp.concatenate(held, axis=0)
    return held, lax.ppermute(held, "sub", [(0, 1), (1, 0)])


def block_place(chip, chips):
    offset = lax.bitwise_xor(lax.axis_index("dap"), chip)
    half = chips // 2
    return jnp.where(offset >= half, 2 * (offset - half) + 1, 2 * offset)


def shards_replicated(
    pairwise_state,
    alignment_state,
    alignment_mask,
    residue_crop_mask,
    outer_input_weight,
    outer_output_weight,
    triangle_input_weight,
    triangle_gate,
    triangle_output_weight,
    transition_up_weight,
    transition_down_weight,
):
    rows, residues, wide = pairwise_state.shape
    sequences = alignment_state.shape[0]
    channels = outer_input_weight.shape[2]
    vector = pl.BlockSpec(memory_space=pltpu.VMEM)
    params = pltpu.CompilerParams(vmem_limit_bytes=40 << 20)
    hbm = pl.BlockSpec(memory_space=pltpu.HBM)
    packed = pl.pallas_call(
        pack_kernel,
        out_shape=jax.ShapeDtypeStruct((rows * residues + sequences + 16, wide), jnp.bfloat16),
        in_specs=[hbm] * 5,
        out_specs=hbm,
        scratch_shapes=[
            pltpu.SMEM((residues,), jnp.int32),
            pltpu.VMEM((rows, sequences), jnp.int32),
            pltpu.VMEM(alignment_state.shape, jnp.bfloat16),
            pltpu.VMEM((2, channels, alignment_state.shape[2]), jnp.bfloat16),
            pltpu.VMEM(alignment_state.shape, jnp.float32),
            pltpu.VMEM((sequences + 16, wide), jnp.bfloat16),
            pltpu.SemaphoreType.DMA((5 + rows,)),
        ],
        compiler_params=pltpu.CompilerParams(vmem_limit_bytes=63 << 20),
    )(
        residue_crop_mask,
        alignment_mask.T,
        alignment_state,
        outer_input_weight.transpose(0, 2, 1),
        pairwise_state,
    )
    held, other = gather_all(packed)
    cores, chips = lax.axis_size("sub"), lax.axis_size("dap")
    group = cores * rows
    parts = 2
    return pl.pallas_call(
        update_kernel,
        out_shape=jax.ShapeDtypeStruct(pairwise_state.shape, jnp.bfloat16),
        in_specs=[vector] * 8,
        out_specs=vector,
        scratch_shapes=[
            pltpu.VMEM((parts, (channels // parts + 1) * 2 * channels, 2 * wide), jnp.bfloat16),
            pltpu.VMEM((residues, channels, wide), jnp.float32),
            pltpu.VMEM((2, group * sequences, chips * wide), jnp.bfloat16),
            pltpu.VMEM((residues, wide), jnp.float32),
            pltpu.VMEM((parts, chips * residues, channels // parts * wide // 2), jnp.bfloat16),
            pltpu.VMEM((parts, chips * residues, channels // parts * wide // 2), jnp.bfloat16),
            pltpu.VMEM((residues, residues, wide), jnp.float32),
            pltpu.VMEM((residues, residues, wide), jnp.float32),
            pltpu.VMEM((residues, residues, wide), jnp.float32),
        ],
        compiler_params=params,
    )(
        held,
        other,
        outer_output_weight,
        triangle_input_weight,
        triangle_gate,
        triangle_output_weight,
        transition_up_weight,
        transition_down_weight,
    )


def shards(
    pairwise_state,
    alignment_state,
    alignment_mask,
    residue_crop_mask,
    outer_input_weight,
    outer_output_weight,
    triangle_input_weight,
    triangle_gate,
    triangle_output_weight,
    transition_up_weight,
    transition_down_weight,
):
    row_count = pairwise_state.shape[0]
    start_row = lax.axis_index(("dap", "sub")) * row_count
    row_presence_mask = lax.dynamic_slice_in_dim(residue_crop_mask, start_row, row_count, 0).astype(
        jnp.float32
    )
    full_mask = residue_crop_mask.astype(jnp.float32)
    alignment_keep = alignment_mask.astype(jnp.float32) * row_presence_mask[None, :]
    alignment_normed = norm_layer(alignment_state.astype(jnp.float32), -1).astype(jnp.bfloat16)
    left_alignment = (
        jnp.einsum(
            "pxm,my->pxy",
            alignment_normed,
            outer_input_weight[0],
            preferred_element_type=jnp.float32,
        )
        * alignment_keep[:, :, None]
    ).astype(jnp.bfloat16)
    right_alignment = (
        jnp.einsum(
            "pxm,my->pxy",
            alignment_normed,
            outer_input_weight[1],
            preferred_element_type=jnp.float32,
        )
        * alignment_keep[:, :, None]
    ).astype(jnp.bfloat16)
    inner_alignment = jnp.einsum(
        "tqu,ulx->tqlx", left_alignment, outer_output_weight, preferred_element_type=jnp.float32
    ).astype(jnp.bfloat16)
    right_portion = lax.all_gather(right_alignment, ("dap", "sub"), axis=1, tiled=True)
    keep_portion = lax.all_gather(
        alignment_keep.astype(jnp.bfloat16), ("dap", "sub"), axis=1, tiled=True
    )
    numerator_sum = jnp.einsum(
        "zkwv,znw->knv", inner_alignment, right_portion, preferred_element_type=jnp.float32
    )
    pair_norm_count = jnp.einsum("cf,cg->fg", alignment_keep, keep_portion.astype(jnp.float32))
    block_part = numerator_sum / jnp.maximum(pair_norm_count, 1.0)[:, :, None]
    pair_one = (pairwise_state.astype(jnp.float32) + block_part).astype(jnp.bfloat16)
    ln_one = norm_layer(pair_one.astype(jnp.float32), -1).astype(jnp.bfloat16)
    pair_keep = row_presence_mask[:, None] * full_mask[None, :]

    def operand(gate_w, proj_w):
        gate_val = jnp.einsum("ijc,cd->dij", ln_one, gate_w, preferred_element_type=jnp.float32)
        proj_val = jnp.einsum("ijc,cd->dij", ln_one, proj_w, preferred_element_type=jnp.float32)
        return (jax.nn.sigmoid(gate_val) * proj_val * pair_keep[None]).astype(jnp.bfloat16)

    left_tri = operand(triangle_input_weight[0], triangle_input_weight[1])
    right_tri = operand(triangle_input_weight[2], triangle_input_weight[3])
    near_right = lax.all_gather(right_tri, "sub", axis=1, tiled=True)
    left_cols, right_all = (
        lax.all_to_all(left_tri, "dap", split_axis=0, concat_axis=1, tiled=True),
        lax.all_to_all(near_right, "dap", split_axis=0, concat_axis=1, tiled=True),
    )
    product = jnp.einsum(
        "cik,cjk->cij", left_cols, right_all, preferred_element_type=jnp.float32
    ).astype(jnp.bfloat16)
    returned = lax.all_to_all(product, "dap", split_axis=1, concat_axis=0, tiled=True)
    normed = norm_layer(returned.astype(jnp.float32), 0).astype(jnp.bfloat16)
    update = jnp.einsum(
        "cij,cd->ijd", normed, triangle_output_weight, preferred_element_type=jnp.float32
    )
    gate_out = jax.nn.sigmoid(
        jnp.einsum("ijc,cd->ijd", ln_one, triangle_gate, preferred_element_type=jnp.float32)
    )
    pair_two = (pair_one.astype(jnp.float32) + gate_out * update).astype(jnp.bfloat16)
    ln_two = norm_layer(pair_two.astype(jnp.float32), -1).astype(jnp.bfloat16)

    def step(row_pair):
        return transition(*row_pair, transition_up_weight, transition_down_weight)

    return lax.map(step, (ln_two, pair_two))


def solution(mesh):
    placed = (
        P(("crop", "dap", "sub"), None, None),
        P("crop", ("dap", "sub"), None),
        P("crop", ("dap", "sub")),
        P("crop"),
        P(),
        P(),
        P(),
        P(),
        P(),
        P(),
        P(),
    )

    small = mesh.shape["sub"] == 2 and mesh.shape["dap"] == 8

    def body(pairwise_state, *rest):
        residues, channels = pairwise_state.shape[1:]
        if small and residues * residues * channels * 2 <= REPLICATED_PAIR_BYTES:
            return shards_replicated(pairwise_state, *rest)
        return shards(pairwise_state, *rest)

    return jax.shard_map(
        body,
        mesh=mesh,
        in_specs=placed,
        out_specs=P(("crop", "dap", "sub"), None, None),
        check_vma=False,
    )
```

```python
import jax
import jax.numpy as jnp
from jax import lax
from jax.experimental import pallas as pl
from jax.experimental.pallas import tpu as pltpu
from jax.sharding import PartitionSpec as P

REPLICATED_PAIR_BYTES = 1 << 20


def norm_layer(values, reduce_axis):
    average = jnp.mean(values, axis=reduce_axis, keepdims=True)
    centered = values - average
    variance = jnp.mean(centered * centered, axis=reduce_axis, keepdims=True)
    return centered * lax.rsqrt(variance + 1e-05)


def transition(ln_two, pair_two, transition_up_weight, transition_down_weight):
    hidden = jax.nn.relu(
        jnp.dot(ln_two, transition_up_weight, preferred_element_type=jnp.float32)
    ).astype(jnp.bfloat16)
    return (
        pair_two.astype(jnp.float32)
        + jnp.dot(hidden, transition_down_weight, preferred_element_type=jnp.float32)
    ).astype(jnp.bfloat16)


def layer_norm(values):
    count = values.shape[-1]
    centered = values - jnp.sum(values, axis=-1, keepdims=True) * (1.0 / count)
    variance = jnp.sum(centered * centered, axis=-1, keepdims=True) * (1.0 / count)
    return centered * lax.rsqrt(variance + 1e-05)


def first_row(rows):
    return (lax.axis_index("dap") * lax.axis_size("sub") + lax.axis_index("sub")) * rows


def pack_kernel(
    mask_hbm,
    keep_hbm,
    state_hbm,
    weight_hbm,
    pair_hbm,
    out_hbm,
    mask_ref,
    keep_ref,
    state_ref,
    weight_ref,
    wide_ref,
    out_ref,
    sems,
):
    rows, residues, wide = pair_hbm.shape
    sequences = state_ref.shape[0]
    base = rows * residues
    start = first_row(rows)
    second_core = lax.axis_index("sub") == 1
    loads = [
        pltpu.make_async_copy(state_hbm, state_ref, sems.at[0]),
        pltpu.make_async_copy(weight_hbm, weight_ref, sems.at[1]),
        pltpu.make_async_copy(keep_hbm, keep_ref, sems.at[2]),
        pltpu.make_async_copy(mask_hbm, mask_ref, sems.at[3]),
    ] + [
        pltpu.make_async_copy(
            pair_hbm.at[row], out_hbm.at[pl.ds(row * residues, residues)], sems.at[5 + row]
        )
        for row in range(rows)
    ]
    for load in loads:
        load.start()
    loads[0].wait()
    wide_ref[...] = state_ref[...].astype(jnp.float32)
    normed_rows = [layer_norm(wide_ref[:, row]).astype(jnp.bfloat16) for row in range(rows)]
    eye = lax.broadcasted_iota(jnp.int32, (sequences, sequences), 0) == lax.broadcasted_iota(
        jnp.int32, (sequences, sequences), 1
    )
    lefts, rights, keeps = [], [], []
    for load in loads[1:4]:
        load.wait()
    for row in range(rows):
        present = mask_ref[start + row].astype(jnp.float32)
        keep_row = keep_ref[row : row + 1].astype(jnp.float32) * present
        keep_column = jnp.sum(
            jnp.where(eye, jnp.broadcast_to(keep_row, eye.shape), 0.0), axis=1, keepdims=True
        )
        normed = normed_rows[row]
        last = (((1,), (1,)), ((), ()))
        left = lax.dot_general(weight_ref[0], normed, last, preferred_element_type=jnp.float32)
        right = lax.dot_general(normed, weight_ref[1], last, preferred_element_type=jnp.float32)
        lefts.append(left * keep_row)
        rights.append(right * keep_column)
        keeps.append(
            jnp.concatenate(
                [keep_row, jnp.full((1, wide - sequences), present, jnp.float32)], axis=1
            )
        )
    left = jnp.concatenate(lefts, axis=1)
    right = jnp.concatenate(rights, axis=1)
    first = jnp.concatenate([right, left], axis=1)
    other = jnp.concatenate([left, right], axis=1)
    out_ref[:sequences] = jnp.where(second_core, other, first).astype(jnp.bfloat16)
    out_ref[sequences:] = jnp.concatenate(
        keeps + [jnp.zeros((16 - rows, wide), jnp.float32)], axis=0
    ).astype(jnp.bfloat16)
    store = pltpu.make_async_copy(
        out_ref, out_hbm.at[pl.ds(base, sequences + 16)], sems.at[4]
    )
    store.start()
    store.wait()
    for load in loads[4:]:
        load.wait()


def sigmoid(values):
    return 0.5 * jnp.tanh(0.5 * values) + 0.5


def update_kernel(
    held_ref,
    other_ref,
    outer_ref,
    triangle_ref,
    gate_ref,
    output_ref,
    up_ref,
    down_ref,
    out_ref,
    block_ref,
    left_ref,
    right_ref,
    keep_ref,
    first_ref,
    second_ref,
    pair_ref,
    pair_one_ref,
    ln_one_ref,
):
    rows, residues, wide = out_ref.shape
    cores, chips = 2, lax.axis_size("dap")
    channels = outer_ref.shape[0]
    sequences = channels
    base = rows * residues
    half = wide // 2
    group = cores * rows
    start = first_row(rows)
    second_core = lax.axis_index("sub") == 1
    bf16 = jnp.bfloat16
    f32 = jnp.float32

    parts = block_ref.shape[0]
    span = channels // parts
    nothing = jnp.zeros((channels, wide), bf16)
    for part in range(parts):
        for step in range(span + 1):
            weight = outer_ref[part * span + step % span]
            at = step * 2 * channels
            block_ref[part, at : at + channels, :wide] = weight
            block_ref[part, at : at + channels, wide:] = nothing
            block_ref[part, at + channels : at + 2 * channels, :wide] = nothing
            block_ref[part, at + channels : at + 2 * channels, wide:] = weight

    lane = lax.broadcasted_iota(jnp.int32, (channels, wide), 1)
    lane_block = lane // channels
    low = lane < half
    for chip in range(chips):
        place = block_place(chip, chips)
        mine, other = held_ref[place], other_ref[place]
        blocks = [jnp.where(second_core, other, mine), jnp.where(second_core, mine, other)]
        packed = [block[base : base + sequences].astype(f32) for block in blocks]
        right = jnp.where(low, packed[0], packed[1])
        for turn, value in enumerate((right, pltpu.roll(right, half, 1))):
            for copy in range(group):
                right_ref[
                    turn,
                    copy * sequences : (copy + 1) * sequences,
                    chip * wide : (chip + 1) * wide,
                ] = value.astype(bf16)
        for core in range(cores):
            residue = (chip * cores + core) * rows
            for row in range(rows):
                at = (rows if core == 0 else 0) + row
                left_ref[residue + row] = jnp.where(lane_block == at, packed[core], 0.0)
            keep_ref[residue : residue + rows] = blocks[core][base + sequences :].astype(f32)[:rows]
            pair_ref[residue : residue + rows] = (
                blocks[core][:base].astype(f32).reshape(rows, residues, wide)
            )

    last = (((1,), (1,)), ((), ()))
    keep = keep_ref[...]
    mask = jnp.broadcast_to(keep[:, sequences : sequences + 1], (residues, wide))
    counted = lax.broadcasted_iota(jnp.int32, (residues, wide), 1) < sequences
    count = lax.dot_general(
        jnp.where(counted, keep, 0.0).astype(bf16),
        keep.astype(bf16),
        last,
        preferred_element_type=f32,
    )
    inverse = 1.0 / jnp.maximum(count, 1.0)

    low = lax.broadcasted_iota(jnp.int32, (residues, wide), 1) < half
    totals = [0.0, 0.0]
    for part in range(parts):
        outer = []
        for turn in range(2):
            left = jnp.concatenate(
                [left_ref[:, d] for d in range(part * span + turn, (part + 1) * span, 2)], axis=0
            ).astype(bf16)
            outer.append(jnp.dot(left, right_ref[turn], preferred_element_type=f32))

        def piece(turn, at, chip):
            return outer[turn][
                at * residues : (at + 1) * residues, chip * wide : (chip + 1) * wide
            ]

        for at in range(span // 2):
            follow = (at + 1) % (span // 2)
            for chip in range(chips):
                place = (
                    part,
                    slice(chip * residues, (chip + 1) * residues),
                    slice(at * wide, (at + 1) * wide),
                )
                first_ref[place] = jnp.where(low, piece(0, at, chip), piece(1, at, chip)).astype(bf16)
                second_ref[place] = jnp.where(
                    low, piece(1, at, chip), piece(0, follow, chip)
                ).astype(bf16)
        depth = span * 2 * channels
        totals[0] += jnp.dot(first_ref[part], block_ref[part, :depth], preferred_element_type=f32)
        totals[1] += jnp.dot(
            second_ref[part], block_ref[part, 2 * channels :], preferred_element_type=f32
        )

    right_weight = jnp.concatenate([triangle_ref[2], triangle_ref[3]], axis=1)
    right_tri = []
    stride = 8
    for first in range(0, residues, stride):
        normed = []
        for k in range(first, first + stride):
            chip, pick = k // group, k % group
            at = (pick % 2) * wide
            numerator = totals[pick // 2][chip * residues : (chip + 1) * residues, at : at + wide]
            opm = numerator * jnp.broadcast_to(inverse[:, k : k + 1], (residues, wide))
            pair_one = (pair_ref[:, k] + opm).astype(bf16).astype(f32)
            pair_one_ref[k] = pair_one
            ln_one = layer_norm(pair_one)
            ln_one_ref[k] = ln_one
            normed.append(ln_one.astype(bf16))
        both = jnp.dot(
            jnp.concatenate(normed, axis=0), right_weight, preferred_element_type=f32
        )
        right_tri.append((sigmoid(both[:, :wide]) * both[:, wide:]).astype(bf16).astype(f32))

    own_pair = jnp.concatenate([pair_one_ref[:, start + row] for row in range(rows)], axis=0)
    own_ln = jnp.concatenate([ln_one_ref[:, start + row] for row in range(rows)], axis=0).astype(bf16)
    left_weight = jnp.concatenate([triangle_ref[0], triangle_ref[1]], axis=1)
    both = jnp.dot(own_ln, left_weight, preferred_element_type=f32)
    left_tri = sigmoid(both[:, :wide]) * both[:, wide:] * jnp.concatenate([mask] * rows, axis=0)
    left_tri = left_tri.astype(bf16).astype(f32)
    products = []
    for row in range(rows):
        sums = [jnp.zeros((residues, wide), f32) for _ in range(4)]
        for k in range(residues):
            at = row * residues + k
            place = (k % stride) * residues
            sums[k % 4] += left_tri[at : at + 1] * right_tri[k // stride][place : place + residues]
        total = (sums[0] + sums[1]) + (sums[2] + sums[3])
        own_mask = keep_ref[pl.ds(start + row, 1), :][:, sequences : sequences + 1]
        products.append(total * (mask * own_mask))
    product = jnp.concatenate(products, axis=0).astype(bf16).astype(f32)
    normed = layer_norm(product).astype(bf16)
    update = jnp.dot(normed, output_ref[...], preferred_element_type=f32)
    gate_out = sigmoid(jnp.dot(own_ln, gate_ref[...], preferred_element_type=f32))
    pair_two = (own_pair + gate_out * update).astype(bf16).astype(f32)
    ln_two = layer_norm(pair_two).astype(bf16)
    hidden = jnp.maximum(jnp.dot(ln_two, up_ref[...], preferred_element_type=f32), 0.0).astype(bf16)
    result = pair_two + jnp.dot(hidden, down_ref[...], preferred_element_type=f32)
    out_ref[...] = result.astype(bf16).reshape(rows, residues, wide)


def copy_kernel(packed_ref, out_ref):
    out_ref[0] = packed_ref[...]


def gather_all(packed):
    dap_count = lax.axis_size("dap")
    half = dap_count // 2
    far = lax.ppermute(packed[None], "dap", [(src, src ^ half) for src in range(dap_count)])
    own = pl.pallas_call(
        copy_kernel,
        out_shape=jax.ShapeDtypeStruct((1,) + packed.shape, packed.dtype),
        in_specs=[pl.BlockSpec(memory_space=pltpu.VMEM)],
        out_specs=pl.BlockSpec(memory_space=pltpu.VMEM),
        compiler_params=pltpu.CompilerParams(vmem_limit_bytes=4 << 20),
    )(packed)
    both = jnp.concatenate([own, far], axis=0)
    swaps = {
        offset: lax.ppermute(both, "dap", [(src, src ^ offset) for src in range(dap_count)])
        for offset in range(half - 1, 0, -1)
    }
    held = [both] + [swaps[offset] for offset in range(1, half)]
    held = jnp.concatenate(held, axis=0)
    return held, lax.ppermute(held, "sub", [(0, 1), (1, 0)])


def block_place(chip, chips):
    offset = lax.bitwise_xor(lax.axis_index("dap"), chip)
    half = chips // 2
    return jnp.where(offset >= half, 2 * (offset - half) + 1, 2 * offset)


def shards_replicated(
    pairwise_state,
    alignment_state,
    alignment_mask,
    residue_crop_mask,
    outer_input_weight,
    outer_output_weight,
    triangle_input_weight,
    triangle_gate,
    triangle_output_weight,
    transition_up_weight,
    transition_down_weight,
):
    rows, residues, wide = pairwise_state.shape
    sequences = alignment_state.shape[0]
    channels = outer_input_weight.shape[2]
    vector = pl.BlockSpec(memory_space=pltpu.VMEM)
    params = pltpu.CompilerParams(vmem_limit_bytes=40 << 20)
    hbm = pl.BlockSpec(memory_space=pltpu.HBM)
    packed = pl.pallas_call(
        pack_kernel,
        out_shape=jax.ShapeDtypeStruct((rows * residues + sequences + 16, wide), jnp.bfloat16),
        in_specs=[hbm] * 5,
        out_specs=hbm,
        scratch_shapes=[
            pltpu.SMEM((residues,), jnp.int32),
            pltpu.VMEM((rows, sequences), jnp.int32),
            pltpu.VMEM(alignment_state.shape, jnp.bfloat16),
            pltpu.VMEM((2, channels, alignment_state.shape[2]), jnp.bfloat16),
            pltpu.VMEM(alignment_state.shape, jnp.float32),
            pltpu.VMEM((sequences + 16, wide), jnp.bfloat16),
            pltpu.SemaphoreType.DMA((5 + rows,)),
        ],
        compiler_params=pltpu.CompilerParams(vmem_limit_bytes=63 << 20),
    )(
        residue_crop_mask,
        alignment_mask.T,
        alignment_state,
        outer_input_weight.transpose(0, 2, 1),
        pairwise_state,
    )
    held, other = gather_all(packed)
    cores, chips = lax.axis_size("sub"), lax.axis_size("dap")
    group = cores * rows
    parts = 2
    return pl.pallas_call(
        update_kernel,
        out_shape=jax.ShapeDtypeStruct(pairwise_state.shape, jnp.bfloat16),
        in_specs=[vector] * 8,
        out_specs=vector,
        scratch_shapes=[
            pltpu.VMEM((parts, (channels // parts + 1) * 2 * channels, 2 * wide), jnp.bfloat16),
            pltpu.VMEM((residues, channels, wide), jnp.float32),
            pltpu.VMEM((2, group * sequences, chips * wide), jnp.bfloat16),
            pltpu.VMEM((residues, wide), jnp.float32),
            pltpu.VMEM((parts, chips * residues, channels // parts * wide // 2), jnp.bfloat16),
            pltpu.VMEM((parts, chips * residues, channels // parts * wide // 2), jnp.bfloat16),
            pltpu.VMEM((residues, residues, wide), jnp.float32),
            pltpu.VMEM((residues, residues, wide), jnp.float32),
            pltpu.VMEM((residues, residues, wide), jnp.float32),
        ],
        compiler_params=params,
    )(
        held,
        other,
        outer_output_weight,
        triangle_input_weight,
        triangle_gate,
        triangle_output_weight,
        transition_up_weight,
        transition_down_weight,
    )


def shards(
    pairwise_state,
    alignment_state,
    alignment_mask,
    residue_crop_mask,
    outer_input_weight,
    outer_output_weight,
    triangle_input_weight,
    triangle_gate,
    triangle_output_weight,
    transition_up_weight,
    transition_down_weight,
):
    row_count = pairwise_state.shape[0]
    start_row = lax.axis_index(("dap", "sub")) * row_count
    row_presence_mask = lax.dynamic_slice_in_dim(residue_crop_mask, start_row, row_count, 0).astype(
        jnp.float32
    )
    full_mask = residue_crop_mask.astype(jnp.float32)
    alignment_keep = alignment_mask.astype(jnp.float32) * row_presence_mask[None, :]
    alignment_normed = norm_layer(alignment_state.astype(jnp.float32), -1).astype(jnp.bfloat16)
    left_alignment = (
        jnp.einsum(
            "pxm,my->pxy",
            alignment_normed,
            outer_input_weight[0],
            preferred_element_type=jnp.float32,
        )
        * alignment_keep[:, :, None]
    ).astype(jnp.bfloat16)
    right_alignment = (
        jnp.einsum(
            "pxm,my->pxy",
            alignment_normed,
            outer_input_weight[1],
            preferred_element_type=jnp.float32,
        )
        * alignment_keep[:, :, None]
    ).astype(jnp.bfloat16)
    inner_alignment = jnp.einsum(
        "tqu,ulx->tqlx", left_alignment, outer_output_weight, preferred_element_type=jnp.float32
    ).astype(jnp.bfloat16)
    right_portion = lax.all_gather(right_alignment, ("dap", "sub"), axis=1, tiled=True)
    keep_portion = lax.all_gather(
        alignment_keep.astype(jnp.bfloat16), ("dap", "sub"), axis=1, tiled=True
    )
    numerator_sum = jnp.einsum(
        "zkwv,znw->knv", inner_alignment, right_portion, preferred_element_type=jnp.float32
    )
    pair_norm_count = jnp.einsum("cf,cg->fg", alignment_keep, keep_portion.astype(jnp.float32))
    block_part = numerator_sum / jnp.maximum(pair_norm_count, 1.0)[:, :, None]
    pair_one = (pairwise_state.astype(jnp.float32) + block_part).astype(jnp.bfloat16)
    ln_one = norm_layer(pair_one.astype(jnp.float32), -1).astype(jnp.bfloat16)
    pair_keep = row_presence_mask[:, None] * full_mask[None, :]

    def operand(gate_w, proj_w):
        gate_val = jnp.einsum("ijc,cd->dij", ln_one, gate_w, preferred_element_type=jnp.float32)
        proj_val = jnp.einsum("ijc,cd->dij", ln_one, proj_w, preferred_element_type=jnp.float32)
        return (jax.nn.sigmoid(gate_val) * proj_val * pair_keep[None]).astype(jnp.bfloat16)

    left_tri = operand(triangle_input_weight[0], triangle_input_weight[1])
    right_tri = operand(triangle_input_weight[2], triangle_input_weight[3])
    near_right = lax.all_gather(right_tri, "sub", axis=1, tiled=True)
    left_cols, right_all = (
        lax.all_to_all(left_tri, "dap", split_axis=0, concat_axis=1, tiled=True),
        lax.all_to_all(near_right, "dap", split_axis=0, concat_axis=1, tiled=True),
    )
    product = jnp.einsum(
        "cik,cjk->cij", left_cols, right_all, preferred_element_type=jnp.float32
    ).astype(jnp.bfloat16)
    returned = lax.all_to_all(product, "dap", split_axis=1, concat_axis=0, tiled=True)
    normed = norm_layer(returned.astype(jnp.float32), 0).astype(jnp.bfloat16)
    update = jnp.einsum(
        "cij,cd->ijd", normed, triangle_output_weight, preferred_element_type=jnp.float32
    )
    gate_out = jax.nn.sigmoid(
        jnp.einsum("ijc,cd->ijd", ln_one, triangle_gate, preferred_element_type=jnp.float32)
    )
    pair_two = (pair_one.astype(jnp.float32) + gate_out * update).astype(jnp.bfloat16)
    ln_two = norm_layer(pair_two.astype(jnp.float32), -1).astype(jnp.bfloat16)

    def step(row_pair):
        return transition(*row_pair, transition_up_weight, transition_down_weight)

    return lax.map(step, (ln_two, pair_two))


def solution(mesh):
    placed = (
        P(("crop", "dap", "sub"), None, None),
        P("crop", ("dap", "sub"), None),
        P("crop", ("dap", "sub")),
        P("crop"),
        P(),
        P(),
        P(),
        P(),
        P(),
        P(),
        P(),
    )

    small = mesh.shape["sub"] == 2 and mesh.shape["dap"] == 8

    def body(pairwise_state, *rest):
        residues, channels = pairwise_state.shape[1:]
        if small and residues * residues * channels * 2 <= REPLICATED_PAIR_BYTES:
            return shards_replicated(pairwise_state, *rest)
        return shards(pairwise_state, *rest)

    return jax.shard_map(
        body,
        mesh=mesh,
        in_specs=placed,
        out_specs=P(("crop", "dap", "sub"), None, None),
        check_vma=False,
    )
```

```python
import jax
import jax.numpy as jnp
from jax import lax
from jax.experimental import pallas as pl
from jax.experimental.pallas import tpu as pltpu
from jax.sharding import PartitionSpec as P

REPLICATED_PAIR_BYTES = 1 << 20


def norm_layer(values, reduce_axis):
    average = jnp.mean(values, axis=reduce_axis, keepdims=True)
    centered = values - average
    variance = jnp.mean(centered * centered, axis=reduce_axis, keepdims=True)
    return centered * lax.rsqrt(variance + 1e-05)


def transition(ln_two, pair_two, transition_up_weight, transition_down_weight):
    hidden = jax.nn.relu(
        jnp.dot(ln_two, transition_up_weight, preferred_element_type=jnp.float32)
    ).astype(jnp.bfloat16)
    return (
        pair_two.astype(jnp.float32)
        + jnp.dot(hidden, transition_down_weight, preferred_element_type=jnp.float32)
    ).astype(jnp.bfloat16)


def layer_norm(values):
    count = values.shape[-1]
    centered = values - jnp.sum(values, axis=-1, keepdims=True) * (1.0 / count)
    variance = jnp.sum(centered * centered, axis=-1, keepdims=True) * (1.0 / count)
    return centered * lax.rsqrt(variance + 1e-05)


def first_row(rows):
    return (lax.axis_index("dap") * lax.axis_size("sub") + lax.axis_index("sub")) * rows


def pack_kernel(
    mask_hbm,
    keep_hbm,
    state_hbm,
    weight_hbm,
    pair_hbm,
    out_hbm,
    mask_ref,
    keep_ref,
    state_ref,
    weight_ref,
    wide_ref,
    out_ref,
    sems,
):
    rows, residues, wide = pair_hbm.shape
    sequences = state_ref.shape[0]
    base = rows * residues
    start = first_row(rows)
    second_core = lax.axis_index("sub") == 1
    loads = [
        pltpu.make_async_copy(state_hbm, state_ref, sems.at[0]),
        pltpu.make_async_copy(weight_hbm, weight_ref, sems.at[1]),
        pltpu.make_async_copy(keep_hbm, keep_ref, sems.at[2]),
        pltpu.make_async_copy(mask_hbm, mask_ref, sems.at[3]),
    ] + [
        pltpu.make_async_copy(
            pair_hbm.at[row], out_hbm.at[pl.ds(row * residues, residues)], sems.at[5 + row]
        )
        for row in range(rows)
    ]
    for load in loads:
        load.start()
    loads[0].wait()
    wide_ref[...] = state_ref[...].astype(jnp.float32)
    normed_rows = [layer_norm(wide_ref[:, row]).astype(jnp.bfloat16) for row in range(rows)]
    eye = lax.broadcasted_iota(jnp.int32, (sequences, sequences), 0) == lax.broadcasted_iota(
        jnp.int32, (sequences, sequences), 1
    )
    lefts, rights, keeps = [], [], []
    for load in loads[1:4]:
        load.wait()
    for row in range(rows):
        present = mask_ref[start + row].astype(jnp.float32)
        keep_row = keep_ref[row : row + 1].astype(jnp.float32) * present
        keep_column = jnp.sum(
            jnp.where(eye, jnp.broadcast_to(keep_row, eye.shape), 0.0), axis=1, keepdims=True
        )
        normed = normed_rows[row]
        last = (((1,), (1,)), ((), ()))
        left = lax.dot_general(weight_ref[0], normed, last, preferred_element_type=jnp.float32)
        right = lax.dot_general(normed, weight_ref[1], last, preferred_element_type=jnp.float32)
        lefts.append(left * keep_row)
        rights.append(right * keep_column)
        keeps.append(
            jnp.concatenate(
                [keep_row, jnp.full((1, wide - sequences), present, jnp.float32)], axis=1
            )
        )
    left = jnp.concatenate(lefts, axis=1)
    right = jnp.concatenate(rights, axis=1)
    first = jnp.concatenate([right, left], axis=1)
    other = jnp.concatenate([left, right], axis=1)
    out_ref[:sequences] = jnp.where(second_core, other, first).astype(jnp.bfloat16)
    out_ref[sequences:] = jnp.concatenate(
        keeps + [jnp.zeros((16 - rows, wide), jnp.float32)], axis=0
    ).astype(jnp.bfloat16)
    store = pltpu.make_async_copy(
        out_ref, out_hbm.at[pl.ds(base, sequences + 16)], sems.at[4]
    )
    store.start()
    store.wait()
    for load in loads[4:]:
        load.wait()


def sigmoid(values):
    return 0.5 * jnp.tanh(0.5 * values) + 0.5


def update_kernel(
    held_ref,
    other_ref,
    outer_ref,
    triangle_ref,
    gate_ref,
    output_ref,
    up_ref,
    down_ref,
    out_ref,
    block_ref,
    left_ref,
    right_ref,
    keep_ref,
    first_ref,
    second_ref,
    pair_ref,
    pair_one_ref,
    ln_one_ref,
):
    rows, residues, wide = out_ref.shape
    cores, chips = 2, lax.axis_size("dap")
    channels = outer_ref.shape[0]
    sequences = channels
    base = rows * residues
    half = wide // 2
    group = cores * rows
    start = first_row(rows)
    second_core = lax.axis_index("sub") == 1
    bf16 = jnp.bfloat16
    f32 = jnp.float32

    parts = block_ref.shape[0]
    span = channels // parts
    nothing = jnp.zeros((channels, wide), bf16)
    for part in range(parts):
        for step in range(span + 1):
            weight = outer_ref[part * span + step % span]
            at = step * 2 * channels
            block_ref[part, at : at + channels, :wide] = weight
            block_ref[part, at : at + channels, wide:] = nothing
            block_ref[part, at + channels : at + 2 * channels, :wide] = nothing
            block_ref[part, at + channels : at + 2 * channels, wide:] = weight

    lane = lax.broadcasted_iota(jnp.int32, (channels, wide), 1)
    lane_block = lane // channels
    low = lane < half
    for chip in range(chips):
        place = block_place(chip, chips)
        mine, other = held_ref[place], other_ref[place]
        blocks = [jnp.where(second_core, other, mine), jnp.where(second_core, mine, other)]
        packed = [block[base : base + sequences].astype(f32) for block in blocks]
        right = jnp.where(low, packed[0], packed[1])
        for turn, value in enumerate((right, pltpu.roll(right, half, 1))):
            for copy in range(group):
                right_ref[
                    turn,
                    copy * sequences : (copy + 1) * sequences,
                    chip * wide : (chip + 1) * wide,
                ] = value.astype(bf16)
        for core in range(cores):
            residue = (chip * cores + core) * rows
            for row in range(rows):
                at = (rows if core == 0 else 0) + row
                left_ref[residue + row] = jnp.where(lane_block == at, packed[core], 0.0)
            keep_ref[residue : residue + rows] = blocks[core][base + sequences :].astype(f32)[:rows]
            pair_ref[residue : residue + rows] = (
                blocks[core][:base].astype(f32).reshape(rows, residues, wide)
            )

    last = (((1,), (1,)), ((), ()))
    keep = keep_ref[...]
    mask = jnp.broadcast_to(keep[:, sequences : sequences + 1], (residues, wide))
    counted = lax.broadcasted_iota(jnp.int32, (residues, wide), 1) < sequences
    count = lax.dot_general(
        jnp.where(counted, keep, 0.0).astype(bf16),
        keep.astype(bf16),
        last,
        preferred_element_type=f32,
    )
    inverse = 1.0 / jnp.maximum(count, 1.0)

    low = lax.broadcasted_iota(jnp.int32, (residues, wide), 1) < half
    totals = [0.0, 0.0]
    for part in range(parts):
        outer = []
        for turn in range(2):
            left = jnp.concatenate(
                [left_ref[:, d] for d in range(part * span + turn, (part + 1) * span, 2)], axis=0
            ).astype(bf16)
            outer.append(jnp.dot(left, right_ref[turn], preferred_element_type=f32))

        def piece(turn, at, chip):
            return outer[turn][
                at * residues : (at + 1) * residues, chip * wide : (chip + 1) * wide
            ]

        for at in range(span // 2):
            follow = (at + 1) % (span // 2)
            for chip in range(chips):
                place = (
                    part,
                    slice(chip * residues, (chip + 1) * residues),
                    slice(at * wide, (at + 1) * wide),
                )
                first_ref[place] = jnp.where(low, piece(0, at, chip), piece(1, at, chip)).astype(bf16)
                second_ref[place] = jnp.where(
                    low, piece(1, at, chip), piece(0, follow, chip)
                ).astype(bf16)
        depth = span * 2 * channels
        totals[0] += jnp.dot(first_ref[part], block_ref[part, :depth], preferred_element_type=f32)
        totals[1] += jnp.dot(
            second_ref[part], block_ref[part, 2 * channels :], preferred_element_type=f32
        )

    right_weight = jnp.concatenate([triangle_ref[2], triangle_ref[3]], axis=1)
    right_tri = []
    stride = 8
    for first in range(0, residues, stride):
        normed = []
        for k in range(first, first + stride):
            chip, pick = k // group, k % group
            at = (pick % 2) * wide
            numerator = totals[pick // 2][chip * residues : (chip + 1) * residues, at : at + wide]
            opm = numerator * jnp.broadcast_to(inverse[:, k : k + 1], (residues, wide))
            pair_one = (pair_ref[:, k] + opm).astype(bf16).astype(f32)
            pair_one_ref[k] = pair_one
            ln_one = layer_norm(pair_one)
            ln_one_ref[k] = ln_one
            normed.append(ln_one.astype(bf16))
        both = jnp.dot(
            jnp.concatenate(normed, axis=0), right_weight, preferred_element_type=f32
        )
        right_tri.append((sigmoid(both[:, :wide]) * both[:, wide:]).astype(bf16).astype(f32))

    own_pair = jnp.concatenate([pair_one_ref[:, start + row] for row in range(rows)], axis=0)
    own_ln = jnp.concatenate([ln_one_ref[:, start + row] for row in range(rows)], axis=0).astype(bf16)
    left_weight = jnp.concatenate([triangle_ref[0], triangle_ref[1]], axis=1)
    both = jnp.dot(own_ln, left_weight, preferred_element_type=f32)
    left_tri = sigmoid(both[:, :wide]) * both[:, wide:] * jnp.concatenate([mask] * rows, axis=0)
    left_tri = left_tri.astype(bf16).astype(f32)
    products = []
    for row in range(rows):
        sums = [jnp.zeros((residues, wide), f32) for _ in range(4)]
        for k in range(residues):
            at = row * residues + k
            place = (k % stride) * residues
            sums[k % 4] += left_tri[at : at + 1] * right_tri[k // stride][place : place + residues]
        total = (sums[0] + sums[1]) + (sums[2] + sums[3])
        own_mask = keep_ref[pl.ds(start + row, 1), :][:, sequences : sequences + 1]
        products.append(total * (mask * own_mask))
    product = jnp.concatenate(products, axis=0).astype(bf16).astype(f32)
    normed = layer_norm(product).astype(bf16)
    update = jnp.dot(normed, output_ref[...], preferred_element_type=f32)
    gate_out = sigmoid(jnp.dot(own_ln, gate_ref[...], preferred_element_type=f32))
    pair_two = (own_pair + gate_out * update).astype(bf16).astype(f32)
    ln_two = layer_norm(pair_two).astype(bf16)
    hidden = jnp.maximum(jnp.dot(ln_two, up_ref[...], preferred_element_type=f32), 0.0).astype(bf16)
    result = pair_two + jnp.dot(hidden, down_ref[...], preferred_element_type=f32)
    out_ref[...] = result.astype(bf16).reshape(rows, residues, wide)


def copy_kernel(packed_ref, out_ref):
    out_ref[0] = packed_ref[...]


def gather_all(packed):
    dap_count = lax.axis_size("dap")
    half = dap_count // 2
    far = lax.ppermute(packed[None], "dap", [(src, src ^ half) for src in range(dap_count)])
    own = pl.pallas_call(
        copy_kernel,
        out_shape=jax.ShapeDtypeStruct((1,) + packed.shape, packed.dtype),
        in_specs=[pl.BlockSpec(memory_space=pltpu.VMEM)],
        out_specs=pl.BlockSpec(memory_space=pltpu.VMEM),
        compiler_params=pltpu.CompilerParams(vmem_limit_bytes=4 << 20),
    )(packed)
    both = jnp.concatenate([own, far], axis=0)
    held = [both] + [
        lax.ppermute(both, "dap", [(src, src ^ offset) for src in range(dap_count)])
        for offset in swap_order(dap_count)
    ]
    held = jnp.concatenate(held, axis=0)
    return held, lax.ppermute(held, "sub", [(0, 1), (1, 0)])


def swap_order(dap_count):
    return list(range(dap_count // 2 - 1, 0, -1))


def block_place(chip, chips):
    offset = lax.bitwise_xor(lax.axis_index("dap"), chip)
    half = chips // 2
    near = jnp.where(offset >= half, offset - half, offset)
    turn = jnp.where(near == 0, 0, half - near)
    return 2 * turn + jnp.where(offset >= half, 1, 0)


def shards_replicated(
    pairwise_state,
    alignment_state,
    alignment_mask,
    residue_crop_mask,
    outer_input_weight,
    outer_output_weight,
    triangle_input_weight,
    triangle_gate,
    triangle_output_weight,
    transition_up_weight,
    transition_down_weight,
):
    rows, residues, wide = pairwise_state.shape
    sequences = alignment_state.shape[0]
    channels = outer_input_weight.shape[2]
    vector = pl.BlockSpec(memory_space=pltpu.VMEM)
    params = pltpu.CompilerParams(vmem_limit_bytes=40 << 20)
    hbm = pl.BlockSpec(memory_space=pltpu.HBM)
    packed = pl.pallas_call(
        pack_kernel,
        out_shape=jax.ShapeDtypeStruct((rows * residues + sequences + 16, wide), jnp.bfloat16),
        in_specs=[hbm] * 5,
        out_specs=hbm,
        scratch_shapes=[
            pltpu.SMEM((residues,), jnp.int32),
            pltpu.VMEM((rows, sequences), jnp.int32),
            pltpu.VMEM(alignment_state.shape, jnp.bfloat16),
            pltpu.VMEM((2, channels, alignment_state.shape[2]), jnp.bfloat16),
            pltpu.VMEM(alignment_state.shape, jnp.float32),
            pltpu.VMEM((sequences + 16, wide), jnp.bfloat16),
            pltpu.SemaphoreType.DMA((5 + rows,)),
        ],
        compiler_params=pltpu.CompilerParams(vmem_limit_bytes=63 << 20),
    )(
        residue_crop_mask,
        alignment_mask.T,
        alignment_state,
        outer_input_weight.transpose(0, 2, 1),
        pairwise_state,
    )
    held, other = gather_all(packed)
    cores, chips = lax.axis_size("sub"), lax.axis_size("dap")
    group = cores * rows
    parts = 2
    return pl.pallas_call(
        update_kernel,
        out_shape=jax.ShapeDtypeStruct(pairwise_state.shape, jnp.bfloat16),
        in_specs=[vector] * 8,
        out_specs=vector,
        scratch_shapes=[
            pltpu.VMEM((parts, (channels // parts + 1) * 2 * channels, 2 * wide), jnp.bfloat16),
            pltpu.VMEM((residues, channels, wide), jnp.float32),
            pltpu.VMEM((2, group * sequences, chips * wide), jnp.bfloat16),
            pltpu.VMEM((residues, wide), jnp.float32),
            pltpu.VMEM((parts, chips * residues, channels // parts * wide // 2), jnp.bfloat16),
            pltpu.VMEM((parts, chips * residues, channels // parts * wide // 2), jnp.bfloat16),
            pltpu.VMEM((residues, residues, wide), jnp.float32),
            pltpu.VMEM((residues, residues, wide), jnp.float32),
            pltpu.VMEM((residues, residues, wide), jnp.float32),
        ],
        compiler_params=params,
    )(
        held,
        other,
        outer_output_weight,
        triangle_input_weight,
        triangle_gate,
        triangle_output_weight,
        transition_up_weight,
        transition_down_weight,
    )


def shards(
    pairwise_state,
    alignment_state,
    alignment_mask,
    residue_crop_mask,
    outer_input_weight,
    outer_output_weight,
    triangle_input_weight,
    triangle_gate,
    triangle_output_weight,
    transition_up_weight,
    transition_down_weight,
):
    row_count = pairwise_state.shape[0]
    start_row = lax.axis_index(("dap", "sub")) * row_count
    row_presence_mask = lax.dynamic_slice_in_dim(residue_crop_mask, start_row, row_count, 0).astype(
        jnp.float32
    )
    full_mask = residue_crop_mask.astype(jnp.float32)
    alignment_keep = alignment_mask.astype(jnp.float32) * row_presence_mask[None, :]
    alignment_normed = norm_layer(alignment_state.astype(jnp.float32), -1).astype(jnp.bfloat16)
    left_alignment = (
        jnp.einsum(
            "pxm,my->pxy",
            alignment_normed,
            outer_input_weight[0],
            preferred_element_type=jnp.float32,
        )
        * alignment_keep[:, :, None]
    ).astype(jnp.bfloat16)
    right_alignment = (
        jnp.einsum(
            "pxm,my->pxy",
            alignment_normed,
            outer_input_weight[1],
            preferred_element_type=jnp.float32,
        )
        * alignment_keep[:, :, None]
    ).astype(jnp.bfloat16)
    inner_alignment = jnp.einsum(
        "tqu,ulx->tqlx", left_alignment, outer_output_weight, preferred_element_type=jnp.float32
    ).astype(jnp.bfloat16)
    right_portion = lax.all_gather(right_alignment, ("dap", "sub"), axis=1, tiled=True)
    keep_portion = lax.all_gather(
        alignment_keep.astype(jnp.bfloat16), ("dap", "sub"), axis=1, tiled=True
    )
    numerator_sum = jnp.einsum(
        "zkwv,znw->knv", inner_alignment, right_portion, preferred_element_type=jnp.float32
    )
    pair_norm_count = jnp.einsum("cf,cg->fg", alignment_keep, keep_portion.astype(jnp.float32))
    block_part = numerator_sum / jnp.maximum(pair_norm_count, 1.0)[:, :, None]
    pair_one = (pairwise_state.astype(jnp.float32) + block_part).astype(jnp.bfloat16)
    ln_one = norm_layer(pair_one.astype(jnp.float32), -1).astype(jnp.bfloat16)
    pair_keep = row_presence_mask[:, None] * full_mask[None, :]

    def operand(gate_w, proj_w):
        gate_val = jnp.einsum("ijc,cd->dij", ln_one, gate_w, preferred_element_type=jnp.float32)
        proj_val = jnp.einsum("ijc,cd->dij", ln_one, proj_w, preferred_element_type=jnp.float32)
        return (jax.nn.sigmoid(gate_val) * proj_val * pair_keep[None]).astype(jnp.bfloat16)

    left_tri = operand(triangle_input_weight[0], triangle_input_weight[1])
    right_tri = operand(triangle_input_weight[2], triangle_input_weight[3])
    near_right = lax.all_gather(right_tri, "sub", axis=1, tiled=True)
    left_cols, right_all = (
        lax.all_to_all(left_tri, "dap", split_axis=0, concat_axis=1, tiled=True),
        lax.all_to_all(near_right, "dap", split_axis=0, concat_axis=1, tiled=True),
    )
    product = jnp.einsum(
        "cik,cjk->cij", left_cols, right_all, preferred_element_type=jnp.float32
    ).astype(jnp.bfloat16)
    returned = lax.all_to_all(product, "dap", split_axis=1, concat_axis=0, tiled=True)
    normed = norm_layer(returned.astype(jnp.float32), 0).astype(jnp.bfloat16)
    update = jnp.einsum(
        "cij,cd->ijd", normed, triangle_output_weight, preferred_element_type=jnp.float32
    )
    gate_out = jax.nn.sigmoid(
        jnp.einsum("ijc,cd->ijd", ln_one, triangle_gate, preferred_element_type=jnp.float32)
    )
    pair_two = (pair_one.astype(jnp.float32) + gate_out * update).astype(jnp.bfloat16)
    ln_two = norm_layer(pair_two.astype(jnp.float32), -1).astype(jnp.bfloat16)

    def step(row_pair):
        return transition(*row_pair, transition_up_weight, transition_down_weight)

    return lax.map(step, (ln_two, pair_two))


def solution(mesh):
    placed = (
        P(("crop", "dap", "sub"), None, None),
        P("crop", ("dap", "sub"), None),
        P("crop", ("dap", "sub")),
        P("crop"),
        P(),
        P(),
        P(),
        P(),
        P(),
        P(),
        P(),
    )

    small = mesh.shape["sub"] == 2 and mesh.shape["dap"] == 8

    def body(pairwise_state, *rest):
        residues, channels = pairwise_state.shape[1:]
        if small and residues * residues * channels * 2 <= REPLICATED_PAIR_BYTES:
            return shards_replicated(pairwise_state, *rest)
        return shards(pairwise_state, *rest)

    return jax.shard_map(
        body,
        mesh=mesh,
        in_specs=placed,
        out_specs=P(("crop", "dap", "sub"), None, None),
        check_vma=False,
    )
```

```python
import jax
import jax.numpy as jnp
from jax import lax
from jax.experimental import pallas as pl
from jax.experimental.pallas import tpu as pltpu
from jax.sharding import PartitionSpec as P

REPLICATED_PAIR_BYTES = 1 << 20


def norm_layer(values, reduce_axis):
    average = jnp.mean(values, axis=reduce_axis, keepdims=True)
    centered = values - average
    variance = jnp.mean(centered * centered, axis=reduce_axis, keepdims=True)
    return centered * lax.rsqrt(variance + 1e-05)


def transition(ln_two, pair_two, transition_up_weight, transition_down_weight):
    hidden = jax.nn.relu(
        jnp.dot(ln_two, transition_up_weight, preferred_element_type=jnp.float32)
    ).astype(jnp.bfloat16)
    return (
        pair_two.astype(jnp.float32)
        + jnp.dot(hidden, transition_down_weight, preferred_element_type=jnp.float32)
    ).astype(jnp.bfloat16)


def layer_norm(values):
    count = values.shape[-1]
    centered = values - jnp.sum(values, axis=-1, keepdims=True) * (1.0 / count)
    variance = jnp.sum(centered * centered, axis=-1, keepdims=True) * (1.0 / count)
    return centered * lax.rsqrt(variance + 1e-05)


def first_row(rows):
    return (lax.axis_index("dap") * lax.axis_size("sub") + lax.axis_index("sub")) * rows


def pack_kernel(
    mask_hbm,
    keep_hbm,
    state_hbm,
    weight_hbm,
    pair_hbm,
    out_hbm,
    mask_ref,
    keep_ref,
    state_ref,
    weight_ref,
    wide_ref,
    out_ref,
    sems,
):
    rows, residues, wide = pair_hbm.shape
    sequences = state_ref.shape[0]
    base = rows * residues
    start = first_row(rows)
    second_core = lax.axis_index("sub") == 1
    loads = [
        pltpu.make_async_copy(state_hbm, state_ref, sems.at[0]),
        pltpu.make_async_copy(weight_hbm, weight_ref, sems.at[1]),
        pltpu.make_async_copy(keep_hbm, keep_ref, sems.at[2]),
        pltpu.make_async_copy(mask_hbm, mask_ref, sems.at[3]),
    ] + [
        pltpu.make_async_copy(
            pair_hbm.at[row], out_hbm.at[pl.ds(row * residues, residues)], sems.at[5 + row]
        )
        for row in range(rows)
    ]
    for load in loads:
        load.start()
    loads[0].wait()
    wide_ref[...] = state_ref[...].astype(jnp.float32)
    normed_rows = [layer_norm(wide_ref[:, row]).astype(jnp.bfloat16) for row in range(rows)]
    eye = lax.broadcasted_iota(jnp.int32, (sequences, sequences), 0) == lax.broadcasted_iota(
        jnp.int32, (sequences, sequences), 1
    )
    lefts, rights, keeps = [], [], []
    for load in loads[1:4]:
        load.wait()
    for row in range(rows):
        present = mask_ref[start + row].astype(jnp.float32)
        keep_row = keep_ref[row : row + 1].astype(jnp.float32) * present
        keep_column = jnp.sum(
            jnp.where(eye, jnp.broadcast_to(keep_row, eye.shape), 0.0), axis=1, keepdims=True
        )
        normed = normed_rows[row]
        last = (((1,), (1,)), ((), ()))
        left = lax.dot_general(weight_ref[0], normed, last, preferred_element_type=jnp.float32)
        right = lax.dot_general(normed, weight_ref[1], last, preferred_element_type=jnp.float32)
        lefts.append(left * keep_row)
        rights.append(right * keep_column)
        keeps.append(
            jnp.concatenate(
                [keep_row, jnp.full((1, wide - sequences), present, jnp.float32)], axis=1
            )
        )
    left = jnp.concatenate(lefts, axis=1)
    right = jnp.concatenate(rights, axis=1)
    first = jnp.concatenate([right, left], axis=1)
    other = jnp.concatenate([left, right], axis=1)
    out_ref[:sequences] = jnp.where(second_core, other, first).astype(jnp.bfloat16)
    out_ref[sequences:] = jnp.concatenate(
        keeps + [jnp.zeros((16 - rows, wide), jnp.float32)], axis=0
    ).astype(jnp.bfloat16)
    store = pltpu.make_async_copy(
        out_ref, out_hbm.at[pl.ds(base, sequences + 16)], sems.at[4]
    )
    store.start()
    store.wait()
    for load in loads[4:]:
        load.wait()


def sigmoid(values):
    return 0.5 * jnp.tanh(0.5 * values) + 0.5


def update_kernel(
    held_ref,
    other_ref,
    outer_ref,
    triangle_ref,
    gate_ref,
    output_ref,
    up_ref,
    down_ref,
    out_ref,
    block_ref,
    left_ref,
    right_ref,
    keep_ref,
    first_ref,
    second_ref,
    pair_ref,
    pair_one_ref,
    ln_one_ref,
):
    rows, residues, wide = out_ref.shape
    cores, chips = 2, lax.axis_size("dap")
    channels = outer_ref.shape[0]
    sequences = channels
    base = rows * residues
    half = wide // 2
    group = cores * rows
    start = first_row(rows)
    second_core = lax.axis_index("sub") == 1
    bf16 = jnp.bfloat16
    f32 = jnp.float32

    parts = block_ref.shape[0]
    span = channels // parts
    nothing = jnp.zeros((channels, wide), bf16)
    for part in range(parts):
        for step in range(span + 1):
            weight = outer_ref[part * span + step % span]
            at = step * 2 * channels
            block_ref[part, at : at + channels, :wide] = weight
            block_ref[part, at : at + channels, wide:] = nothing
            block_ref[part, at + channels : at + 2 * channels, :wide] = nothing
            block_ref[part, at + channels : at + 2 * channels, wide:] = weight

    lane = lax.broadcasted_iota(jnp.int32, (channels, wide), 1)
    lane_block = lane // channels
    low = lane < half
    for chip in range(chips):
        place = block_place(chip, chips)
        mine, other = held_ref[place], other_ref[place]
        blocks = [jnp.where(second_core, other, mine), jnp.where(second_core, mine, other)]
        packed = [block[base : base + sequences].astype(f32) for block in blocks]
        right = jnp.where(low, packed[0], packed[1])
        turned = pltpu.roll(right, half, 1)
        for turn, (near, far) in enumerate(((right, turned), (turned, right))):
            near = jnp.where(low, near, 0.0).astype(bf16)
            far = jnp.where(low, 0.0, far).astype(bf16)
            for copy in range(2 * group):
                right_ref[
                    turn,
                    copy * sequences : (copy + 1) * sequences,
                    chip * wide : (chip + 1) * wide,
                ] = near if copy < group else far
        for core in range(cores):
            residue = (chip * cores + core) * rows
            for row in range(rows):
                at = (rows if core == 0 else 0) + row
                left_ref[residue + row] = jnp.where(lane_block == at, packed[core], 0.0)
            keep_ref[residue : residue + rows] = blocks[core][base + sequences :].astype(f32)[:rows]
            pair_ref[residue : residue + rows] = (
                blocks[core][:base].astype(f32).reshape(rows, residues, wide)
            )

    last = (((1,), (1,)), ((), ()))
    keep = keep_ref[...]
    mask = jnp.broadcast_to(keep[:, sequences : sequences + 1], (residues, wide))
    counted = lax.broadcasted_iota(jnp.int32, (residues, wide), 1) < sequences
    count = lax.dot_general(
        jnp.where(counted, keep, 0.0).astype(bf16),
        keep.astype(bf16),
        last,
        preferred_element_type=f32,
    )
    inverse = 1.0 / jnp.maximum(count, 1.0)

    totals = [0.0, 0.0]
    for part in range(parts):
        left = [left_ref[:, d].astype(bf16) for d in range(part * span, (part + 1) * span)]
        for turn, outer_ref_part in enumerate((first_ref, second_ref)):
            pairs = jnp.concatenate(
                [
                    jnp.concatenate([left[d], left[(d + 1) % span]], axis=1)
                    for d in range(turn, span, 2)
                ],
                axis=0,
            )
            outer = jnp.dot(pairs, right_ref[turn], preferred_element_type=f32).astype(bf16)
            for at in range(span // 2):
                for chip in range(chips):
                    outer_ref_part[
                        part,
                        chip * residues : (chip + 1) * residues,
                        at * wide : (at + 1) * wide,
                    ] = outer[
                        at * residues : (at + 1) * residues, chip * wide : (chip + 1) * wide
                    ]
        depth = span * 2 * channels
        totals[0] += jnp.dot(first_ref[part], block_ref[part, :depth], preferred_element_type=f32)
        totals[1] += jnp.dot(
            second_ref[part], block_ref[part, 2 * channels :], preferred_element_type=f32
        )

    right_weight = jnp.concatenate([triangle_ref[2], triangle_ref[3]], axis=1)
    right_tri = []
    stride = 8
    for first in range(0, residues, stride):
        normed = []
        for k in range(first, first + stride):
            chip, pick = k // group, k % group
            at = (pick % 2) * wide
            numerator = totals[pick // 2][chip * residues : (chip + 1) * residues, at : at + wide]
            opm = numerator * jnp.broadcast_to(inverse[:, k : k + 1], (residues, wide))
            pair_one = (pair_ref[:, k] + opm).astype(bf16).astype(f32)
            pair_one_ref[k] = pair_one
            ln_one = layer_norm(pair_one)
            ln_one_ref[k] = ln_one
            normed.append(ln_one.astype(bf16))
        both = jnp.dot(
            jnp.concatenate(normed, axis=0), right_weight, preferred_element_type=f32
        )
        right_tri.append((sigmoid(both[:, :wide]) * both[:, wide:]).astype(bf16).astype(f32))

    own_pair = jnp.concatenate([pair_one_ref[:, start + row] for row in range(rows)], axis=0)
    own_ln = jnp.concatenate([ln_one_ref[:, start + row] for row in range(rows)], axis=0).astype(bf16)
    left_weight = jnp.concatenate([triangle_ref[0], triangle_ref[1]], axis=1)
    both = jnp.dot(own_ln, left_weight, preferred_element_type=f32)
    left_tri = sigmoid(both[:, :wide]) * both[:, wide:] * jnp.concatenate([mask] * rows, axis=0)
    left_tri = left_tri.astype(bf16).astype(f32)
    products = []
    for row in range(rows):
        sums = [jnp.zeros((residues, wide), f32) for _ in range(4)]
        for k in range(residues):
            at = row * residues + k
            place = (k % stride) * residues
            sums[k % 4] += left_tri[at : at + 1] * right_tri[k // stride][place : place + residues]
        total = (sums[0] + sums[1]) + (sums[2] + sums[3])
        own_mask = keep_ref[pl.ds(start + row, 1), :][:, sequences : sequences + 1]
        products.append(total * (mask * own_mask))
    product = jnp.concatenate(products, axis=0).astype(bf16).astype(f32)
    normed = layer_norm(product).astype(bf16)
    update = jnp.dot(normed, output_ref[...], preferred_element_type=f32)
    gate_out = sigmoid(jnp.dot(own_ln, gate_ref[...], preferred_element_type=f32))
    pair_two = (own_pair + gate_out * update).astype(bf16).astype(f32)
    ln_two = layer_norm(pair_two).astype(bf16)
    hidden = jnp.maximum(jnp.dot(ln_two, up_ref[...], preferred_element_type=f32), 0.0).astype(bf16)
    result = pair_two + jnp.dot(hidden, down_ref[...], preferred_element_type=f32)
    out_ref[...] = result.astype(bf16).reshape(rows, residues, wide)


def copy_kernel(packed_ref, out_ref):
    out_ref[0] = packed_ref[...]


def gather_all(packed):
    dap_count = lax.axis_size("dap")
    half = dap_count // 2
    far = lax.ppermute(packed[None], "dap", [(src, src ^ half) for src in range(dap_count)])
    own = pl.pallas_call(
        copy_kernel,
        out_shape=jax.ShapeDtypeStruct((1,) + packed.shape, packed.dtype),
        in_specs=[pl.BlockSpec(memory_space=pltpu.VMEM)],
        out_specs=pl.BlockSpec(memory_space=pltpu.VMEM),
        compiler_params=pltpu.CompilerParams(vmem_limit_bytes=4 << 20),
    )(packed)
    both = jnp.concatenate([own, far], axis=0)
    held = [both] + [
        lax.ppermute(both, "dap", [(src, src ^ offset) for src in range(dap_count)])
        for offset in swap_order(dap_count)
    ]
    sibling = [(0, 1), (1, 0)]
    early = lax.ppermute(jnp.concatenate(held[:-1], axis=0), "sub", sibling)
    late = lax.ppermute(held[-1], "sub", sibling)
    return jnp.concatenate(held, axis=0), jnp.concatenate([early, late], axis=0)


def swap_order(dap_count):
    return list(range(dap_count // 2 - 1, 0, -1))


def block_place(chip, chips):
    offset = lax.bitwise_xor(lax.axis_index("dap"), chip)
    half = chips // 2
    near = jnp.where(offset >= half, offset - half, offset)
    turn = jnp.where(near == 0, 0, half - near)
    return 2 * turn + jnp.where(offset >= half, 1, 0)


def shards_replicated(
    pairwise_state,
    alignment_state,
    alignment_mask,
    residue_crop_mask,
    outer_input_weight,
    outer_output_weight,
    triangle_input_weight,
    triangle_gate,
    triangle_output_weight,
    transition_up_weight,
    transition_down_weight,
):
    rows, residues, wide = pairwise_state.shape
    sequences = alignment_state.shape[0]
    channels = outer_input_weight.shape[2]
    vector = pl.BlockSpec(memory_space=pltpu.VMEM)
    params = pltpu.CompilerParams(vmem_limit_bytes=40 << 20)
    hbm = pl.BlockSpec(memory_space=pltpu.HBM)
    packed = pl.pallas_call(
        pack_kernel,
        out_shape=jax.ShapeDtypeStruct((rows * residues + sequences + 16, wide), jnp.bfloat16),
        in_specs=[hbm] * 5,
        out_specs=hbm,
        scratch_shapes=[
            pltpu.SMEM((residues,), jnp.int32),
            pltpu.VMEM((rows, sequences), jnp.int32),
            pltpu.VMEM(alignment_state.shape, jnp.bfloat16),
            pltpu.VMEM((2, channels, alignment_state.shape[2]), jnp.bfloat16),
            pltpu.VMEM(alignment_state.shape, jnp.float32),
            pltpu.VMEM((sequences + 16, wide), jnp.bfloat16),
            pltpu.SemaphoreType.DMA((5 + rows,)),
        ],
        compiler_params=pltpu.CompilerParams(vmem_limit_bytes=63 << 20),
    )(
        residue_crop_mask,
        alignment_mask.T,
        alignment_state,
        outer_input_weight.transpose(0, 2, 1),
        pairwise_state,
    )
    held, other = gather_all(packed)
    cores, chips = lax.axis_size("sub"), lax.axis_size("dap")
    group = cores * rows
    parts = 2
    return pl.pallas_call(
        update_kernel,
        out_shape=jax.ShapeDtypeStruct(pairwise_state.shape, jnp.bfloat16),
        in_specs=[vector] * 8,
        out_specs=vector,
        scratch_shapes=[
            pltpu.VMEM((parts, (channels // parts + 1) * 2 * channels, 2 * wide), jnp.bfloat16),
            pltpu.VMEM((residues, channels, wide), jnp.float32),
            pltpu.VMEM((2, 2 * group * sequences, chips * wide), jnp.bfloat16),
            pltpu.VMEM((residues, wide), jnp.float32),
            pltpu.VMEM((parts, chips * residues, channels // parts * wide // 2), jnp.bfloat16),
            pltpu.VMEM((parts, chips * residues, channels // parts * wide // 2), jnp.bfloat16),
            pltpu.VMEM((residues, residues, wide), jnp.float32),
            pltpu.VMEM((residues, residues, wide), jnp.float32),
            pltpu.VMEM((residues, residues, wide), jnp.float32),
        ],
        compiler_params=params,
    )(
        held,
        other,
        outer_output_weight,
        triangle_input_weight,
        triangle_gate,
        triangle_output_weight,
        transition_up_weight,
        transition_down_weight,
    )


def shards(
    pairwise_state,
    alignment_state,
    alignment_mask,
    residue_crop_mask,
    outer_input_weight,
    outer_output_weight,
    triangle_input_weight,
    triangle_gate,
    triangle_output_weight,
    transition_up_weight,
    transition_down_weight,
):
    row_count = pairwise_state.shape[0]
    start_row = lax.axis_index(("dap", "sub")) * row_count
    row_presence_mask = lax.dynamic_slice_in_dim(residue_crop_mask, start_row, row_count, 0).astype(
        jnp.float32
    )
    full_mask = residue_crop_mask.astype(jnp.float32)
    alignment_keep = alignment_mask.astype(jnp.float32) * row_presence_mask[None, :]
    alignment_normed = norm_layer(alignment_state.astype(jnp.float32), -1).astype(jnp.bfloat16)
    left_alignment = (
        jnp.einsum(
            "pxm,my->pxy",
            alignment_normed,
            outer_input_weight[0],
            preferred_element_type=jnp.float32,
        )
        * alignment_keep[:, :, None]
    ).astype(jnp.bfloat16)
    right_alignment = (
        jnp.einsum(
            "pxm,my->pxy",
            alignment_normed,
            outer_input_weight[1],
            preferred_element_type=jnp.float32,
        )
        * alignment_keep[:, :, None]
    ).astype(jnp.bfloat16)
    inner_alignment = jnp.einsum(
        "tqu,ulx->tqlx", left_alignment, outer_output_weight, preferred_element_type=jnp.float32
    ).astype(jnp.bfloat16)
    right_portion = lax.all_gather(right_alignment, ("dap", "sub"), axis=1, tiled=True)
    keep_portion = lax.all_gather(
        alignment_keep.astype(jnp.bfloat16), ("dap", "sub"), axis=1, tiled=True
    )
    numerator_sum = jnp.einsum(
        "zkwv,znw->knv", inner_alignment, right_portion, preferred_element_type=jnp.float32
    )
    pair_norm_count = jnp.einsum("cf,cg->fg", alignment_keep, keep_portion.astype(jnp.float32))
    block_part = numerator_sum / jnp.maximum(pair_norm_count, 1.0)[:, :, None]
    pair_one = (pairwise_state.astype(jnp.float32) + block_part).astype(jnp.bfloat16)
    ln_one = norm_layer(pair_one.astype(jnp.float32), -1).astype(jnp.bfloat16)
    pair_keep = row_presence_mask[:, None] * full_mask[None, :]

    def operand(gate_w, proj_w):
        gate_val = jnp.einsum("ijc,cd->dij", ln_one, gate_w, preferred_element_type=jnp.float32)
        proj_val = jnp.einsum("ijc,cd->dij", ln_one, proj_w, preferred_element_type=jnp.float32)
        return (jax.nn.sigmoid(gate_val) * proj_val * pair_keep[None]).astype(jnp.bfloat16)

    left_tri = operand(triangle_input_weight[0], triangle_input_weight[1])
    right_tri = operand(triangle_input_weight[2], triangle_input_weight[3])
    near_right = lax.all_gather(right_tri, "sub", axis=1, tiled=True)
    left_cols, right_all = (
        lax.all_to_all(left_tri, "dap", split_axis=0, concat_axis=1, tiled=True),
        lax.all_to_all(near_right, "dap", split_axis=0, concat_axis=1, tiled=True),
    )
    product = jnp.einsum(
        "cik,cjk->cij", left_cols, right_all, preferred_element_type=jnp.float32
    ).astype(jnp.bfloat16)
    returned = lax.all_to_all(product, "dap", split_axis=1, concat_axis=0, tiled=True)
    normed = norm_layer(returned.astype(jnp.float32), 0).astype(jnp.bfloat16)
    update = jnp.einsum(
        "cij,cd->ijd", normed, triangle_output_weight, preferred_element_type=jnp.float32
    )
    gate_out = jax.nn.sigmoid(
        jnp.einsum("ijc,cd->ijd", ln_one, triangle_gate, preferred_element_type=jnp.float32)
    )
    pair_two = (pair_one.astype(jnp.float32) + gate_out * update).astype(jnp.bfloat16)
    ln_two = norm_layer(pair_two.astype(jnp.float32), -1).astype(jnp.bfloat16)

    def step(row_pair):
        return transition(*row_pair, transition_up_weight, transition_down_weight)

    return lax.map(step, (ln_two, pair_two))


def solution(mesh):
    placed = (
        P(("crop", "dap", "sub"), None, None),
        P("crop", ("dap", "sub"), None),
        P("crop", ("dap", "sub")),
        P("crop"),
        P(),
        P(),
        P(),
        P(),
        P(),
        P(),
        P(),
    )

    small = mesh.shape["sub"] == 2 and mesh.shape["dap"] == 8

    def body(pairwise_state, *rest):
        residues, channels = pairwise_state.shape[1:]
        if small and residues * residues * channels * 2 <= REPLICATED_PAIR_BYTES:
            return shards_replicated(pairwise_state, *rest)
        return shards(pairwise_state, *rest)

    return jax.shard_map(
        body,
        mesh=mesh,
        in_specs=placed,
        out_specs=P(("crop", "dap", "sub"), None, None),
        check_vma=False,
    )
```

```python
import jax
import jax.numpy as jnp
from jax import lax
from jax.experimental import pallas as pl
from jax.experimental.pallas import tpu as pltpu
from jax.sharding import PartitionSpec as P

REPLICATED_PAIR_BYTES = 1 << 20


def norm_layer(values, reduce_axis):
    average = jnp.mean(values, axis=reduce_axis, keepdims=True)
    centered = values - average
    variance = jnp.mean(centered * centered, axis=reduce_axis, keepdims=True)
    return centered * lax.rsqrt(variance + 1e-05)


def transition(ln_two, pair_two, transition_up_weight, transition_down_weight):
    hidden = jax.nn.relu(
        jnp.dot(ln_two, transition_up_weight, preferred_element_type=jnp.float32)
    ).astype(jnp.bfloat16)
    return (
        pair_two.astype(jnp.float32)
        + jnp.dot(hidden, transition_down_weight, preferred_element_type=jnp.float32)
    ).astype(jnp.bfloat16)


def layer_norm(values):
    count = values.shape[-1]
    centered = values - jnp.sum(values, axis=-1, keepdims=True) * (1.0 / count)
    variance = jnp.sum(centered * centered, axis=-1, keepdims=True) * (1.0 / count)
    return centered * lax.rsqrt(variance + 1e-05)


def first_row(rows):
    return (lax.axis_index("dap") * lax.axis_size("sub") + lax.axis_index("sub")) * rows


def pack_kernel(
    mask_hbm,
    keep_hbm,
    state_hbm,
    weight_hbm,
    pair_hbm,
    out_ref,
    mask_ref,
    keep_ref,
    state_ref,
    weight_ref,
    wide_ref,
    sems,
):
    rows, residues, wide = pair_hbm.shape
    sequences = state_ref.shape[0]
    base = rows * residues
    start = first_row(rows)
    second_core = lax.axis_index("sub") == 1
    loads = [
        pltpu.make_async_copy(state_hbm, state_ref, sems.at[0]),
        pltpu.make_async_copy(weight_hbm, weight_ref, sems.at[1]),
        pltpu.make_async_copy(keep_hbm, keep_ref, sems.at[2]),
        pltpu.make_async_copy(mask_hbm, mask_ref, sems.at[3]),
    ] + [
        pltpu.make_async_copy(
            pair_hbm.at[row], out_ref.at[pl.ds(row * residues, residues)], sems.at[4 + row]
        )
        for row in range(rows)
    ]
    for load in loads:
        load.start()
    loads[0].wait()
    wide_ref[...] = state_ref[...].astype(jnp.float32)
    normed_rows = [layer_norm(wide_ref[:, row]).astype(jnp.bfloat16) for row in range(rows)]
    eye = lax.broadcasted_iota(jnp.int32, (sequences, sequences), 0) == lax.broadcasted_iota(
        jnp.int32, (sequences, sequences), 1
    )
    lefts, rights, keeps = [], [], []
    for load in loads[1:4]:
        load.wait()
    for row in range(rows):
        present = mask_ref[start + row].astype(jnp.float32)
        keep_row = keep_ref[row : row + 1].astype(jnp.float32) * present
        keep_column = jnp.sum(
            jnp.where(eye, jnp.broadcast_to(keep_row, eye.shape), 0.0), axis=1, keepdims=True
        )
        normed = normed_rows[row]
        last = (((1,), (1,)), ((), ()))
        left = lax.dot_general(weight_ref[0], normed, last, preferred_element_type=jnp.float32)
        right = lax.dot_general(normed, weight_ref[1], last, preferred_element_type=jnp.float32)
        lefts.append(left * keep_row)
        rights.append(right * keep_column)
        keeps.append(
            jnp.concatenate(
                [keep_row, jnp.full((1, wide - sequences), present, jnp.float32)], axis=1
            )
        )
    left = jnp.concatenate(lefts, axis=1)
    right = jnp.concatenate(rights, axis=1)
    first = jnp.concatenate([right, left], axis=1)
    other = jnp.concatenate([left, right], axis=1)
    out_ref[base : base + sequences] = jnp.where(second_core, other, first).astype(jnp.bfloat16)
    out_ref[base + sequences :] = jnp.concatenate(
        keeps + [jnp.zeros((16 - rows, wide), jnp.float32)], axis=0
    ).astype(jnp.bfloat16)
    for load in loads[4:]:
        load.wait()


def sigmoid(values):
    return 0.5 * jnp.tanh(0.5 * values) + 0.5


def update_kernel(
    held_ref,
    other_ref,
    outer_ref,
    triangle_ref,
    gate_ref,
    output_ref,
    up_ref,
    down_ref,
    out_ref,
    block_ref,
    left_ref,
    right_ref,
    keep_ref,
    first_ref,
    second_ref,
    pair_ref,
    pair_one_ref,
    ln_one_ref,
):
    rows, residues, wide = out_ref.shape
    cores, chips = 2, lax.axis_size("dap")
    channels = outer_ref.shape[0]
    sequences = channels
    base = rows * residues
    half = wide // 2
    group = cores * rows
    start = first_row(rows)
    second_core = lax.axis_index("sub") == 1
    bf16 = jnp.bfloat16
    f32 = jnp.float32

    parts = block_ref.shape[0]
    span = channels // parts
    nothing = jnp.zeros((channels, wide), bf16)
    for part in range(parts):
        for step in range(span + 1):
            weight = outer_ref[part * span + step % span]
            at = step * 2 * channels
            block_ref[part, at : at + channels, :wide] = weight
            block_ref[part, at : at + channels, wide:] = nothing
            block_ref[part, at + channels : at + 2 * channels, :wide] = nothing
            block_ref[part, at + channels : at + 2 * channels, wide:] = weight

    lane = lax.broadcasted_iota(jnp.int32, (channels, wide), 1)
    lane_block = lane // channels
    low = lane < half
    for chip in range(chips):
        place = block_place(chip, chips)
        mine, other = held_ref[place], other_ref[place]
        blocks = [jnp.where(second_core, other, mine), jnp.where(second_core, mine, other)]
        packed = [block[base : base + sequences].astype(f32) for block in blocks]
        right = jnp.where(low, packed[0], packed[1])
        for turn, value in enumerate((right, pltpu.roll(right, half, 1))):
            for copy in range(group):
                right_ref[
                    turn,
                    copy * sequences : (copy + 1) * sequences,
                    chip * wide : (chip + 1) * wide,
                ] = value.astype(bf16)
        for core in range(cores):
            residue = (chip * cores + core) * rows
            for row in range(rows):
                at = (rows if core == 0 else 0) + row
                left_ref[residue + row] = jnp.where(lane_block == at, packed[core], 0.0)
            keep_ref[residue : residue + rows] = blocks[core][base + sequences :].astype(f32)[:rows]
            pair_ref[residue : residue + rows] = (
                blocks[core][:base].astype(f32).reshape(rows, residues, wide)
            )

    last = (((1,), (1,)), ((), ()))
    keep = keep_ref[...]
    mask = jnp.broadcast_to(keep[:, sequences : sequences + 1], (residues, wide))
    counted = lax.broadcasted_iota(jnp.int32, (residues, wide), 1) < sequences
    count = lax.dot_general(
        jnp.where(counted, keep, 0.0).astype(bf16),
        keep.astype(bf16),
        last,
        preferred_element_type=f32,
    )
    inverse = 1.0 / jnp.maximum(count, 1.0)

    low = lax.broadcasted_iota(jnp.int32, (residues, wide), 1) < half
    totals = [0.0, 0.0]
    for part in range(parts):
        outer = []
        for turn in range(2):
            left = jnp.concatenate(
                [left_ref[:, d] for d in range(part * span + turn, (part + 1) * span, 2)], axis=0
            ).astype(bf16)
            outer.append(jnp.dot(left, right_ref[turn], preferred_element_type=f32))

        def piece(turn, at, chip):
            return outer[turn][
                at * residues : (at + 1) * residues, chip * wide : (chip + 1) * wide
            ]

        for at in range(span // 2):
            follow = (at + 1) % (span // 2)
            for chip in range(chips):
                place = (
                    part,
                    slice(chip * residues, (chip + 1) * residues),
                    slice(at * wide, (at + 1) * wide),
                )
                first_ref[place] = jnp.where(low, piece(0, at, chip), piece(1, at, chip)).astype(bf16)
                second_ref[place] = jnp.where(
                    low, piece(1, at, chip), piece(0, follow, chip)
                ).astype(bf16)
        depth = span * 2 * channels
        totals[0] += jnp.dot(first_ref[part], block_ref[part, :depth], preferred_element_type=f32)
        totals[1] += jnp.dot(
            second_ref[part], block_ref[part, 2 * channels :], preferred_element_type=f32
        )

    right_weight = jnp.concatenate([triangle_ref[2], triangle_ref[3]], axis=1)
    right_tri = []
    stride = 8
    for first in range(0, residues, stride):
        normed = []
        for k in range(first, first + stride):
            chip, pick = k // group, k % group
            at = (pick % 2) * wide
            numerator = totals[pick // 2][chip * residues : (chip + 1) * residues, at : at + wide]
            opm = numerator * jnp.broadcast_to(inverse[:, k : k + 1], (residues, wide))
            pair_one = (pair_ref[:, k] + opm).astype(bf16).astype(f32)
            pair_one_ref[k] = pair_one
            ln_one = layer_norm(pair_one)
            ln_one_ref[k] = ln_one
            normed.append(ln_one.astype(bf16))
        both = jnp.dot(
            jnp.concatenate(normed, axis=0), right_weight, preferred_element_type=f32
        )
        right_tri.append((sigmoid(both[:, :wide]) * both[:, wide:]).astype(bf16).astype(f32))

    own_pair = jnp.concatenate([pair_one_ref[:, start + row] for row in range(rows)], axis=0)
    own_ln = jnp.concatenate([ln_one_ref[:, start + row] for row in range(rows)], axis=0).astype(bf16)
    left_weight = jnp.concatenate([triangle_ref[0], triangle_ref[1]], axis=1)
    both = jnp.dot(own_ln, left_weight, preferred_element_type=f32)
    left_tri = sigmoid(both[:, :wide]) * both[:, wide:] * jnp.concatenate([mask] * rows, axis=0)
    left_tri = left_tri.astype(bf16).astype(f32)
    products = []
    for row in range(rows):
        sums = [jnp.zeros((residues, wide), f32) for _ in range(4)]
        for k in range(residues):
            at = row * residues + k
            place = (k % stride) * residues
            sums[k % 4] += left_tri[at : at + 1] * right_tri[k // stride][place : place + residues]
        total = (sums[0] + sums[1]) + (sums[2] + sums[3])
        own_mask = keep_ref[pl.ds(start + row, 1), :][:, sequences : sequences + 1]
        products.append(total * (mask * own_mask))
    product = jnp.concatenate(products, axis=0).astype(bf16).astype(f32)
    normed = layer_norm(product).astype(bf16)
    update = jnp.dot(normed, output_ref[...], preferred_element_type=f32)
    gate_out = sigmoid(jnp.dot(own_ln, gate_ref[...], preferred_element_type=f32))
    pair_two = (own_pair + gate_out * update).astype(bf16).astype(f32)
    ln_two = layer_norm(pair_two).astype(bf16)
    hidden = jnp.maximum(jnp.dot(ln_two, up_ref[...], preferred_element_type=f32), 0.0).astype(bf16)
    result = pair_two + jnp.dot(hidden, down_ref[...], preferred_element_type=f32)
    out_ref[...] = result.astype(bf16).reshape(rows, residues, wide)


def gather_all(packed):
    dap_count = lax.axis_size("dap")
    half = dap_count // 2
    far = lax.ppermute(packed[None], "dap", [(src, src ^ half) for src in range(dap_count)])
    both = jnp.concatenate([packed[None], far], axis=0)
    held = [both] + [
        lax.ppermute(both, "dap", [(src, src ^ offset) for src in range(dap_count)])
        for offset in swap_order(dap_count)
    ]
    sibling = [(0, 1), (1, 0)]
    early = lax.ppermute(jnp.concatenate(held[:-1], axis=0), "sub", sibling)
    late = lax.ppermute(held[-1], "sub", sibling)
    return jnp.concatenate(held, axis=0), jnp.concatenate([early, late], axis=0)


def swap_order(dap_count):
    return list(range(dap_count // 2 - 1, 0, -1))


def block_place(chip, chips):
    offset = lax.bitwise_xor(lax.axis_index("dap"), chip)
    half = chips // 2
    near = jnp.where(offset >= half, offset - half, offset)
    turn = jnp.where(near == 0, 0, half - near)
    return 2 * turn + jnp.where(offset >= half, 1, 0)


def shards_replicated(
    pairwise_state,
    alignment_state,
    alignment_mask,
    residue_crop_mask,
    outer_input_weight,
    outer_output_weight,
    triangle_input_weight,
    triangle_gate,
    triangle_output_weight,
    transition_up_weight,
    transition_down_weight,
):
    rows, residues, wide = pairwise_state.shape
    sequences = alignment_state.shape[0]
    channels = outer_input_weight.shape[2]
    vector = pl.BlockSpec(memory_space=pltpu.VMEM)
    params = pltpu.CompilerParams(vmem_limit_bytes=40 << 20)
    hbm = pl.BlockSpec(memory_space=pltpu.HBM)
    packed = pl.pallas_call(
        pack_kernel,
        out_shape=jax.ShapeDtypeStruct((rows * residues + sequences + 16, wide), jnp.bfloat16),
        in_specs=[hbm] * 5,
        out_specs=vector,
        scratch_shapes=[
            pltpu.SMEM((residues,), jnp.int32),
            pltpu.VMEM((rows, sequences), jnp.int32),
            pltpu.VMEM(alignment_state.shape, jnp.bfloat16),
            pltpu.VMEM((2, channels, alignment_state.shape[2]), jnp.bfloat16),
            pltpu.VMEM(alignment_state.shape, jnp.float32),
            pltpu.SemaphoreType.DMA((4 + rows,)),
        ],
        compiler_params=pltpu.CompilerParams(vmem_limit_bytes=8 << 20),
    )(
        *(
            pltpu.with_memory_space_constraint(array, pltpu.HBM)
            for array in (
                residue_crop_mask,
                alignment_mask.T,
                alignment_state,
                outer_input_weight.transpose(0, 2, 1),
                pairwise_state,
            )
        )
    )
    held, other = gather_all(packed)
    cores, chips = lax.axis_size("sub"), lax.axis_size("dap")
    group = cores * rows
    parts = 2
    return pl.pallas_call(
        update_kernel,
        out_shape=jax.ShapeDtypeStruct(pairwise_state.shape, jnp.bfloat16),
        in_specs=[vector] * 8,
        out_specs=vector,
        scratch_shapes=[
            pltpu.VMEM((parts, (channels // parts + 1) * 2 * channels, 2 * wide), jnp.bfloat16),
            pltpu.VMEM((residues, channels, wide), jnp.float32),
            pltpu.VMEM((2, group * sequences, chips * wide), jnp.bfloat16),
            pltpu.VMEM((residues, wide), jnp.float32),
            pltpu.VMEM((parts, chips * residues, channels // parts * wide // 2), jnp.bfloat16),
            pltpu.VMEM((parts, chips * residues, channels // parts * wide // 2), jnp.bfloat16),
            pltpu.VMEM((residues, residues, wide), jnp.float32),
            pltpu.VMEM((residues, residues, wide), jnp.float32),
            pltpu.VMEM((residues, residues, wide), jnp.float32),
        ],
        compiler_params=params,
    )(
        held,
        other,
        outer_output_weight,
        triangle_input_weight,
        triangle_gate,
        triangle_output_weight,
        transition_up_weight,
        transition_down_weight,
    )


def shards(
    pairwise_state,
    alignment_state,
    alignment_mask,
    residue_crop_mask,
    outer_input_weight,
    outer_output_weight,
    triangle_input_weight,
    triangle_gate,
    triangle_output_weight,
    transition_up_weight,
    transition_down_weight,
):
    row_count = pairwise_state.shape[0]
    start_row = lax.axis_index(("dap", "sub")) * row_count
    row_presence_mask = lax.dynamic_slice_in_dim(residue_crop_mask, start_row, row_count, 0).astype(
        jnp.float32
    )
    full_mask = residue_crop_mask.astype(jnp.float32)
    alignment_keep = alignment_mask.astype(jnp.float32) * row_presence_mask[None, :]
    alignment_normed = norm_layer(alignment_state.astype(jnp.float32), -1).astype(jnp.bfloat16)
    left_alignment = (
        jnp.einsum(
            "pxm,my->pxy",
            alignment_normed,
            outer_input_weight[0],
            preferred_element_type=jnp.float32,
        )
        * alignment_keep[:, :, None]
    ).astype(jnp.bfloat16)
    right_alignment = (
        jnp.einsum(
            "pxm,my->pxy",
            alignment_normed,
            outer_input_weight[1],
            preferred_element_type=jnp.float32,
        )
        * alignment_keep[:, :, None]
    ).astype(jnp.bfloat16)
    inner_alignment = jnp.einsum(
        "tqu,ulx->tqlx", left_alignment, outer_output_weight, preferred_element_type=jnp.float32
    ).astype(jnp.bfloat16)
    right_portion = lax.all_gather(right_alignment, ("dap", "sub"), axis=1, tiled=True)
    keep_portion = lax.all_gather(
        alignment_keep.astype(jnp.bfloat16), ("dap", "sub"), axis=1, tiled=True
    )
    numerator_sum = jnp.einsum(
        "zkwv,znw->knv", inner_alignment, right_portion, preferred_element_type=jnp.float32
    )
    pair_norm_count = jnp.einsum("cf,cg->fg", alignment_keep, keep_portion.astype(jnp.float32))
    block_part = numerator_sum / jnp.maximum(pair_norm_count, 1.0)[:, :, None]
    pair_one = (pairwise_state.astype(jnp.float32) + block_part).astype(jnp.bfloat16)
    ln_one = norm_layer(pair_one.astype(jnp.float32), -1).astype(jnp.bfloat16)
    pair_keep = row_presence_mask[:, None] * full_mask[None, :]

    def operand(gate_w, proj_w):
        gate_val = jnp.einsum("ijc,cd->dij", ln_one, gate_w, preferred_element_type=jnp.float32)
        proj_val = jnp.einsum("ijc,cd->dij", ln_one, proj_w, preferred_element_type=jnp.float32)
        return (jax.nn.sigmoid(gate_val) * proj_val * pair_keep[None]).astype(jnp.bfloat16)

    left_tri = operand(triangle_input_weight[0], triangle_input_weight[1])
    right_tri = operand(triangle_input_weight[2], triangle_input_weight[3])
    near_right = lax.all_gather(right_tri, "sub", axis=1, tiled=True)
    left_cols, right_all = (
        lax.all_to_all(left_tri, "dap", split_axis=0, concat_axis=1, tiled=True),
        lax.all_to_all(near_right, "dap", split_axis=0, concat_axis=1, tiled=True),
    )
    product = jnp.einsum(
        "cik,cjk->cij", left_cols, right_all, preferred_element_type=jnp.float32
    ).astype(jnp.bfloat16)
    returned = lax.all_to_all(product, "dap", split_axis=1, concat_axis=0, tiled=True)
    normed = norm_layer(returned.astype(jnp.float32), 0).astype(jnp.bfloat16)
    update = jnp.einsum(
        "cij,cd->ijd", normed, triangle_output_weight, preferred_element_type=jnp.float32
    )
    gate_out = jax.nn.sigmoid(
        jnp.einsum("ijc,cd->ijd", ln_one, triangle_gate, preferred_element_type=jnp.float32)
    )
    pair_two = (pair_one.astype(jnp.float32) + gate_out * update).astype(jnp.bfloat16)
    ln_two = norm_layer(pair_two.astype(jnp.float32), -1).astype(jnp.bfloat16)

    def step(row_pair):
        return transition(*row_pair, transition_up_weight, transition_down_weight)

    return lax.map(step, (ln_two, pair_two))


def solution(mesh):
    placed = (
        P(("crop", "dap", "sub"), None, None),
        P("crop", ("dap", "sub"), None),
        P("crop", ("dap", "sub")),
        P("crop"),
        P(),
        P(),
        P(),
        P(),
        P(),
        P(),
        P(),
    )

    small = mesh.shape["sub"] == 2 and mesh.shape["dap"] == 8

    def body(pairwise_state, *rest):
        residues, channels = pairwise_state.shape[1:]
        if small and residues * residues * channels * 2 <= REPLICATED_PAIR_BYTES:
            return shards_replicated(pairwise_state, *rest)
        return shards(pairwise_state, *rest)

    return jax.shard_map(
        body,
        mesh=mesh,
        in_specs=placed,
        out_specs=P(("crop", "dap", "sub"), None, None),
        check_vma=False,
    )
```

```python
import jax
import jax.numpy as jnp
from jax import lax
from jax.experimental import pallas as pl
from jax.experimental.pallas import tpu as pltpu
from jax.sharding import PartitionSpec as P

REPLICATED_PAIR_BYTES = 1 << 20


def norm_layer(values, reduce_axis):
    average = jnp.mean(values, axis=reduce_axis, keepdims=True)
    centered = values - average
    variance = jnp.mean(centered * centered, axis=reduce_axis, keepdims=True)
    return centered * lax.rsqrt(variance + 1e-05)


def transition(ln_two, pair_two, transition_up_weight, transition_down_weight):
    hidden = jax.nn.relu(
        jnp.dot(ln_two, transition_up_weight, preferred_element_type=jnp.float32)
    ).astype(jnp.bfloat16)
    return (
        pair_two.astype(jnp.float32)
        + jnp.dot(hidden, transition_down_weight, preferred_element_type=jnp.float32)
    ).astype(jnp.bfloat16)


def layer_norm(values):
    count = values.shape[-1]
    centered = values - jnp.sum(values, axis=-1, keepdims=True) * (1.0 / count)
    variance = jnp.sum(centered * centered, axis=-1, keepdims=True) * (1.0 / count)
    return centered * lax.rsqrt(variance + 1e-05)


def first_row(rows):
    return (lax.axis_index("dap") * lax.axis_size("sub") + lax.axis_index("sub")) * rows


def pack_kernel(
    mask_hbm,
    keep_hbm,
    state_hbm,
    weight_hbm,
    pair_hbm,
    out_ref,
    mask_ref,
    keep_ref,
    state_ref,
    weight_ref,
    wide_ref,
    sems,
):
    rows, residues, wide = pair_hbm.shape
    sequences = state_ref.shape[0]
    base = rows * residues
    start = first_row(rows)
    second_core = lax.axis_index("sub") == 1
    loads = [
        pltpu.make_async_copy(state_hbm, state_ref, sems.at[0]),
        pltpu.make_async_copy(weight_hbm, weight_ref, sems.at[1]),
        pltpu.make_async_copy(keep_hbm, keep_ref, sems.at[2]),
        pltpu.make_async_copy(mask_hbm, mask_ref, sems.at[3]),
    ] + [
        pltpu.make_async_copy(
            pair_hbm.at[row], out_ref.at[pl.ds(row * residues, residues)], sems.at[4 + row]
        )
        for row in range(rows)
    ]
    for load in loads:
        load.start()
    loads[0].wait()
    wide_ref[...] = state_ref[...].astype(jnp.float32)
    normed_rows = [layer_norm(wide_ref[:, row]).astype(jnp.bfloat16) for row in range(rows)]
    eye = lax.broadcasted_iota(jnp.int32, (sequences, sequences), 0) == lax.broadcasted_iota(
        jnp.int32, (sequences, sequences), 1
    )
    lefts, rights, keeps = [], [], []
    for load in loads[1:4]:
        load.wait()
    for row in range(rows):
        present = mask_ref[start + row].astype(jnp.float32)
        keep_row = keep_ref[row : row + 1].astype(jnp.float32) * present
        keep_column = jnp.sum(
            jnp.where(eye, jnp.broadcast_to(keep_row, eye.shape), 0.0), axis=1, keepdims=True
        )
        normed = normed_rows[row]
        last = (((1,), (1,)), ((), ()))
        left = lax.dot_general(weight_ref[0], normed, last, preferred_element_type=jnp.float32)
        right = lax.dot_general(normed, weight_ref[1], last, preferred_element_type=jnp.float32)
        lefts.append(left * keep_row)
        rights.append(right * keep_column)
        keeps.append(
            jnp.concatenate(
                [keep_row, jnp.full((1, wide - sequences), present, jnp.float32)], axis=1
            )
        )
    left = jnp.concatenate(lefts, axis=1)
    right = jnp.concatenate(rights, axis=1)
    first = jnp.concatenate([right, left], axis=1)
    other = jnp.concatenate([left, right], axis=1)
    out_ref[base : base + sequences] = jnp.where(second_core, other, first).astype(jnp.bfloat16)
    out_ref[base + sequences :] = jnp.concatenate(
        keeps + [jnp.zeros((16 - rows, wide), jnp.float32)], axis=0
    ).astype(jnp.bfloat16)
    for load in loads[4:]:
        load.wait()


def sigmoid(values):
    return 0.5 * jnp.tanh(0.5 * values) + 0.5


def weight_kernel(
    outer_hbm,
    triangle_hbm,
    gate_hbm,
    output_hbm,
    up_hbm,
    down_hbm,
    packed_hbm,
    block_ref,
    right_ref,
    left_ref,
    output_ref,
    up_ref,
    down_ref,
    outer_ref,
    sems,
):
    channels, _, wide = outer_hbm.shape
    loads = [
        pltpu.make_async_copy(source, target, sems.at[place])
        for place, (source, target) in enumerate(
            (
                (outer_hbm, outer_ref),
                (triangle_hbm.at[2], right_ref.at[:, pl.ds(0, wide)]),
                (triangle_hbm.at[3], right_ref.at[:, pl.ds(wide, wide)]),
                (triangle_hbm.at[0], left_ref.at[:, pl.ds(0, wide)]),
                (triangle_hbm.at[1], left_ref.at[:, pl.ds(wide, wide)]),
                (gate_hbm, left_ref.at[:, pl.ds(2 * wide, wide)]),
                (output_hbm, output_ref),
                (up_hbm, up_ref),
                (down_hbm, down_ref),
            )
        )
    ]
    for load in loads:
        load.start()
    parts = block_ref.shape[0]
    span = channels // parts
    nothing = jnp.zeros((channels, wide), block_ref.dtype)
    loads[0].wait()
    for part in range(parts):
        for step in range(span + 1):
            weight = outer_ref[part * span + step % span]
            at = step * 2 * channels
            block_ref[part, at : at + channels, :wide] = weight
            block_ref[part, at : at + channels, wide:] = nothing
            block_ref[part, at + channels : at + 2 * channels, :wide] = nothing
            block_ref[part, at + channels : at + 2 * channels, wide:] = weight
    for load in loads[1:]:
        load.wait()


def update_kernel(
    held_ref,
    other_ref,
    block_ref,
    right_weight_ref,
    left_weight_ref,
    output_ref,
    up_ref,
    down_ref,
    out_ref,
    left_ref,
    right_ref,
    keep_ref,
    first_ref,
    second_ref,
    pair_ref,
    pair_one_ref,
    ln_one_ref,
):
    rows, residues, wide = out_ref.shape
    cores, chips = 2, lax.axis_size("dap")
    channels = left_ref.shape[1]
    sequences = channels
    parts = block_ref.shape[0]
    span = channels // parts
    base = rows * residues
    half = wide // 2
    group = cores * rows
    start = first_row(rows)
    second_core = lax.axis_index("sub") == 1
    bf16 = jnp.bfloat16
    f32 = jnp.float32

    lane = lax.broadcasted_iota(jnp.int32, (channels, wide), 1)
    lane_block = lane // channels
    low = lane < half
    for chip in range(chips):
        place = block_place(chip, chips)
        mine, other = held_ref[place], other_ref[place]
        blocks = [jnp.where(second_core, other, mine), jnp.where(second_core, mine, other)]
        packed = [block[base : base + sequences].astype(f32) for block in blocks]
        right = jnp.where(low, packed[0], packed[1])
        for turn, value in enumerate((right, pltpu.roll(right, half, 1))):
            for copy in range(group):
                right_ref[
                    turn,
                    copy * sequences : (copy + 1) * sequences,
                    chip * wide : (chip + 1) * wide,
                ] = value.astype(bf16)
        for core in range(cores):
            residue = (chip * cores + core) * rows
            for row in range(rows):
                at = (rows if core == 0 else 0) + row
                left_ref[residue + row] = jnp.where(lane_block == at, packed[core], 0.0)
            keep_ref[residue : residue + rows] = blocks[core][base + sequences :].astype(f32)[:rows]
            pair_ref[residue : residue + rows] = (
                blocks[core][:base].astype(f32).reshape(rows, residues, wide)
            )

    last = (((1,), (1,)), ((), ()))
    keep = keep_ref[...]
    mask = jnp.broadcast_to(keep[:, sequences : sequences + 1], (residues, wide))
    counted = lax.broadcasted_iota(jnp.int32, (residues, wide), 1) < sequences
    count = lax.dot_general(
        jnp.where(counted, keep, 0.0).astype(bf16),
        keep.astype(bf16),
        last,
        preferred_element_type=f32,
    )
    inverse = 1.0 / jnp.maximum(count, 1.0)

    low = lax.broadcasted_iota(jnp.int32, (residues, wide), 1) < half
    totals = [0.0, 0.0]
    for part in range(parts):
        outer = []
        for turn in range(2):
            left = jnp.concatenate(
                [left_ref[:, d] for d in range(part * span + turn, (part + 1) * span, 2)], axis=0
            ).astype(bf16)
            outer.append(jnp.dot(left, right_ref[turn], preferred_element_type=f32))

        def piece(turn, at, chip):
            return outer[turn][
                at * residues : (at + 1) * residues, chip * wide : (chip + 1) * wide
            ]

        for at in range(span // 2):
            follow = (at + 1) % (span // 2)
            for chip in range(chips):
                place = (
                    part,
                    slice(chip * residues, (chip + 1) * residues),
                    slice(at * wide, (at + 1) * wide),
                )
                first_ref[place] = jnp.where(low, piece(0, at, chip), piece(1, at, chip)).astype(bf16)
                second_ref[place] = jnp.where(
                    low, piece(1, at, chip), piece(0, follow, chip)
                ).astype(bf16)
        depth = span * 2 * channels
        totals[0] += jnp.dot(first_ref[part], block_ref[part, :depth], preferred_element_type=f32)
        totals[1] += jnp.dot(
            second_ref[part], block_ref[part, 2 * channels :], preferred_element_type=f32
        )

    stride = 8
    sums = [[jnp.zeros((residues, wide), f32) for _ in range(2)] for _ in range(rows)]
    gates = [[] for _ in range(rows)]
    for first in range(0, residues, stride):
        normed = []
        for k in range(first, first + stride):
            chip, pick = k // group, k % group
            at = (pick % 2) * wide
            numerator = totals[pick // 2][chip * residues : (chip + 1) * residues, at : at + wide]
            opm = numerator * jnp.broadcast_to(inverse[:, k : k + 1], (residues, wide))
            pair_one = (pair_ref[:, k] + opm).astype(bf16).astype(f32)
            pair_one_ref[k] = pair_one
            ln_one = layer_norm(pair_one)
            ln_one_ref[k] = ln_one
            normed.append(ln_one.astype(bf16))
        own_ln = jnp.concatenate(
            [ln_one_ref[first : first + stride, start + row] for row in range(rows)], axis=0
        ).astype(bf16)
        both = jnp.dot(own_ln, left_weight_ref[...], preferred_element_type=f32)
        own_mask = jnp.concatenate([mask[first : first + stride]] * rows, axis=0)
        left_tri = sigmoid(both[:, :wide]) * both[:, wide : 2 * wide] * own_mask
        left_tri = left_tri.astype(bf16).astype(f32)
        gate_out = sigmoid(both[:, 2 * wide :])
        both = jnp.dot(
            jnp.concatenate(normed, axis=0), right_weight_ref[...], preferred_element_type=f32
        )
        right_tri = (sigmoid(both[:, :wide]) * both[:, wide:]).astype(bf16).astype(f32)
        for row in range(rows):
            gates[row].append(gate_out[row * stride : (row + 1) * stride])
            for k in range(stride):
                at = row * stride + k
                sums[row][k % 2] += (
                    left_tri[at : at + 1] * right_tri[k * residues : (k + 1) * residues]
                )

    own_pair = jnp.concatenate([pair_one_ref[:, start + row] for row in range(rows)], axis=0)
    gate_out = jnp.concatenate(sum(gates, []), axis=0)
    products = []
    for row in range(rows):
        own_mask = keep_ref[pl.ds(start + row, 1), :][:, sequences : sequences + 1]
        products.append((sums[row][0] + sums[row][1]) * (mask * own_mask))
    product = jnp.concatenate(products, axis=0).astype(bf16).astype(f32)
    normed = layer_norm(product).astype(bf16)
    update = jnp.dot(normed, output_ref[...], preferred_element_type=f32)
    pair_two = (own_pair + gate_out * update).astype(bf16).astype(f32)
    ln_two = layer_norm(pair_two).astype(bf16)
    hidden = jnp.maximum(jnp.dot(ln_two, up_ref[...], preferred_element_type=f32), 0.0).astype(bf16)
    result = pair_two + jnp.dot(hidden, down_ref[...], preferred_element_type=f32)
    out_ref[...] = result.astype(bf16).reshape(rows, residues, wide)


def gather_all(packed):
    dap_count = lax.axis_size("dap")
    half = dap_count // 2
    far = lax.ppermute(packed[None], "dap", [(src, src ^ half) for src in range(dap_count)])
    both = jnp.concatenate([packed[None], far], axis=0)
    held = [both] + [
        lax.ppermute(both, "dap", [(src, src ^ offset) for src in range(dap_count)])
        for offset in swap_order(dap_count)
    ]
    sibling = [(0, 1), (1, 0)]
    early = lax.ppermute(jnp.concatenate(held[:-1], axis=0), "sub", sibling)
    late = lax.ppermute(held[-1], "sub", sibling)
    return jnp.concatenate(held, axis=0), jnp.concatenate([early, late], axis=0)


def swap_order(dap_count):
    return list(range(dap_count // 2 - 1, 0, -1))


def block_place(chip, chips):
    offset = lax.bitwise_xor(lax.axis_index("dap"), chip)
    half = chips // 2
    near = jnp.where(offset >= half, offset - half, offset)
    turn = jnp.where(near == 0, 0, half - near)
    return 2 * turn + jnp.where(offset >= half, 1, 0)


def shards_replicated(
    pairwise_state,
    alignment_state,
    alignment_mask,
    residue_crop_mask,
    outer_input_weight,
    outer_output_weight,
    triangle_input_weight,
    triangle_gate,
    triangle_output_weight,
    transition_up_weight,
    transition_down_weight,
):
    rows, residues, wide = pairwise_state.shape
    sequences = alignment_state.shape[0]
    channels = outer_input_weight.shape[2]
    vector = pl.BlockSpec(memory_space=pltpu.VMEM)
    params = pltpu.CompilerParams(vmem_limit_bytes=40 << 20)
    hbm = pl.BlockSpec(memory_space=pltpu.HBM)
    packed = pl.pallas_call(
        pack_kernel,
        out_shape=jax.ShapeDtypeStruct((rows * residues + sequences + 16, wide), jnp.bfloat16),
        in_specs=[hbm] * 5,
        out_specs=vector,
        scratch_shapes=[
            pltpu.SMEM((residues,), jnp.int32),
            pltpu.VMEM((rows, sequences), jnp.int32),
            pltpu.VMEM(alignment_state.shape, jnp.bfloat16),
            pltpu.VMEM((2, channels, alignment_state.shape[2]), jnp.bfloat16),
            pltpu.VMEM(alignment_state.shape, jnp.float32),
            pltpu.SemaphoreType.DMA((4 + rows,)),
        ],
        compiler_params=pltpu.CompilerParams(vmem_limit_bytes=8 << 20),
    )(
        *(
            pltpu.with_memory_space_constraint(array, pltpu.HBM)
            for array in (
                residue_crop_mask,
                alignment_mask.T,
                alignment_state,
                outer_input_weight.transpose(0, 2, 1),
                pairwise_state,
            )
        )
    )
    cores, chips = lax.axis_size("sub"), lax.axis_size("dap")
    group = cores * rows
    parts = 2
    hidden = transition_up_weight.shape[1]
    weights = pl.pallas_call(
        weight_kernel,
        out_shape=(
            pltpu.VMEM((parts, (channels // parts + 1) * 2 * channels, 2 * wide), jnp.bfloat16),
            pltpu.VMEM((wide, 2 * wide), jnp.bfloat16),
            pltpu.VMEM((wide, 3 * wide), jnp.bfloat16),
            pltpu.VMEM((wide, wide), jnp.bfloat16),
            pltpu.VMEM((wide, hidden), jnp.bfloat16),
            pltpu.VMEM((hidden, wide), jnp.bfloat16),
        ),
        in_specs=[hbm] * 6 + [pl.BlockSpec(memory_space=pl.ANY)],
        out_specs=(vector,) * 6,
        scratch_shapes=[
            pltpu.VMEM(outer_output_weight.shape, jnp.bfloat16),
            pltpu.SemaphoreType.DMA((9,)),
        ],
        compiler_params=pltpu.CompilerParams(vmem_limit_bytes=8 << 20),
    )(
        *(
            pltpu.with_memory_space_constraint(array, pltpu.HBM)
            for array in (
                outer_output_weight,
                triangle_input_weight,
                triangle_gate,
                triangle_output_weight,
                transition_up_weight,
                transition_down_weight,
            )
        ),
        packed,
    )
    held, other = gather_all(packed)
    return pl.pallas_call(
        update_kernel,
        out_shape=jax.ShapeDtypeStruct(pairwise_state.shape, jnp.bfloat16),
        in_specs=[vector] * 8,
        out_specs=vector,
        scratch_shapes=[
            pltpu.VMEM((residues, channels, wide), jnp.float32),
            pltpu.VMEM((2, group * sequences, chips * wide), jnp.bfloat16),
            pltpu.VMEM((residues, wide), jnp.float32),
            pltpu.VMEM((parts, chips * residues, channels // parts * wide // 2), jnp.bfloat16),
            pltpu.VMEM((parts, chips * residues, channels // parts * wide // 2), jnp.bfloat16),
            pltpu.VMEM((residues, residues, wide), jnp.float32),
            pltpu.VMEM((residues, residues, wide), jnp.float32),
            pltpu.VMEM((residues, residues, wide), jnp.float32),
        ],
        compiler_params=params,
    )(
        held,
        other,
        *weights,
    )


def shards(
    pairwise_state,
    alignment_state,
    alignment_mask,
    residue_crop_mask,
    outer_input_weight,
    outer_output_weight,
    triangle_input_weight,
    triangle_gate,
    triangle_output_weight,
    transition_up_weight,
    transition_down_weight,
):
    row_count = pairwise_state.shape[0]
    start_row = lax.axis_index(("dap", "sub")) * row_count
    row_presence_mask = lax.dynamic_slice_in_dim(residue_crop_mask, start_row, row_count, 0).astype(
        jnp.float32
    )
    full_mask = residue_crop_mask.astype(jnp.float32)
    alignment_keep = alignment_mask.astype(jnp.float32) * row_presence_mask[None, :]
    alignment_normed = norm_layer(alignment_state.astype(jnp.float32), -1).astype(jnp.bfloat16)
    left_alignment = (
        jnp.einsum(
            "pxm,my->pxy",
            alignment_normed,
            outer_input_weight[0],
            preferred_element_type=jnp.float32,
        )
        * alignment_keep[:, :, None]
    ).astype(jnp.bfloat16)
    right_alignment = (
        jnp.einsum(
            "pxm,my->pxy",
            alignment_normed,
            outer_input_weight[1],
            preferred_element_type=jnp.float32,
        )
        * alignment_keep[:, :, None]
    ).astype(jnp.bfloat16)
    inner_alignment = jnp.einsum(
        "tqu,ulx->tqlx", left_alignment, outer_output_weight, preferred_element_type=jnp.float32
    ).astype(jnp.bfloat16)
    right_portion = lax.all_gather(right_alignment, ("dap", "sub"), axis=1, tiled=True)
    keep_portion = lax.all_gather(
        alignment_keep.astype(jnp.bfloat16), ("dap", "sub"), axis=1, tiled=True
    )
    numerator_sum = jnp.einsum(
        "zkwv,znw->knv", inner_alignment, right_portion, preferred_element_type=jnp.float32
    )
    pair_norm_count = jnp.einsum("cf,cg->fg", alignment_keep, keep_portion.astype(jnp.float32))
    block_part = numerator_sum / jnp.maximum(pair_norm_count, 1.0)[:, :, None]
    pair_one = (pairwise_state.astype(jnp.float32) + block_part).astype(jnp.bfloat16)
    ln_one = norm_layer(pair_one.astype(jnp.float32), -1).astype(jnp.bfloat16)
    pair_keep = row_presence_mask[:, None] * full_mask[None, :]

    def operand(gate_w, proj_w):
        gate_val = jnp.einsum("ijc,cd->dij", ln_one, gate_w, preferred_element_type=jnp.float32)
        proj_val = jnp.einsum("ijc,cd->dij", ln_one, proj_w, preferred_element_type=jnp.float32)
        return (jax.nn.sigmoid(gate_val) * proj_val * pair_keep[None]).astype(jnp.bfloat16)

    left_tri = operand(triangle_input_weight[0], triangle_input_weight[1])
    right_tri = operand(triangle_input_weight[2], triangle_input_weight[3])
    near_right = lax.all_gather(right_tri, "sub", axis=1, tiled=True)
    left_cols, right_all = (
        lax.all_to_all(left_tri, "dap", split_axis=0, concat_axis=1, tiled=True),
        lax.all_to_all(near_right, "dap", split_axis=0, concat_axis=1, tiled=True),
    )
    product = jnp.einsum(
        "cik,cjk->cij", left_cols, right_all, preferred_element_type=jnp.float32
    ).astype(jnp.bfloat16)
    returned = lax.all_to_all(product, "dap", split_axis=1, concat_axis=0, tiled=True)
    normed = norm_layer(returned.astype(jnp.float32), 0).astype(jnp.bfloat16)
    update = jnp.einsum(
        "cij,cd->ijd", normed, triangle_output_weight, preferred_element_type=jnp.float32
    )
    gate_out = jax.nn.sigmoid(
        jnp.einsum("ijc,cd->ijd", ln_one, triangle_gate, preferred_element_type=jnp.float32)
    )
    pair_two = (pair_one.astype(jnp.float32) + gate_out * update).astype(jnp.bfloat16)
    ln_two = norm_layer(pair_two.astype(jnp.float32), -1).astype(jnp.bfloat16)

    def step(row_pair):
        return transition(*row_pair, transition_up_weight, transition_down_weight)

    return lax.map(step, (ln_two, pair_two))


def solution(mesh):
    placed = (
        P(("crop", "dap", "sub"), None, None),
        P("crop", ("dap", "sub"), None),
        P("crop", ("dap", "sub")),
        P("crop"),
        P(),
        P(),
        P(),
        P(),
        P(),
        P(),
        P(),
    )

    small = mesh.shape["sub"] == 2 and mesh.shape["dap"] == 8

    def body(pairwise_state, *rest):
        residues, channels = pairwise_state.shape[1:]
        if small and residues * residues * channels * 2 <= REPLICATED_PAIR_BYTES:
            return shards_replicated(pairwise_state, *rest)
        return shards(pairwise_state, *rest)

    return jax.shard_map(
        body,
        mesh=mesh,
        in_specs=placed,
        out_specs=P(("crop", "dap", "sub"), None, None),
        check_vma=False,
    )
```

```python
import jax
import jax.numpy as jnp
from jax import lax
from jax.experimental import pallas as pl
from jax.experimental.pallas import tpu as pltpu
from jax.sharding import Mesh, PartitionSpec as P

REPLICATED_PAIR_BYTES = 1 << 20


def norm_layer(values, reduce_axis):
    average = jnp.mean(values, axis=reduce_axis, keepdims=True)
    centered = values - average
    variance = jnp.mean(centered * centered, axis=reduce_axis, keepdims=True)
    return centered * lax.rsqrt(variance + 1e-05)


def transition(ln_two, pair_two, transition_up_weight, transition_down_weight):
    hidden = jax.nn.relu(
        jnp.dot(ln_two, transition_up_weight, preferred_element_type=jnp.float32)
    ).astype(jnp.bfloat16)
    return (
        pair_two.astype(jnp.float32)
        + jnp.dot(hidden, transition_down_weight, preferred_element_type=jnp.float32)
    ).astype(jnp.bfloat16)


def layer_norm(values):
    count = values.shape[-1]
    centered = values - jnp.sum(values, axis=-1, keepdims=True) * (1.0 / count)
    variance = jnp.sum(centered * centered, axis=-1, keepdims=True) * (1.0 / count)
    return centered * lax.rsqrt(variance + 1e-05)


def first_row(rows):
    chip = lax.axis_index("far") * lax.axis_size("near") + lax.axis_index("near")
    return (chip * lax.axis_size("sub") + lax.axis_index("sub")) * rows


def pack_kernel(
    mask_hbm,
    keep_hbm,
    state_hbm,
    weight_hbm,
    pair_hbm,
    out_ref,
    mask_ref,
    keep_ref,
    state_ref,
    weight_ref,
    wide_ref,
    sems,
):
    rows, residues, wide = pair_hbm.shape
    sequences = state_ref.shape[0]
    base = rows * residues
    start = first_row(rows)
    second_core = lax.axis_index("sub") == 1
    loads = [
        pltpu.make_async_copy(state_hbm, state_ref, sems.at[0]),
        pltpu.make_async_copy(weight_hbm, weight_ref, sems.at[1]),
        pltpu.make_async_copy(keep_hbm, keep_ref, sems.at[2]),
        pltpu.make_async_copy(mask_hbm, mask_ref, sems.at[3]),
    ] + [
        pltpu.make_async_copy(
            pair_hbm.at[row], out_ref.at[pl.ds(row * residues, residues)], sems.at[4 + row]
        )
        for row in range(rows)
    ]
    for load in loads:
        load.start()
    loads[0].wait()
    wide_ref[...] = state_ref[...].astype(jnp.float32)
    normed_rows = [layer_norm(wide_ref[:, row]).astype(jnp.bfloat16) for row in range(rows)]
    eye = lax.broadcasted_iota(jnp.int32, (sequences, sequences), 0) == lax.broadcasted_iota(
        jnp.int32, (sequences, sequences), 1
    )
    lefts, rights, keeps = [], [], []
    for load in loads[1:4]:
        load.wait()
    for row in range(rows):
        present = mask_ref[start + row].astype(jnp.float32)
        keep_row = keep_ref[row : row + 1].astype(jnp.float32) * present
        keep_column = jnp.sum(
            jnp.where(eye, jnp.broadcast_to(keep_row, eye.shape), 0.0), axis=1, keepdims=True
        )
        normed = normed_rows[row]
        last = (((1,), (1,)), ((), ()))
        left = lax.dot_general(weight_ref[0], normed, last, preferred_element_type=jnp.float32)
        right = lax.dot_general(normed, weight_ref[1], last, preferred_element_type=jnp.float32)
        lefts.append(left * keep_row)
        rights.append(right * keep_column)
        keeps.append(
            jnp.concatenate(
                [keep_row, jnp.full((1, wide - sequences), present, jnp.float32)], axis=1
            )
        )
    left = jnp.concatenate(lefts, axis=1)
    right = jnp.concatenate(rights, axis=1)
    first = jnp.concatenate([right, left], axis=1)
    other = jnp.concatenate([left, right], axis=1)
    out_ref[base : base + sequences] = jnp.where(second_core, other, first).astype(jnp.bfloat16)
    out_ref[base + sequences :] = jnp.concatenate(
        keeps + [jnp.zeros((16 - rows, wide), jnp.float32)], axis=0
    ).astype(jnp.bfloat16)
    for load in loads[4:]:
        load.wait()


def sigmoid(values):
    return 0.5 * jnp.tanh(0.5 * values) + 0.5


def weight_kernel(
    outer_hbm,
    triangle_hbm,
    gate_hbm,
    output_hbm,
    up_hbm,
    down_hbm,
    packed_hbm,
    block_ref,
    right_ref,
    left_ref,
    output_ref,
    up_ref,
    down_ref,
    outer_ref,
    sems,
):
    channels, _, wide = outer_hbm.shape
    loads = [
        pltpu.make_async_copy(source, target, sems.at[place])
        for place, (source, target) in enumerate(
            (
                (outer_hbm, outer_ref),
                (triangle_hbm.at[2], right_ref.at[:, pl.ds(0, wide)]),
                (triangle_hbm.at[3], right_ref.at[:, pl.ds(wide, wide)]),
                (triangle_hbm.at[0], left_ref.at[:, pl.ds(0, wide)]),
                (triangle_hbm.at[1], left_ref.at[:, pl.ds(wide, wide)]),
                (gate_hbm, left_ref.at[:, pl.ds(2 * wide, wide)]),
                (output_hbm, output_ref),
                (up_hbm, up_ref),
                (down_hbm, down_ref),
            )
        )
    ]
    for load in loads:
        load.start()
    parts = block_ref.shape[0]
    span = channels // parts
    nothing = jnp.zeros((channels, wide), block_ref.dtype)
    loads[0].wait()
    for part in range(parts):
        for step in range(span + 1):
            weight = outer_ref[part * span + step % span]
            at = step * 2 * channels
            block_ref[part, at : at + channels, :wide] = weight
            block_ref[part, at : at + channels, wide:] = nothing
            block_ref[part, at + channels : at + 2 * channels, :wide] = nothing
            block_ref[part, at + channels : at + 2 * channels, wide:] = weight
    for load in loads[1:]:
        load.wait()


def update_kernel(
    held_ref,
    other_ref,
    block_ref,
    right_weight_ref,
    left_weight_ref,
    output_ref,
    up_ref,
    down_ref,
    out_ref,
    left_ref,
    right_ref,
    keep_ref,
    first_ref,
    second_ref,
    pair_ref,
    pair_one_ref,
    ln_one_ref,
):
    rows, residues, wide = out_ref.shape
    cores, chips = 2, held_ref.shape[0]
    channels = left_ref.shape[1]
    sequences = channels
    parts = block_ref.shape[0]
    span = channels // parts
    base = rows * residues
    half = wide // 2
    group = cores * rows
    start = first_row(rows)
    second_core = lax.axis_index("sub") == 1
    bf16 = jnp.bfloat16
    f32 = jnp.float32

    lane = lax.broadcasted_iota(jnp.int32, (channels, wide), 1)
    lane_block = lane // channels
    low = lane < half
    for chip in range(chips):
        place = block_place(chip, chips)
        mine, other = held_ref[place], other_ref[place]
        blocks = [jnp.where(second_core, other, mine), jnp.where(second_core, mine, other)]
        packed = [block[base : base + sequences].astype(f32) for block in blocks]
        right = jnp.where(low, packed[0], packed[1])
        for turn, value in enumerate((right, pltpu.roll(right, half, 1))):
            for copy in range(group):
                right_ref[
                    turn,
                    copy * sequences : (copy + 1) * sequences,
                    chip * wide : (chip + 1) * wide,
                ] = value.astype(bf16)
        for core in range(cores):
            residue = (chip * cores + core) * rows
            for row in range(rows):
                at = (rows if core == 0 else 0) + row
                left_ref[residue + row] = jnp.where(lane_block == at, packed[core], 0.0)
            keep_ref[residue : residue + rows] = blocks[core][base + sequences :].astype(f32)[:rows]
            pair_ref[residue : residue + rows] = (
                blocks[core][:base].astype(f32).reshape(rows, residues, wide)
            )

    last = (((1,), (1,)), ((), ()))
    keep = keep_ref[...]
    mask = jnp.broadcast_to(keep[:, sequences : sequences + 1], (residues, wide))
    counted = lax.broadcasted_iota(jnp.int32, (residues, wide), 1) < sequences
    count = lax.dot_general(
        jnp.where(counted, keep, 0.0).astype(bf16),
        keep.astype(bf16),
        last,
        preferred_element_type=f32,
    )
    inverse = 1.0 / jnp.maximum(count, 1.0)

    low = lax.broadcasted_iota(jnp.int32, (residues, wide), 1) < half
    totals = [0.0, 0.0]
    for part in range(parts):
        outer = []
        for turn in range(2):
            left = jnp.concatenate(
                [left_ref[:, d] for d in range(part * span + turn, (part + 1) * span, 2)], axis=0
            ).astype(bf16)
            outer.append(jnp.dot(left, right_ref[turn], preferred_element_type=f32))

        def piece(turn, at, chip):
            return outer[turn][
                at * residues : (at + 1) * residues, chip * wide : (chip + 1) * wide
            ]

        for at in range(span // 2):
            follow = (at + 1) % (span // 2)
            for chip in range(chips):
                place = (
                    part,
                    slice(chip * residues, (chip + 1) * residues),
                    slice(at * wide, (at + 1) * wide),
                )
                first_ref[place] = jnp.where(low, piece(0, at, chip), piece(1, at, chip)).astype(bf16)
                second_ref[place] = jnp.where(
                    low, piece(1, at, chip), piece(0, follow, chip)
                ).astype(bf16)
        depth = span * 2 * channels
        totals[0] += jnp.dot(first_ref[part], block_ref[part, :depth], preferred_element_type=f32)
        totals[1] += jnp.dot(
            second_ref[part], block_ref[part, 2 * channels :], preferred_element_type=f32
        )

    stride = 8
    sums = [[jnp.zeros((residues, wide), f32) for _ in range(2)] for _ in range(rows)]
    gates = [[] for _ in range(rows)]
    for first in range(0, residues, stride):
        normed = []
        for k in range(first, first + stride):
            chip, pick = k // group, k % group
            at = (pick % 2) * wide
            numerator = totals[pick // 2][chip * residues : (chip + 1) * residues, at : at + wide]
            opm = numerator * jnp.broadcast_to(inverse[:, k : k + 1], (residues, wide))
            pair_one = (pair_ref[:, k] + opm).astype(bf16).astype(f32)
            pair_one_ref[k] = pair_one
            ln_one = layer_norm(pair_one)
            ln_one_ref[k] = ln_one
            normed.append(ln_one.astype(bf16))
        own_ln = jnp.concatenate(
            [ln_one_ref[first : first + stride, start + row] for row in range(rows)], axis=0
        ).astype(bf16)
        both = jnp.dot(own_ln, left_weight_ref[...], preferred_element_type=f32)
        own_mask = jnp.concatenate([mask[first : first + stride]] * rows, axis=0)
        left_tri = sigmoid(both[:, :wide]) * both[:, wide : 2 * wide] * own_mask
        left_tri = left_tri.astype(bf16).astype(f32)
        gate_out = sigmoid(both[:, 2 * wide :])
        both = jnp.dot(
            jnp.concatenate(normed, axis=0), right_weight_ref[...], preferred_element_type=f32
        )
        right_tri = (sigmoid(both[:, :wide]) * both[:, wide:]).astype(bf16).astype(f32)
        for row in range(rows):
            gates[row].append(gate_out[row * stride : (row + 1) * stride])
            for k in range(stride):
                at = row * stride + k
                sums[row][k % 2] += (
                    left_tri[at : at + 1] * right_tri[k * residues : (k + 1) * residues]
                )

    own_pair = jnp.concatenate([pair_one_ref[:, start + row] for row in range(rows)], axis=0)
    gate_out = jnp.concatenate(sum(gates, []), axis=0)
    products = []
    for row in range(rows):
        own_mask = keep_ref[pl.ds(start + row, 1), :][:, sequences : sequences + 1]
        products.append((sums[row][0] + sums[row][1]) * (mask * own_mask))
    product = jnp.concatenate(products, axis=0).astype(bf16).astype(f32)
    normed = layer_norm(product).astype(bf16)
    update = jnp.dot(normed, output_ref[...], preferred_element_type=f32)
    pair_two = (own_pair + gate_out * update).astype(bf16).astype(f32)
    ln_two = layer_norm(pair_two).astype(bf16)
    hidden = jnp.maximum(jnp.dot(ln_two, up_ref[...], preferred_element_type=f32), 0.0).astype(bf16)
    result = pair_two + jnp.dot(hidden, down_ref[...], preferred_element_type=f32)
    out_ref[...] = result.astype(bf16).reshape(rows, residues, wide)


def gather_all(packed):
    near_count = lax.axis_size("near")
    sibling = [(0, 1), (1, 0)]
    far = lax.ppermute(packed[None], "far", sibling)
    both = jnp.concatenate([packed[None], far], axis=0)
    copies = jnp.broadcast_to(both, (near_count,) + both.shape)
    held = lax.all_to_all(copies, "near", split_axis=0, concat_axis=0)
    held = held.reshape((-1,) + packed.shape)
    return held, lax.ppermute(held, "sub", sibling)


def block_place(chip, chips):
    half = chips // 2
    return 2 * (chip % half) + lax.bitwise_xor(lax.axis_index("far"), chip // half)


def shards_replicated(
    pairwise_state,
    alignment_state,
    alignment_mask,
    residue_crop_mask,
    outer_input_weight,
    outer_output_weight,
    triangle_input_weight,
    triangle_gate,
    triangle_output_weight,
    transition_up_weight,
    transition_down_weight,
):
    rows, residues, wide = pairwise_state.shape
    sequences = alignment_state.shape[0]
    channels = outer_input_weight.shape[2]
    vector = pl.BlockSpec(memory_space=pltpu.VMEM)
    params = pltpu.CompilerParams(vmem_limit_bytes=40 << 20)
    hbm = pl.BlockSpec(memory_space=pltpu.HBM)
    packed = pl.pallas_call(
        pack_kernel,
        out_shape=jax.ShapeDtypeStruct((rows * residues + sequences + 16, wide), jnp.bfloat16),
        in_specs=[hbm] * 5,
        out_specs=vector,
        scratch_shapes=[
            pltpu.SMEM((residues,), jnp.int32),
            pltpu.VMEM((rows, sequences), jnp.int32),
            pltpu.VMEM(alignment_state.shape, jnp.bfloat16),
            pltpu.VMEM((2, channels, alignment_state.shape[2]), jnp.bfloat16),
            pltpu.VMEM(alignment_state.shape, jnp.float32),
            pltpu.SemaphoreType.DMA((4 + rows,)),
        ],
        compiler_params=pltpu.CompilerParams(vmem_limit_bytes=8 << 20),
    )(
        *(
            pltpu.with_memory_space_constraint(array, pltpu.HBM)
            for array in (
                residue_crop_mask,
                alignment_mask.T,
                alignment_state,
                outer_input_weight.transpose(0, 2, 1),
                pairwise_state,
            )
        )
    )
    cores, chips = lax.axis_size("sub"), lax.axis_size("far") * lax.axis_size("near")
    group = cores * rows
    parts = 2
    hidden = transition_up_weight.shape[1]
    weights = pl.pallas_call(
        weight_kernel,
        out_shape=(
            pltpu.VMEM((parts, (channels // parts + 1) * 2 * channels, 2 * wide), jnp.bfloat16),
            pltpu.VMEM((wide, 2 * wide), jnp.bfloat16),
            pltpu.VMEM((wide, 3 * wide), jnp.bfloat16),
            pltpu.VMEM((wide, wide), jnp.bfloat16),
            pltpu.VMEM((wide, hidden), jnp.bfloat16),
            pltpu.VMEM((hidden, wide), jnp.bfloat16),
        ),
        in_specs=[hbm] * 6 + [pl.BlockSpec(memory_space=pl.ANY)],
        out_specs=(vector,) * 6,
        scratch_shapes=[
            pltpu.VMEM(outer_output_weight.shape, jnp.bfloat16),
            pltpu.SemaphoreType.DMA((9,)),
        ],
        compiler_params=pltpu.CompilerParams(vmem_limit_bytes=8 << 20),
    )(
        *(
            pltpu.with_memory_space_constraint(array, pltpu.HBM)
            for array in (
                outer_output_weight,
                triangle_input_weight,
                triangle_gate,
                triangle_output_weight,
                transition_up_weight,
                transition_down_weight,
            )
        ),
        packed,
    )
    held, other = gather_all(packed)
    return pl.pallas_call(
        update_kernel,
        out_shape=jax.ShapeDtypeStruct(pairwise_state.shape, jnp.bfloat16),
        in_specs=[vector] * 8,
        out_specs=vector,
        scratch_shapes=[
            pltpu.VMEM((residues, channels, wide), jnp.float32),
            pltpu.VMEM((2, group * sequences, chips * wide), jnp.bfloat16),
            pltpu.VMEM((residues, wide), jnp.float32),
            pltpu.VMEM((parts, chips * residues, channels // parts * wide // 2), jnp.bfloat16),
            pltpu.VMEM((parts, chips * residues, channels // parts * wide // 2), jnp.bfloat16),
            pltpu.VMEM((residues, residues, wide), jnp.float32),
            pltpu.VMEM((residues, residues, wide), jnp.float32),
            pltpu.VMEM((residues, residues, wide), jnp.float32),
        ],
        compiler_params=params,
    )(
        held,
        other,
        *weights,
    )


def shards(
    pairwise_state,
    alignment_state,
    alignment_mask,
    residue_crop_mask,
    outer_input_weight,
    outer_output_weight,
    triangle_input_weight,
    triangle_gate,
    triangle_output_weight,
    transition_up_weight,
    transition_down_weight,
):
    row_count = pairwise_state.shape[0]
    start_row = lax.axis_index(("dap", "sub")) * row_count
    row_presence_mask = lax.dynamic_slice_in_dim(residue_crop_mask, start_row, row_count, 0).astype(
        jnp.float32
    )
    full_mask = residue_crop_mask.astype(jnp.float32)
    alignment_keep = alignment_mask.astype(jnp.float32) * row_presence_mask[None, :]
    alignment_normed = norm_layer(alignment_state.astype(jnp.float32), -1).astype(jnp.bfloat16)
    left_alignment = (
        jnp.einsum(
            "pxm,my->pxy",
            alignment_normed,
            outer_input_weight[0],
            preferred_element_type=jnp.float32,
        )
        * alignment_keep[:, :, None]
    ).astype(jnp.bfloat16)
    right_alignment = (
        jnp.einsum(
            "pxm,my->pxy",
            alignment_normed,
            outer_input_weight[1],
            preferred_element_type=jnp.float32,
        )
        * alignment_keep[:, :, None]
    ).astype(jnp.bfloat16)
    inner_alignment = jnp.einsum(
        "tqu,ulx->tqlx", left_alignment, outer_output_weight, preferred_element_type=jnp.float32
    ).astype(jnp.bfloat16)
    right_portion = lax.all_gather(right_alignment, ("dap", "sub"), axis=1, tiled=True)
    keep_portion = lax.all_gather(
        alignment_keep.astype(jnp.bfloat16), ("dap", "sub"), axis=1, tiled=True
    )
    numerator_sum = jnp.einsum(
        "zkwv,znw->knv", inner_alignment, right_portion, preferred_element_type=jnp.float32
    )
    pair_norm_count = jnp.einsum("cf,cg->fg", alignment_keep, keep_portion.astype(jnp.float32))
    block_part = numerator_sum / jnp.maximum(pair_norm_count, 1.0)[:, :, None]
    pair_one = (pairwise_state.astype(jnp.float32) + block_part).astype(jnp.bfloat16)
    ln_one = norm_layer(pair_one.astype(jnp.float32), -1).astype(jnp.bfloat16)
    pair_keep = row_presence_mask[:, None] * full_mask[None, :]

    def operand(gate_w, proj_w):
        gate_val = jnp.einsum("ijc,cd->dij", ln_one, gate_w, preferred_element_type=jnp.float32)
        proj_val = jnp.einsum("ijc,cd->dij", ln_one, proj_w, preferred_element_type=jnp.float32)
        return (jax.nn.sigmoid(gate_val) * proj_val * pair_keep[None]).astype(jnp.bfloat16)

    left_tri = operand(triangle_input_weight[0], triangle_input_weight[1])
    right_tri = operand(triangle_input_weight[2], triangle_input_weight[3])
    near_right = lax.all_gather(right_tri, "sub", axis=1, tiled=True)
    left_cols, right_all = (
        lax.all_to_all(left_tri, "dap", split_axis=0, concat_axis=1, tiled=True),
        lax.all_to_all(near_right, "dap", split_axis=0, concat_axis=1, tiled=True),
    )
    product = jnp.einsum(
        "cik,cjk->cij", left_cols, right_all, preferred_element_type=jnp.float32
    ).astype(jnp.bfloat16)
    returned = lax.all_to_all(product, "dap", split_axis=1, concat_axis=0, tiled=True)
    normed = norm_layer(returned.astype(jnp.float32), 0).astype(jnp.bfloat16)
    update = jnp.einsum(
        "cij,cd->ijd", normed, triangle_output_weight, preferred_element_type=jnp.float32
    )
    gate_out = jax.nn.sigmoid(
        jnp.einsum("ijc,cd->ijd", ln_one, triangle_gate, preferred_element_type=jnp.float32)
    )
    pair_two = (pair_one.astype(jnp.float32) + gate_out * update).astype(jnp.bfloat16)
    ln_two = norm_layer(pair_two.astype(jnp.float32), -1).astype(jnp.bfloat16)

    def step(row_pair):
        return transition(*row_pair, transition_up_weight, transition_down_weight)

    return lax.map(step, (ln_two, pair_two))


def solution(mesh):
    placed = (
        P(("crop", "dap", "sub"), None, None),
        P("crop", ("dap", "sub"), None),
        P("crop", ("dap", "sub")),
        P("crop"),
        P(),
        P(),
        P(),
        P(),
        P(),
        P(),
        P(),
    )

    small = mesh.shape["sub"] == 2 and mesh.shape["dap"] == 8

    def distributed(*arrays):
        return jax.shard_map(
            shards,
            mesh=mesh,
            in_specs=placed,
            out_specs=P(("crop", "dap", "sub"), None, None),
            check_vma=False,
        )(*arrays)

    def replicated(*arrays):
        rows = ("far", "near", "sub")
        fine = Mesh(
            mesh.devices.reshape(mesh.shape["crop"], 2, -1, mesh.shape["sub"]), ("crop",) + rows
        )
        return jax.shard_map(
            shards_replicated,
            mesh=fine,
            in_specs=(P(("crop",) + rows, None, None), P("crop", rows, None), P("crop", rows))
            + placed[3:],
            out_specs=P(("crop",) + rows, None, None),
            check_vma=False,
        )(*arrays)

    def whole(pairwise_state, *rest):
        residues, channels = pairwise_state.shape[1:]
        if small and residues * residues * channels * 2 <= REPLICATED_PAIR_BYTES:
            return replicated(pairwise_state, *rest)
        return distributed(pairwise_state, *rest)

    return whole
```

```python
import jax
import jax.numpy as jnp
from jax import lax
from jax.experimental import pallas as pl
from jax.experimental.pallas import tpu as pltpu
from jax.sharding import PartitionSpec as P

REPLICATED_PAIR_BYTES = 1 << 20


def norm_layer(values, reduce_axis):
    average = jnp.mean(values, axis=reduce_axis, keepdims=True)
    centered = values - average
    variance = jnp.mean(centered * centered, axis=reduce_axis, keepdims=True)
    return centered * lax.rsqrt(variance + 1e-05)


def transition(ln_two, pair_two, transition_up_weight, transition_down_weight):
    hidden = jax.nn.relu(
        jnp.dot(ln_two, transition_up_weight, preferred_element_type=jnp.float32)
    ).astype(jnp.bfloat16)
    return (
        pair_two.astype(jnp.float32)
        + jnp.dot(hidden, transition_down_weight, preferred_element_type=jnp.float32)
    ).astype(jnp.bfloat16)


def layer_norm(values):
    count = values.shape[-1]
    centered = values - jnp.sum(values, axis=-1, keepdims=True) * (1.0 / count)
    variance = jnp.sum(centered * centered, axis=-1, keepdims=True) * (1.0 / count)
    return centered * lax.rsqrt(variance + 1e-05)


def first_row(rows):
    return (lax.axis_index("dap") * lax.axis_size("sub") + lax.axis_index("sub")) * rows


def pack_kernel(
    mask_hbm,
    keep_hbm,
    state_hbm,
    weight_hbm,
    pair_hbm,
    out_ref,
    mask_ref,
    keep_ref,
    state_ref,
    weight_ref,
    wide_ref,
    sems,
):
    rows, residues, wide = pair_hbm.shape
    sequences = state_ref.shape[0]
    base = rows * residues
    start = first_row(rows)
    second_core = lax.axis_index("sub") == 1
    loads = [
        pltpu.make_async_copy(state_hbm, state_ref, sems.at[0]),
        pltpu.make_async_copy(weight_hbm, weight_ref, sems.at[1]),
        pltpu.make_async_copy(keep_hbm, keep_ref, sems.at[2]),
        pltpu.make_async_copy(mask_hbm, mask_ref, sems.at[3]),
    ] + [
        pltpu.make_async_copy(
            pair_hbm.at[row], out_ref.at[pl.ds(row * residues, residues)], sems.at[4 + row]
        )
        for row in range(rows)
    ]
    for load in loads:
        load.start()
    loads[0].wait()
    wide_ref[...] = state_ref[...].astype(jnp.float32)
    normed_rows = [layer_norm(wide_ref[:, row]).astype(jnp.bfloat16) for row in range(rows)]
    eye = lax.broadcasted_iota(jnp.int32, (sequences, sequences), 0) == lax.broadcasted_iota(
        jnp.int32, (sequences, sequences), 1
    )
    lefts, rights, keeps = [], [], []
    for load in loads[1:4]:
        load.wait()
    for row in range(rows):
        present = mask_ref[start + row].astype(jnp.float32)
        keep_row = keep_ref[row : row + 1].astype(jnp.float32) * present
        keep_column = jnp.sum(
            jnp.where(eye, jnp.broadcast_to(keep_row, eye.shape), 0.0), axis=1, keepdims=True
        )
        normed = normed_rows[row]
        last = (((1,), (1,)), ((), ()))
        left = lax.dot_general(weight_ref[0], normed, last, preferred_element_type=jnp.float32)
        right = lax.dot_general(normed, weight_ref[1], last, preferred_element_type=jnp.float32)
        lefts.append(left * keep_row)
        rights.append(right * keep_column)
        keeps.append(
            jnp.concatenate(
                [keep_row, jnp.full((1, wide - sequences), present, jnp.float32)], axis=1
            )
        )
    left = jnp.concatenate(lefts, axis=1)
    right = jnp.concatenate(rights, axis=1)
    first = jnp.concatenate([right, left], axis=1)
    other = jnp.concatenate([left, right], axis=1)
    out_ref[base : base + sequences] = jnp.where(second_core, other, first).astype(jnp.bfloat16)
    out_ref[base + sequences :] = jnp.concatenate(
        keeps + [jnp.zeros((16 - rows, wide), jnp.float32)], axis=0
    ).astype(jnp.bfloat16)
    for load in loads[4:]:
        load.wait()


def sigmoid(values):
    return 0.5 * jnp.tanh(0.5 * values) + 0.5


def update_kernel(
    held_ref,
    other_ref,
    outer_ref,
    triangle_ref,
    gate_ref,
    output_ref,
    up_ref,
    down_ref,
    out_ref,
    block_ref,
    left_ref,
    right_ref,
    keep_ref,
    first_ref,
    second_ref,
    pair_ref,
    pair_one_ref,
    ln_one_ref,
):
    rows, residues, wide = out_ref.shape
    cores, chips = 2, lax.axis_size("dap")
    channels = outer_ref.shape[0]
    sequences = channels
    base = rows * residues
    half = wide // 2
    group = cores * rows
    start = first_row(rows)
    second_core = lax.axis_index("sub") == 1
    bf16 = jnp.bfloat16
    f32 = jnp.float32

    parts = block_ref.shape[0]
    span = channels // parts
    nothing = jnp.zeros((channels, wide), bf16)
    for part in range(parts):
        for step in range(span + 1):
            weight = outer_ref[part * span + step % span]
            at = step * 2 * channels
            block_ref[part, at : at + channels, :wide] = weight
            block_ref[part, at : at + channels, wide:] = nothing
            block_ref[part, at + channels : at + 2 * channels, :wide] = nothing
            block_ref[part, at + channels : at + 2 * channels, wide:] = weight

    lane = lax.broadcasted_iota(jnp.int32, (channels, wide), 1)
    lane_block = lane // channels
    low = lane < half
    for chip in range(chips):
        place = block_place(chip, chips)
        mine, other = held_ref[place], other_ref[place]
        blocks = [jnp.where(second_core, other, mine), jnp.where(second_core, mine, other)]
        packed = [block[base : base + sequences].astype(f32) for block in blocks]
        right = jnp.where(low, packed[0], packed[1])
        for turn, value in enumerate((right, pltpu.roll(right, half, 1))):
            for copy in range(group):
                right_ref[
                    turn,
                    copy * sequences : (copy + 1) * sequences,
                    chip * wide : (chip + 1) * wide,
                ] = value.astype(bf16)
        for core in range(cores):
            residue = (chip * cores + core) * rows
            for row in range(rows):
                at = (rows if core == 0 else 0) + row
                left_ref[residue + row] = jnp.where(lane_block == at, packed[core], 0.0)
            keep_ref[residue : residue + rows] = blocks[core][base + sequences :].astype(f32)[:rows]
            pair_ref[residue : residue + rows] = (
                blocks[core][:base].astype(f32).reshape(rows, residues, wide)
            )

    last = (((1,), (1,)), ((), ()))
    keep = keep_ref[...]
    mask = jnp.broadcast_to(keep[:, sequences : sequences + 1], (residues, wide))
    counted = lax.broadcasted_iota(jnp.int32, (residues, wide), 1) < sequences
    count = lax.dot_general(
        jnp.where(counted, keep, 0.0).astype(bf16),
        keep.astype(bf16),
        last,
        preferred_element_type=f32,
    )
    inverse = 1.0 / jnp.maximum(count, 1.0)

    low = lax.broadcasted_iota(jnp.int32, (residues, wide), 1) < half
    totals = [0.0, 0.0]
    for part in range(parts):
        outer = []
        for turn in range(2):
            left = jnp.concatenate(
                [left_ref[:, d] for d in range(part * span + turn, (part + 1) * span, 2)], axis=0
            ).astype(bf16)
            outer.append(jnp.dot(left, right_ref[turn], preferred_element_type=f32))

        def piece(turn, at, chip):
            return outer[turn][
                at * residues : (at + 1) * residues, chip * wide : (chip + 1) * wide
            ]

        for at in range(span // 2):
            follow = (at + 1) % (span // 2)
            for chip in range(chips):
                place = (
                    part,
                    slice(chip * residues, (chip + 1) * residues),
                    slice(at * wide, (at + 1) * wide),
                )
                first_ref[place] = jnp.where(low, piece(0, at, chip), piece(1, at, chip)).astype(bf16)
                second_ref[place] = jnp.where(
                    low, piece(1, at, chip), piece(0, follow, chip)
                ).astype(bf16)
        depth = span * 2 * channels
        totals[0] += jnp.dot(first_ref[part], block_ref[part, :depth], preferred_element_type=f32)
        totals[1] += jnp.dot(
            second_ref[part], block_ref[part, 2 * channels :], preferred_element_type=f32
        )

    right_weight = jnp.concatenate([triangle_ref[2], triangle_ref[3]], axis=1)
    right_tri = []
    stride = 8
    for first in range(0, residues, stride):
        normed = []
        for k in range(first, first + stride):
            chip, pick = k // group, k % group
            at = (pick % 2) * wide
            numerator = totals[pick // 2][chip * residues : (chip + 1) * residues, at : at + wide]
            opm = numerator * jnp.broadcast_to(inverse[:, k : k + 1], (residues, wide))
            pair_one = (pair_ref[:, k] + opm).astype(bf16).astype(f32)
            pair_one_ref[k] = pair_one
            ln_one = layer_norm(pair_one)
            ln_one_ref[k] = ln_one
            normed.append(ln_one.astype(bf16))
        both = jnp.dot(
            jnp.concatenate(normed, axis=0), right_weight, preferred_element_type=f32
        )
        right_tri.append((sigmoid(both[:, :wide]) * both[:, wide:]).astype(bf16).astype(f32))

    own_pair = jnp.concatenate([pair_one_ref[:, start + row] for row in range(rows)], axis=0)
    own_ln = jnp.concatenate([ln_one_ref[:, start + row] for row in range(rows)], axis=0).astype(bf16)
    left_weight = jnp.concatenate([triangle_ref[0], triangle_ref[1]], axis=1)
    both = jnp.dot(own_ln, left_weight, preferred_element_type=f32)
    left_tri = sigmoid(both[:, :wide]) * both[:, wide:] * jnp.concatenate([mask] * rows, axis=0)
    left_tri = left_tri.astype(bf16).astype(f32)
    products = []
    for row in range(rows):
        sums = [jnp.zeros((residues, wide), f32) for _ in range(4)]
        for k in range(residues):
            at = row * residues + k
            place = (k % stride) * residues
            sums[k % 4] += left_tri[at : at + 1] * right_tri[k // stride][place : place + residues]
        total = (sums[0] + sums[1]) + (sums[2] + sums[3])
        own_mask = keep_ref[pl.ds(start + row, 1), :][:, sequences : sequences + 1]
        products.append(total * (mask * own_mask))
    product = jnp.concatenate(products, axis=0).astype(bf16).astype(f32)
    normed = layer_norm(product).astype(bf16)
    update = jnp.dot(normed, output_ref[...], preferred_element_type=f32)
    gate_out = sigmoid(jnp.dot(own_ln, gate_ref[...], preferred_element_type=f32))
    pair_two = (own_pair + gate_out * update).astype(bf16).astype(f32)
    ln_two = layer_norm(pair_two).astype(bf16)
    hidden = jnp.maximum(jnp.dot(ln_two, up_ref[...], preferred_element_type=f32), 0.0).astype(bf16)
    result = pair_two + jnp.dot(hidden, down_ref[...], preferred_element_type=f32)
    out_ref[...] = result.astype(bf16).reshape(rows, residues, wide)


def gather_all(packed):
    dap_count = lax.axis_size("dap")
    half = dap_count // 2
    far = lax.ppermute(packed[None], "dap", [(src, src ^ half) for src in range(dap_count)])
    both = jnp.concatenate([packed[None], far], axis=0)
    held = [both] + [
        lax.ppermute(both, "dap", [(src, src ^ offset) for src in range(dap_count)])
        for offset in swap_order(dap_count)
    ]
    sibling = [(0, 1), (1, 0)]
    early = lax.ppermute(jnp.concatenate(held[:-1], axis=0), "sub", sibling)
    late = lax.ppermute(held[-1], "sub", sibling)
    return jnp.concatenate(held, axis=0), jnp.concatenate([early, late], axis=0)


def swap_order(dap_count):
    near = dap_count // 2
    return [1, near - 1] + list(range(2, near - 1))


def block_place(chip, chips):
    offset = lax.bitwise_xor(lax.axis_index("dap"), chip)
    half = chips // 2
    near = jnp.where(offset >= half, offset - half, offset)
    turn = jnp.where(near > 1, jnp.where(near == half - 1, 2, near + 1), near)
    return 2 * turn + jnp.where(offset >= half, 1, 0)


def shards_replicated(
    pairwise_state,
    alignment_state,
    alignment_mask,
    residue_crop_mask,
    outer_input_weight,
    outer_output_weight,
    triangle_input_weight,
    triangle_gate,
    triangle_output_weight,
    transition_up_weight,
    transition_down_weight,
):
    rows, residues, wide = pairwise_state.shape
    sequences = alignment_state.shape[0]
    channels = outer_input_weight.shape[2]
    vector = pl.BlockSpec(memory_space=pltpu.VMEM)
    params = pltpu.CompilerParams(vmem_limit_bytes=40 << 20)
    hbm = pl.BlockSpec(memory_space=pltpu.HBM)
    packed = pl.pallas_call(
        pack_kernel,
        out_shape=jax.ShapeDtypeStruct((rows * residues + sequences + 16, wide), jnp.bfloat16),
        in_specs=[hbm] * 5,
        out_specs=vector,
        scratch_shapes=[
            pltpu.SMEM((residues,), jnp.int32),
            pltpu.VMEM((rows, sequences), jnp.int32),
            pltpu.VMEM(alignment_state.shape, jnp.bfloat16),
            pltpu.VMEM((2, channels, alignment_state.shape[2]), jnp.bfloat16),
            pltpu.VMEM(alignment_state.shape, jnp.float32),
            pltpu.SemaphoreType.DMA((4 + rows,)),
        ],
        compiler_params=pltpu.CompilerParams(vmem_limit_bytes=8 << 20),
    )(
        *(
            pltpu.with_memory_space_constraint(array, pltpu.HBM)
            for array in (
                residue_crop_mask,
                alignment_mask.T,
                alignment_state,
                outer_input_weight.transpose(0, 2, 1),
                pairwise_state,
            )
        )
    )
    held, other = gather_all(packed)
    cores, chips = lax.axis_size("sub"), lax.axis_size("dap")
    group = cores * rows
    parts = 1
    return pl.pallas_call(
        update_kernel,
        out_shape=jax.ShapeDtypeStruct(pairwise_state.shape, jnp.bfloat16),
        in_specs=[vector] * 8,
        out_specs=vector,
        scratch_shapes=[
            pltpu.VMEM((parts, (channels // parts + 1) * 2 * channels, 2 * wide), jnp.bfloat16),
            pltpu.VMEM((residues, channels, wide), jnp.float32),
            pltpu.VMEM((2, group * sequences, chips * wide), jnp.bfloat16),
            pltpu.VMEM((residues, wide), jnp.float32),
            pltpu.VMEM((parts, chips * residues, channels // parts * wide // 2), jnp.bfloat16),
            pltpu.VMEM((parts, chips * residues, channels // parts * wide // 2), jnp.bfloat16),
            pltpu.VMEM((residues, residues, wide), jnp.float32),
            pltpu.VMEM((residues, residues, wide), jnp.float32),
            pltpu.VMEM((residues, residues, wide), jnp.float32),
        ],
        compiler_params=params,
    )(
        held,
        other,
        outer_output_weight,
        triangle_input_weight,
        triangle_gate,
        triangle_output_weight,
        transition_up_weight,
        transition_down_weight,
    )


def shards(
    pairwise_state,
    alignment_state,
    alignment_mask,
    residue_crop_mask,
    outer_input_weight,
    outer_output_weight,
    triangle_input_weight,
    triangle_gate,
    triangle_output_weight,
    transition_up_weight,
    transition_down_weight,
):
    row_count = pairwise_state.shape[0]
    start_row = lax.axis_index(("dap", "sub")) * row_count
    row_presence_mask = lax.dynamic_slice_in_dim(residue_crop_mask, start_row, row_count, 0).astype(
        jnp.float32
    )
    full_mask = residue_crop_mask.astype(jnp.float32)
    alignment_keep = alignment_mask.astype(jnp.float32) * row_presence_mask[None, :]
    alignment_normed = norm_layer(alignment_state.astype(jnp.float32), -1).astype(jnp.bfloat16)
    left_alignment = (
        jnp.einsum(
            "pxm,my->pxy",
            alignment_normed,
            outer_input_weight[0],
            preferred_element_type=jnp.float32,
        )
        * alignment_keep[:, :, None]
    ).astype(jnp.bfloat16)
    right_alignment = (
        jnp.einsum(
            "pxm,my->pxy",
            alignment_normed,
            outer_input_weight[1],
            preferred_element_type=jnp.float32,
        )
        * alignment_keep[:, :, None]
    ).astype(jnp.bfloat16)
    inner_alignment = jnp.einsum(
        "tqu,ulx->tqlx", left_alignment, outer_output_weight, preferred_element_type=jnp.float32
    ).astype(jnp.bfloat16)
    right_portion = lax.all_gather(right_alignment, ("dap", "sub"), axis=1, tiled=True)
    keep_portion = lax.all_gather(
        alignment_keep.astype(jnp.bfloat16), ("dap", "sub"), axis=1, tiled=True
    )
    numerator_sum = jnp.einsum(
        "zkwv,znw->knv", inner_alignment, right_portion, preferred_element_type=jnp.float32
    )
    pair_norm_count = jnp.einsum("cf,cg->fg", alignment_keep, keep_portion.astype(jnp.float32))
    block_part = numerator_sum / jnp.maximum(pair_norm_count, 1.0)[:, :, None]
    pair_one = (pairwise_state.astype(jnp.float32) + block_part).astype(jnp.bfloat16)
    ln_one = norm_layer(pair_one.astype(jnp.float32), -1).astype(jnp.bfloat16)
    pair_keep = row_presence_mask[:, None] * full_mask[None, :]

    def operand(gate_w, proj_w):
        gate_val = jnp.einsum("ijc,cd->dij", ln_one, gate_w, preferred_element_type=jnp.float32)
        proj_val = jnp.einsum("ijc,cd->dij", ln_one, proj_w, preferred_element_type=jnp.float32)
        return (jax.nn.sigmoid(gate_val) * proj_val * pair_keep[None]).astype(jnp.bfloat16)

    left_tri = operand(triangle_input_weight[0], triangle_input_weight[1])
    right_tri = operand(triangle_input_weight[2], triangle_input_weight[3])
    near_right = lax.all_gather(right_tri, "sub", axis=1, tiled=True)
    left_cols, right_all = (
        lax.all_to_all(left_tri, "dap", split_axis=0, concat_axis=1, tiled=True),
        lax.all_to_all(near_right, "dap", split_axis=0, concat_axis=1, tiled=True),
    )
    product = jnp.einsum(
        "cik,cjk->cij", left_cols, right_all, preferred_element_type=jnp.float32
    ).astype(jnp.bfloat16)
    returned = lax.all_to_all(product, "dap", split_axis=1, concat_axis=0, tiled=True)
    normed = norm_layer(returned.astype(jnp.float32), 0).astype(jnp.bfloat16)
    update = jnp.einsum(
        "cij,cd->ijd", normed, triangle_output_weight, preferred_element_type=jnp.float32
    )
    gate_out = jax.nn.sigmoid(
        jnp.einsum("ijc,cd->ijd", ln_one, triangle_gate, preferred_element_type=jnp.float32)
    )
    pair_two = (pair_one.astype(jnp.float32) + gate_out * update).astype(jnp.bfloat16)
    ln_two = norm_layer(pair_two.astype(jnp.float32), -1).astype(jnp.bfloat16)

    def step(row_pair):
        return transition(*row_pair, transition_up_weight, transition_down_weight)

    return lax.map(step, (ln_two, pair_two))


def solution(mesh):
    placed = (
        P(("crop", "dap", "sub"), None, None),
        P("crop", ("dap", "sub"), None),
        P("crop", ("dap", "sub")),
        P("crop"),
        P(),
        P(),
        P(),
        P(),
        P(),
        P(),
        P(),
    )

    small = mesh.shape["sub"] == 2 and mesh.shape["dap"] == 8

    def body(pairwise_state, *rest):
        residues, channels = pairwise_state.shape[1:]
        if small and residues * residues * channels * 2 <= REPLICATED_PAIR_BYTES:
            return shards_replicated(pairwise_state, *rest)
        return shards(pairwise_state, *rest)

    return jax.shard_map(
        body,
        mesh=mesh,
        in_specs=placed,
        out_specs=P(("crop", "dap", "sub"), None, None),
        check_vma=False,
    )
```

```python
import jax
import jax.numpy as jnp
from jax import lax
from jax.experimental import pallas as pl
from jax.experimental.pallas import tpu as pltpu
from jax.sharding import PartitionSpec as P

REPLICATED_PAIR_BYTES = 1 << 20


def norm_layer(values, reduce_axis):
    average = jnp.mean(values, axis=reduce_axis, keepdims=True)
    centered = values - average
    variance = jnp.mean(centered * centered, axis=reduce_axis, keepdims=True)
    return centered * lax.rsqrt(variance + 1e-05)


def transition(ln_two, pair_two, transition_up_weight, transition_down_weight):
    hidden = jax.nn.relu(
        jnp.dot(ln_two, transition_up_weight, preferred_element_type=jnp.float32)
    ).astype(jnp.bfloat16)
    return (
        pair_two.astype(jnp.float32)
        + jnp.dot(hidden, transition_down_weight, preferred_element_type=jnp.float32)
    ).astype(jnp.bfloat16)


def layer_norm(values):
    count = values.shape[-1]
    centered = values - jnp.sum(values, axis=-1, keepdims=True) * (1.0 / count)
    variance = jnp.sum(centered * centered, axis=-1, keepdims=True) * (1.0 / count)
    return centered * lax.rsqrt(variance + 1e-05)


def first_row(rows):
    return (lax.axis_index("dap") * lax.axis_size("sub") + lax.axis_index("sub")) * rows


def pack_kernel(
    mask_hbm,
    keep_hbm,
    state_hbm,
    weight_hbm,
    pair_hbm,
    out_ref,
    mask_ref,
    keep_ref,
    state_ref,
    weight_ref,
    wide_ref,
    sems,
):
    rows, residues, wide = pair_hbm.shape
    sequences = state_ref.shape[0]
    base = rows * residues
    start = first_row(rows)
    second_core = lax.axis_index("sub") == 1
    loads = [
        pltpu.make_async_copy(state_hbm, state_ref, sems.at[0]),
        pltpu.make_async_copy(weight_hbm, weight_ref, sems.at[1]),
        pltpu.make_async_copy(keep_hbm, keep_ref, sems.at[2]),
        pltpu.make_async_copy(mask_hbm, mask_ref, sems.at[3]),
    ] + [
        pltpu.make_async_copy(
            pair_hbm.at[row], out_ref.at[pl.ds(row * residues, residues)], sems.at[4 + row]
        )
        for row in range(rows)
    ]
    for load in loads:
        load.start()
    loads[0].wait()
    wide_ref[...] = state_ref[...].astype(jnp.float32)
    normed_rows = [layer_norm(wide_ref[:, row]).astype(jnp.bfloat16) for row in range(rows)]
    eye = lax.broadcasted_iota(jnp.int32, (sequences, sequences), 0) == lax.broadcasted_iota(
        jnp.int32, (sequences, sequences), 1
    )
    lefts, rights, keeps = [], [], []
    for load in loads[1:4]:
        load.wait()
    for row in range(rows):
        present = mask_ref[start + row].astype(jnp.float32)
        keep_row = keep_ref[row : row + 1].astype(jnp.float32) * present
        keep_column = jnp.sum(
            jnp.where(eye, jnp.broadcast_to(keep_row, eye.shape), 0.0), axis=1, keepdims=True
        )
        normed = normed_rows[row]
        last = (((1,), (1,)), ((), ()))
        left = lax.dot_general(weight_ref[0], normed, last, preferred_element_type=jnp.float32)
        right = lax.dot_general(normed, weight_ref[1], last, preferred_element_type=jnp.float32)
        lefts.append(left * keep_row)
        rights.append(right * keep_column)
        keeps.append(
            jnp.concatenate(
                [keep_row, jnp.full((1, wide - sequences), present, jnp.float32)], axis=1
            )
        )
    left = jnp.concatenate(lefts, axis=1)
    right = jnp.concatenate(rights, axis=1)
    first = jnp.concatenate([right, left], axis=1)
    other = jnp.concatenate([left, right], axis=1)
    out_ref[base : base + sequences] = jnp.where(second_core, other, first).astype(jnp.bfloat16)
    out_ref[base + sequences :] = jnp.concatenate(
        keeps + [jnp.zeros((16 - rows, wide), jnp.float32)], axis=0
    ).astype(jnp.bfloat16)
    for load in loads[4:]:
        load.wait()


def sigmoid(values):
    return 0.5 * jnp.tanh(0.5 * values) + 0.5


def update_kernel(
    held_ref,
    other_ref,
    outer_ref,
    triangle_ref,
    gate_ref,
    output_ref,
    up_ref,
    down_ref,
    out_ref,
    block_ref,
    left_ref,
    right_ref,
    keep_ref,
    first_ref,
    second_ref,
    pair_ref,
):
    rows, residues, wide = out_ref.shape
    cores, chips = 2, lax.axis_size("dap")
    channels = outer_ref.shape[0]
    sequences = channels
    base = rows * residues
    half = wide // 2
    group = cores * rows
    start = first_row(rows)
    second_core = lax.axis_index("sub") == 1
    bf16 = jnp.bfloat16
    f32 = jnp.float32

    parts = block_ref.shape[0]
    span = channels // parts
    nothing = jnp.zeros((channels, wide), bf16)
    for part in range(parts):
        for step in range(span + 1):
            weight = outer_ref[part * span + step % span]
            at = step * 2 * channels
            block_ref[part, at : at + channels, :wide] = weight
            block_ref[part, at : at + channels, wide:] = nothing
            block_ref[part, at + channels : at + 2 * channels, :wide] = nothing
            block_ref[part, at + channels : at + 2 * channels, wide:] = weight

    lane = lax.broadcasted_iota(jnp.int32, (channels, wide), 1)
    lane_block = lane // channels
    low = lane < half
    for chip in range(chips):
        place = block_place(chip, chips)
        mine, other = held_ref[place], other_ref[place]
        blocks = [jnp.where(second_core, other, mine), jnp.where(second_core, mine, other)]
        packed = [block[base : base + sequences].astype(f32) for block in blocks]
        right = jnp.where(low, packed[0], packed[1])
        for turn, value in enumerate((right, pltpu.roll(right, half, 1))):
            for copy in range(group):
                right_ref[
                    turn,
                    copy * sequences : (copy + 1) * sequences,
                    chip * wide : (chip + 1) * wide,
                ] = value.astype(bf16)
        for core in range(cores):
            residue = (chip * cores + core) * rows
            for row in range(rows):
                at = (rows if core == 0 else 0) + row
                left_ref[residue + row] = jnp.where(lane_block == at, packed[core], 0.0)
            keep_ref[residue : residue + rows] = blocks[core][base + sequences :].astype(f32)[:rows]
            pair_ref[residue : residue + rows] = (
                blocks[core][:base].astype(f32).reshape(rows, residues, wide)
            )

    last = (((1,), (1,)), ((), ()))
    keep = keep_ref[...]
    mask = jnp.broadcast_to(keep[:, sequences : sequences + 1], (residues, wide))
    counted = lax.broadcasted_iota(jnp.int32, (residues, wide), 1) < sequences
    count = lax.dot_general(
        jnp.where(counted, keep, 0.0).astype(bf16),
        keep.astype(bf16),
        last,
        preferred_element_type=f32,
    )
    inverse = 1.0 / jnp.maximum(count, 1.0)

    low = lax.broadcasted_iota(jnp.int32, (residues, wide), 1) < half
    totals = [0.0, 0.0]
    for part in range(parts):
        outer = []
        for turn in range(2):
            left = jnp.concatenate(
                [left_ref[:, d] for d in range(part * span + turn, (part + 1) * span, 2)], axis=0
            ).astype(bf16)
            outer.append(jnp.dot(left, right_ref[turn], preferred_element_type=f32).astype(bf16))

        def piece(turn, at, chip):
            return outer[turn][
                at * residues : (at + 1) * residues, chip * wide : (chip + 1) * wide
            ]

        for at in range(span // 2):
            follow = (at + 1) % (span // 2)
            for chip in range(chips):
                place = (
                    part,
                    slice(chip * residues, (chip + 1) * residues),
                    slice(at * wide, (at + 1) * wide),
                )
                first_ref[place] = jnp.where(low, piece(0, at, chip), piece(1, at, chip))
                second_ref[place] = jnp.where(low, piece(1, at, chip), piece(0, follow, chip))
        depth = span * 2 * channels
        totals[0] += jnp.dot(first_ref[part], block_ref[part, :depth], preferred_element_type=f32)
        totals[1] += jnp.dot(
            second_ref[part], block_ref[part, 2 * channels :], preferred_element_type=f32
        )

    pairs = residues * residues
    pair_one = []
    for k in range(residues):
        chip, pick = k // group, k % group
        at = (pick % 2) * wide
        numerator = totals[pick // 2][chip * residues : (chip + 1) * residues, at : at + wide]
        opm = numerator * jnp.broadcast_to(inverse[:, k : k + 1], (residues, wide))
        pair_one.append((pair_ref[:, k] + opm).astype(bf16))
    pair_one = jnp.concatenate(pair_one, axis=0)
    average = jnp.full((2 * wide, wide), 1.0 / wide, bf16)
    mean = jnp.dot(pair_one, average[:wide], preferred_element_type=f32)
    centered = pair_one.astype(f32) - mean
    square = centered * centered
    coarse = square.astype(bf16)
    fine = (square - coarse.astype(f32)).astype(bf16)
    variance = jnp.dot(
        jnp.concatenate([coarse, fine], axis=1), average, preferred_element_type=f32
    )
    ln_all = (centered * lax.rsqrt(variance + 1e-05)).astype(bf16)
    both = jnp.dot(
        ln_all,
        jnp.concatenate([triangle_ref[2], triangle_ref[3]], axis=1),
        preferred_element_type=f32,
    )
    right_tri = (sigmoid(both[:, :wide]) * both[:, wide:]).astype(bf16).astype(f32)

    own = lax.broadcasted_iota(jnp.int32, (rows * residues, pairs), 0)
    own = (own % residues) * residues + own // residues + start
    chosen = (lax.broadcasted_iota(jnp.int32, (rows * residues, pairs), 1) == own).astype(bf16)
    own = jnp.dot(
        chosen, jnp.concatenate([ln_all, pair_one], axis=1), preferred_element_type=f32
    )
    own_ln, own_pair = own[:, :wide].astype(bf16), own[:, wide:]
    left_weight = jnp.concatenate([triangle_ref[0], triangle_ref[1]], axis=1)
    both = jnp.dot(own_ln, left_weight, preferred_element_type=f32)
    left_tri = sigmoid(both[:, :wide]) * both[:, wide:] * jnp.concatenate([mask] * rows, axis=0)
    left_tri = left_tri.astype(bf16).astype(f32)
    products = []
    for row in range(rows):
        sums = [jnp.zeros((residues, wide), f32) for _ in range(4)]
        for k in range(residues):
            at = row * residues + k
            sums[k % 4] += left_tri[at : at + 1] * right_tri[k * residues : (k + 1) * residues]
        total = (sums[0] + sums[1]) + (sums[2] + sums[3])
        own_mask = keep_ref[pl.ds(start + row, 1), :][:, sequences : sequences + 1]
        products.append(total * (mask * own_mask))
    product = jnp.concatenate(products, axis=0).astype(bf16).astype(f32)
    normed = layer_norm(product).astype(bf16)
    update = jnp.dot(normed, output_ref[...], preferred_element_type=f32)
    gate_out = sigmoid(jnp.dot(own_ln, gate_ref[...], preferred_element_type=f32))
    pair_two = (own_pair + gate_out * update).astype(bf16).astype(f32)
    ln_two = layer_norm(pair_two).astype(bf16)
    hidden = jnp.maximum(jnp.dot(ln_two, up_ref[...], preferred_element_type=f32), 0.0).astype(bf16)
    result = pair_two + jnp.dot(hidden, down_ref[...], preferred_element_type=f32)
    out_ref[...] = result.astype(bf16).reshape(rows, residues, wide)


def gather_all(packed):
    dap_count = lax.axis_size("dap")
    half = dap_count // 2
    far = lax.ppermute(packed[None], "dap", [(src, src ^ half) for src in range(dap_count)])
    both = jnp.concatenate([packed[None], far], axis=0)
    held = [both] + [
        lax.ppermute(both, "dap", [(src, src ^ offset) for src in range(dap_count)])
        for offset in swap_order(dap_count)
    ]
    sibling = [(0, 1), (1, 0)]
    early = lax.ppermute(jnp.concatenate(held[:-1], axis=0), "sub", sibling)
    late = lax.ppermute(held[-1], "sub", sibling)
    return jnp.concatenate(held, axis=0), jnp.concatenate([early, late], axis=0)


def swap_order(dap_count):
    near = dap_count // 2
    return [1, near - 1] + list(range(2, near - 1))


def block_place(chip, chips):
    offset = lax.bitwise_xor(lax.axis_index("dap"), chip)
    half = chips // 2
    near = jnp.where(offset >= half, offset - half, offset)
    turn = jnp.where(near > 1, jnp.where(near == half - 1, 2, near + 1), near)
    return 2 * turn + jnp.where(offset >= half, 1, 0)


def shards_replicated(
    pairwise_state,
    alignment_state,
    alignment_mask,
    residue_crop_mask,
    outer_input_weight,
    outer_output_weight,
    triangle_input_weight,
    triangle_gate,
    triangle_output_weight,
    transition_up_weight,
    transition_down_weight,
):
    rows, residues, wide = pairwise_state.shape
    sequences = alignment_state.shape[0]
    channels = outer_input_weight.shape[2]
    vector = pl.BlockSpec(memory_space=pltpu.VMEM)
    params = pltpu.CompilerParams(vmem_limit_bytes=40 << 20)
    hbm = pl.BlockSpec(memory_space=pltpu.HBM)
    packed = pl.pallas_call(
        pack_kernel,
        out_shape=jax.ShapeDtypeStruct((rows * residues + sequences + 16, wide), jnp.bfloat16),
        in_specs=[hbm] * 5,
        out_specs=vector,
        scratch_shapes=[
            pltpu.SMEM((residues,), jnp.int32),
            pltpu.VMEM((rows, sequences), jnp.int32),
            pltpu.VMEM(alignment_state.shape, jnp.bfloat16),
            pltpu.VMEM((2, channels, alignment_state.shape[2]), jnp.bfloat16),
            pltpu.VMEM(alignment_state.shape, jnp.float32),
            pltpu.SemaphoreType.DMA((4 + rows,)),
        ],
        compiler_params=pltpu.CompilerParams(vmem_limit_bytes=8 << 20),
    )(
        *(
            pltpu.with_memory_space_constraint(array, pltpu.HBM)
            for array in (
                residue_crop_mask,
                alignment_mask.T,
                alignment_state,
                outer_input_weight.transpose(0, 2, 1),
                pairwise_state,
            )
        )
    )
    held, other = gather_all(packed)
    cores, chips = lax.axis_size("sub"), lax.axis_size("dap")
    group = cores * rows
    parts = 1
    return pl.pallas_call(
        update_kernel,
        out_shape=jax.ShapeDtypeStruct(pairwise_state.shape, jnp.bfloat16),
        in_specs=[vector] * 8,
        out_specs=vector,
        scratch_shapes=[
            pltpu.VMEM((parts, (channels // parts + 1) * 2 * channels, 2 * wide), jnp.bfloat16),
            pltpu.VMEM((residues, channels, wide), jnp.float32),
            pltpu.VMEM((2, group * sequences, chips * wide), jnp.bfloat16),
            pltpu.VMEM((residues, wide), jnp.float32),
            pltpu.VMEM((parts, chips * residues, channels // parts * wide // 2), jnp.bfloat16),
            pltpu.VMEM((parts, chips * residues, channels // parts * wide // 2), jnp.bfloat16),
            pltpu.VMEM((residues, residues, wide), jnp.float32),
        ],
        compiler_params=params,
    )(
        held,
        other,
        outer_output_weight,
        triangle_input_weight,
        triangle_gate,
        triangle_output_weight,
        transition_up_weight,
        transition_down_weight,
    )


def shards(
    pairwise_state,
    alignment_state,
    alignment_mask,
    residue_crop_mask,
    outer_input_weight,
    outer_output_weight,
    triangle_input_weight,
    triangle_gate,
    triangle_output_weight,
    transition_up_weight,
    transition_down_weight,
):
    row_count = pairwise_state.shape[0]
    start_row = lax.axis_index(("dap", "sub")) * row_count
    row_presence_mask = lax.dynamic_slice_in_dim(residue_crop_mask, start_row, row_count, 0).astype(
        jnp.float32
    )
    full_mask = residue_crop_mask.astype(jnp.float32)
    alignment_keep = alignment_mask.astype(jnp.float32) * row_presence_mask[None, :]
    alignment_normed = norm_layer(alignment_state.astype(jnp.float32), -1).astype(jnp.bfloat16)
    left_alignment = (
        jnp.einsum(
            "pxm,my->pxy",
            alignment_normed,
            outer_input_weight[0],
            preferred_element_type=jnp.float32,
        )
        * alignment_keep[:, :, None]
    ).astype(jnp.bfloat16)
    right_alignment = (
        jnp.einsum(
            "pxm,my->pxy",
            alignment_normed,
            outer_input_weight[1],
            preferred_element_type=jnp.float32,
        )
        * alignment_keep[:, :, None]
    ).astype(jnp.bfloat16)
    inner_alignment = jnp.einsum(
        "tqu,ulx->tqlx", left_alignment, outer_output_weight, preferred_element_type=jnp.float32
    ).astype(jnp.bfloat16)
    right_portion = lax.all_gather(right_alignment, ("dap", "sub"), axis=1, tiled=True)
    keep_portion = lax.all_gather(
        alignment_keep.astype(jnp.bfloat16), ("dap", "sub"), axis=1, tiled=True
    )
    numerator_sum = jnp.einsum(
        "zkwv,znw->knv", inner_alignment, right_portion, preferred_element_type=jnp.float32
    )
    pair_norm_count = jnp.einsum("cf,cg->fg", alignment_keep, keep_portion.astype(jnp.float32))
    block_part = numerator_sum / jnp.maximum(pair_norm_count, 1.0)[:, :, None]
    pair_one = (pairwise_state.astype(jnp.float32) + block_part).astype(jnp.bfloat16)
    ln_one = norm_layer(pair_one.astype(jnp.float32), -1).astype(jnp.bfloat16)
    pair_keep = row_presence_mask[:, None] * full_mask[None, :]

    def operand(gate_w, proj_w):
        gate_val = jnp.einsum("ijc,cd->dij", ln_one, gate_w, preferred_element_type=jnp.float32)
        proj_val = jnp.einsum("ijc,cd->dij", ln_one, proj_w, preferred_element_type=jnp.float32)
        return (jax.nn.sigmoid(gate_val) * proj_val * pair_keep[None]).astype(jnp.bfloat16)

    left_tri = operand(triangle_input_weight[0], triangle_input_weight[1])
    right_tri = operand(triangle_input_weight[2], triangle_input_weight[3])
    near_right = lax.all_gather(right_tri, "sub", axis=1, tiled=True)
    left_cols, right_all = (
        lax.all_to_all(left_tri, "dap", split_axis=0, concat_axis=1, tiled=True),
        lax.all_to_all(near_right, "dap", split_axis=0, concat_axis=1, tiled=True),
    )
    product = jnp.einsum(
        "cik,cjk->cij", left_cols, right_all, preferred_element_type=jnp.float32
    ).astype(jnp.bfloat16)
    returned = lax.all_to_all(product, "dap", split_axis=1, concat_axis=0, tiled=True)
    normed = norm_layer(returned.astype(jnp.float32), 0).astype(jnp.bfloat16)
    update = jnp.einsum(
        "cij,cd->ijd", normed, triangle_output_weight, preferred_element_type=jnp.float32
    )
    gate_out = jax.nn.sigmoid(
        jnp.einsum("ijc,cd->ijd", ln_one, triangle_gate, preferred_element_type=jnp.float32)
    )
    pair_two = (pair_one.astype(jnp.float32) + gate_out * update).astype(jnp.bfloat16)
    ln_two = norm_layer(pair_two.astype(jnp.float32), -1).astype(jnp.bfloat16)

    def step(row_pair):
        return transition(*row_pair, transition_up_weight, transition_down_weight)

    return lax.map(step, (ln_two, pair_two))


def solution(mesh):
    placed = (
        P(("crop", "dap", "sub"), None, None),
        P("crop", ("dap", "sub"), None),
        P("crop", ("dap", "sub")),
        P("crop"),
        P(),
        P(),
        P(),
        P(),
        P(),
        P(),
        P(),
    )

    small = mesh.shape["sub"] == 2 and mesh.shape["dap"] == 8

    def body(pairwise_state, *rest):
        residues, channels = pairwise_state.shape[1:]
        if small and residues * residues * channels * 2 <= REPLICATED_PAIR_BYTES:
            return shards_replicated(pairwise_state, *rest)
        return shards(pairwise_state, *rest)

    return jax.shard_map(
        body,
        mesh=mesh,
        in_specs=placed,
        out_specs=P(("crop", "dap", "sub"), None, None),
        check_vma=False,
    )
```

```python
import jax
import jax.numpy as jnp
from jax import lax
from jax.experimental import pallas as pl
from jax.experimental.pallas import tpu as pltpu
from jax.sharding import PartitionSpec as P

REPLICATED_PAIR_BYTES = 1 << 20


def norm_layer(values, reduce_axis):
    average = jnp.mean(values, axis=reduce_axis, keepdims=True)
    centered = values - average
    variance = jnp.mean(centered * centered, axis=reduce_axis, keepdims=True)
    return centered * lax.rsqrt(variance + 1e-05)


def transition(ln_two, pair_two, transition_up_weight, transition_down_weight):
    hidden = jax.nn.relu(
        jnp.dot(ln_two, transition_up_weight, preferred_element_type=jnp.float32)
    ).astype(jnp.bfloat16)
    return (
        pair_two.astype(jnp.float32)
        + jnp.dot(hidden, transition_down_weight, preferred_element_type=jnp.float32)
    ).astype(jnp.bfloat16)


def layer_norm(values):
    count = values.shape[-1]
    centered = values - jnp.sum(values, axis=-1, keepdims=True) * (1.0 / count)
    variance = jnp.sum(centered * centered, axis=-1, keepdims=True) * (1.0 / count)
    return centered * lax.rsqrt(variance + 1e-05)


def first_row(rows):
    return (lax.axis_index("dap") * lax.axis_size("sub") + lax.axis_index("sub")) * rows


def pack_kernel(
    mask_hbm,
    keep_hbm,
    state_hbm,
    weight_hbm,
    pair_hbm,
    out_ref,
    mask_ref,
    keep_ref,
    state_ref,
    weight_ref,
    wide_ref,
    sems,
):
    rows, residues, wide = pair_hbm.shape
    sequences = state_ref.shape[0]
    base = rows * residues
    start = first_row(rows)
    second_core = lax.axis_index("sub") == 1
    loads = [
        pltpu.make_async_copy(state_hbm, state_ref, sems.at[0]),
        pltpu.make_async_copy(weight_hbm, weight_ref, sems.at[1]),
        pltpu.make_async_copy(keep_hbm, keep_ref, sems.at[2]),
        pltpu.make_async_copy(mask_hbm, mask_ref, sems.at[3]),
    ] + [
        pltpu.make_async_copy(
            pair_hbm.at[row], out_ref.at[pl.ds(row * residues, residues)], sems.at[4 + row]
        )
        for row in range(rows)
    ]
    for load in loads:
        load.start()
    for load in loads[:4]:
        load.wait()
    f32, bf16 = jnp.float32, jnp.bfloat16
    wide_ref[...] = state_ref[...].astype(f32)
    eye = lax.broadcasted_iota(jnp.int32, (sequences, sequences), 0) == lax.broadcasted_iota(
        jnp.int32, (sequences, sequences), 1
    )
    last = (((1,), (1,)), ((), ()))
    weight = weight_ref[1]
    nothing = jnp.zeros_like(weight)
    here = jnp.where(second_core, nothing, weight), jnp.where(second_core, weight, nothing)
    keeps, fronts, backs = [], [], []
    projected = 0.0
    for row in range(rows):
        present = mask_ref[start + row].astype(f32)
        keep_row = keep_ref[row : row + 1].astype(f32) * present
        keep_column = jnp.sum(
            jnp.where(eye, jnp.broadcast_to(keep_row, eye.shape), 0.0), axis=1, keepdims=True
        )
        normed = (layer_norm(wide_ref[:, row]) * keep_column).astype(bf16)
        fronts.append(jnp.where(second_core, normed, jnp.zeros_like(normed)))
        backs.append(jnp.where(second_core, jnp.zeros_like(normed), normed))
        placed = [here[0] if at == row else here[1] if at == rows + row else nothing for at in range(2 * rows)]
        projected += lax.dot_general(
            normed, jnp.concatenate(placed, axis=0), last, preferred_element_type=f32
        )
        keeps.append(
            jnp.concatenate([keep_row, jnp.full((1, wide - sequences), present, f32)], axis=1)
        )
    projected += lax.dot_general(
        weight_ref[0], jnp.concatenate(fronts + backs, axis=0), last, preferred_element_type=f32
    )
    out_ref[base : base + sequences] = projected.astype(bf16)
    out_ref[base + sequences :] = jnp.concatenate(
        keeps + [jnp.zeros((16 - rows, wide), jnp.float32)], axis=0
    ).astype(jnp.bfloat16)
    for load in loads[4:]:
        load.wait()


def sigmoid(values):
    return 0.5 * jnp.tanh(0.5 * values) + 0.5


def update_kernel(
    held_ref,
    other_ref,
    outer_ref,
    triangle_ref,
    gate_ref,
    output_ref,
    up_ref,
    down_ref,
    out_ref,
    block_ref,
    left_ref,
    right_ref,
    keep_ref,
    first_ref,
    second_ref,
    pair_ref,
    pair_one_ref,
    ln_one_ref,
):
    rows, residues, wide = out_ref.shape
    cores, chips = 2, lax.axis_size("dap")
    channels = outer_ref.shape[0]
    sequences = channels
    base = rows * residues
    half = wide // 2
    group = cores * rows
    start = first_row(rows)
    second_core = lax.axis_index("sub") == 1
    bf16 = jnp.bfloat16
    f32 = jnp.float32

    parts = block_ref.shape[0]
    span = channels // parts
    nothing = jnp.zeros((channels, wide), bf16)
    for part in range(parts):
        for step in range(span + 1):
            weight = outer_ref[part * span + step % span]
            at = step * 2 * channels
            block_ref[part, at : at + channels, :wide] = weight
            block_ref[part, at : at + channels, wide:] = nothing
            block_ref[part, at + channels : at + 2 * channels, :wide] = nothing
            block_ref[part, at + channels : at + 2 * channels, wide:] = weight

    lane = lax.broadcasted_iota(jnp.int32, (channels, wide), 1)
    lane_block = lane // channels
    low = lane < half
    for chip in range(chips):
        place = block_place(chip, chips)
        mine, other = held_ref[place], other_ref[place]
        blocks = [jnp.where(second_core, other, mine), jnp.where(second_core, mine, other)]
        packed = [block[base : base + sequences].astype(f32) for block in blocks]
        right = jnp.where(low, packed[0], packed[1])
        for turn, value in enumerate((right, pltpu.roll(right, half, 1))):
            for copy in range(group):
                right_ref[
                    turn,
                    copy * sequences : (copy + 1) * sequences,
                    chip * wide : (chip + 1) * wide,
                ] = value.astype(bf16)
        for core in range(cores):
            residue = (chip * cores + core) * rows
            for row in range(rows):
                at = (rows if core == 0 else 0) + row
                left_ref[residue + row] = jnp.where(lane_block == at, packed[core], 0.0)
            keep_ref[residue : residue + rows] = blocks[core][base + sequences :].astype(f32)[:rows]
            pair_ref[residue : residue + rows] = (
                blocks[core][:base].astype(f32).reshape(rows, residues, wide)
            )

    last = (((1,), (1,)), ((), ()))
    keep = keep_ref[...]
    mask = jnp.broadcast_to(keep[:, sequences : sequences + 1], (residues, wide))
    counted = lax.broadcasted_iota(jnp.int32, (residues, wide), 1) < sequences
    count = lax.dot_general(
        jnp.where(counted, keep, 0.0).astype(bf16),
        keep.astype(bf16),
        last,
        preferred_element_type=f32,
    )
    inverse = 1.0 / jnp.maximum(count, 1.0)

    low = lax.broadcasted_iota(jnp.int32, (residues, wide), 1) < half
    totals = [0.0, 0.0]
    for part in range(parts):
        outer = []
        for turn in range(2):
            left = jnp.concatenate(
                [left_ref[:, d] for d in range(part * span + turn, (part + 1) * span, 2)], axis=0
            ).astype(bf16)
            outer.append(jnp.dot(left, right_ref[turn], preferred_element_type=f32).astype(bf16))

        def piece(turn, at, chip):
            return outer[turn][
                at * residues : (at + 1) * residues, chip * wide : (chip + 1) * wide
            ]

        for at in range(span // 2):
            follow = (at + 1) % (span // 2)
            for chip in range(chips):
                place = (
                    part,
                    slice(chip * residues, (chip + 1) * residues),
                    slice(at * wide, (at + 1) * wide),
                )
                first_ref[place] = jnp.where(low, piece(0, at, chip), piece(1, at, chip))
                second_ref[place] = jnp.where(low, piece(1, at, chip), piece(0, follow, chip))
        depth = span * 2 * channels
        totals[0] += jnp.dot(first_ref[part], block_ref[part, :depth], preferred_element_type=f32)
        totals[1] += jnp.dot(
            second_ref[part], block_ref[part, 2 * channels :], preferred_element_type=f32
        )

    right_weight = jnp.concatenate([triangle_ref[2], triangle_ref[3]], axis=1)
    right_tri = []
    stride = 8
    for first in range(0, residues, stride):
        normed = []
        for k in range(first, first + stride):
            chip, pick = k // group, k % group
            at = (pick % 2) * wide
            numerator = totals[pick // 2][chip * residues : (chip + 1) * residues, at : at + wide]
            opm = numerator * jnp.broadcast_to(inverse[:, k : k + 1], (residues, wide))
            pair_one = (pair_ref[:, k] + opm).astype(bf16).astype(f32)
            pair_one_ref[k] = pair_one
            ln_one = layer_norm(pair_one)
            ln_one_ref[k] = ln_one
            normed.append(ln_one.astype(bf16))
        both = jnp.dot(
            jnp.concatenate(normed, axis=0), right_weight, preferred_element_type=f32
        )
        right_tri.append((sigmoid(both[:, :wide]) * both[:, wide:]).astype(bf16).astype(f32))

    own_pair = jnp.concatenate([pair_one_ref[:, start + row] for row in range(rows)], axis=0)
    own_ln = jnp.concatenate([ln_one_ref[:, start + row] for row in range(rows)], axis=0).astype(bf16)
    left_weight = jnp.concatenate([triangle_ref[0], triangle_ref[1]], axis=1)
    both = jnp.dot(own_ln, left_weight, preferred_element_type=f32)
    left_tri = sigmoid(both[:, :wide]) * both[:, wide:] * jnp.concatenate([mask] * rows, axis=0)
    left_tri = left_tri.astype(bf16).astype(f32)
    products = []
    for row in range(rows):
        sums = [jnp.zeros((residues, wide), f32) for _ in range(4)]
        for k in range(residues):
            at = row * residues + k
            place = (k % stride) * residues
            sums[k % 4] += left_tri[at : at + 1] * right_tri[k // stride][place : place + residues]
        total = (sums[0] + sums[1]) + (sums[2] + sums[3])
        own_mask = keep_ref[pl.ds(start + row, 1), :][:, sequences : sequences + 1]
        products.append(total * (mask * own_mask))
    product = jnp.concatenate(products, axis=0).astype(bf16).astype(f32)
    normed = layer_norm(product).astype(bf16)
    update = jnp.dot(normed, output_ref[...], preferred_element_type=f32)
    gate_out = sigmoid(jnp.dot(own_ln, gate_ref[...], preferred_element_type=f32))
    pair_two = (own_pair + gate_out * update).astype(bf16).astype(f32)
    ln_two = layer_norm(pair_two).astype(bf16)
    hidden = jnp.maximum(jnp.dot(ln_two, up_ref[...], preferred_element_type=f32), 0.0).astype(bf16)
    result = pair_two + jnp.dot(hidden, down_ref[...], preferred_element_type=f32)
    out_ref[...] = result.astype(bf16).reshape(rows, residues, wide)


def gather_all(packed):
    dap_count = lax.axis_size("dap")
    half = dap_count // 2
    far = lax.ppermute(packed[None], "dap", [(src, src ^ half) for src in range(dap_count)])
    both = jnp.concatenate([packed[None], far], axis=0)
    held = [both] + [
        lax.ppermute(both, "dap", [(src, src ^ offset) for src in range(dap_count)])
        for offset in swap_order(dap_count)
    ]
    sibling = [(0, 1), (1, 0)]
    early = lax.ppermute(jnp.concatenate(held[:-1], axis=0), "sub", sibling)
    late = lax.ppermute(held[-1], "sub", sibling)
    return jnp.concatenate(held, axis=0), jnp.concatenate([early, late], axis=0)


def swap_order(dap_count):
    near = dap_count // 2
    return [1, near - 1] + list(range(2, near - 1))


def block_place(chip, chips):
    offset = lax.bitwise_xor(lax.axis_index("dap"), chip)
    half = chips // 2
    near = jnp.where(offset >= half, offset - half, offset)
    turn = jnp.where(near > 1, jnp.where(near == half - 1, 2, near + 1), near)
    return 2 * turn + jnp.where(offset >= half, 1, 0)


def shards_replicated(
    pairwise_state,
    alignment_state,
    alignment_mask,
    residue_crop_mask,
    outer_input_weight,
    outer_output_weight,
    triangle_input_weight,
    triangle_gate,
    triangle_output_weight,
    transition_up_weight,
    transition_down_weight,
):
    rows, residues, wide = pairwise_state.shape
    sequences = alignment_state.shape[0]
    channels = outer_input_weight.shape[2]
    vector = pl.BlockSpec(memory_space=pltpu.VMEM)
    params = pltpu.CompilerParams(vmem_limit_bytes=40 << 20)
    hbm = pl.BlockSpec(memory_space=pltpu.HBM)
    packed = pl.pallas_call(
        pack_kernel,
        out_shape=jax.ShapeDtypeStruct((rows * residues + sequences + 16, wide), jnp.bfloat16),
        in_specs=[hbm] * 5,
        out_specs=vector,
        scratch_shapes=[
            pltpu.SMEM((residues,), jnp.int32),
            pltpu.VMEM((rows, sequences), jnp.int32),
            pltpu.VMEM(alignment_state.shape, jnp.bfloat16),
            pltpu.VMEM((2, channels, alignment_state.shape[2]), jnp.bfloat16),
            pltpu.VMEM(alignment_state.shape, jnp.float32),
            pltpu.SemaphoreType.DMA((4 + rows,)),
        ],
        compiler_params=pltpu.CompilerParams(vmem_limit_bytes=8 << 20),
    )(
        *(
            pltpu.with_memory_space_constraint(array, pltpu.HBM)
            for array in (
                residue_crop_mask,
                alignment_mask.T,
                alignment_state,
                outer_input_weight.transpose(0, 2, 1),
                pairwise_state,
            )
        )
    )
    held, other = gather_all(packed)
    cores, chips = lax.axis_size("sub"), lax.axis_size("dap")
    group = cores * rows
    parts = 1
    return pl.pallas_call(
        update_kernel,
        out_shape=jax.ShapeDtypeStruct(pairwise_state.shape, jnp.bfloat16),
        in_specs=[vector] * 8,
        out_specs=vector,
        scratch_shapes=[
            pltpu.VMEM((parts, (channels // parts + 1) * 2 * channels, 2 * wide), jnp.bfloat16),
            pltpu.VMEM((residues, channels, wide), jnp.float32),
            pltpu.VMEM((2, group * sequences, chips * wide), jnp.bfloat16),
            pltpu.VMEM((residues, wide), jnp.float32),
            pltpu.VMEM((parts, chips * residues, channels // parts * wide // 2), jnp.bfloat16),
            pltpu.VMEM((parts, chips * residues, channels // parts * wide // 2), jnp.bfloat16),
            pltpu.VMEM((residues, residues, wide), jnp.float32),
            pltpu.VMEM((residues, residues, wide), jnp.float32),
            pltpu.VMEM((residues, residues, wide), jnp.float32),
        ],
        compiler_params=params,
    )(
        held,
        other,
        outer_output_weight,
        triangle_input_weight,
        triangle_gate,
        triangle_output_weight,
        transition_up_weight,
        transition_down_weight,
    )


def shards(
    pairwise_state,
    alignment_state,
    alignment_mask,
    residue_crop_mask,
    outer_input_weight,
    outer_output_weight,
    triangle_input_weight,
    triangle_gate,
    triangle_output_weight,
    transition_up_weight,
    transition_down_weight,
):
    row_count = pairwise_state.shape[0]
    start_row = lax.axis_index(("dap", "sub")) * row_count
    row_presence_mask = lax.dynamic_slice_in_dim(residue_crop_mask, start_row, row_count, 0).astype(
        jnp.float32
    )
    full_mask = residue_crop_mask.astype(jnp.float32)
    alignment_keep = alignment_mask.astype(jnp.float32) * row_presence_mask[None, :]
    alignment_normed = norm_layer(alignment_state.astype(jnp.float32), -1).astype(jnp.bfloat16)
    left_alignment = (
        jnp.einsum(
            "pxm,my->pxy",
            alignment_normed,
            outer_input_weight[0],
            preferred_element_type=jnp.float32,
        )
        * alignment_keep[:, :, None]
    ).astype(jnp.bfloat16)
    right_alignment = (
        jnp.einsum(
            "pxm,my->pxy",
            alignment_normed,
            outer_input_weight[1],
            preferred_element_type=jnp.float32,
        )
        * alignment_keep[:, :, None]
    ).astype(jnp.bfloat16)
    inner_alignment = jnp.einsum(
        "tqu,ulx->tqlx", left_alignment, outer_output_weight, preferred_element_type=jnp.float32
    ).astype(jnp.bfloat16)
    right_portion = lax.all_gather(right_alignment, ("dap", "sub"), axis=1, tiled=True)
    keep_portion = lax.all_gather(
        alignment_keep.astype(jnp.bfloat16), ("dap", "sub"), axis=1, tiled=True
    )
    numerator_sum = jnp.einsum(
        "zkwv,znw->knv", inner_alignment, right_portion, preferred_element_type=jnp.float32
    )
    pair_norm_count = jnp.einsum("cf,cg->fg", alignment_keep, keep_portion.astype(jnp.float32))
    block_part = numerator_sum / jnp.maximum(pair_norm_count, 1.0)[:, :, None]
    pair_one = (pairwise_state.astype(jnp.float32) + block_part).astype(jnp.bfloat16)
    ln_one = norm_layer(pair_one.astype(jnp.float32), -1).astype(jnp.bfloat16)
    pair_keep = row_presence_mask[:, None] * full_mask[None, :]

    def operand(gate_w, proj_w):
        gate_val = jnp.einsum("ijc,cd->dij", ln_one, gate_w, preferred_element_type=jnp.float32)
        proj_val = jnp.einsum("ijc,cd->dij", ln_one, proj_w, preferred_element_type=jnp.float32)
        return (jax.nn.sigmoid(gate_val) * proj_val * pair_keep[None]).astype(jnp.bfloat16)

    left_tri = operand(triangle_input_weight[0], triangle_input_weight[1])
    right_tri = operand(triangle_input_weight[2], triangle_input_weight[3])
    near_right = lax.all_gather(right_tri, "sub", axis=1, tiled=True)
    left_cols, right_all = (
        lax.all_to_all(left_tri, "dap", split_axis=0, concat_axis=1, tiled=True),
        lax.all_to_all(near_right, "dap", split_axis=0, concat_axis=1, tiled=True),
    )
    product = jnp.einsum(
        "cik,cjk->cij", left_cols, right_all, preferred_element_type=jnp.float32
    ).astype(jnp.bfloat16)
    returned = lax.all_to_all(product, "dap", split_axis=1, concat_axis=0, tiled=True)
    normed = norm_layer(returned.astype(jnp.float32), 0).astype(jnp.bfloat16)
    update = jnp.einsum(
        "cij,cd->ijd", normed, triangle_output_weight, preferred_element_type=jnp.float32
    )
    gate_out = jax.nn.sigmoid(
        jnp.einsum("ijc,cd->ijd", ln_one, triangle_gate, preferred_element_type=jnp.float32)
    )
    pair_two = (pair_one.astype(jnp.float32) + gate_out * update).astype(jnp.bfloat16)
    ln_two = norm_layer(pair_two.astype(jnp.float32), -1).astype(jnp.bfloat16)

    def step(row_pair):
        return transition(*row_pair, transition_up_weight, transition_down_weight)

    return lax.map(step, (ln_two, pair_two))


def solution(mesh):
    placed = (
        P(("crop", "dap", "sub"), None, None),
        P("crop", ("dap", "sub"), None),
        P("crop", ("dap", "sub")),
        P("crop"),
        P(),
        P(),
        P(),
        P(),
        P(),
        P(),
        P(),
    )

    small = mesh.shape["sub"] == 2 and mesh.shape["dap"] == 8

    def body(pairwise_state, *rest):
        residues, channels = pairwise_state.shape[1:]
        if small and residues * residues * channels * 2 <= REPLICATED_PAIR_BYTES:
            return shards_replicated(pairwise_state, *rest)
        return shards(pairwise_state, *rest)

    return jax.shard_map(
        body,
        mesh=mesh,
        in_specs=placed,
        out_specs=P(("crop", "dap", "sub"), None, None),
        check_vma=False,
    )
```

```python
import jax
import jax.numpy as jnp
from jax import lax
from jax.experimental import pallas as pl
from jax.experimental.pallas import tpu as pltpu
from jax.sharding import PartitionSpec as P

REPLICATED_PAIR_BYTES = 1 << 20


def norm_layer(values, reduce_axis):
    average = jnp.mean(values, axis=reduce_axis, keepdims=True)
    centered = values - average
    variance = jnp.mean(centered * centered, axis=reduce_axis, keepdims=True)
    return centered * lax.rsqrt(variance + 1e-05)


def transition(ln_two, pair_two, transition_up_weight, transition_down_weight):
    hidden = jax.nn.relu(
        jnp.dot(ln_two, transition_up_weight, preferred_element_type=jnp.float32)
    ).astype(jnp.bfloat16)
    return (
        pair_two.astype(jnp.float32)
        + jnp.dot(hidden, transition_down_weight, preferred_element_type=jnp.float32)
    ).astype(jnp.bfloat16)


def layer_norm(values):
    count = values.shape[-1]
    centered = values - jnp.sum(values, axis=-1, keepdims=True) * (1.0 / count)
    variance = jnp.sum(centered * centered, axis=-1, keepdims=True) * (1.0 / count)
    return centered * lax.rsqrt(variance + 1e-05)


def first_row(rows):
    return (lax.axis_index("dap") * lax.axis_size("sub") + lax.axis_index("sub")) * rows


def pack_kernel(
    mask_hbm,
    keep_hbm,
    state_hbm,
    weight_hbm,
    pair_hbm,
    out_ref,
    mask_ref,
    keep_ref,
    state_ref,
    weight_ref,
    wide_ref,
    sems,
):
    rows, residues, wide = pair_hbm.shape
    sequences = state_ref.shape[0]
    base = rows * residues
    start = first_row(rows)
    second_core = lax.axis_index("sub") == 1
    loads = [
        pltpu.make_async_copy(state_hbm, state_ref, sems.at[0]),
        pltpu.make_async_copy(weight_hbm, weight_ref, sems.at[1]),
        pltpu.make_async_copy(keep_hbm, keep_ref, sems.at[2]),
        pltpu.make_async_copy(mask_hbm, mask_ref, sems.at[3]),
    ] + [
        pltpu.make_async_copy(
            pair_hbm.at[row], out_ref.at[pl.ds(row * residues, residues)], sems.at[4 + row]
        )
        for row in range(rows)
    ]
    for load in loads:
        load.start()
    for load in loads[:4]:
        load.wait()
    f32, bf16 = jnp.float32, jnp.bfloat16
    wide_ref[...] = state_ref[...].astype(f32)
    eye = lax.broadcasted_iota(jnp.int32, (sequences, sequences), 0) == lax.broadcasted_iota(
        jnp.int32, (sequences, sequences), 1
    )
    last = (((1,), (1,)), ((), ()))
    weight = weight_ref[1]
    nothing = jnp.zeros_like(weight)
    here = jnp.where(second_core, nothing, weight), jnp.where(second_core, weight, nothing)
    keeps, fronts, backs = [], [], []
    projected = 0.0
    for row in range(rows):
        present = mask_ref[start + row].astype(f32)
        keep_row = keep_ref[row : row + 1].astype(f32) * present
        keep_column = jnp.sum(
            jnp.where(eye, jnp.broadcast_to(keep_row, eye.shape), 0.0), axis=1, keepdims=True
        )
        normed = (layer_norm(wide_ref[:, row]) * keep_column).astype(bf16)
        fronts.append(jnp.where(second_core, normed, jnp.zeros_like(normed)))
        backs.append(jnp.where(second_core, jnp.zeros_like(normed), normed))
        placed = [here[0] if at == row else here[1] if at == rows + row else nothing for at in range(2 * rows)]
        projected += lax.dot_general(
            normed, jnp.concatenate(placed, axis=0), last, preferred_element_type=f32
        )
        keeps.append(
            jnp.concatenate([keep_row, jnp.full((1, wide - sequences), present, f32)], axis=1)
        )
    projected += lax.dot_general(
        weight_ref[0], jnp.concatenate(fronts + backs, axis=0), last, preferred_element_type=f32
    )
    out_ref[base : base + sequences] = projected.astype(bf16)
    out_ref[base + sequences :] = jnp.concatenate(
        keeps + [jnp.zeros((16 - rows, wide), jnp.float32)], axis=0
    ).astype(jnp.bfloat16)
    for load in loads[4:]:
        load.wait()


def sigmoid(values):
    return 0.5 * jnp.tanh(0.5 * values) + 0.5


def update_kernel(
    held_ref,
    other_ref,
    outer_ref,
    triangle_ref,
    gate_ref,
    output_ref,
    up_ref,
    down_ref,
    out_ref,
    block_ref,
    left_ref,
    right_ref,
    keep_ref,
    first_ref,
    second_ref,
    pair_ref,
    pair_one_ref,
    ln_one_ref,
):
    rows, residues, wide = out_ref.shape
    cores, chips = 2, lax.axis_size("dap")
    channels = outer_ref.shape[0]
    sequences = channels
    base = rows * residues
    half = wide // 2
    group = cores * rows
    start = first_row(rows)
    second_core = lax.axis_index("sub") == 1
    bf16 = jnp.bfloat16
    f32 = jnp.float32

    parts = block_ref.shape[0]
    span = channels // parts
    nothing = jnp.zeros((channels, wide), bf16)
    for part in range(parts):
        for step in range(span + 1):
            weight = outer_ref[part * span + step % span]
            at = step * 2 * channels
            block_ref[part, at : at + channels, :wide] = weight
            block_ref[part, at : at + channels, wide:] = nothing
            block_ref[part, at + channels : at + 2 * channels, :wide] = nothing
            block_ref[part, at + channels : at + 2 * channels, wide:] = weight

    lane = lax.broadcasted_iota(jnp.int32, (channels, wide), 1)
    lane_block = lane // channels
    low = lane < half
    for chip in range(chips):
        places = [block_place(chip, chips, core) for core in range(cores)]
        blocks = [
            jnp.where(second_core, other_ref[places[0]], held_ref[places[0]]),
            jnp.where(second_core, held_ref[places[1]], other_ref[places[1]]),
        ]
        packed = [block[base : base + sequences].astype(f32) for block in blocks]
        right = jnp.where(low, packed[0], packed[1])
        for turn, value in enumerate((right, pltpu.roll(right, half, 1))):
            for copy in range(group):
                right_ref[
                    turn,
                    copy * sequences : (copy + 1) * sequences,
                    chip * wide : (chip + 1) * wide,
                ] = value.astype(bf16)
        for core in range(cores):
            residue = (chip * cores + core) * rows
            for row in range(rows):
                at = (rows if core == 0 else 0) + row
                left_ref[residue + row] = jnp.where(lane_block == at, packed[core], 0.0)
            keep_ref[residue : residue + rows] = blocks[core][base + sequences :].astype(f32)[:rows]
            pair_ref[residue : residue + rows] = (
                blocks[core][:base].astype(f32).reshape(rows, residues, wide)
            )

    last = (((1,), (1,)), ((), ()))
    keep = keep_ref[...]
    mask = jnp.broadcast_to(keep[:, sequences : sequences + 1], (residues, wide))
    counted = lax.broadcasted_iota(jnp.int32, (residues, wide), 1) < sequences
    count = lax.dot_general(
        jnp.where(counted, keep, 0.0).astype(bf16),
        keep.astype(bf16),
        last,
        preferred_element_type=f32,
    )
    inverse = 1.0 / jnp.maximum(count, 1.0)

    low = lax.broadcasted_iota(jnp.int32, (residues, wide), 1) < half
    totals = [0.0, 0.0]
    for part in range(parts):
        outer = []
        for turn in range(2):
            left = jnp.concatenate(
                [left_ref[:, d] for d in range(part * span + turn, (part + 1) * span, 2)], axis=0
            ).astype(bf16)
            outer.append(jnp.dot(left, right_ref[turn], preferred_element_type=f32).astype(bf16))

        def piece(turn, at, chip):
            return outer[turn][
                at * residues : (at + 1) * residues, chip * wide : (chip + 1) * wide
            ]

        for at in range(span // 2):
            follow = (at + 1) % (span // 2)
            for chip in range(chips):
                place = (
                    part,
                    slice(chip * residues, (chip + 1) * residues),
                    slice(at * wide, (at + 1) * wide),
                )
                first_ref[place] = jnp.where(low, piece(0, at, chip), piece(1, at, chip))
                second_ref[place] = jnp.where(low, piece(1, at, chip), piece(0, follow, chip))
        depth = span * 2 * channels
        totals[0] += jnp.dot(first_ref[part], block_ref[part, :depth], preferred_element_type=f32)
        totals[1] += jnp.dot(
            second_ref[part], block_ref[part, 2 * channels :], preferred_element_type=f32
        )

    right_weight = jnp.concatenate([triangle_ref[2], triangle_ref[3]], axis=1)
    right_tri = []
    stride = 8
    for first in range(0, residues, stride):
        normed = []
        for k in range(first, first + stride):
            chip, pick = k // group, k % group
            at = (pick % 2) * wide
            numerator = totals[pick // 2][chip * residues : (chip + 1) * residues, at : at + wide]
            opm = numerator * jnp.broadcast_to(inverse[:, k : k + 1], (residues, wide))
            pair_one = (pair_ref[:, k] + opm).astype(bf16).astype(f32)
            pair_one_ref[k] = pair_one
            ln_one = layer_norm(pair_one)
            ln_one_ref[k] = ln_one
            normed.append(ln_one.astype(bf16))
        both = jnp.dot(
            jnp.concatenate(normed, axis=0), right_weight, preferred_element_type=f32
        )
        right_tri.append((sigmoid(both[:, :wide]) * both[:, wide:]).astype(bf16).astype(f32))

    own_pair = jnp.concatenate([pair_one_ref[:, start + row] for row in range(rows)], axis=0)
    own_ln = jnp.concatenate([ln_one_ref[:, start + row] for row in range(rows)], axis=0).astype(bf16)
    left_weight = jnp.concatenate([triangle_ref[0], triangle_ref[1]], axis=1)
    both = jnp.dot(own_ln, left_weight, preferred_element_type=f32)
    left_tri = sigmoid(both[:, :wide]) * both[:, wide:] * jnp.concatenate([mask] * rows, axis=0)
    left_tri = left_tri.astype(bf16).astype(f32)
    products = []
    for row in range(rows):
        sums = [jnp.zeros((residues, wide), f32) for _ in range(4)]
        for k in range(residues):
            at = row * residues + k
            place = (k % stride) * residues
            sums[k % 4] += left_tri[at : at + 1] * right_tri[k // stride][place : place + residues]
        total = (sums[0] + sums[1]) + (sums[2] + sums[3])
        own_mask = keep_ref[pl.ds(start + row, 1), :][:, sequences : sequences + 1]
        products.append(total * (mask * own_mask))
    product = jnp.concatenate(products, axis=0).astype(bf16).astype(f32)
    normed = layer_norm(product).astype(bf16)
    update = jnp.dot(normed, output_ref[...], preferred_element_type=f32)
    gate_out = sigmoid(jnp.dot(own_ln, gate_ref[...], preferred_element_type=f32))
    pair_two = (own_pair + gate_out * update).astype(bf16).astype(f32)
    ln_two = layer_norm(pair_two).astype(bf16)
    hidden = jnp.maximum(jnp.dot(ln_two, up_ref[...], preferred_element_type=f32), 0.0).astype(bf16)
    result = pair_two + jnp.dot(hidden, down_ref[...], preferred_element_type=f32)
    out_ref[...] = result.astype(bf16).reshape(rows, residues, wide)


def gather_all(packed):
    dap_count = lax.axis_size("dap")
    half = dap_count // 2
    far = lax.ppermute(packed[None], "dap", [(src, src ^ half) for src in range(dap_count)])
    both = jnp.concatenate([packed[None], far], axis=0)
    orders = [swap_order(dap_count, core) for core in range(2)]
    held = [both]
    for turn in range(half - 1):
        pairs = [
            (2 * chip + core, 2 * (chip ^ orders[core][turn]) + core)
            for core in range(2)
            for chip in range(dap_count)
        ]
        held.append(lax.ppermute(both, ("dap", "sub"), pairs))
    sibling = [(0, 1), (1, 0)]
    early = lax.ppermute(jnp.concatenate(held[:-1], axis=0), "sub", sibling)
    late = lax.ppermute(held[-1], "sub", sibling)
    return jnp.concatenate(held, axis=0), jnp.concatenate([early, late], axis=0)


def swap_order(dap_count, core):
    near = dap_count // 2
    order = [1, near - 1] + list(range(2, near - 1))
    return order if core == 0 else order[::-1]


def block_place(chip, chips, core):
    offset = lax.bitwise_xor(lax.axis_index("dap"), chip)
    half = chips // 2
    near = jnp.where(offset >= half, offset - half, offset)
    turn = 0
    for place, one in enumerate(swap_order(chips, core)):
        turn = turn + jnp.where(near == one, place + 1, 0)
    return 2 * turn + jnp.where(offset >= half, 1, 0)


def shards_replicated(
    pairwise_state,
    alignment_state,
    alignment_mask,
    residue_crop_mask,
    outer_input_weight,
    outer_output_weight,
    triangle_input_weight,
    triangle_gate,
    triangle_output_weight,
    transition_up_weight,
    transition_down_weight,
):
    rows, residues, wide = pairwise_state.shape
    sequences = alignment_state.shape[0]
    channels = outer_input_weight.shape[2]
    vector = pl.BlockSpec(memory_space=pltpu.VMEM)
    params = pltpu.CompilerParams(vmem_limit_bytes=40 << 20)
    hbm = pl.BlockSpec(memory_space=pltpu.HBM)
    packed = pl.pallas_call(
        pack_kernel,
        out_shape=jax.ShapeDtypeStruct((rows * residues + sequences + 16, wide), jnp.bfloat16),
        in_specs=[hbm] * 5,
        out_specs=vector,
        scratch_shapes=[
            pltpu.SMEM((residues,), jnp.int32),
            pltpu.VMEM((rows, sequences), jnp.int32),
            pltpu.VMEM(alignment_state.shape, jnp.bfloat16),
            pltpu.VMEM((2, channels, alignment_state.shape[2]), jnp.bfloat16),
            pltpu.VMEM(alignment_state.shape, jnp.float32),
            pltpu.SemaphoreType.DMA((4 + rows,)),
        ],
        compiler_params=pltpu.CompilerParams(vmem_limit_bytes=8 << 20),
    )(
        *(
            pltpu.with_memory_space_constraint(array, pltpu.HBM)
            for array in (
                residue_crop_mask,
                alignment_mask.T,
                alignment_state,
                outer_input_weight.transpose(0, 2, 1),
                pairwise_state,
            )
        )
    )
    held, other = gather_all(packed)
    cores, chips = lax.axis_size("sub"), lax.axis_size("dap")
    group = cores * rows
    parts = 1
    return pl.pallas_call(
        update_kernel,
        out_shape=jax.ShapeDtypeStruct(pairwise_state.shape, jnp.bfloat16),
        in_specs=[vector] * 8,
        out_specs=vector,
        scratch_shapes=[
            pltpu.VMEM((parts, (channels // parts + 1) * 2 * channels, 2 * wide), jnp.bfloat16),
            pltpu.VMEM((residues, channels, wide), jnp.float32),
            pltpu.VMEM((2, group * sequences, chips * wide), jnp.bfloat16),
            pltpu.VMEM((residues, wide), jnp.float32),
            pltpu.VMEM((parts, chips * residues, channels // parts * wide // 2), jnp.bfloat16),
            pltpu.VMEM((parts, chips * residues, channels // parts * wide // 2), jnp.bfloat16),
            pltpu.VMEM((residues, residues, wide), jnp.float32),
            pltpu.VMEM((residues, residues, wide), jnp.float32),
            pltpu.VMEM((residues, residues, wide), jnp.float32),
        ],
        compiler_params=params,
    )(
        held,
        other,
        outer_output_weight,
        triangle_input_weight,
        triangle_gate,
        triangle_output_weight,
        transition_up_weight,
        transition_down_weight,
    )


def shards(
    pairwise_state,
    alignment_state,
    alignment_mask,
    residue_crop_mask,
    outer_input_weight,
    outer_output_weight,
    triangle_input_weight,
    triangle_gate,
    triangle_output_weight,
    transition_up_weight,
    transition_down_weight,
):
    row_count = pairwise_state.shape[0]
    start_row = lax.axis_index(("dap", "sub")) * row_count
    row_presence_mask = lax.dynamic_slice_in_dim(residue_crop_mask, start_row, row_count, 0).astype(
        jnp.float32
    )
    full_mask = residue_crop_mask.astype(jnp.float32)
    alignment_keep = alignment_mask.astype(jnp.float32) * row_presence_mask[None, :]
    alignment_normed = norm_layer(alignment_state.astype(jnp.float32), -1).astype(jnp.bfloat16)
    left_alignment = (
        jnp.einsum(
            "pxm,my->pxy",
            alignment_normed,
            outer_input_weight[0],
            preferred_element_type=jnp.float32,
        )
        * alignment_keep[:, :, None]
    ).astype(jnp.bfloat16)
    right_alignment = (
        jnp.einsum(
            "pxm,my->pxy",
            alignment_normed,
            outer_input_weight[1],
            preferred_element_type=jnp.float32,
        )
        * alignment_keep[:, :, None]
    ).astype(jnp.bfloat16)
    inner_alignment = jnp.einsum(
        "tqu,ulx->tqlx", left_alignment, outer_output_weight, preferred_element_type=jnp.float32
    ).astype(jnp.bfloat16)
    right_portion = lax.all_gather(right_alignment, ("dap", "sub"), axis=1, tiled=True)
    keep_portion = lax.all_gather(
        alignment_keep.astype(jnp.bfloat16), ("dap", "sub"), axis=1, tiled=True
    )
    numerator_sum = jnp.einsum(
        "zkwv,znw->knv", inner_alignment, right_portion, preferred_element_type=jnp.float32
    )
    pair_norm_count = jnp.einsum("cf,cg->fg", alignment_keep, keep_portion.astype(jnp.float32))
    block_part = numerator_sum / jnp.maximum(pair_norm_count, 1.0)[:, :, None]
    pair_one = (pairwise_state.astype(jnp.float32) + block_part).astype(jnp.bfloat16)
    ln_one = norm_layer(pair_one.astype(jnp.float32), -1).astype(jnp.bfloat16)
    pair_keep = row_presence_mask[:, None] * full_mask[None, :]

    def operand(gate_w, proj_w):
        gate_val = jnp.einsum("ijc,cd->dij", ln_one, gate_w, preferred_element_type=jnp.float32)
        proj_val = jnp.einsum("ijc,cd->dij", ln_one, proj_w, preferred_element_type=jnp.float32)
        return (jax.nn.sigmoid(gate_val) * proj_val * pair_keep[None]).astype(jnp.bfloat16)

    left_tri = operand(triangle_input_weight[0], triangle_input_weight[1])
    right_tri = operand(triangle_input_weight[2], triangle_input_weight[3])
    near_right = lax.all_gather(right_tri, "sub", axis=1, tiled=True)
    left_cols, right_all = (
        lax.all_to_all(left_tri, "dap", split_axis=0, concat_axis=1, tiled=True),
        lax.all_to_all(near_right, "dap", split_axis=0, concat_axis=1, tiled=True),
    )
    product = jnp.einsum(
        "cik,cjk->cij", left_cols, right_all, preferred_element_type=jnp.float32
    ).astype(jnp.bfloat16)
    returned = lax.all_to_all(product, "dap", split_axis=1, concat_axis=0, tiled=True)
    normed = norm_layer(returned.astype(jnp.float32), 0).astype(jnp.bfloat16)
    update = jnp.einsum(
        "cij,cd->ijd", normed, triangle_output_weight, preferred_element_type=jnp.float32
    )
    gate_out = jax.nn.sigmoid(
        jnp.einsum("ijc,cd->ijd", ln_one, triangle_gate, preferred_element_type=jnp.float32)
    )
    pair_two = (pair_one.astype(jnp.float32) + gate_out * update).astype(jnp.bfloat16)
    ln_two = norm_layer(pair_two.astype(jnp.float32), -1).astype(jnp.bfloat16)

    def step(row_pair):
        return transition(*row_pair, transition_up_weight, transition_down_weight)

    return lax.map(step, (ln_two, pair_two))


def solution(mesh):
    placed = (
        P(("crop", "dap", "sub"), None, None),
        P("crop", ("dap", "sub"), None),
        P("crop", ("dap", "sub")),
        P("crop"),
        P(),
        P(),
        P(),
        P(),
        P(),
        P(),
        P(),
    )

    small = mesh.shape["sub"] == 2 and mesh.shape["dap"] == 8

    def body(pairwise_state, *rest):
        residues, channels = pairwise_state.shape[1:]
        if small and residues * residues * channels * 2 <= REPLICATED_PAIR_BYTES:
            return shards_replicated(pairwise_state, *rest)
        return shards(pairwise_state, *rest)

    return jax.shard_map(
        body,
        mesh=mesh,
        in_specs=placed,
        out_specs=P(("crop", "dap", "sub"), None, None),
        check_vma=False,
    )
```

```python
import jax
import jax.numpy as jnp
from jax import lax
from jax.experimental import pallas as pl
from jax.experimental.pallas import tpu as pltpu
from jax.sharding import PartitionSpec as P

REPLICATED_PAIR_BYTES = 1 << 20


def norm_layer(values, reduce_axis):
    average = jnp.mean(values, axis=reduce_axis, keepdims=True)
    centered = values - average
    variance = jnp.mean(centered * centered, axis=reduce_axis, keepdims=True)
    return centered * lax.rsqrt(variance + 1e-05)


def transition(ln_two, pair_two, transition_up_weight, transition_down_weight):
    hidden = jax.nn.relu(
        jnp.dot(ln_two, transition_up_weight, preferred_element_type=jnp.float32)
    ).astype(jnp.bfloat16)
    return (
        pair_two.astype(jnp.float32)
        + jnp.dot(hidden, transition_down_weight, preferred_element_type=jnp.float32)
    ).astype(jnp.bfloat16)


def layer_norm(values):
    count = values.shape[-1]
    centered = values - jnp.sum(values, axis=-1, keepdims=True) * (1.0 / count)
    variance = jnp.sum(centered * centered, axis=-1, keepdims=True) * (1.0 / count)
    return centered * lax.rsqrt(variance + 1e-05)


def first_row(rows):
    return (lax.axis_index("dap") * lax.axis_size("sub") + lax.axis_index("sub")) * rows


def pack_kernel(
    mask_hbm,
    keep_hbm,
    state_hbm,
    weight_hbm,
    pair_hbm,
    out_ref,
    mask_ref,
    keep_ref,
    state_ref,
    weight_ref,
    wide_ref,
    sems,
):
    rows, residues, wide = pair_hbm.shape
    sequences = state_ref.shape[0]
    base = rows * residues
    start = first_row(rows)
    second_core = lax.axis_index("sub") == 1
    loads = [
        pltpu.make_async_copy(state_hbm, state_ref, sems.at[0]),
        pltpu.make_async_copy(weight_hbm, weight_ref, sems.at[1]),
        pltpu.make_async_copy(keep_hbm, keep_ref, sems.at[2]),
        pltpu.make_async_copy(mask_hbm, mask_ref, sems.at[3]),
    ] + [
        pltpu.make_async_copy(
            pair_hbm.at[row], out_ref.at[pl.ds(row * residues, residues)], sems.at[4 + row]
        )
        for row in range(rows)
    ]
    for load in loads:
        load.start()
    for load in loads[:4]:
        load.wait()
    f32, bf16 = jnp.float32, jnp.bfloat16
    wide_ref[...] = state_ref[...].astype(f32)
    eye = lax.broadcasted_iota(jnp.int32, (sequences, sequences), 0) == lax.broadcasted_iota(
        jnp.int32, (sequences, sequences), 1
    )
    last = (((1,), (1,)), ((), ()))
    weight = weight_ref[1]
    nothing = jnp.zeros_like(weight)
    here = jnp.where(second_core, nothing, weight), jnp.where(second_core, weight, nothing)
    keeps, fronts, backs = [], [], []
    projected = 0.0
    for row in range(rows):
        present = mask_ref[start + row].astype(f32)
        keep_row = keep_ref[row : row + 1].astype(f32) * present
        keep_column = jnp.sum(
            jnp.where(eye, jnp.broadcast_to(keep_row, eye.shape), 0.0), axis=1, keepdims=True
        )
        normed = (layer_norm(wide_ref[:, row]) * keep_column).astype(bf16)
        fronts.append(jnp.where(second_core, normed, jnp.zeros_like(normed)))
        backs.append(jnp.where(second_core, jnp.zeros_like(normed), normed))
        placed = [here[0] if at == row else here[1] if at == rows + row else nothing for at in range(2 * rows)]
        projected += lax.dot_general(
            normed, jnp.concatenate(placed, axis=0), last, preferred_element_type=f32
        )
        keeps.append(
            jnp.concatenate([keep_row, jnp.full((1, wide - sequences), present, f32)], axis=1)
        )
    projected += lax.dot_general(
        weight_ref[0], jnp.concatenate(fronts + backs, axis=0), last, preferred_element_type=f32
    )
    out_ref[base : base + sequences] = projected.astype(bf16)
    out_ref[base + sequences :] = jnp.concatenate(
        keeps + [jnp.zeros((16 - rows, wide), jnp.float32)], axis=0
    ).astype(jnp.bfloat16)
    for load in loads[4:]:
        load.wait()


def sigmoid(values):
    return 0.5 * jnp.tanh(0.5 * values) + 0.5


def update_kernel(
    held_ref,
    other_ref,
    outer_ref,
    triangle_ref,
    gate_ref,
    output_ref,
    up_ref,
    down_ref,
    out_ref,
    block_ref,
    left_ref,
    right_ref,
    keep_ref,
    first_ref,
    second_ref,
    pair_ref,
    pair_one_ref,
    ln_one_ref,
):
    rows, residues, wide = out_ref.shape
    cores, chips = 2, lax.axis_size("dap")
    channels = outer_ref.shape[0]
    sequences = channels
    base = rows * residues
    half = wide // 2
    group = cores * rows
    start = first_row(rows)
    second_core = lax.axis_index("sub") == 1
    bf16 = jnp.bfloat16
    f32 = jnp.float32

    parts = block_ref.shape[0]
    span = channels // parts
    nothing = jnp.zeros((channels, wide), bf16)
    for part in range(parts):
        for step in range(span + 1):
            weight = outer_ref[part * span + step % span]
            at = step * 2 * channels
            block_ref[part, at : at + channels, :wide] = weight
            block_ref[part, at : at + channels, wide:] = nothing
            block_ref[part, at + channels : at + 2 * channels, :wide] = nothing
            block_ref[part, at + channels : at + 2 * channels, wide:] = weight

    lane = lax.broadcasted_iota(jnp.int32, (channels, wide), 1)
    lane_block = lane // channels
    low = lane < half
    for chip in range(chips):
        place = block_place(chip, chips)
        mine, other = held_ref[place], other_ref[place]
        blocks = [jnp.where(second_core, other, mine), jnp.where(second_core, mine, other)]
        packed = [block[base : base + sequences].astype(f32) for block in blocks]
        right = jnp.where(low, packed[0], packed[1])
        for turn, value in enumerate((right, pltpu.roll(right, half, 1))):
            for copy in range(group):
                right_ref[
                    turn,
                    copy * sequences : (copy + 1) * sequences,
                    chip * wide : (chip + 1) * wide,
                ] = value.astype(bf16)
        for core in range(cores):
            residue = (chip * cores + core) * rows
            for row in range(rows):
                at = (rows if core == 0 else 0) + row
                left_ref[residue + row] = jnp.where(lane_block == at, packed[core], 0.0)
            keep_ref[residue : residue + rows] = blocks[core][base + sequences :].astype(f32)[:rows]
            pair_ref[residue : residue + rows] = (
                blocks[core][:base].astype(f32).reshape(rows, residues, wide)
            )

    last = (((1,), (1,)), ((), ()))
    keep = keep_ref[...]
    mask = jnp.broadcast_to(keep[:, sequences : sequences + 1], (residues, wide))
    counted = lax.broadcasted_iota(jnp.int32, (residues, wide), 1) < sequences
    count = lax.dot_general(
        jnp.where(counted, keep, 0.0).astype(bf16),
        keep.astype(bf16),
        last,
        preferred_element_type=f32,
    )
    inverse = 1.0 / jnp.maximum(count, 1.0)

    low = lax.broadcasted_iota(jnp.int32, (residues, wide), 1) < half
    totals = [0.0, 0.0]
    for part in range(parts):
        outer = []
        for turn in range(2):
            left = jnp.concatenate(
                [left_ref[:, d] for d in range(part * span + turn, (part + 1) * span, 2)], axis=0
            ).astype(bf16)
            outer.append(jnp.dot(left, right_ref[turn], preferred_element_type=f32).astype(bf16))

        def piece(turn, at, chip):
            return outer[turn][
                at * residues : (at + 1) * residues, chip * wide : (chip + 1) * wide
            ]

        for at in range(span // 2):
            follow = (at + 1) % (span // 2)
            for chip in range(chips):
                place = (
                    part,
                    slice(chip * residues, (chip + 1) * residues),
                    slice(at * wide, (at + 1) * wide),
                )
                first_ref[place] = jnp.where(low, piece(0, at, chip), piece(1, at, chip))
                second_ref[place] = jnp.where(low, piece(1, at, chip), piece(0, follow, chip))
        depth = span * 2 * channels
        totals[0] += jnp.dot(first_ref[part], block_ref[part, :depth], preferred_element_type=f32)
        totals[1] += jnp.dot(
            second_ref[part], block_ref[part, 2 * channels :], preferred_element_type=f32
        )

    right_weight = jnp.concatenate([triangle_ref[2], triangle_ref[3]], axis=1)
    right_tri = []
    stride = 8
    for first in range(0, residues, stride):
        normed = []
        for k in range(first, first + stride):
            chip, pick = k // group, k % group
            at = (pick % 2) * wide
            numerator = totals[pick // 2][chip * residues : (chip + 1) * residues, at : at + wide]
            opm = numerator * jnp.broadcast_to(inverse[:, k : k + 1], (residues, wide))
            pair_one = (pair_ref[:, k] + opm).astype(bf16).astype(f32)
            pair_one_ref[k] = pair_one
            ln_one = layer_norm(pair_one)
            ln_one_ref[k] = ln_one
            normed.append(ln_one.astype(bf16))
        both = jnp.dot(
            jnp.concatenate(normed, axis=0), right_weight, preferred_element_type=f32
        )
        right_tri.append((sigmoid(both[:, :wide]) * both[:, wide:]).astype(bf16).astype(f32))

    own_pair = jnp.concatenate([pair_one_ref[:, start + row] for row in range(rows)], axis=0)
    own_ln = jnp.concatenate([ln_one_ref[:, start + row] for row in range(rows)], axis=0).astype(bf16)
    left_weight = jnp.concatenate([triangle_ref[0], triangle_ref[1]], axis=1)
    both = jnp.dot(own_ln, left_weight, preferred_element_type=f32)
    left_tri = sigmoid(both[:, :wide]) * both[:, wide:] * jnp.concatenate([mask] * rows, axis=0)
    left_tri = left_tri.astype(bf16).astype(f32)
    products = []
    for row in range(rows):
        sums = [jnp.zeros((residues, wide), f32) for _ in range(4)]
        for k in range(residues):
            at = row * residues + k
            place = (k % stride) * residues
            sums[k % 4] += left_tri[at : at + 1] * right_tri[k // stride][place : place + residues]
        total = (sums[0] + sums[1]) + (sums[2] + sums[3])
        own_mask = keep_ref[pl.ds(start + row, 1), :][:, sequences : sequences + 1]
        products.append(total * (mask * own_mask))
    product = jnp.concatenate(products, axis=0).astype(bf16).astype(f32)
    normed = layer_norm(product).astype(bf16)
    update = jnp.dot(normed, output_ref[...], preferred_element_type=f32)
    gate_out = sigmoid(jnp.dot(own_ln, gate_ref[...], preferred_element_type=f32))
    pair_two = (own_pair + gate_out * update).astype(bf16).astype(f32)
    ln_two = layer_norm(pair_two).astype(bf16)
    hidden = jnp.maximum(jnp.dot(ln_two, up_ref[...], preferred_element_type=f32), 0.0).astype(bf16)
    result = pair_two + jnp.dot(hidden, down_ref[...], preferred_element_type=f32)
    out_ref[...] = result.astype(bf16).reshape(rows, residues, wide)


def gather_all(packed):
    dap_count = lax.axis_size("dap")
    half = dap_count // 2
    far = lax.ppermute(packed[None], "dap", [(src, src ^ half) for src in range(dap_count)])
    both = jnp.concatenate([packed[None], far], axis=0)
    held = [both] + [
        lax.ppermute(both, "dap", [(src, src ^ offset) for src in range(dap_count)])
        for offset in swap_order(dap_count)
    ]
    sibling = [(0, 1), (1, 0)]
    first = lax.ppermute(both, "sub", sibling)
    early = lax.ppermute(jnp.concatenate(held[1:-1], axis=0), "sub", sibling)
    late = lax.ppermute(held[-1], "sub", sibling)
    return jnp.concatenate(held, axis=0), jnp.concatenate([first, early, late], axis=0)


def swap_order(dap_count):
    near = dap_count // 2
    return [1, near - 1] + list(range(2, near - 1))


def block_place(chip, chips):
    offset = lax.bitwise_xor(lax.axis_index("dap"), chip)
    half = chips // 2
    near = jnp.where(offset >= half, offset - half, offset)
    turn = jnp.where(near > 1, jnp.where(near == half - 1, 2, near + 1), near)
    return 2 * turn + jnp.where(offset >= half, 1, 0)


def shards_replicated(
    pairwise_state,
    alignment_state,
    alignment_mask,
    residue_crop_mask,
    outer_input_weight,
    outer_output_weight,
    triangle_input_weight,
    triangle_gate,
    triangle_output_weight,
    transition_up_weight,
    transition_down_weight,
):
    rows, residues, wide = pairwise_state.shape
    sequences = alignment_state.shape[0]
    channels = outer_input_weight.shape[2]
    vector = pl.BlockSpec(memory_space=pltpu.VMEM)
    params = pltpu.CompilerParams(vmem_limit_bytes=40 << 20)
    hbm = pl.BlockSpec(memory_space=pltpu.HBM)
    packed = pl.pallas_call(
        pack_kernel,
        out_shape=jax.ShapeDtypeStruct((rows * residues + sequences + 16, wide), jnp.bfloat16),
        in_specs=[hbm] * 5,
        out_specs=vector,
        scratch_shapes=[
            pltpu.SMEM((residues,), jnp.int32),
            pltpu.VMEM((rows, sequences), jnp.int32),
            pltpu.VMEM(alignment_state.shape, jnp.bfloat16),
            pltpu.VMEM((2, channels, alignment_state.shape[2]), jnp.bfloat16),
            pltpu.VMEM(alignment_state.shape, jnp.float32),
            pltpu.SemaphoreType.DMA((4 + rows,)),
        ],
        compiler_params=pltpu.CompilerParams(vmem_limit_bytes=8 << 20),
    )(
        *(
            pltpu.with_memory_space_constraint(array, pltpu.HBM)
            for array in (
                residue_crop_mask,
                alignment_mask.T,
                alignment_state,
                outer_input_weight.transpose(0, 2, 1),
                pairwise_state,
            )
        )
    )
    held, other = gather_all(packed)
    cores, chips = lax.axis_size("sub"), lax.axis_size("dap")
    group = cores * rows
    parts = 1
    return pl.pallas_call(
        update_kernel,
        out_shape=jax.ShapeDtypeStruct(pairwise_state.shape, jnp.bfloat16),
        in_specs=[vector] * 8,
        out_specs=vector,
        scratch_shapes=[
            pltpu.VMEM((parts, (channels // parts + 1) * 2 * channels, 2 * wide), jnp.bfloat16),
            pltpu.VMEM((residues, channels, wide), jnp.float32),
            pltpu.VMEM((2, group * sequences, chips * wide), jnp.bfloat16),
            pltpu.VMEM((residues, wide), jnp.float32),
            pltpu.VMEM((parts, chips * residues, channels // parts * wide // 2), jnp.bfloat16),
            pltpu.VMEM((parts, chips * residues, channels // parts * wide // 2), jnp.bfloat16),
            pltpu.VMEM((residues, residues, wide), jnp.float32),
            pltpu.VMEM((residues, residues, wide), jnp.float32),
            pltpu.VMEM((residues, residues, wide), jnp.float32),
        ],
        compiler_params=params,
    )(
        held,
        other,
        outer_output_weight,
        triangle_input_weight,
        triangle_gate,
        triangle_output_weight,
        transition_up_weight,
        transition_down_weight,
    )


def shards(
    pairwise_state,
    alignment_state,
    alignment_mask,
    residue_crop_mask,
    outer_input_weight,
    outer_output_weight,
    triangle_input_weight,
    triangle_gate,
    triangle_output_weight,
    transition_up_weight,
    transition_down_weight,
):
    row_count = pairwise_state.shape[0]
    start_row = lax.axis_index(("dap", "sub")) * row_count
    row_presence_mask = lax.dynamic_slice_in_dim(residue_crop_mask, start_row, row_count, 0).astype(
        jnp.float32
    )
    full_mask = residue_crop_mask.astype(jnp.float32)
    alignment_keep = alignment_mask.astype(jnp.float32) * row_presence_mask[None, :]
    alignment_normed = norm_layer(alignment_state.astype(jnp.float32), -1).astype(jnp.bfloat16)
    left_alignment = (
        jnp.einsum(
            "pxm,my->pxy",
            alignment_normed,
            outer_input_weight[0],
            preferred_element_type=jnp.float32,
        )
        * alignment_keep[:, :, None]
    ).astype(jnp.bfloat16)
    right_alignment = (
        jnp.einsum(
            "pxm,my->pxy",
            alignment_normed,
            outer_input_weight[1],
            preferred_element_type=jnp.float32,
        )
        * alignment_keep[:, :, None]
    ).astype(jnp.bfloat16)
    inner_alignment = jnp.einsum(
        "tqu,ulx->tqlx", left_alignment, outer_output_weight, preferred_element_type=jnp.float32
    ).astype(jnp.bfloat16)
    right_portion = lax.all_gather(right_alignment, ("dap", "sub"), axis=1, tiled=True)
    keep_portion = lax.all_gather(
        alignment_keep.astype(jnp.bfloat16), ("dap", "sub"), axis=1, tiled=True
    )
    numerator_sum = jnp.einsum(
        "zkwv,znw->knv", inner_alignment, right_portion, preferred_element_type=jnp.float32
    )
    pair_norm_count = jnp.einsum("cf,cg->fg", alignment_keep, keep_portion.astype(jnp.float32))
    block_part = numerator_sum / jnp.maximum(pair_norm_count, 1.0)[:, :, None]
    pair_one = (pairwise_state.astype(jnp.float32) + block_part).astype(jnp.bfloat16)
    ln_one = norm_layer(pair_one.astype(jnp.float32), -1).astype(jnp.bfloat16)
    pair_keep = row_presence_mask[:, None] * full_mask[None, :]

    def operand(gate_w, proj_w):
        gate_val = jnp.einsum("ijc,cd->dij", ln_one, gate_w, preferred_element_type=jnp.float32)
        proj_val = jnp.einsum("ijc,cd->dij", ln_one, proj_w, preferred_element_type=jnp.float32)
        return (jax.nn.sigmoid(gate_val) * proj_val * pair_keep[None]).astype(jnp.bfloat16)

    left_tri = operand(triangle_input_weight[0], triangle_input_weight[1])
    right_tri = operand(triangle_input_weight[2], triangle_input_weight[3])
    near_right = lax.all_gather(right_tri, "sub", axis=1, tiled=True)
    left_cols, right_all = (
        lax.all_to_all(left_tri, "dap", split_axis=0, concat_axis=1, tiled=True),
        lax.all_to_all(near_right, "dap", split_axis=0, concat_axis=1, tiled=True),
    )
    product = jnp.einsum(
        "cik,cjk->cij", left_cols, right_all, preferred_element_type=jnp.float32
    ).astype(jnp.bfloat16)
    returned = lax.all_to_all(product, "dap", split_axis=1, concat_axis=0, tiled=True)
    normed = norm_layer(returned.astype(jnp.float32), 0).astype(jnp.bfloat16)
    update = jnp.einsum(
        "cij,cd->ijd", normed, triangle_output_weight, preferred_element_type=jnp.float32
    )
    gate_out = jax.nn.sigmoid(
        jnp.einsum("ijc,cd->ijd", ln_one, triangle_gate, preferred_element_type=jnp.float32)
    )
    pair_two = (pair_one.astype(jnp.float32) + gate_out * update).astype(jnp.bfloat16)
    ln_two = norm_layer(pair_two.astype(jnp.float32), -1).astype(jnp.bfloat16)

    def step(row_pair):
        return transition(*row_pair, transition_up_weight, transition_down_weight)

    return lax.map(step, (ln_two, pair_two))


def solution(mesh):
    placed = (
        P(("crop", "dap", "sub"), None, None),
        P("crop", ("dap", "sub"), None),
        P("crop", ("dap", "sub")),
        P("crop"),
        P(),
        P(),
        P(),
        P(),
        P(),
        P(),
        P(),
    )

    small = mesh.shape["sub"] == 2 and mesh.shape["dap"] == 8

    def body(pairwise_state, *rest):
        residues, channels = pairwise_state.shape[1:]
        if small and residues * residues * channels * 2 <= REPLICATED_PAIR_BYTES:
            return shards_replicated(pairwise_state, *rest)
        return shards(pairwise_state, *rest)

    return jax.shard_map(
        body,
        mesh=mesh,
        in_specs=placed,
        out_specs=P(("crop", "dap", "sub"), None, None),
        check_vma=False,
    )
```

```python
import jax
import jax.numpy as jnp
from jax import lax
from jax.experimental import pallas as pl
from jax.experimental.pallas import tpu as pltpu
from jax.sharding import PartitionSpec as P

REPLICATED_PAIR_BYTES = 1 << 20


def norm_layer(values, reduce_axis):
    average = jnp.mean(values, axis=reduce_axis, keepdims=True)
    centered = values - average
    variance = jnp.mean(centered * centered, axis=reduce_axis, keepdims=True)
    return centered * lax.rsqrt(variance + 1e-05)


def transition(ln_two, pair_two, transition_up_weight, transition_down_weight):
    hidden = jax.nn.relu(
        jnp.dot(ln_two, transition_up_weight, preferred_element_type=jnp.float32)
    ).astype(jnp.bfloat16)
    return (
        pair_two.astype(jnp.float32)
        + jnp.dot(hidden, transition_down_weight, preferred_element_type=jnp.float32)
    ).astype(jnp.bfloat16)


def layer_norm(values):
    count = values.shape[-1]
    centered = values - jnp.sum(values, axis=-1, keepdims=True) * (1.0 / count)
    variance = jnp.sum(centered * centered, axis=-1, keepdims=True) * (1.0 / count)
    return centered * lax.rsqrt(variance + 1e-05)


def first_row(rows):
    return (lax.axis_index("dap") * lax.axis_size("sub") + lax.axis_index("sub")) * rows


def pack_kernel(
    mask_hbm,
    keep_hbm,
    state_hbm,
    weight_hbm,
    pair_hbm,
    out_ref,
    mask_ref,
    keep_ref,
    state_ref,
    weight_ref,
    wide_ref,
    sems,
):
    rows, residues, wide = pair_hbm.shape
    sequences = state_ref.shape[0]
    base = rows * residues
    start = first_row(rows)
    second_core = lax.axis_index("sub") == 1
    loads = [
        pltpu.make_async_copy(state_hbm, state_ref, sems.at[0]),
        pltpu.make_async_copy(weight_hbm, weight_ref, sems.at[1]),
        pltpu.make_async_copy(keep_hbm, keep_ref, sems.at[2]),
        pltpu.make_async_copy(mask_hbm, mask_ref, sems.at[3]),
    ] + [
        pltpu.make_async_copy(
            pair_hbm.at[row], out_ref.at[pl.ds(row * residues, residues)], sems.at[4 + row]
        )
        for row in range(rows)
    ]
    for load in loads:
        load.start()
    for load in loads[:4]:
        load.wait()
    f32, bf16 = jnp.float32, jnp.bfloat16
    wide_ref[...] = state_ref[...].astype(f32)
    eye = lax.broadcasted_iota(jnp.int32, (sequences, sequences), 0) == lax.broadcasted_iota(
        jnp.int32, (sequences, sequences), 1
    )
    last = (((1,), (1,)), ((), ()))
    weight = weight_ref[1]
    nothing = jnp.zeros_like(weight)
    here = jnp.where(second_core, nothing, weight), jnp.where(second_core, weight, nothing)
    keeps, fronts, backs = [], [], []
    projected = 0.0
    for row in range(rows):
        present = mask_ref[start + row].astype(f32)
        keep_row = keep_ref[row : row + 1].astype(f32) * present
        keep_column = jnp.sum(
            jnp.where(eye, jnp.broadcast_to(keep_row, eye.shape), 0.0), axis=1, keepdims=True
        )
        normed = (layer_norm(wide_ref[:, row]) * keep_column).astype(bf16)
        fronts.append(jnp.where(second_core, normed, jnp.zeros_like(normed)))
        backs.append(jnp.where(second_core, jnp.zeros_like(normed), normed))
        placed = [here[0] if at == row else here[1] if at == rows + row else nothing for at in range(2 * rows)]
        projected += lax.dot_general(
            normed, jnp.concatenate(placed, axis=0), last, preferred_element_type=f32
        )
        keeps.append(
            jnp.concatenate([keep_row, jnp.full((1, wide - sequences), present, f32)], axis=1)
        )
    projected += lax.dot_general(
        weight_ref[0], jnp.concatenate(fronts + backs, axis=0), last, preferred_element_type=f32
    )
    out_ref[base : base + sequences] = projected.astype(bf16)
    out_ref[base + sequences :] = jnp.concatenate(
        keeps + [jnp.zeros((16 - rows, wide), jnp.float32)], axis=0
    ).astype(jnp.bfloat16)
    for load in loads[4:]:
        load.wait()


def sigmoid(values):
    return 0.5 * jnp.tanh(0.5 * values) + 0.5


def update_kernel(
    held_ref,
    other_ref,
    outer_ref,
    triangle_ref,
    gate_ref,
    output_ref,
    up_ref,
    down_ref,
    out_ref,
    block_ref,
    left_ref,
    right_ref,
    keep_ref,
    first_ref,
    second_ref,
    pair_ref,
    pair_one_ref,
    ln_one_ref,
):
    rows, residues, wide = out_ref.shape
    cores, chips = 2, lax.axis_size("dap")
    channels = outer_ref.shape[0]
    sequences = channels
    base = rows * residues
    half = wide // 2
    group = cores * rows
    start = first_row(rows)
    second_core = lax.axis_index("sub") == 1
    bf16 = jnp.bfloat16
    f32 = jnp.float32

    parts = block_ref.shape[0]
    span = channels // parts
    lane = lax.broadcasted_iota(jnp.int32, (channels, wide), 1)
    lane_block = lane // channels
    low = lane < half
    for chip in range(chips):
        place = block_place(chip, chips)
        mine, other = held_ref[place], other_ref[place]
        blocks = [jnp.where(second_core, other, mine), jnp.where(second_core, mine, other)]
        packed = [block[base : base + sequences].astype(f32) for block in blocks]
        right = jnp.where(low, packed[0], packed[1])
        for turn, value in enumerate((right, pltpu.roll(right, half, 1))):
            for copy in range(group):
                right_ref[
                    turn,
                    copy * sequences : (copy + 1) * sequences,
                    chip * wide : (chip + 1) * wide,
                ] = value.astype(bf16)
        for core in range(cores):
            residue = (chip * cores + core) * rows
            for row in range(rows):
                at = (rows if core == 0 else 0) + row
                left_ref[residue + row] = jnp.where(lane_block == at, packed[core], 0.0)
            keep_ref[residue : residue + rows] = blocks[core][base + sequences :].astype(f32)[:rows]
            pair_ref[residue : residue + rows] = (
                blocks[core][:base].astype(f32).reshape(rows, residues, wide)
            )

    last = (((1,), (1,)), ((), ()))
    keep = keep_ref[...]
    mask = jnp.broadcast_to(keep[:, sequences : sequences + 1], (residues, wide))
    counted = lax.broadcasted_iota(jnp.int32, (residues, wide), 1) < sequences
    count = lax.dot_general(
        jnp.where(counted, keep, 0.0).astype(bf16),
        keep.astype(bf16),
        last,
        preferred_element_type=f32,
    )
    inverse = 1.0 / jnp.maximum(count, 1.0)

    low = lax.broadcasted_iota(jnp.int32, (residues, wide), 1) < half
    totals = [0.0, 0.0]
    for part in range(parts):
        outer = []
        for turn in range(2):
            left = jnp.concatenate(
                [left_ref[:, d] for d in range(part * span + turn, (part + 1) * span, 2)], axis=0
            ).astype(bf16)
            outer.append(jnp.dot(left, right_ref[turn], preferred_element_type=f32).astype(bf16))

        nothing = jnp.zeros((channels, wide), bf16)
        for step in range(span + 1):
            weight = outer_ref[part * span + step % span]
            at = step * 2 * channels
            block_ref[part, at : at + channels, :wide] = weight
            block_ref[part, at : at + channels, wide:] = nothing
            block_ref[part, at + channels : at + 2 * channels, :wide] = nothing
            block_ref[part, at + channels : at + 2 * channels, wide:] = weight

        def piece(turn, at, chip):
            return outer[turn][
                at * residues : (at + 1) * residues, chip * wide : (chip + 1) * wide
            ]

        for at in range(span // 2):
            follow = (at + 1) % (span // 2)
            for chip in range(chips):
                place = (
                    part,
                    slice(chip * residues, (chip + 1) * residues),
                    slice(at * wide, (at + 1) * wide),
                )
                first_ref[place] = jnp.where(low, piece(0, at, chip), piece(1, at, chip))
                second_ref[place] = jnp.where(low, piece(1, at, chip), piece(0, follow, chip))
        depth = span * 2 * channels
        totals[0] += jnp.dot(first_ref[part], block_ref[part, :depth], preferred_element_type=f32)
        totals[1] += jnp.dot(
            second_ref[part], block_ref[part, 2 * channels :], preferred_element_type=f32
        )

    right_weight = jnp.concatenate([triangle_ref[2], triangle_ref[3]], axis=1)
    right_tri = []
    stride = 8
    for first in range(0, residues, stride):
        normed = []
        for k in range(first, first + stride):
            chip, pick = k // group, k % group
            at = (pick % 2) * wide
            numerator = totals[pick // 2][chip * residues : (chip + 1) * residues, at : at + wide]
            opm = numerator * jnp.broadcast_to(inverse[:, k : k + 1], (residues, wide))
            pair_one = (pair_ref[:, k] + opm).astype(bf16).astype(f32)
            pair_one_ref[k] = pair_one
            ln_one = layer_norm(pair_one)
            ln_one_ref[k] = ln_one
            normed.append(ln_one.astype(bf16))
        both = jnp.dot(
            jnp.concatenate(normed, axis=0), right_weight, preferred_element_type=f32
        )
        right_tri.append((sigmoid(both[:, :wide]) * both[:, wide:]).astype(bf16).astype(f32))

    own_pair = jnp.concatenate([pair_one_ref[:, start + row] for row in range(rows)], axis=0)
    own_ln = jnp.concatenate([ln_one_ref[:, start + row] for row in range(rows)], axis=0).astype(bf16)
    left_weight = jnp.concatenate([triangle_ref[0], triangle_ref[1]], axis=1)
    both = jnp.dot(own_ln, left_weight, preferred_element_type=f32)
    left_tri = sigmoid(both[:, :wide]) * both[:, wide:] * jnp.concatenate([mask] * rows, axis=0)
    left_tri = left_tri.astype(bf16).astype(f32)
    products = []
    for row in range(rows):
        sums = [jnp.zeros((residues, wide), f32) for _ in range(4)]
        for k in range(residues):
            at = row * residues + k
            place = (k % stride) * residues
            sums[k % 4] += left_tri[at : at + 1] * right_tri[k // stride][place : place + residues]
        total = (sums[0] + sums[1]) + (sums[2] + sums[3])
        own_mask = keep_ref[pl.ds(start + row, 1), :][:, sequences : sequences + 1]
        products.append(total * (mask * own_mask))
    product = jnp.concatenate(products, axis=0).astype(bf16).astype(f32)
    normed = layer_norm(product).astype(bf16)
    update = jnp.dot(normed, output_ref[...], preferred_element_type=f32)
    gate_out = sigmoid(jnp.dot(own_ln, gate_ref[...], preferred_element_type=f32))
    pair_two = (own_pair + gate_out * update).astype(bf16).astype(f32)
    ln_two = layer_norm(pair_two).astype(bf16)
    hidden = jnp.maximum(jnp.dot(ln_two, up_ref[...], preferred_element_type=f32), 0.0).astype(bf16)
    result = pair_two + jnp.dot(hidden, down_ref[...], preferred_element_type=f32)
    out_ref[...] = result.astype(bf16).reshape(rows, residues, wide)


def gather_all(packed):
    dap_count = lax.axis_size("dap")
    half = dap_count // 2
    far = lax.ppermute(packed[None], "dap", [(src, src ^ half) for src in range(dap_count)])
    both = jnp.concatenate([packed[None], far], axis=0)
    held = [both] + [
        lax.ppermute(both, "dap", [(src, src ^ offset) for src in range(dap_count)])
        for offset in swap_order(dap_count)
    ]
    sibling = [(0, 1), (1, 0)]
    first = lax.ppermute(both, "sub", sibling)
    early = lax.ppermute(jnp.concatenate(held[1:-1], axis=0), "sub", sibling)
    late = lax.ppermute(held[-1], "sub", sibling)
    return jnp.concatenate(held, axis=0), jnp.concatenate([first, early, late], axis=0)


def swap_order(dap_count):
    near = dap_count // 2
    return [1, near - 1] + list(range(2, near - 1))


def block_place(chip, chips):
    offset = lax.bitwise_xor(lax.axis_index("dap"), chip)
    half = chips // 2
    near = jnp.where(offset >= half, offset - half, offset)
    turn = jnp.where(near > 1, jnp.where(near == half - 1, 2, near + 1), near)
    return 2 * turn + jnp.where(offset >= half, 1, 0)


def shards_replicated(
    pairwise_state,
    alignment_state,
    alignment_mask,
    residue_crop_mask,
    outer_input_weight,
    outer_output_weight,
    triangle_input_weight,
    triangle_gate,
    triangle_output_weight,
    transition_up_weight,
    transition_down_weight,
):
    rows, residues, wide = pairwise_state.shape
    sequences = alignment_state.shape[0]
    channels = outer_input_weight.shape[2]
    vector = pl.BlockSpec(memory_space=pltpu.VMEM)
    params = pltpu.CompilerParams(vmem_limit_bytes=40 << 20)
    hbm = pl.BlockSpec(memory_space=pltpu.HBM)
    packed = pl.pallas_call(
        pack_kernel,
        out_shape=jax.ShapeDtypeStruct((rows * residues + sequences + 16, wide), jnp.bfloat16),
        in_specs=[hbm] * 5,
        out_specs=vector,
        scratch_shapes=[
            pltpu.SMEM((residues,), jnp.int32),
            pltpu.VMEM((rows, sequences), jnp.int32),
            pltpu.VMEM(alignment_state.shape, jnp.bfloat16),
            pltpu.VMEM((2, channels, alignment_state.shape[2]), jnp.bfloat16),
            pltpu.VMEM(alignment_state.shape, jnp.float32),
            pltpu.SemaphoreType.DMA((4 + rows,)),
        ],
        compiler_params=pltpu.CompilerParams(vmem_limit_bytes=8 << 20),
    )(
        *(
            pltpu.with_memory_space_constraint(array, pltpu.HBM)
            for array in (
                residue_crop_mask,
                alignment_mask.T,
                alignment_state,
                outer_input_weight.transpose(0, 2, 1),
                pairwise_state,
            )
        )
    )
    held, other = gather_all(packed)
    cores, chips = lax.axis_size("sub"), lax.axis_size("dap")
    group = cores * rows
    parts = 1
    return pl.pallas_call(
        update_kernel,
        out_shape=jax.ShapeDtypeStruct(pairwise_state.shape, jnp.bfloat16),
        in_specs=[vector] * 8,
        out_specs=vector,
        scratch_shapes=[
            pltpu.VMEM((parts, (channels // parts + 1) * 2 * channels, 2 * wide), jnp.bfloat16),
            pltpu.VMEM((residues, channels, wide), jnp.float32),
            pltpu.VMEM((2, group * sequences, chips * wide), jnp.bfloat16),
            pltpu.VMEM((residues, wide), jnp.float32),
            pltpu.VMEM((parts, chips * residues, channels // parts * wide // 2), jnp.bfloat16),
            pltpu.VMEM((parts, chips * residues, channels // parts * wide // 2), jnp.bfloat16),
            pltpu.VMEM((residues, residues, wide), jnp.float32),
            pltpu.VMEM((residues, residues, wide), jnp.float32),
            pltpu.VMEM((residues, residues, wide), jnp.float32),
        ],
        compiler_params=params,
    )(
        held,
        other,
        outer_output_weight,
        triangle_input_weight,
        triangle_gate,
        triangle_output_weight,
        transition_up_weight,
        transition_down_weight,
    )


def shards(
    pairwise_state,
    alignment_state,
    alignment_mask,
    residue_crop_mask,
    outer_input_weight,
    outer_output_weight,
    triangle_input_weight,
    triangle_gate,
    triangle_output_weight,
    transition_up_weight,
    transition_down_weight,
):
    row_count = pairwise_state.shape[0]
    start_row = lax.axis_index(("dap", "sub")) * row_count
    row_presence_mask = lax.dynamic_slice_in_dim(residue_crop_mask, start_row, row_count, 0).astype(
        jnp.float32
    )
    full_mask = residue_crop_mask.astype(jnp.float32)
    alignment_keep = alignment_mask.astype(jnp.float32) * row_presence_mask[None, :]
    alignment_normed = norm_layer(alignment_state.astype(jnp.float32), -1).astype(jnp.bfloat16)
    left_alignment = (
        jnp.einsum(
            "pxm,my->pxy",
            alignment_normed,
            outer_input_weight[0],
            preferred_element_type=jnp.float32,
        )
        * alignment_keep[:, :, None]
    ).astype(jnp.bfloat16)
    right_alignment = (
        jnp.einsum(
            "pxm,my->pxy",
            alignment_normed,
            outer_input_weight[1],
            preferred_element_type=jnp.float32,
        )
        * alignment_keep[:, :, None]
    ).astype(jnp.bfloat16)
    inner_alignment = jnp.einsum(
        "tqu,ulx->tqlx", left_alignment, outer_output_weight, preferred_element_type=jnp.float32
    ).astype(jnp.bfloat16)
    right_portion = lax.all_gather(right_alignment, ("dap", "sub"), axis=1, tiled=True)
    keep_portion = lax.all_gather(
        alignment_keep.astype(jnp.bfloat16), ("dap", "sub"), axis=1, tiled=True
    )
    numerator_sum = jnp.einsum(
        "zkwv,znw->knv", inner_alignment, right_portion, preferred_element_type=jnp.float32
    )
    pair_norm_count = jnp.einsum("cf,cg->fg", alignment_keep, keep_portion.astype(jnp.float32))
    block_part = numerator_sum / jnp.maximum(pair_norm_count, 1.0)[:, :, None]
    pair_one = (pairwise_state.astype(jnp.float32) + block_part).astype(jnp.bfloat16)
    ln_one = norm_layer(pair_one.astype(jnp.float32), -1).astype(jnp.bfloat16)
    pair_keep = row_presence_mask[:, None] * full_mask[None, :]

    def operand(gate_w, proj_w):
        gate_val = jnp.einsum("ijc,cd->dij", ln_one, gate_w, preferred_element_type=jnp.float32)
        proj_val = jnp.einsum("ijc,cd->dij", ln_one, proj_w, preferred_element_type=jnp.float32)
        return (jax.nn.sigmoid(gate_val) * proj_val * pair_keep[None]).astype(jnp.bfloat16)

    left_tri = operand(triangle_input_weight[0], triangle_input_weight[1])
    right_tri = operand(triangle_input_weight[2], triangle_input_weight[3])
    near_right = lax.all_gather(right_tri, "sub", axis=1, tiled=True)
    left_cols, right_all = (
        lax.all_to_all(left_tri, "dap", split_axis=0, concat_axis=1, tiled=True),
        lax.all_to_all(near_right, "dap", split_axis=0, concat_axis=1, tiled=True),
    )
    product = jnp.einsum(
        "cik,cjk->cij", left_cols, right_all, preferred_element_type=jnp.float32
    ).astype(jnp.bfloat16)
    returned = lax.all_to_all(product, "dap", split_axis=1, concat_axis=0, tiled=True)
    normed = norm_layer(returned.astype(jnp.float32), 0).astype(jnp.bfloat16)
    update = jnp.einsum(
        "cij,cd->ijd", normed, triangle_output_weight, preferred_element_type=jnp.float32
    )
    gate_out = jax.nn.sigmoid(
        jnp.einsum("ijc,cd->ijd", ln_one, triangle_gate, preferred_element_type=jnp.float32)
    )
    pair_two = (pair_one.astype(jnp.float32) + gate_out * update).astype(jnp.bfloat16)
    ln_two = norm_layer(pair_two.astype(jnp.float32), -1).astype(jnp.bfloat16)

    def step(row_pair):
        return transition(*row_pair, transition_up_weight, transition_down_weight)

    return lax.map(step, (ln_two, pair_two))


def solution(mesh):
    placed = (
        P(("crop", "dap", "sub"), None, None),
        P("crop", ("dap", "sub"), None),
        P("crop", ("dap", "sub")),
        P("crop"),
        P(),
        P(),
        P(),
        P(),
        P(),
        P(),
        P(),
    )

    small = mesh.shape["sub"] == 2 and mesh.shape["dap"] == 8

    def body(pairwise_state, *rest):
        residues, channels = pairwise_state.shape[1:]
        if small and residues * residues * channels * 2 <= REPLICATED_PAIR_BYTES:
            return shards_replicated(pairwise_state, *rest)
        return shards(pairwise_state, *rest)

    return jax.shard_map(
        body,
        mesh=mesh,
        in_specs=placed,
        out_specs=P(("crop", "dap", "sub"), None, None),
        check_vma=False,
    )
```

```python
import jax
import jax.numpy as jnp
from jax import lax
from jax.experimental import pallas as pl
from jax.experimental.pallas import tpu as pltpu
from jax.sharding import PartitionSpec as P

REPLICATED_PAIR_BYTES = 1 << 20


def norm_layer(values, reduce_axis):
    average = jnp.mean(values, axis=reduce_axis, keepdims=True)
    centered = values - average
    variance = jnp.mean(centered * centered, axis=reduce_axis, keepdims=True)
    return centered * lax.rsqrt(variance + 1e-05)


def transition(ln_two, pair_two, transition_up_weight, transition_down_weight):
    hidden = jax.nn.relu(
        jnp.dot(ln_two, transition_up_weight, preferred_element_type=jnp.float32)
    ).astype(jnp.bfloat16)
    return (
        pair_two.astype(jnp.float32)
        + jnp.dot(hidden, transition_down_weight, preferred_element_type=jnp.float32)
    ).astype(jnp.bfloat16)


def layer_norm(values):
    count = values.shape[-1]
    centered = values - jnp.sum(values, axis=-1, keepdims=True) * (1.0 / count)
    variance = jnp.sum(centered * centered, axis=-1, keepdims=True) * (1.0 / count)
    return centered * lax.rsqrt(variance + 1e-05)


def first_row(rows):
    return (lax.axis_index("dap") * lax.axis_size("sub") + lax.axis_index("sub")) * rows


def pack_kernel(
    mask_hbm,
    keep_hbm,
    state_hbm,
    weight_hbm,
    pair_hbm,
    out_ref,
    mask_ref,
    keep_ref,
    state_ref,
    weight_ref,
    wide_ref,
    sems,
):
    rows, residues, wide = pair_hbm.shape
    sequences = state_ref.shape[0]
    base = rows * residues
    start = first_row(rows)
    second_core = lax.axis_index("sub") == 1
    loads = [
        pltpu.make_async_copy(state_hbm, state_ref, sems.at[0]),
        pltpu.make_async_copy(weight_hbm, weight_ref, sems.at[1]),
        pltpu.make_async_copy(keep_hbm, keep_ref, sems.at[2]),
        pltpu.make_async_copy(mask_hbm, mask_ref, sems.at[3]),
    ] + [
        pltpu.make_async_copy(
            pair_hbm.at[row], out_ref.at[pl.ds(row * residues, residues)], sems.at[4 + row]
        )
        for row in range(rows)
    ]
    for load in loads:
        load.start()
    for load in loads[:4]:
        load.wait()
    f32, bf16 = jnp.float32, jnp.bfloat16
    wide_ref[...] = state_ref[...].astype(f32)
    eye = lax.broadcasted_iota(jnp.int32, (sequences, sequences), 0) == lax.broadcasted_iota(
        jnp.int32, (sequences, sequences), 1
    )
    last = (((1,), (1,)), ((), ()))
    weight = weight_ref[1]
    nothing = jnp.zeros_like(weight)
    here = jnp.where(second_core, nothing, weight), jnp.where(second_core, weight, nothing)
    keeps, fronts, backs = [], [], []
    projected = 0.0
    for row in range(rows):
        present = mask_ref[start + row].astype(f32)
        keep_row = keep_ref[row : row + 1].astype(f32) * present
        keep_column = jnp.sum(
            jnp.where(eye, jnp.broadcast_to(keep_row, eye.shape), 0.0), axis=1, keepdims=True
        )
        normed = (layer_norm(wide_ref[:, row]) * keep_column).astype(bf16)
        fronts.append(jnp.where(second_core, normed, jnp.zeros_like(normed)))
        backs.append(jnp.where(second_core, jnp.zeros_like(normed), normed))
        placed = [here[0] if at == row else here[1] if at == rows + row else nothing for at in range(2 * rows)]
        projected += lax.dot_general(
            normed, jnp.concatenate(placed, axis=0), last, preferred_element_type=f32
        )
        keeps.append(
            jnp.concatenate([keep_row, jnp.full((1, wide - sequences), present, f32)], axis=1)
        )
    projected += lax.dot_general(
        weight_ref[0], jnp.concatenate(fronts + backs, axis=0), last, preferred_element_type=f32
    )
    out_ref[base : base + sequences] = projected.astype(bf16)
    out_ref[base + sequences :] = jnp.concatenate(
        keeps + [jnp.zeros((16 - rows, wide), jnp.float32)], axis=0
    ).astype(jnp.bfloat16)
    for load in loads[4:]:
        load.wait()


def sigmoid(values):
    return 0.5 * jnp.tanh(0.5 * values) + 0.5


def update_kernel(
    held_ref,
    other_ref,
    outer_ref,
    triangle_ref,
    gate_ref,
    output_ref,
    up_ref,
    down_ref,
    out_ref,
    block_ref,
    left_ref,
    right_ref,
    keep_ref,
    first_ref,
    second_ref,
    pair_ref,
    pair_one_ref,
    ln_one_ref,
):
    rows, residues, wide = out_ref.shape
    cores, chips = 2, lax.axis_size("dap")
    channels = outer_ref.shape[0]
    sequences = channels
    base = rows * residues
    half = wide // 2
    group = cores * rows
    start = first_row(rows)
    second_core = lax.axis_index("sub") == 1
    bf16 = jnp.bfloat16
    f32 = jnp.float32

    parts = block_ref.shape[0]
    span = channels // parts
    nothing = jnp.zeros((channels, wide), bf16)
    for part in range(parts):
        for step in range(span + 1):
            weight = outer_ref[part * span + step % span]
            at = step * 2 * channels
            block_ref[part, at : at + channels, :wide] = weight
            block_ref[part, at : at + channels, wide:] = nothing
            block_ref[part, at + channels : at + 2 * channels, :wide] = nothing
            block_ref[part, at + channels : at + 2 * channels, wide:] = weight

    lane = lax.broadcasted_iota(jnp.int32, (channels, wide), 1)
    lane_block = lane // channels
    low = lane < half
    for chip in range(chips):
        place = block_place(chip, chips)
        mine, other = held_ref[place], other_ref[place]
        blocks = [jnp.where(second_core, other, mine), jnp.where(second_core, mine, other)]
        packed = [block[base : base + sequences].astype(f32) for block in blocks]
        right = jnp.where(low, packed[0], packed[1])
        for turn, value in enumerate((right, pltpu.roll(right, half, 1))):
            for copy in range(group):
                right_ref[
                    turn,
                    copy * sequences : (copy + 1) * sequences,
                    chip * wide : (chip + 1) * wide,
                ] = value.astype(bf16)
        for core in range(cores):
            residue = (chip * cores + core) * rows
            for row in range(rows):
                at = (rows if core == 0 else 0) + row
                left_ref[residue + row] = jnp.where(lane_block == at, packed[core], 0.0)
            keep_ref[residue : residue + rows] = blocks[core][base + sequences :].astype(f32)[:rows]
            pair_ref[residue : residue + rows] = (
                blocks[core][:base].astype(f32).reshape(rows, residues, wide)
            )

    last = (((1,), (1,)), ((), ()))
    keep = keep_ref[...]
    mask = jnp.broadcast_to(keep[:, sequences : sequences + 1], (residues, wide))
    counted = lax.broadcasted_iota(jnp.int32, (residues, wide), 1) < sequences
    count = lax.dot_general(
        jnp.where(counted, keep, 0.0).astype(bf16),
        keep.astype(bf16),
        last,
        preferred_element_type=f32,
    )
    inverse = 1.0 / jnp.maximum(count, 1.0)

    low = lax.broadcasted_iota(jnp.int32, (residues, wide), 1) < half
    totals = [0.0, 0.0]
    for part in range(parts):
        outer = []
        for turn in range(2):
            left = jnp.concatenate(
                [left_ref[:, d] for d in range(part * span + turn, (part + 1) * span, 2)], axis=0
            ).astype(bf16)
            outer.append(jnp.dot(left, right_ref[turn], preferred_element_type=f32).astype(bf16))

        def piece(turn, at, chip):
            return outer[turn][
                at * residues : (at + 1) * residues, chip * wide : (chip + 1) * wide
            ]

        for at in range(span // 2):
            follow = (at + 1) % (span // 2)
            for chip in range(chips):
                place = (
                    part,
                    slice(chip * residues, (chip + 1) * residues),
                    slice(at * wide, (at + 1) * wide),
                )
                first_ref[place] = jnp.where(low, piece(0, at, chip), piece(1, at, chip))
                second_ref[place] = jnp.where(low, piece(1, at, chip), piece(0, follow, chip))
        depth = span * 2 * channels
        totals[0] += jnp.dot(first_ref[part], block_ref[part, :depth], preferred_element_type=f32)
        totals[1] += jnp.dot(
            second_ref[part], block_ref[part, 2 * channels :], preferred_element_type=f32
        )

    left_weight = jnp.concatenate([triangle_ref[0], triangle_ref[1], gate_ref[...]], axis=1)
    right_weight = jnp.concatenate([triangle_ref[2], triangle_ref[3]], axis=1)
    stride = 8
    sums = [[jnp.zeros((residues, wide), f32) for _ in range(2)] for _ in range(rows)]
    gates = [[] for _ in range(rows)]
    for first in range(0, residues, stride):
        normed = []
        for k in range(first, first + stride):
            chip, pick = k // group, k % group
            at = (pick % 2) * wide
            numerator = totals[pick // 2][chip * residues : (chip + 1) * residues, at : at + wide]
            opm = numerator * jnp.broadcast_to(inverse[:, k : k + 1], (residues, wide))
            pair_one = (pair_ref[:, k] + opm).astype(bf16).astype(f32)
            pair_one_ref[k] = pair_one
            ln_one = layer_norm(pair_one)
            ln_one_ref[k] = ln_one
            normed.append(ln_one.astype(bf16))
        own_ln = jnp.concatenate(
            [ln_one_ref[first : first + stride, start + row] for row in range(rows)], axis=0
        ).astype(bf16)
        both = jnp.dot(own_ln, left_weight, preferred_element_type=f32)
        own_mask = jnp.concatenate([mask[first : first + stride]] * rows, axis=0)
        left_tri = sigmoid(both[:, :wide]) * both[:, wide : 2 * wide] * own_mask
        left_tri = left_tri.astype(bf16).astype(f32)
        gate_out = sigmoid(both[:, 2 * wide :])
        both = jnp.dot(
            jnp.concatenate(normed, axis=0), right_weight, preferred_element_type=f32
        )
        right_tri = (sigmoid(both[:, :wide]) * both[:, wide:]).astype(bf16).astype(f32)
        for row in range(rows):
            gates[row].append(gate_out[row * stride : (row + 1) * stride])
            for k in range(stride):
                at = row * stride + k
                sums[row][k % 2] += (
                    left_tri[at : at + 1] * right_tri[k * residues : (k + 1) * residues]
                )

    own_pair = jnp.concatenate([pair_one_ref[:, start + row] for row in range(rows)], axis=0)
    gate_out = jnp.concatenate(sum(gates, []), axis=0)
    products = []
    for row in range(rows):
        own_mask = keep_ref[pl.ds(start + row, 1), :][:, sequences : sequences + 1]
        products.append((sums[row][0] + sums[row][1]) * (mask * own_mask))
    product = jnp.concatenate(products, axis=0).astype(bf16).astype(f32)
    normed = layer_norm(product).astype(bf16)
    update = jnp.dot(normed, output_ref[...], preferred_element_type=f32)
    pair_two = (own_pair + gate_out * update).astype(bf16).astype(f32)
    ln_two = layer_norm(pair_two).astype(bf16)
    hidden = jnp.maximum(jnp.dot(ln_two, up_ref[...], preferred_element_type=f32), 0.0).astype(bf16)
    result = pair_two + jnp.dot(hidden, down_ref[...], preferred_element_type=f32)
    out_ref[...] = result.astype(bf16).reshape(rows, residues, wide)


def gather_all(packed):
    dap_count = lax.axis_size("dap")
    half = dap_count // 2
    far = lax.ppermute(packed[None], "dap", [(src, src ^ half) for src in range(dap_count)])
    both = jnp.concatenate([packed[None], far], axis=0)
    held = [both] + [
        lax.ppermute(both, "dap", [(src, src ^ offset) for src in range(dap_count)])
        for offset in swap_order(dap_count)
    ]
    sibling = [(0, 1), (1, 0)]
    first = lax.ppermute(both, "sub", sibling)
    early = lax.ppermute(jnp.concatenate(held[1:-1], axis=0), "sub", sibling)
    late = lax.ppermute(held[-1], "sub", sibling)
    return jnp.concatenate(held, axis=0), jnp.concatenate([first, early, late], axis=0)


def swap_order(dap_count):
    near = dap_count // 2
    return [1, near - 1] + list(range(2, near - 1))


def block_place(chip, chips):
    offset = lax.bitwise_xor(lax.axis_index("dap"), chip)
    half = chips // 2
    near = jnp.where(offset >= half, offset - half, offset)
    turn = jnp.where(near > 1, jnp.where(near == half - 1, 2, near + 1), near)
    return 2 * turn + jnp.where(offset >= half, 1, 0)


def shards_replicated(
    pairwise_state,
    alignment_state,
    alignment_mask,
    residue_crop_mask,
    outer_input_weight,
    outer_output_weight,
    triangle_input_weight,
    triangle_gate,
    triangle_output_weight,
    transition_up_weight,
    transition_down_weight,
):
    rows, residues, wide = pairwise_state.shape
    sequences = alignment_state.shape[0]
    channels = outer_input_weight.shape[2]
    vector = pl.BlockSpec(memory_space=pltpu.VMEM)
    params = pltpu.CompilerParams(vmem_limit_bytes=40 << 20)
    hbm = pl.BlockSpec(memory_space=pltpu.HBM)
    packed = pl.pallas_call(
        pack_kernel,
        out_shape=jax.ShapeDtypeStruct((rows * residues + sequences + 16, wide), jnp.bfloat16),
        in_specs=[hbm] * 5,
        out_specs=vector,
        scratch_shapes=[
            pltpu.SMEM((residues,), jnp.int32),
            pltpu.VMEM((rows, sequences), jnp.int32),
            pltpu.VMEM(alignment_state.shape, jnp.bfloat16),
            pltpu.VMEM((2, channels, alignment_state.shape[2]), jnp.bfloat16),
            pltpu.VMEM(alignment_state.shape, jnp.float32),
            pltpu.SemaphoreType.DMA((4 + rows,)),
        ],
        compiler_params=pltpu.CompilerParams(vmem_limit_bytes=8 << 20),
    )(
        *(
            pltpu.with_memory_space_constraint(array, pltpu.HBM)
            for array in (
                residue_crop_mask,
                alignment_mask.T,
                alignment_state,
                outer_input_weight.transpose(0, 2, 1),
                pairwise_state,
            )
        )
    )
    held, other = gather_all(packed)
    cores, chips = lax.axis_size("sub"), lax.axis_size("dap")
    group = cores * rows
    parts = 1
    return pl.pallas_call(
        update_kernel,
        out_shape=jax.ShapeDtypeStruct(pairwise_state.shape, jnp.bfloat16),
        in_specs=[vector] * 8,
        out_specs=vector,
        scratch_shapes=[
            pltpu.VMEM((parts, (channels // parts + 1) * 2 * channels, 2 * wide), jnp.bfloat16),
            pltpu.VMEM((residues, channels, wide), jnp.float32),
            pltpu.VMEM((2, group * sequences, chips * wide), jnp.bfloat16),
            pltpu.VMEM((residues, wide), jnp.float32),
            pltpu.VMEM((parts, chips * residues, channels // parts * wide // 2), jnp.bfloat16),
            pltpu.VMEM((parts, chips * residues, channels // parts * wide // 2), jnp.bfloat16),
            pltpu.VMEM((residues, residues, wide), jnp.float32),
            pltpu.VMEM((residues, residues, wide), jnp.float32),
            pltpu.VMEM((residues, residues, wide), jnp.float32),
        ],
        compiler_params=params,
    )(
        held,
        other,
        outer_output_weight,
        triangle_input_weight,
        triangle_gate,
        triangle_output_weight,
        transition_up_weight,
        transition_down_weight,
    )


def shards(
    pairwise_state,
    alignment_state,
    alignment_mask,
    residue_crop_mask,
    outer_input_weight,
    outer_output_weight,
    triangle_input_weight,
    triangle_gate,
    triangle_output_weight,
    transition_up_weight,
    transition_down_weight,
):
    row_count = pairwise_state.shape[0]
    start_row = lax.axis_index(("dap", "sub")) * row_count
    row_presence_mask = lax.dynamic_slice_in_dim(residue_crop_mask, start_row, row_count, 0).astype(
        jnp.float32
    )
    full_mask = residue_crop_mask.astype(jnp.float32)
    alignment_keep = alignment_mask.astype(jnp.float32) * row_presence_mask[None, :]
    alignment_normed = norm_layer(alignment_state.astype(jnp.float32), -1).astype(jnp.bfloat16)
    left_alignment = (
        jnp.einsum(
            "pxm,my->pxy",
            alignment_normed,
            outer_input_weight[0],
            preferred_element_type=jnp.float32,
        )
        * alignment_keep[:, :, None]
    ).astype(jnp.bfloat16)
    right_alignment = (
        jnp.einsum(
            "pxm,my->pxy",
            alignment_normed,
            outer_input_weight[1],
            preferred_element_type=jnp.float32,
        )
        * alignment_keep[:, :, None]
    ).astype(jnp.bfloat16)
    inner_alignment = jnp.einsum(
        "tqu,ulx->tqlx", left_alignment, outer_output_weight, preferred_element_type=jnp.float32
    ).astype(jnp.bfloat16)
    right_portion = lax.all_gather(right_alignment, ("dap", "sub"), axis=1, tiled=True)
    keep_portion = lax.all_gather(
        alignment_keep.astype(jnp.bfloat16), ("dap", "sub"), axis=1, tiled=True
    )
    numerator_sum = jnp.einsum(
        "zkwv,znw->knv", inner_alignment, right_portion, preferred_element_type=jnp.float32
    )
    pair_norm_count = jnp.einsum("cf,cg->fg", alignment_keep, keep_portion.astype(jnp.float32))
    block_part = numerator_sum / jnp.maximum(pair_norm_count, 1.0)[:, :, None]
    pair_one = (pairwise_state.astype(jnp.float32) + block_part).astype(jnp.bfloat16)
    ln_one = norm_layer(pair_one.astype(jnp.float32), -1).astype(jnp.bfloat16)
    pair_keep = row_presence_mask[:, None] * full_mask[None, :]

    def operand(gate_w, proj_w):
        gate_val = jnp.einsum("ijc,cd->dij", ln_one, gate_w, preferred_element_type=jnp.float32)
        proj_val = jnp.einsum("ijc,cd->dij", ln_one, proj_w, preferred_element_type=jnp.float32)
        return (jax.nn.sigmoid(gate_val) * proj_val * pair_keep[None]).astype(jnp.bfloat16)

    left_tri = operand(triangle_input_weight[0], triangle_input_weight[1])
    right_tri = operand(triangle_input_weight[2], triangle_input_weight[3])
    near_right = lax.all_gather(right_tri, "sub", axis=1, tiled=True)
    left_cols, right_all = (
        lax.all_to_all(left_tri, "dap", split_axis=0, concat_axis=1, tiled=True),
        lax.all_to_all(near_right, "dap", split_axis=0, concat_axis=1, tiled=True),
    )
    product = jnp.einsum(
        "cik,cjk->cij", left_cols, right_all, preferred_element_type=jnp.float32
    ).astype(jnp.bfloat16)
    returned = lax.all_to_all(product, "dap", split_axis=1, concat_axis=0, tiled=True)
    normed = norm_layer(returned.astype(jnp.float32), 0).astype(jnp.bfloat16)
    update = jnp.einsum(
        "cij,cd->ijd", normed, triangle_output_weight, preferred_element_type=jnp.float32
    )
    gate_out = jax.nn.sigmoid(
        jnp.einsum("ijc,cd->ijd", ln_one, triangle_gate, preferred_element_type=jnp.float32)
    )
    pair_two = (pair_one.astype(jnp.float32) + gate_out * update).astype(jnp.bfloat16)
    ln_two = norm_layer(pair_two.astype(jnp.float32), -1).astype(jnp.bfloat16)

    def step(row_pair):
        return transition(*row_pair, transition_up_weight, transition_down_weight)

    return lax.map(step, (ln_two, pair_two))


def solution(mesh):
    placed = (
        P(("crop", "dap", "sub"), None, None),
        P("crop", ("dap", "sub"), None),
        P("crop", ("dap", "sub")),
        P("crop"),
        P(),
        P(),
        P(),
        P(),
        P(),
        P(),
        P(),
    )

    small = mesh.shape["sub"] == 2 and mesh.shape["dap"] == 8

    def body(pairwise_state, *rest):
        residues, channels = pairwise_state.shape[1:]
        if small and residues * residues * channels * 2 <= REPLICATED_PAIR_BYTES:
            return shards_replicated(pairwise_state, *rest)
        return shards(pairwise_state, *rest)

    return jax.shard_map(
        body,
        mesh=mesh,
        in_specs=placed,
        out_specs=P(("crop", "dap", "sub"), None, None),
        check_vma=False,
    )
```

```python
import jax
import jax.numpy as jnp
from jax import lax
from jax.experimental import pallas as pl
from jax.experimental.pallas import tpu as pltpu
from jax.sharding import PartitionSpec as P

REPLICATED_PAIR_BYTES = 1 << 20


def norm_layer(values, reduce_axis):
    average = jnp.mean(values, axis=reduce_axis, keepdims=True)
    centered = values - average
    variance = jnp.mean(centered * centered, axis=reduce_axis, keepdims=True)
    return centered * lax.rsqrt(variance + 1e-05)


def transition(ln_two, pair_two, transition_up_weight, transition_down_weight):
    hidden = jax.nn.relu(
        jnp.dot(ln_two, transition_up_weight, preferred_element_type=jnp.float32)
    ).astype(jnp.bfloat16)
    return (
        pair_two.astype(jnp.float32)
        + jnp.dot(hidden, transition_down_weight, preferred_element_type=jnp.float32)
    ).astype(jnp.bfloat16)


def layer_norm(values):
    count = values.shape[-1]
    centered = values - jnp.sum(values, axis=-1, keepdims=True) * (1.0 / count)
    variance = jnp.sum(centered * centered, axis=-1, keepdims=True) * (1.0 / count)
    return centered * lax.rsqrt(variance + 1e-05)


def first_row(rows):
    return (lax.axis_index("dap") * lax.axis_size("sub") + lax.axis_index("sub")) * rows


def pack_kernel(
    mask_hbm,
    keep_hbm,
    state_hbm,
    weight_hbm,
    pair_hbm,
    out_ref,
    mask_ref,
    keep_ref,
    state_ref,
    weight_ref,
    wide_ref,
    sems,
):
    rows, residues, wide = pair_hbm.shape
    sequences = state_ref.shape[0]
    base = rows * residues
    start = first_row(rows)
    second_core = lax.axis_index("sub") == 1
    loads = [
        pltpu.make_async_copy(state_hbm, state_ref, sems.at[0]),
        pltpu.make_async_copy(weight_hbm, weight_ref, sems.at[1]),
        pltpu.make_async_copy(keep_hbm, keep_ref, sems.at[2]),
        pltpu.make_async_copy(mask_hbm, mask_ref, sems.at[3]),
    ] + [
        pltpu.make_async_copy(
            pair_hbm.at[row], out_ref.at[pl.ds(row * residues, residues)], sems.at[4 + row]
        )
        for row in range(rows)
    ]
    for load in loads:
        load.start()
    for load in loads[:4]:
        load.wait()
    f32, bf16 = jnp.float32, jnp.bfloat16
    wide_ref[...] = state_ref[...].astype(f32)
    eye = lax.broadcasted_iota(jnp.int32, (sequences, sequences), 0) == lax.broadcasted_iota(
        jnp.int32, (sequences, sequences), 1
    )
    last = (((1,), (1,)), ((), ()))
    weight = weight_ref[1]
    nothing = jnp.zeros_like(weight)
    here = jnp.where(second_core, nothing, weight), jnp.where(second_core, weight, nothing)
    keeps, fronts, backs = [], [], []
    projected = 0.0
    for row in range(rows):
        present = mask_ref[start + row].astype(f32)
        keep_row = keep_ref[row : row + 1].astype(f32) * present
        keep_column = jnp.sum(
            jnp.where(eye, jnp.broadcast_to(keep_row, eye.shape), 0.0), axis=1, keepdims=True
        )
        normed = (layer_norm(wide_ref[:, row]) * keep_column).astype(bf16)
        fronts.append(jnp.where(second_core, normed, jnp.zeros_like(normed)))
        backs.append(jnp.where(second_core, jnp.zeros_like(normed), normed))
        placed = [here[0] if at == row else here[1] if at == rows + row else nothing for at in range(2 * rows)]
        projected += lax.dot_general(
            normed, jnp.concatenate(placed, axis=0), last, preferred_element_type=f32
        )
        keeps.append(
            jnp.concatenate([keep_row, jnp.full((1, wide - sequences), present, f32)], axis=1)
        )
    projected += lax.dot_general(
        weight_ref[0], jnp.concatenate(fronts + backs, axis=0), last, preferred_element_type=f32
    )
    out_ref[base : base + sequences] = projected.astype(bf16)
    out_ref[base + sequences :] = jnp.concatenate(
        keeps + [jnp.zeros((16 - rows, wide), jnp.float32)], axis=0
    ).astype(jnp.bfloat16)
    for load in loads[4:]:
        load.wait()


def sigmoid(values):
    return 0.5 * jnp.tanh(0.5 * values) + 0.5


def update_kernel(
    held_ref,
    other_ref,
    outer_ref,
    triangle_ref,
    gate_ref,
    output_ref,
    up_ref,
    down_ref,
    out_ref,
    block_ref,
    left_ref,
    right_ref,
    keep_ref,
    first_ref,
    second_ref,
    pair_ref,
    pair_one_ref,
    ln_one_ref,
):
    rows, residues, wide = out_ref.shape
    cores, chips = 2, lax.axis_size("dap")
    channels = outer_ref.shape[0]
    sequences = channels
    base = rows * residues
    half = wide // 2
    group = cores * rows
    start = first_row(rows)
    second_core = lax.axis_index("sub") == 1
    bf16 = jnp.bfloat16
    f32 = jnp.float32

    parts = block_ref.shape[0]
    span = channels // parts
    nothing = jnp.zeros((channels, wide), bf16)
    for part in range(parts):
        for step in range(span + 1):
            weight = outer_ref[part * span + step % span]
            at = step * 2 * channels
            block_ref[part, at : at + channels, :wide] = weight
            block_ref[part, at : at + channels, wide:] = nothing
            block_ref[part, at + channels : at + 2 * channels, :wide] = nothing
            block_ref[part, at + channels : at + 2 * channels, wide:] = weight

    lane = lax.broadcasted_iota(jnp.int32, (channels, wide), 1)
    lane_block = lane // channels
    low = lane < half
    for chip in range(chips):
        place = block_place(chip, chips)
        mine, other = held_ref[place], other_ref[place]
        blocks = [jnp.where(second_core, other, mine), jnp.where(second_core, mine, other)]
        packed = [block[base : base + sequences].astype(f32) for block in blocks]
        right = jnp.where(low, packed[0], packed[1])
        for turn, value in enumerate((right, pltpu.roll(right, half, 1))):
            for copy in range(group):
                right_ref[
                    turn,
                    copy * sequences : (copy + 1) * sequences,
                    chip * wide : (chip + 1) * wide,
                ] = value.astype(bf16)
        for core in range(cores):
            residue = (chip * cores + core) * rows
            for row in range(rows):
                at = (rows if core == 0 else 0) + row
                left_ref[residue + row] = jnp.where(lane_block == at, packed[core], 0.0)
            keep_ref[residue : residue + rows] = blocks[core][base + sequences :].astype(f32)[:rows]
            pair_ref[residue : residue + rows] = (
                blocks[core][:base].astype(f32).reshape(rows, residues, wide)
            )

    last = (((1,), (1,)), ((), ()))
    keep = keep_ref[...]
    mask = jnp.broadcast_to(keep[:, sequences : sequences + 1], (residues, wide))
    counted = lax.broadcasted_iota(jnp.int32, (residues, wide), 1) < sequences
    count = lax.dot_general(
        jnp.where(counted, keep, 0.0).astype(bf16),
        keep.astype(bf16),
        last,
        preferred_element_type=f32,
    )
    inverse = 1.0 / jnp.maximum(count, 1.0)

    low = lax.broadcasted_iota(jnp.int32, (residues, wide), 1) < half
    totals = [0.0, 0.0]
    for part in range(parts):
        outer = []
        for turn in range(2):
            left = jnp.concatenate(
                [left_ref[:, d] for d in range(part * span + turn, (part + 1) * span, 2)], axis=0
            ).astype(bf16)
            outer.append(jnp.dot(left, right_ref[turn], preferred_element_type=f32).astype(bf16))

        def piece(turn, at, chip):
            return outer[turn][
                at * residues : (at + 1) * residues, chip * wide : (chip + 1) * wide
            ]

        for at in range(span // 2):
            follow = (at + 1) % (span // 2)
            for chip in range(chips):
                place = (
                    part,
                    slice(chip * residues, (chip + 1) * residues),
                    slice(at * wide, (at + 1) * wide),
                )
                first_ref[place] = jnp.where(low, piece(0, at, chip), piece(1, at, chip))
                second_ref[place] = jnp.where(low, piece(1, at, chip), piece(0, follow, chip))
        depth = span * 2 * channels
        totals[0] += jnp.dot(first_ref[part], block_ref[part, :depth], preferred_element_type=f32)
        totals[1] += jnp.dot(
            second_ref[part], block_ref[part, 2 * channels :], preferred_element_type=f32
        )

    right_weight = jnp.concatenate([triangle_ref[2], triangle_ref[3]], axis=1)
    right_tri = []
    stride = 8
    for first in range(0, residues, stride):
        normed = []
        for k in range(first, first + stride):
            chip, pick = k // group, k % group
            at = (pick % 2) * wide
            numerator = totals[pick // 2][chip * residues : (chip + 1) * residues, at : at + wide]
            opm = numerator * jnp.broadcast_to(inverse[:, k : k + 1], (residues, wide))
            pair_one = (pair_ref[:, k] + opm).astype(bf16).astype(f32)
            pair_one_ref[k] = pair_one
            ln_one = layer_norm(pair_one)
            ln_one_ref[k] = ln_one
            normed.append(ln_one.astype(bf16))
        both = jnp.dot(
            jnp.concatenate(normed, axis=0), right_weight, preferred_element_type=f32
        )
        right_tri.append((sigmoid(both[:, :wide]) * both[:, wide:]).astype(bf16).astype(f32))

    own_pair = jnp.concatenate([pair_one_ref[:, start + row] for row in range(rows)], axis=0)
    own_ln = jnp.concatenate([ln_one_ref[:, start + row] for row in range(rows)], axis=0).astype(bf16)
    left_weight = jnp.concatenate([triangle_ref[0], triangle_ref[1]], axis=1)
    both = jnp.dot(own_ln, left_weight, preferred_element_type=f32)
    left_tri = sigmoid(both[:, :wide]) * both[:, wide:] * jnp.concatenate([mask] * rows, axis=0)
    left_tri = left_tri.astype(bf16).astype(f32)
    products = []
    for row in range(rows):
        sums = [jnp.zeros((residues, wide), f32) for _ in range(4)]
        for k in range(residues):
            at = row * residues + k
            place = (k % stride) * residues
            sums[k % 4] += left_tri[at : at + 1] * right_tri[k // stride][place : place + residues]
        total = (sums[0] + sums[1]) + (sums[2] + sums[3])
        own_mask = keep_ref[pl.ds(start + row, 1), :][:, sequences : sequences + 1]
        products.append(total * (mask * own_mask))
    product = jnp.concatenate(products, axis=0).astype(bf16).astype(f32)
    normed = layer_norm(product).astype(bf16)
    update = jnp.dot(normed, output_ref[...], preferred_element_type=f32)
    gate_out = sigmoid(jnp.dot(own_ln, gate_ref[...], preferred_element_type=f32))
    pair_two = (own_pair + gate_out * update).astype(bf16).astype(f32)
    ln_two = layer_norm(pair_two).astype(bf16)
    hidden = jnp.maximum(jnp.dot(ln_two, up_ref[...], preferred_element_type=f32), 0.0).astype(bf16)
    result = pair_two + jnp.dot(hidden, down_ref[...], preferred_element_type=f32)
    out_ref[...] = result.astype(bf16).reshape(rows, residues, wide)


def gather_all(packed):
    dap_count = lax.axis_size("dap")
    half = dap_count // 2
    far = lax.ppermute(packed[None], "dap", [(src, src ^ half) for src in range(dap_count)])
    both = jnp.concatenate([packed[None], far], axis=0)
    held = [both] + [
        lax.ppermute(both, "dap", [(src, src ^ offset) for src in range(dap_count)])
        for offset in swap_order(dap_count)
    ]
    sibling = [(0, 1), (1, 0)]
    first = lax.ppermute(both, "sub", sibling)
    early = lax.ppermute(jnp.concatenate(held[1:-1], axis=0), "sub", sibling)
    late = lax.ppermute(held[-1], "sub", sibling)
    return jnp.concatenate(held, axis=0), jnp.concatenate([first, early, late], axis=0)


def swap_order(dap_count):
    near = dap_count // 2
    return list(range(2, near - 1)) + [near - 1, 1]


def block_place(chip, chips):
    offset = lax.bitwise_xor(lax.axis_index("dap"), chip)
    half = chips // 2
    near = jnp.where(offset >= half, offset - half, offset)
    turn = 0
    for place, one in enumerate(swap_order(chips)):
        turn = turn + jnp.where(near == one, place + 1, 0)
    return 2 * turn + jnp.where(offset >= half, 1, 0)


def shards_replicated(
    pairwise_state,
    alignment_state,
    alignment_mask,
    residue_crop_mask,
    outer_input_weight,
    outer_output_weight,
    triangle_input_weight,
    triangle_gate,
    triangle_output_weight,
    transition_up_weight,
    transition_down_weight,
):
    rows, residues, wide = pairwise_state.shape
    sequences = alignment_state.shape[0]
    channels = outer_input_weight.shape[2]
    vector = pl.BlockSpec(memory_space=pltpu.VMEM)
    params = pltpu.CompilerParams(vmem_limit_bytes=40 << 20)
    hbm = pl.BlockSpec(memory_space=pltpu.HBM)
    packed = pl.pallas_call(
        pack_kernel,
        out_shape=jax.ShapeDtypeStruct((rows * residues + sequences + 16, wide), jnp.bfloat16),
        in_specs=[hbm] * 5,
        out_specs=vector,
        scratch_shapes=[
            pltpu.SMEM((residues,), jnp.int32),
            pltpu.VMEM((rows, sequences), jnp.int32),
            pltpu.VMEM(alignment_state.shape, jnp.bfloat16),
            pltpu.VMEM((2, channels, alignment_state.shape[2]), jnp.bfloat16),
            pltpu.VMEM(alignment_state.shape, jnp.float32),
            pltpu.SemaphoreType.DMA((4 + rows,)),
        ],
        compiler_params=pltpu.CompilerParams(vmem_limit_bytes=8 << 20),
    )(
        *(
            pltpu.with_memory_space_constraint(array, pltpu.HBM)
            for array in (
                residue_crop_mask,
                alignment_mask.T,
                alignment_state,
                outer_input_weight.transpose(0, 2, 1),
                pairwise_state,
            )
        )
    )
    held, other = gather_all(packed)
    cores, chips = lax.axis_size("sub"), lax.axis_size("dap")
    group = cores * rows
    parts = 1
    return pl.pallas_call(
        update_kernel,
        out_shape=jax.ShapeDtypeStruct(pairwise_state.shape, jnp.bfloat16),
        in_specs=[vector] * 8,
        out_specs=vector,
        scratch_shapes=[
            pltpu.VMEM((parts, (channels // parts + 1) * 2 * channels, 2 * wide), jnp.bfloat16),
            pltpu.VMEM((residues, channels, wide), jnp.float32),
            pltpu.VMEM((2, group * sequences, chips * wide), jnp.bfloat16),
            pltpu.VMEM((residues, wide), jnp.float32),
            pltpu.VMEM((parts, chips * residues, channels // parts * wide // 2), jnp.bfloat16),
            pltpu.VMEM((parts, chips * residues, channels // parts * wide // 2), jnp.bfloat16),
            pltpu.VMEM((residues, residues, wide), jnp.float32),
            pltpu.VMEM((residues, residues, wide), jnp.float32),
            pltpu.VMEM((residues, residues, wide), jnp.float32),
        ],
        compiler_params=params,
    )(
        held,
        other,
        outer_output_weight,
        triangle_input_weight,
        triangle_gate,
        triangle_output_weight,
        transition_up_weight,
        transition_down_weight,
    )


def shards(
    pairwise_state,
    alignment_state,
    alignment_mask,
    residue_crop_mask,
    outer_input_weight,
    outer_output_weight,
    triangle_input_weight,
    triangle_gate,
    triangle_output_weight,
    transition_up_weight,
    transition_down_weight,
):
    row_count = pairwise_state.shape[0]
    start_row = lax.axis_index(("dap", "sub")) * row_count
    row_presence_mask = lax.dynamic_slice_in_dim(residue_crop_mask, start_row, row_count, 0).astype(
        jnp.float32
    )
    full_mask = residue_crop_mask.astype(jnp.float32)
    alignment_keep = alignment_mask.astype(jnp.float32) * row_presence_mask[None, :]
    alignment_normed = norm_layer(alignment_state.astype(jnp.float32), -1).astype(jnp.bfloat16)
    left_alignment = (
        jnp.einsum(
            "pxm,my->pxy",
            alignment_normed,
            outer_input_weight[0],
            preferred_element_type=jnp.float32,
        )
        * alignment_keep[:, :, None]
    ).astype(jnp.bfloat16)
    right_alignment = (
        jnp.einsum(
            "pxm,my->pxy",
            alignment_normed,
            outer_input_weight[1],
            preferred_element_type=jnp.float32,
        )
        * alignment_keep[:, :, None]
    ).astype(jnp.bfloat16)
    inner_alignment = jnp.einsum(
        "tqu,ulx->tqlx", left_alignment, outer_output_weight, preferred_element_type=jnp.float32
    ).astype(jnp.bfloat16)
    right_portion = lax.all_gather(right_alignment, ("dap", "sub"), axis=1, tiled=True)
    keep_portion = lax.all_gather(
        alignment_keep.astype(jnp.bfloat16), ("dap", "sub"), axis=1, tiled=True
    )
    numerator_sum = jnp.einsum(
        "zkwv,znw->knv", inner_alignment, right_portion, preferred_element_type=jnp.float32
    )
    pair_norm_count = jnp.einsum("cf,cg->fg", alignment_keep, keep_portion.astype(jnp.float32))
    block_part = numerator_sum / jnp.maximum(pair_norm_count, 1.0)[:, :, None]
    pair_one = (pairwise_state.astype(jnp.float32) + block_part).astype(jnp.bfloat16)
    ln_one = norm_layer(pair_one.astype(jnp.float32), -1).astype(jnp.bfloat16)
    pair_keep = row_presence_mask[:, None] * full_mask[None, :]

    def operand(gate_w, proj_w):
        gate_val = jnp.einsum("ijc,cd->dij", ln_one, gate_w, preferred_element_type=jnp.float32)
        proj_val = jnp.einsum("ijc,cd->dij", ln_one, proj_w, preferred_element_type=jnp.float32)
        return (jax.nn.sigmoid(gate_val) * proj_val * pair_keep[None]).astype(jnp.bfloat16)

    left_tri = operand(triangle_input_weight[0], triangle_input_weight[1])
    right_tri = operand(triangle_input_weight[2], triangle_input_weight[3])
    near_right = lax.all_gather(right_tri, "sub", axis=1, tiled=True)
    left_cols, right_all = (
        lax.all_to_all(left_tri, "dap", split_axis=0, concat_axis=1, tiled=True),
        lax.all_to_all(near_right, "dap", split_axis=0, concat_axis=1, tiled=True),
    )
    product = jnp.einsum(
        "cik,cjk->cij", left_cols, right_all, preferred_element_type=jnp.float32
    ).astype(jnp.bfloat16)
    returned = lax.all_to_all(product, "dap", split_axis=1, concat_axis=0, tiled=True)
    normed = norm_layer(returned.astype(jnp.float32), 0).astype(jnp.bfloat16)
    update = jnp.einsum(
        "cij,cd->ijd", normed, triangle_output_weight, preferred_element_type=jnp.float32
    )
    gate_out = jax.nn.sigmoid(
        jnp.einsum("ijc,cd->ijd", ln_one, triangle_gate, preferred_element_type=jnp.float32)
    )
    pair_two = (pair_one.astype(jnp.float32) + gate_out * update).astype(jnp.bfloat16)
    ln_two = norm_layer(pair_two.astype(jnp.float32), -1).astype(jnp.bfloat16)

    def step(row_pair):
        return transition(*row_pair, transition_up_weight, transition_down_weight)

    return lax.map(step, (ln_two, pair_two))


def solution(mesh):
    placed = (
        P(("crop", "dap", "sub"), None, None),
        P("crop", ("dap", "sub"), None),
        P("crop", ("dap", "sub")),
        P("crop"),
        P(),
        P(),
        P(),
        P(),
        P(),
        P(),
        P(),
    )

    small = mesh.shape["sub"] == 2 and mesh.shape["dap"] == 8

    def body(pairwise_state, *rest):
        residues, channels = pairwise_state.shape[1:]
        if small and residues * residues * channels * 2 <= REPLICATED_PAIR_BYTES:
            return shards_replicated(pairwise_state, *rest)
        return shards(pairwise_state, *rest)

    return jax.shard_map(
        body,
        mesh=mesh,
        in_specs=placed,
        out_specs=P(("crop", "dap", "sub"), None, None),
        check_vma=False,
    )
```

```python
import jax
import jax.numpy as jnp
from jax import lax
from jax.experimental import pallas as pl
from jax.experimental.pallas import tpu as pltpu
from jax.sharding import PartitionSpec as P

REPLICATED_PAIR_BYTES = 1 << 20


def norm_layer(values, reduce_axis):
    average = jnp.mean(values, axis=reduce_axis, keepdims=True)
    centered = values - average
    variance = jnp.mean(centered * centered, axis=reduce_axis, keepdims=True)
    return centered * lax.rsqrt(variance + 1e-05)


def transition(ln_two, pair_two, transition_up_weight, transition_down_weight):
    hidden = jax.nn.relu(
        jnp.dot(ln_two, transition_up_weight, preferred_element_type=jnp.float32)
    ).astype(jnp.bfloat16)
    return (
        pair_two.astype(jnp.float32)
        + jnp.dot(hidden, transition_down_weight, preferred_element_type=jnp.float32)
    ).astype(jnp.bfloat16)


def layer_norm(values):
    count = values.shape[-1]
    centered = values - jnp.sum(values, axis=-1, keepdims=True) * (1.0 / count)
    variance = jnp.sum(centered * centered, axis=-1, keepdims=True) * (1.0 / count)
    return centered * lax.rsqrt(variance + 1e-05)


def first_row(rows):
    return (lax.axis_index("dap") * lax.axis_size("sub") + lax.axis_index("sub")) * rows


def pack_kernel(
    mask_hbm,
    keep_hbm,
    state_hbm,
    weight_hbm,
    pair_hbm,
    out_ref,
    mask_ref,
    keep_ref,
    state_ref,
    weight_ref,
    wide_ref,
    sems,
):
    rows, residues, wide = pair_hbm.shape
    sequences = state_ref.shape[0]
    base = rows * residues
    start = first_row(rows)
    second_core = lax.axis_index("sub") == 1
    loads = [
        pltpu.make_async_copy(state_hbm, state_ref, sems.at[0]),
        pltpu.make_async_copy(weight_hbm, weight_ref, sems.at[1]),
        pltpu.make_async_copy(keep_hbm, keep_ref, sems.at[2]),
        pltpu.make_async_copy(mask_hbm, mask_ref, sems.at[3]),
    ] + [
        pltpu.make_async_copy(
            pair_hbm.at[row], out_ref.at[pl.ds(row * residues, residues)], sems.at[4 + row]
        )
        for row in range(rows)
    ]
    for load in loads:
        load.start()
    for load in loads[:4]:
        load.wait()
    f32, bf16 = jnp.float32, jnp.bfloat16
    wide_ref[...] = state_ref[...].astype(f32)
    eye = lax.broadcasted_iota(jnp.int32, (sequences, sequences), 0) == lax.broadcasted_iota(
        jnp.int32, (sequences, sequences), 1
    )
    last = (((1,), (1,)), ((), ()))
    weight = weight_ref[1]
    nothing = jnp.zeros_like(weight)
    here = jnp.where(second_core, nothing, weight), jnp.where(second_core, weight, nothing)
    keeps, fronts, backs = [], [], []
    projected = 0.0
    for row in range(rows):
        present = mask_ref[start + row].astype(f32)
        keep_row = keep_ref[row : row + 1].astype(f32) * present
        keep_column = jnp.sum(
            jnp.where(eye, jnp.broadcast_to(keep_row, eye.shape), 0.0), axis=1, keepdims=True
        )
        normed = (layer_norm(wide_ref[:, row]) * keep_column).astype(bf16)
        fronts.append(jnp.where(second_core, normed, jnp.zeros_like(normed)))
        backs.append(jnp.where(second_core, jnp.zeros_like(normed), normed))
        placed = [here[0] if at == row else here[1] if at == rows + row else nothing for at in range(2 * rows)]
        projected += lax.dot_general(
            normed, jnp.concatenate(placed, axis=0), last, preferred_element_type=f32
        )
        keeps.append(
            jnp.concatenate([keep_row, jnp.full((1, wide - sequences), present, f32)], axis=1)
        )
    projected += lax.dot_general(
        weight_ref[0], jnp.concatenate(fronts + backs, axis=0), last, preferred_element_type=f32
    )
    out_ref[base : base + sequences] = projected.astype(bf16)
    out_ref[base + sequences :] = jnp.concatenate(
        keeps + [jnp.zeros((16 - rows, wide), jnp.float32)], axis=0
    ).astype(jnp.bfloat16)
    for load in loads[4:]:
        load.wait()


def sigmoid(values):
    return 0.5 * jnp.tanh(0.5 * values) + 0.5


def update_kernel(
    held_ref,
    other_ref,
    outer_ref,
    triangle_ref,
    gate_ref,
    output_ref,
    up_ref,
    down_ref,
    out_ref,
    block_ref,
    left_ref,
    right_ref,
    keep_ref,
    first_ref,
    second_ref,
    pair_ref,
    pair_one_ref,
    ln_one_ref,
):
    rows, residues, wide = out_ref.shape
    cores, chips = 2, lax.axis_size("dap")
    channels = outer_ref.shape[0]
    sequences = channels
    base = rows * residues
    half = wide // 2
    group = cores * rows
    start = first_row(rows)
    second_core = lax.axis_index("sub") == 1
    bf16 = jnp.bfloat16
    f32 = jnp.float32

    parts = block_ref.shape[0]
    span = channels // parts
    nothing = jnp.zeros((channels, wide), bf16)
    for part in range(parts):
        for step in range(span + 1):
            weight = outer_ref[part * span + step % span]
            at = step * 2 * channels
            block_ref[part, at : at + channels, :wide] = weight
            block_ref[part, at : at + channels, wide:] = nothing
            block_ref[part, at + channels : at + 2 * channels, :wide] = nothing
            block_ref[part, at + channels : at + 2 * channels, wide:] = weight

    lane = lax.broadcasted_iota(jnp.int32, (channels, wide), 1)
    lane_block = lane // channels
    low = lane < half
    for chip in range(chips):
        place = block_place(chip, chips)
        mine, other = held_ref[place], other_ref[place]
        blocks = [jnp.where(second_core, other, mine), jnp.where(second_core, mine, other)]
        packed = [block[base : base + sequences].astype(f32) for block in blocks]
        right = jnp.where(low, packed[0], packed[1])
        for turn, value in enumerate((right, pltpu.roll(right, half, 1))):
            for copy in range(group):
                right_ref[
                    turn,
                    copy * sequences : (copy + 1) * sequences,
                    chip * wide : (chip + 1) * wide,
                ] = value.astype(bf16)
        for core in range(cores):
            residue = (chip * cores + core) * rows
            for row in range(rows):
                at = (rows if core == 0 else 0) + row
                left_ref[residue + row] = jnp.where(lane_block == at, packed[core], 0.0)
            keep_ref[residue : residue + rows] = blocks[core][base + sequences :].astype(f32)[:rows]
            pair_ref[residue : residue + rows] = (
                blocks[core][:base].astype(f32).reshape(rows, residues, wide)
            )

    last = (((1,), (1,)), ((), ()))
    keep = keep_ref[...]
    mask = jnp.broadcast_to(keep[:, sequences : sequences + 1], (residues, wide))
    counted = lax.broadcasted_iota(jnp.int32, (residues, wide), 1) < sequences
    count = lax.dot_general(
        jnp.where(counted, keep, 0.0).astype(bf16),
        keep.astype(bf16),
        last,
        preferred_element_type=f32,
    )
    inverse = 1.0 / jnp.maximum(count, 1.0)

    low = lax.broadcasted_iota(jnp.int32, (residues, wide), 1) < half
    totals = [0.0, 0.0]
    for part in range(parts):
        outer = []
        for turn in range(2):
            left = jnp.concatenate(
                [left_ref[:, d] for d in range(part * span + turn, (part + 1) * span, 2)], axis=0
            ).astype(bf16)
            outer.append(jnp.dot(left, right_ref[turn], preferred_element_type=f32).astype(bf16))

        def piece(turn, at, chip):
            return outer[turn][
                at * residues : (at + 1) * residues, chip * wide : (chip + 1) * wide
            ]

        for at in range(span // 2):
            follow = (at + 1) % (span // 2)
            for chip in range(chips):
                place = (
                    part,
                    slice(chip * residues, (chip + 1) * residues),
                    slice(at * wide, (at + 1) * wide),
                )
                first_ref[place] = jnp.where(low, piece(0, at, chip), piece(1, at, chip))
                second_ref[place] = jnp.where(low, piece(1, at, chip), piece(0, follow, chip))
        depth = span * 2 * channels
        totals[0] += jnp.dot(first_ref[part], block_ref[part, :depth], preferred_element_type=f32)
        totals[1] += jnp.dot(
            second_ref[part], block_ref[part, 2 * channels :], preferred_element_type=f32
        )

    right_weight = jnp.concatenate([triangle_ref[2], triangle_ref[3]], axis=1)
    right_tri = []
    stride = 8
    for first in range(0, residues, stride):
        normed = []
        for k in range(first, first + stride):
            chip, pick = k // group, k % group
            at = (pick % 2) * wide
            numerator = totals[pick // 2][chip * residues : (chip + 1) * residues, at : at + wide]
            opm = numerator * jnp.broadcast_to(inverse[:, k : k + 1], (residues, wide))
            pair_one = (pair_ref[:, k] + opm).astype(bf16).astype(f32)
            pair_one_ref[k] = pair_one
            ln_one = layer_norm(pair_one)
            ln_one_ref[k] = ln_one
            normed.append(ln_one.astype(bf16))
        both = jnp.dot(
            jnp.concatenate(normed, axis=0), right_weight, preferred_element_type=f32
        )
        right_tri.append((sigmoid(both[:, :wide]) * both[:, wide:]).astype(bf16).astype(f32))

    own_pair = jnp.concatenate([pair_one_ref[:, start + row] for row in range(rows)], axis=0)
    own_ln = jnp.concatenate([ln_one_ref[:, start + row] for row in range(rows)], axis=0).astype(bf16)
    left_weight = jnp.concatenate([triangle_ref[0], triangle_ref[1]], axis=1)
    both = jnp.dot(own_ln, left_weight, preferred_element_type=f32)
    left_tri = sigmoid(both[:, :wide]) * both[:, wide:] * jnp.concatenate([mask] * rows, axis=0)
    left_tri = left_tri.astype(bf16).astype(f32)
    products = []
    for row in range(rows):
        sums = [jnp.zeros((residues, wide), f32) for _ in range(4)]
        for k in range(residues):
            at = row * residues + k
            place = (k % stride) * residues
            sums[k % 4] += left_tri[at : at + 1] * right_tri[k // stride][place : place + residues]
        total = (sums[0] + sums[1]) + (sums[2] + sums[3])
        own_mask = keep_ref[pl.ds(start + row, 1), :][:, sequences : sequences + 1]
        products.append(total * (mask * own_mask))
    product = jnp.concatenate(products, axis=0).astype(bf16).astype(f32)
    normed = layer_norm(product).astype(bf16)
    update = jnp.dot(normed, output_ref[...], preferred_element_type=f32)
    gate_out = sigmoid(jnp.dot(own_ln, gate_ref[...], preferred_element_type=f32))
    pair_two = (own_pair + gate_out * update).astype(bf16).astype(f32)
    ln_two = layer_norm(pair_two).astype(bf16)
    hidden = jnp.maximum(jnp.dot(ln_two, up_ref[...], preferred_element_type=f32), 0.0).astype(bf16)
    result = pair_two + jnp.dot(hidden, down_ref[...], preferred_element_type=f32)
    out_ref[...] = result.astype(bf16).reshape(rows, residues, wide)


def gather_all(packed):
    dap_count = lax.axis_size("dap")
    half = dap_count // 2
    far = lax.ppermute(packed[None], "dap", [(src, src ^ half) for src in range(dap_count)])
    both = jnp.concatenate([packed[None], far], axis=0)
    held = [both] + [
        lax.ppermute(both, "dap", [(src, src ^ offset) for src in range(dap_count)])
        for offset in swap_order(dap_count)
    ]
    sibling = [(0, 1), (1, 0)]
    first = lax.ppermute(both, "sub", sibling)
    early = lax.ppermute(jnp.concatenate(held[1:-1], axis=0), "sub", sibling)
    late = lax.ppermute(held[-1], "sub", sibling)
    return jnp.concatenate(held, axis=0), jnp.concatenate([first, early, late], axis=0)


def swap_order(dap_count):
    near = dap_count // 2
    return [1, near - 1] + list(range(2, near - 1))


def block_place(chip, chips):
    offset = lax.bitwise_xor(lax.axis_index("dap"), chip)
    half = chips // 2
    near = jnp.where(offset >= half, offset - half, offset)
    turn = jnp.where(near > 1, jnp.where(near == half - 1, 2, near + 1), near)
    return 2 * turn + jnp.where(offset >= half, 1, 0)


def shards_replicated(
    pairwise_state,
    alignment_state,
    alignment_mask,
    residue_crop_mask,
    outer_input_weight,
    outer_output_weight,
    triangle_input_weight,
    triangle_gate,
    triangle_output_weight,
    transition_up_weight,
    transition_down_weight,
):
    rows, residues, wide = pairwise_state.shape
    sequences = alignment_state.shape[0]
    channels = outer_input_weight.shape[2]
    vector = pl.BlockSpec(memory_space=pltpu.VMEM)
    params = pltpu.CompilerParams(vmem_limit_bytes=40 << 20)
    hbm = pl.BlockSpec(memory_space=pltpu.HBM)
    packed = pl.pallas_call(
        pack_kernel,
        out_shape=jax.ShapeDtypeStruct((rows * residues + sequences + 16, wide), jnp.bfloat16),
        in_specs=[hbm] * 5,
        out_specs=vector,
        scratch_shapes=[
            pltpu.SMEM((residues,), jnp.int32),
            pltpu.VMEM((rows, sequences), jnp.int32),
            pltpu.VMEM(alignment_state.shape, jnp.bfloat16),
            pltpu.VMEM((2, channels, alignment_state.shape[2]), jnp.bfloat16),
            pltpu.VMEM(alignment_state.shape, jnp.float32),
            pltpu.SemaphoreType.DMA((4 + rows,)),
        ],
        compiler_params=pltpu.CompilerParams(vmem_limit_bytes=8 << 20),
    )(
        *(
            pltpu.with_memory_space_constraint(array, pltpu.HBM)
            for array in (
                residue_crop_mask,
                alignment_mask.T,
                alignment_state,
                outer_input_weight.transpose(0, 2, 1),
                pairwise_state,
            )
        )
    )
    held, other = gather_all(packed)
    cores, chips = lax.axis_size("sub"), lax.axis_size("dap")
    group = cores * rows
    parts = 2
    return pl.pallas_call(
        update_kernel,
        out_shape=jax.ShapeDtypeStruct(pairwise_state.shape, jnp.bfloat16),
        in_specs=[vector] * 8,
        out_specs=vector,
        scratch_shapes=[
            pltpu.VMEM((parts, (channels // parts + 1) * 2 * channels, 2 * wide), jnp.bfloat16),
            pltpu.VMEM((residues, channels, wide), jnp.float32),
            pltpu.VMEM((2, group * sequences, chips * wide), jnp.bfloat16),
            pltpu.VMEM((residues, wide), jnp.float32),
            pltpu.VMEM((parts, chips * residues, channels // parts * wide // 2), jnp.bfloat16),
            pltpu.VMEM((parts, chips * residues, channels // parts * wide // 2), jnp.bfloat16),
            pltpu.VMEM((residues, residues, wide), jnp.float32),
            pltpu.VMEM((residues, residues, wide), jnp.float32),
            pltpu.VMEM((residues, residues, wide), jnp.float32),
        ],
        compiler_params=params,
    )(
        held,
        other,
        outer_output_weight,
        triangle_input_weight,
        triangle_gate,
        triangle_output_weight,
        transition_up_weight,
        transition_down_weight,
    )


def shards(
    pairwise_state,
    alignment_state,
    alignment_mask,
    residue_crop_mask,
    outer_input_weight,
    outer_output_weight,
    triangle_input_weight,
    triangle_gate,
    triangle_output_weight,
    transition_up_weight,
    transition_down_weight,
):
    row_count = pairwise_state.shape[0]
    start_row = lax.axis_index(("dap", "sub")) * row_count
    row_presence_mask = lax.dynamic_slice_in_dim(residue_crop_mask, start_row, row_count, 0).astype(
        jnp.float32
    )
    full_mask = residue_crop_mask.astype(jnp.float32)
    alignment_keep = alignment_mask.astype(jnp.float32) * row_presence_mask[None, :]
    alignment_normed = norm_layer(alignment_state.astype(jnp.float32), -1).astype(jnp.bfloat16)
    left_alignment = (
        jnp.einsum(
            "pxm,my->pxy",
            alignment_normed,
            outer_input_weight[0],
            preferred_element_type=jnp.float32,
        )
        * alignment_keep[:, :, None]
    ).astype(jnp.bfloat16)
    right_alignment = (
        jnp.einsum(
            "pxm,my->pxy",
            alignment_normed,
            outer_input_weight[1],
            preferred_element_type=jnp.float32,
        )
        * alignment_keep[:, :, None]
    ).astype(jnp.bfloat16)
    inner_alignment = jnp.einsum(
        "tqu,ulx->tqlx", left_alignment, outer_output_weight, preferred_element_type=jnp.float32
    ).astype(jnp.bfloat16)
    right_portion = lax.all_gather(right_alignment, ("dap", "sub"), axis=1, tiled=True)
    keep_portion = lax.all_gather(
        alignment_keep.astype(jnp.bfloat16), ("dap", "sub"), axis=1, tiled=True
    )
    numerator_sum = jnp.einsum(
        "zkwv,znw->knv", inner_alignment, right_portion, preferred_element_type=jnp.float32
    )
    pair_norm_count = jnp.einsum("cf,cg->fg", alignment_keep, keep_portion.astype(jnp.float32))
    block_part = numerator_sum / jnp.maximum(pair_norm_count, 1.0)[:, :, None]
    pair_one = (pairwise_state.astype(jnp.float32) + block_part).astype(jnp.bfloat16)
    ln_one = norm_layer(pair_one.astype(jnp.float32), -1).astype(jnp.bfloat16)
    pair_keep = row_presence_mask[:, None] * full_mask[None, :]

    def operand(gate_w, proj_w):
        gate_val = jnp.einsum("ijc,cd->dij", ln_one, gate_w, preferred_element_type=jnp.float32)
        proj_val = jnp.einsum("ijc,cd->dij", ln_one, proj_w, preferred_element_type=jnp.float32)
        return (jax.nn.sigmoid(gate_val) * proj_val * pair_keep[None]).astype(jnp.bfloat16)

    left_tri = operand(triangle_input_weight[0], triangle_input_weight[1])
    right_tri = operand(triangle_input_weight[2], triangle_input_weight[3])
    near_right = lax.all_gather(right_tri, "sub", axis=1, tiled=True)
    left_cols, right_all = (
        lax.all_to_all(left_tri, "dap", split_axis=0, concat_axis=1, tiled=True),
        lax.all_to_all(near_right, "dap", split_axis=0, concat_axis=1, tiled=True),
    )
    product = jnp.einsum(
        "cik,cjk->cij", left_cols, right_all, preferred_element_type=jnp.float32
    ).astype(jnp.bfloat16)
    returned = lax.all_to_all(product, "dap", split_axis=1, concat_axis=0, tiled=True)
    normed = norm_layer(returned.astype(jnp.float32), 0).astype(jnp.bfloat16)
    update = jnp.einsum(
        "cij,cd->ijd", normed, triangle_output_weight, preferred_element_type=jnp.float32
    )
    gate_out = jax.nn.sigmoid(
        jnp.einsum("ijc,cd->ijd", ln_one, triangle_gate, preferred_element_type=jnp.float32)
    )
    pair_two = (pair_one.astype(jnp.float32) + gate_out * update).astype(jnp.bfloat16)
    ln_two = norm_layer(pair_two.astype(jnp.float32), -1).astype(jnp.bfloat16)

    def step(row_pair):
        return transition(*row_pair, transition_up_weight, transition_down_weight)

    return lax.map(step, (ln_two, pair_two))


def solution(mesh):
    placed = (
        P(("crop", "dap", "sub"), None, None),
        P("crop", ("dap", "sub"), None),
        P("crop", ("dap", "sub")),
        P("crop"),
        P(),
        P(),
        P(),
        P(),
        P(),
        P(),
        P(),
    )

    small = mesh.shape["sub"] == 2 and mesh.shape["dap"] == 8

    def body(pairwise_state, *rest):
        residues, channels = pairwise_state.shape[1:]
        if small and residues * residues * channels * 2 <= REPLICATED_PAIR_BYTES:
            return shards_replicated(pairwise_state, *rest)
        return shards(pairwise_state, *rest)

    return jax.shard_map(
        body,
        mesh=mesh,
        in_specs=placed,
        out_specs=P(("crop", "dap", "sub"), None, None),
        check_vma=False,
    )
```
